32 devices in a mesh: dp: 4 (over x, core), dap: 8 (over z, y).
Axes of the slice: x: 2, y: 2, z: 4, core: 2. Of those that a mesh axis runs over, the one named last changes fastest.
Arguments:
- pair_repr: bfloat16 [4, 32, 32, 128], P('dp', 'dap'), may hold values from -16 to 16
- pair_mask: int32 [4, 32, 32], P('dp', 'dap'), may hold values from 0 to 1, as said below
- cotangent: bfloat16 [4, 32, 32, 128], P('dp', 'dap'), may hold values from -6 to 6
- proj_weight: bfloat16 [2, 128, 640], replicated, may hold values from -0.5 to 0.5
- proj_bias: float32 [2, 640], replicated, may hold values from -3 to 3
- norm_gain: float32 [2, 256], replicated, may hold values from 0.1 to 1.9
- norm_shift: float32 [2, 256], replicated, may hold values from -3 to 3
- out_weight: bfloat16 [2, 128, 128], replicated, may hold values from -0.5 to 0.5
- out_bias: float32 [2, 128], replicated, may hold values from -3 to 3
Outputs:
- pair_grad: bfloat16 [4, 32, 32, 128], P('dp', 'dap')
- proj_weight_grad: float32 [2, 128, 640], replicated
- out_weight_grad: float32 [2, 128, 128], replicated
The draws below stay inside these ranges and needn't reach their ends.
Inputs may be any that keep to these rules, and one draw needn't show every extreme that they name: pair_mask[c, i, j] is 1 exactly when residues i and j both lie below crop c's length, which is at least 16 and below 32.
All inputs are finite; a program needn't handle non-finite values.
Results may differ from the reference program's by a relative error of at most 0.015.
Values may be sent and summed in bfloat16 or wider, within the bound.
No kernel may reach another device: no remote copies, remote signals or barrier semaphores. Data moves between devices by JAX's collectives and lax.ppermute only.
A program may use at most 64 MiB of HBM per device.

```python
import math
import jax
import jax.numpy as jnp
from jax import lax

C = 128
CH = 128
N = 32
CROPS = 4


def draw_pair_repr(key, part):
    key = jax.random.fold_in(key, 5)
    key_base, key_scale = jax.random.split(key, 2)
    cell_scale = jnp.exp(jax.random.uniform(key_scale, (CROPS, N, N, 1), jnp.float32, math.log(0.5), math.log(4.0)))
    values = jnp.clip(jax.random.normal(key_base, (CROPS, N, N, C), jnp.float32), -4.0, 4.0) * cell_scale
    return values.astype(jnp.bfloat16)


def draw_pair_mask(key, part):
    key = jax.random.fold_in(key, 11)
    lengths = jax.random.randint(key, (CROPS,), N // 2, N)
    positions = jnp.arange(N, dtype=jnp.int32)
    residue_valid = positions[None, :] < lengths[:, None]
    both_valid = residue_valid[:, :, None] & residue_valid[:, None, :]
    return both_valid.astype(jnp.int32)


def block_levels(own_key, shape, shards, least, high):
    level = 1.0
    for position, parts in shards:
        draws = jax.random.uniform(jax.random.fold_in(jax.random.fold_in(own_key, 6), position), (parts,), jnp.float32, least / len(shards), high / len(shards))
        level = level * jnp.repeat(jnp.exp(draws), shape[position] // parts).reshape((-1,) + (1,) * (len(shape) - 1 - position))
    return level


def bell_draw(key, extent, width, reach, shards=(), held_as=jnp.bfloat16):
    array = width * jax.random.normal(key, extent, jnp.float32)
    if shards:
        array = array * block_levels(key, extent, shards, -0.22, 0.18)
    return jnp.clip(array, -reach, reach).astype(held_as)


def setup_inputs(seed: int = 0) -> dict:
    key_list = jax.random.split(jax.random.key(seed), 10)
    pair_repr = draw_pair_repr(jax.random.fold_in(key_list[9], 71), 0)
    pair_mask = draw_pair_mask(jax.random.fold_in(key_list[9], 71), 0)
    cotangent = bell_draw(key_list[2], (CROPS, N, N, C), 1.0, 6.0, ((0, 4), (1, 8)))
    proj_weight = bell_draw(key_list[3], (2, C, 4 * CH + C), C ** -0.5, 0.5)
    proj_bias = bell_draw(key_list[4], (2, 4 * CH + C), 0.5, 3.0, (), jnp.float32)
    norm_gain = jnp.clip(1.0 + 0.18 * jax.random.normal(key_list[5], (2, C + CH), jnp.float32), 0.1, 1.9)
    norm_shift = bell_draw(key_list[6], (2, C + CH), 0.5, 3.0, (), jnp.float32)
    out_weight = bell_draw(key_list[7], (2, CH, C), CH ** -0.5, 0.5)
    out_bias = bell_draw(key_list[8], (2, C), 0.5, 3.0, (), jnp.float32)
    return {"pair_repr": pair_repr, "pair_mask": pair_mask, "cotangent": cotangent, "proj_weight": proj_weight, "proj_bias": proj_bias, "norm_gain": norm_gain, "norm_shift": norm_shift, "out_weight": out_weight, "out_bias": out_bias}


NORM_EPSILON = 1e-05

def layer_norm(values, gain_vec, shift_vec, norm_axis):
    mean_value = lax.optimization_barrier(jnp.mean(values, axis=norm_axis, keepdims=True))
    centred = values - mean_value
    variance = lax.optimization_barrier(jnp.mean(centred * centred, axis=norm_axis, keepdims=True))
    return centred * lax.rsqrt(variance + NORM_EPSILON) * gain_vec + shift_vec

def norm_pullback(values, gain_vec, shift_vec, norm_axis, upstream):
    _, pull_back = jax.vjp(lambda inner_value: layer_norm(inner_value, gain_vec, shift_vec, norm_axis), values)
    return pull_back(upstream)[0]

def edge_pair(edge_pre, cell_mask):
    left_edge = jax.nn.sigmoid(edge_pre[1]) * edge_pre[0] * cell_mask
    right_edge = jax.nn.sigmoid(edge_pre[3]) * edge_pre[2] * cell_mask
    return jnp.stack([left_edge, right_edge]).astype(jnp.bfloat16)

def edge_pullback(edge_pre, cell_mask, grad_pair):
    sig_left = jax.nn.sigmoid(edge_pre[1])
    sig_right = jax.nn.sigmoid(edge_pre[3])
    grad_left = grad_pair[0].astype(jnp.float32) * cell_mask
    grad_right = grad_pair[1].astype(jnp.float32) * cell_mask
    return jnp.stack([grad_left * sig_left, grad_left * edge_pre[0] * sig_left * (1.0 - sig_left), grad_right * sig_right, grad_right * edge_pre[2] * sig_right * (1.0 - sig_right)]).astype(jnp.bfloat16)

def triangle(pair_edges, outgoing):
    left_edge = pair_edges[0].astype(jnp.float32)
    right_edge = pair_edges[1].astype(jnp.float32)
    if outgoing:
        return jnp.einsum('cik,cjk->cij', left_edge, right_edge).astype(jnp.bfloat16)
    return jnp.einsum('cki,ckj->cij', left_edge, right_edge).astype(jnp.bfloat16)

def triangle_pullback(pair_edges, grad_product, outgoing):
    left_edge = pair_edges[0].astype(jnp.float32)
    right_edge = pair_edges[1].astype(jnp.float32)
    grad_prod = grad_product.astype(jnp.float32)
    if outgoing:
        grad_left = jnp.einsum('cij,cjk->cik', grad_prod, right_edge)
        grad_right = jnp.einsum('cij,cik->cjk', grad_prod, left_edge)
    else:
        grad_left = jnp.einsum('ckj,cij->cki', right_edge, grad_prod)
        grad_right = jnp.einsum('cki,cij->ckj', left_edge, grad_prod)
    return jnp.stack([grad_left, grad_right]).astype(jnp.bfloat16)

def crop_pass(crop_pair, crop_mask, crop_cot, proj_weight, proj_bias, norm_gain, norm_shift, out_weight, out_bias):
    cell_mask = crop_mask.astype(jnp.float32)
    pair_state = crop_pair
    records = []
    for update in range(2):
        w_edge = proj_weight[update, :, :4 * CH].reshape(C, 4, CH).astype(jnp.float32)
        w_gate = proj_weight[update, :, 4 * CH:].astype(jnp.float32)
        state_f = pair_state.astype(jnp.float32)
        normed = layer_norm(state_f, norm_gain[update, :C], norm_shift[update, :C], -1).astype(jnp.bfloat16)
        normed_f = normed.astype(jnp.float32)
        edge_pre = jnp.einsum('rnc,cgh->ghrn', normed_f, w_edge) + proj_bias[update, :4 * CH].reshape(4, CH, 1, 1)
        gate_pre = jnp.einsum('rnc,cd->rnd', normed_f, w_gate) + proj_bias[update, 4 * CH:]
        pair_edges = edge_pair(edge_pre, cell_mask)
        product = triangle(pair_edges, update == 0)
        mixed_norm = layer_norm(product.astype(jnp.float32), norm_gain[update, C:][:, None, None], norm_shift[update, C:][:, None, None], 0).astype(jnp.bfloat16)
        branch = jnp.einsum('hrn,hd->rnd', mixed_norm.astype(jnp.float32), out_weight[update].astype(jnp.float32)) + out_bias[update]
        records.append((state_f, normed, edge_pre, gate_pre, pair_edges, product, mixed_norm, branch))
        pair_state = (state_f + jax.nn.sigmoid(gate_pre) * branch).astype(jnp.bfloat16)
    upstream = crop_cot.astype(jnp.float32)
    proj_grads = []
    out_grads = []
    for update in (1, 0):
        state_f, normed, edge_pre, gate_pre, pair_edges, product, mixed_norm, branch = records[update]
        w_edge = proj_weight[update, :, :4 * CH].reshape(C, 4, CH).astype(jnp.float32)
        w_gate = proj_weight[update, :, 4 * CH:].astype(jnp.float32)
        gate_value = jax.nn.sigmoid(gate_pre)
        grad_branch = (upstream * gate_value).astype(jnp.bfloat16)
        grad_gate = (upstream * branch * gate_value * (1.0 - gate_value)).astype(jnp.bfloat16)
        out_grad = jnp.einsum('hrn,rnd->hd', mixed_norm.astype(jnp.float32), grad_branch.astype(jnp.float32))
        grad_mixed = jnp.einsum('rnd,hd->hrn', grad_branch.astype(jnp.float32), out_weight[update].astype(jnp.float32))
        grad_product = norm_pullback(product.astype(jnp.float32), norm_gain[update, C:][:, None, None], norm_shift[update, C:][:, None, None], 0, grad_mixed).astype(jnp.bfloat16)
        grad_pair = triangle_pullback(pair_edges, grad_product, update == 0)
        grad_edge = edge_pullback(edge_pre, cell_mask, grad_pair).astype(jnp.float32)
        normed_f = normed.astype(jnp.float32)
        grad_gate_f = grad_gate.astype(jnp.float32)
        edge_grad = jnp.einsum('rnc,ghrn->cgh', normed_f, grad_edge).reshape(C, 4 * CH)
        gate_grad = jnp.einsum('rnc,rnd->cd', normed_f, grad_gate_f)
        grad_normed = jnp.einsum('ghrn,cgh->rnc', grad_edge, w_edge) + jnp.einsum('rnd,cd->rnc', grad_gate_f, w_gate)
        upstream = upstream + norm_pullback(state_f, norm_gain[update, :C], norm_shift[update, :C], -1, grad_normed)
        proj_grads.append(jnp.concatenate([edge_grad, gate_grad], axis=1))
        out_grads.append(out_grad)
    return (upstream.astype(jnp.bfloat16), jnp.stack(proj_grads[::-1]), jnp.stack(out_grads[::-1]))

def reference(pair_repr, pair_mask, cotangent, proj_weight, proj_bias, norm_gain, norm_shift, out_weight, out_bias):

    def one_crop(carry, crop_inputs):
        crop_pair, crop_mask, crop_cot = crop_inputs
        crop_grad, proj_part, out_part = crop_pass(crop_pair, crop_mask, crop_cot, proj_weight, proj_bias, norm_gain, norm_shift, out_weight, out_bias)
        return ((carry[0] + proj_part, carry[1] + out_part), crop_grad)
    start = (jnp.zeros((2, C, 4 * CH + C), jnp.float32), jnp.zeros((2, CH, C), jnp.float32))
    totals, pair_grad = lax.scan(one_crop, start, (pair_repr, pair_mask, cotangent))
    return (pair_grad, totals[0], totals[1])
```

```python
import functools

import jax
import jax.numpy as jnp
from jax import lax
from jax.experimental import pallas as pl
from jax.experimental.pallas import tpu as pltpu
from jax.sharding import PartitionSpec as P

NORM_EPSILON = 1e-05
VMEM_BYTES = 48 * 1024 * 1024
CROP_BUDGET = 32 * 1024 * 1024
BLOCK_ROWS = 8
F32 = jnp.float32
BF16 = jnp.bfloat16


def sigmoid(x):
    return 0.5 * jnp.tanh(0.5 * x) + 0.5


def dot(a, b, dims=((1,), (0,))):
    return lax.dot_general(a, b, (dims, ((), ())), preferred_element_type=F32)


def norm_parts(x):
    centred = x - jnp.mean(x, axis=-1, keepdims=True)
    rstd = lax.rsqrt(jnp.mean(centred * centred, axis=-1, keepdims=True) + NORM_EPSILON)
    return centred * rstd, rstd


def norm_vjp(x_hat, rstd, grad):
    mean_grad = jnp.mean(grad, axis=-1, keepdims=True)
    mean_prod = jnp.mean(grad * x_hat, axis=-1, keepdims=True)
    return rstd * (grad - mean_grad - x_hat * mean_prod)


def pair_mask_block(length, first_row, rows, n, lanes):
    shape = (rows, n, lanes)
    i = lax.broadcasted_iota(jnp.int32, shape, 0) + first_row
    j = lax.broadcasted_iota(jnp.int32, shape, 1)
    inside = jnp.where((i < length) & (j < length), 1.0, 0.0)
    return inside.reshape(rows * n, lanes)


def project(x, mask, u, w, b, gain, shift):
    c = x.shape[1]
    x_hat, rstd = norm_parts(x)
    normed = (x_hat * gain[u : u + 1, :c] + shift[u : u + 1, :c]).astype(BF16)
    pre = dot(normed, w[u]) + b[u : u + 1, :]
    h = (pre.shape[1] - c) // 4
    s_left = sigmoid(pre[:, h : 2 * h]) * mask
    s_right = sigmoid(pre[:, 3 * h : 4 * h]) * mask
    left = s_left * pre[:, :h]
    right = s_right * pre[:, 2 * h : 3 * h]
    gate = sigmoid(pre[:, 4 * h :])
    return x_hat, rstd, normed, s_left, s_right, left, right, gate


def mix(product, u, c, gain, shift, w_out, b_out):
    p_hat, p_rstd = norm_parts(product.astype(F32))
    mixed = (p_hat * gain[u : u + 1, c:] + shift[u : u + 1, c:]).astype(BF16)
    branch = dot(mixed, w_out[u]) + b_out[u : u + 1, :]
    return p_hat, p_rstd, mixed, branch


def unmix(up, gate, branch, p_hat, p_rstd, u, c, gain, w_out):
    d_branch = up * gate
    d_gate = (d_branch * branch * (1.0 - gate)).astype(BF16)
    d_branch = d_branch.astype(BF16)
    d_mixed = dot(d_branch, w_out[u], ((1,), (1,))) * gain[u : u + 1, c:]
    return d_branch, d_gate, norm_vjp(p_hat, p_rstd, d_mixed)


def contract(n, first, row_of, x, y):
    lanes = y.shape[1]

    def step(e, totals):
        block = y[pl.ds(pl.multiple_of(e * n, n), n), :]
        return tuple(
            totals[a] + x[pl.ds(row_of(first + a, e), 1), :] * block for a in range(BLOCK_ROWS)
        )

    zero = jnp.zeros((n, lanes), F32)
    totals = lax.fori_loop(0, n, step, (zero,) * BLOCK_ROWS, unroll=4)
    return totals


def edge_grads(d_left, d_right, s_left, s_right, left, right):
    return (
        (d_left * s_left).astype(BF16),
        (d_left * left * (1.0 - s_left)).astype(BF16),
        (d_right * s_right).astype(BF16),
        (d_right * right * (1.0 - s_right)).astype(BF16),
    )


def crop_length(state_ref, cells):
    return jnp.max(state_ref[:, cells:, :].astype(F32)).astype(jnp.int32)


def forward_first(
    n, state_ref, w, b, gain, shift, w_out, b_out, next_ref, product_ref, left_s, right_s, gate_s
):
    parts, cells, c = state_ref.shape
    rows = n // parts
    cells = rows * n
    length = crop_length(state_ref, cells)

    @pl.loop(0, parts)
    def _(t):
        x = state_ref[t, :cells, :].astype(F32)
        mask = pair_mask_block(length, t * rows, rows, n, c)
        _, _, _, _, _, left, right, gate = project(x, mask, 0, w, b, gain, shift)
        here = pl.ds(pl.multiple_of(t * cells, cells), cells)
        left_s[here, :] = left
        gate_s[here, :] = gate
        for r in range(rows):
            right_s[pl.ds(t * rows + r, n, stride=n), :] = right[r * n : (r + 1) * n]

    @pl.loop(0, n // BLOCK_ROWS)
    def _(t):
        totals = contract(n, t * BLOCK_ROWS, lambda i, k: i * n + k, left_s, right_s)
        here = pl.ds(pl.multiple_of(t * BLOCK_ROWS * n, BLOCK_ROWS * n), BLOCK_ROWS * n)
        product = jnp.concatenate(totals, axis=0).astype(BF16)
        product_ref[here, :] = product
        _, _, _, branch = mix(product, 0, c, gain, shift, w_out, b_out)
        per = BLOCK_ROWS // rows
        x = jnp.concatenate([state_ref[t * per + q, :cells, :] for q in range(per)], axis=0)
        next_ref[here, :] = (x.astype(F32) + gate_s[here, :] * branch).astype(BF16)


def weight_grads(index_ref, normed_s, d_pre_s, mixed_s, d_branch_s, grad_s, slice_ref):
    part = slice_ref.shape[0]
    width = d_pre_s.shape[1]
    grad_s[:, :width] = dot(normed_s[...], d_pre_s[...], ((0,), (0,)))
    grad_s[:, width:] = dot(mixed_s[...], d_branch_s[...], ((0,), (0,)))
    own = pl.ds(pl.multiple_of(index_ref[0] * part, part), part)
    slice_ref[...] = grad_s[own, :].astype(BF16)


def update_second(
    n,
    index_ref,
    state_ref,
    next_ref,
    cot_ref,
    w,
    b,
    gain,
    shift,
    w_out,
    b_out,
    up_ref,
    slice_ref,
    left_s,
    right_s,
    s_left_s,
    s_right_s,
    gate_s,
    hat_s,
    rstd_s,
    d_product_s,
    d_product_t_s,
    normed_s,
    mixed_s,
    d_branch_s,
    d_pre_s,
    grad_s,
):
    parts, _, c = state_ref.shape
    rows = n // parts
    cells = rows * n
    h = left_s.shape[1]
    length = crop_length(state_ref, cells)

    @pl.loop(0, parts)
    def _(t):
        here = pl.ds(pl.multiple_of(t * cells, cells), cells)
        x = next_ref[here, :].astype(F32)
        mask = pair_mask_block(length, t * rows, rows, n, c)
        x_hat, rstd, normed, s_left, s_right, left, right, gate = project(
            x, mask, 1, w, b, gain, shift
        )
        left_s[here, :] = left
        right_s[here, :] = right
        s_left_s[here, :] = s_left
        s_right_s[here, :] = s_right
        gate_s[here, :] = gate
        hat_s[here, :] = x_hat
        rstd_s[here, :] = jnp.broadcast_to(rstd, x_hat.shape)
        normed_s[here, :] = normed

    per = BLOCK_ROWS // rows

    @pl.loop(0, n // BLOCK_ROWS)
    def _(t):
        totals = contract(n, t * BLOCK_ROWS, lambda i, k: k * n + i, left_s, right_s)
        here = pl.ds(pl.multiple_of(t * BLOCK_ROWS * n, BLOCK_ROWS * n), BLOCK_ROWS * n)
        product = jnp.concatenate(totals, axis=0).astype(BF16)
        p_hat, p_rstd, mixed, branch = mix(product, 1, c, gain, shift, w_out, b_out)
        up = jnp.concatenate([cot_ref[t * per + q] for q in range(per)], axis=0).astype(F32)
        d_branch, d_gate, d_product = unmix(
            up, gate_s[here, :], branch, p_hat, p_rstd, 1, c, gain, w_out
        )
        mixed_s[here, :] = mixed
        d_branch_s[here, :] = d_branch
        d_pre_s[here, 4 * h :] = d_gate
        d_product_s[here, :] = d_product
        for r in range(BLOCK_ROWS):
            d_product_t_s[pl.ds(t * BLOCK_ROWS + r, n, stride=n), :] = d_product[
                r * n : (r + 1) * n
            ]

    @pl.loop(0, n // BLOCK_ROWS)
    def _(t):
        first = t * BLOCK_ROWS
        here = pl.ds(pl.multiple_of(first * n, BLOCK_ROWS * n), BLOCK_ROWS * n)
        d_left = jnp.concatenate(
            contract(n, first, lambda k, j: k * n + j, right_s, d_product_t_s), axis=0
        )
        d_right = jnp.concatenate(
            contract(n, first, lambda k, i: k * n + i, left_s, d_product_s), axis=0
        )
        grads = edge_grads(
            d_left, d_right, s_left_s[here, :], s_right_s[here, :], left_s[here, :], right_s[here, :]
        )
        for g in range(4):
            d_pre_s[here, g * h : (g + 1) * h] = grads[g]
        d_normed = dot(d_pre_s[here, :], w[1], ((1,), (1,))) * gain[1:2, :c]
        up = jnp.concatenate([cot_ref[t * per + q] for q in range(per)], axis=0).astype(F32)
        up_ref[here, :] = up + norm_vjp(hat_s[here, :], rstd_s[here, :], d_normed)

    weight_grads(index_ref, normed_s, d_pre_s, mixed_s, d_branch_s, grad_s, slice_ref)


def backward_first(
    n,
    index_ref,
    state_ref,
    product_ref,
    up_ref,
    w,
    b,
    gain,
    shift,
    w_out,
    b_out,
    out_ref,
    slice_ref,
    left_s,
    right_s,
    s_left_s,
    s_right_s,
    hat_s,
    rstd_s,
    d_product_s,
    normed_s,
    mixed_s,
    d_branch_s,
    d_pre_s,
    grad_s,
):
    parts, _, c = state_ref.shape
    rows = n // parts
    cells = rows * n
    h = left_s.shape[1]
    length = crop_length(state_ref, cells)

    @pl.loop(0, parts)
    def _(t):
        here = pl.ds(pl.multiple_of(t * cells, cells), cells)
        x = state_ref[t, :cells, :].astype(F32)
        mask = pair_mask_block(length, t * rows, rows, n, c)
        x_hat, rstd, normed, s_left, s_right, left, right, gate = project(
            x, mask, 0, w, b, gain, shift
        )
        left_s[here, :] = left
        right_s[here, :] = right
        s_left_s[here, :] = s_left
        s_right_s[here, :] = s_right
        hat_s[here, :] = x_hat
        rstd_s[here, :] = jnp.broadcast_to(rstd, x_hat.shape)
        normed_s[here, :] = normed
        p_hat, p_rstd, mixed, branch = mix(
            product_ref[here, :], 0, c, gain, shift, w_out, b_out
        )
        d_branch, d_gate, d_product = unmix(
            up_ref[here, :], gate, branch, p_hat, p_rstd, 0, c, gain, w_out
        )
        mixed_s[here, :] = mixed
        d_branch_s[here, :] = d_branch
        d_pre_s[here, 4 * h :] = d_gate
        d_product_s[here, :] = d_product

    @pl.loop(0, n // BLOCK_ROWS)
    def _(t):
        first = t * BLOCK_ROWS
        here = pl.ds(pl.multiple_of(first * n, BLOCK_ROWS * n), BLOCK_ROWS * n)
        d_left = jnp.concatenate(
            contract(n, first, lambda i, j: i * n + j, d_product_s, right_s), axis=0
        )
        d_right = jnp.concatenate(
            contract(n, first, lambda j, i: i * n + j, d_product_s, left_s), axis=0
        )
        grads = edge_grads(
            d_left, d_right, s_left_s[here, :], s_right_s[here, :], left_s[here, :], right_s[here, :]
        )
        for g in range(4):
            d_pre_s[here, g * h : (g + 1) * h] = grads[g]

    own = pl.ds(pl.multiple_of(index_ref[0] * cells, cells), cells)
    d_normed = dot(d_pre_s[own, :], w[0], ((1,), (1,))) * gain[0:1, :c]
    out_ref[...] = (
        up_ref[own, :] + norm_vjp(hat_s[own, :], rstd_s[own, :], d_normed)
    ).astype(BF16)
    weight_grads(index_ref, normed_s, d_pre_s, mixed_s, d_branch_s, grad_s, slice_ref)


def gather_rows(value, axis, size):
    spread = jnp.broadcast_to(value[None], (size,) + value.shape)
    return lax.all_to_all(spread, axis, split_axis=0, concat_axis=0, tiled=True)


def gather_doubling(value, axis, size):
    me = lax.axis_index(axis)
    held = value[None]
    step = 1
    while step < size:
        other = lax.ppermute(held, axis, [(d, d ^ step) for d in range(size)])
        low = (me & step) == 0
        held = jnp.concatenate(
            [jnp.where(low, held, other), jnp.where(low, other, held)], axis=0
        )
        step *= 2
    return held


def sum_exchange(value, axis, size):
    total = value.astype(F32)
    for shift in range(1, size):
        total = total + lax.ppermute(
            value, axis, [(d, (d + shift) % size) for d in range(size)]
        ).astype(F32)
    return total


def crop_shards(
    groups,
    parts,
    pair_repr,
    pair_mask,
    cotangent,
    proj_weight,
    proj_bias,
    norm_gain,
    norm_shift,
    out_weight,
    out_bias,
):
    _, rows, n, c = pair_repr.shape
    h = out_weight.shape[1]
    width = proj_weight.shape[2]
    cells, pairs = rows * n, n * n
    part = c // parts
    plane = pltpu.VMEM((pairs, h), F32)
    narrow = pltpu.VMEM((pairs, h), BF16)
    wide = pltpu.VMEM((pairs, width), BF16)
    grads = pltpu.VMEM((c, width + c), F32)
    vmem = pl.BlockSpec(memory_space=pltpu.VMEM)
    smem = pl.BlockSpec(memory_space=pltpu.SMEM)
    params = pltpu.CompilerParams(vmem_limit_bytes=VMEM_BYTES)
    weights = (proj_weight, proj_bias, norm_gain, norm_shift, out_weight, out_bias)

    index = lax.axis_index("dap").astype(jnp.int32)[None]
    length = jnp.max(jnp.sum(pair_mask[0], axis=1)).astype(BF16)
    sent = jnp.concatenate(
        [pair_repr.reshape(cells, c), jnp.full((16, c), length, BF16)], axis=0
    )
    state = gather_rows(sent, "dap", parts)
    cot = lax.all_gather(cotangent.reshape(cells, c), "dap")

    state_1, product_0 = pl.pallas_call(
        functools.partial(forward_first, n),
        out_shape=(
            jax.ShapeDtypeStruct((pairs, c), BF16),
            jax.ShapeDtypeStruct((pairs, h), BF16),
        ),
        in_specs=[vmem] * 7,
        out_specs=(vmem, vmem),
        scratch_shapes=[plane] * 3,
        compiler_params=params,
        name="forward_first",
    )(state, *weights)

    up_1, slice_1 = pl.pallas_call(
        functools.partial(update_second, n),
        out_shape=(
            jax.ShapeDtypeStruct((pairs, c), F32),
            jax.ShapeDtypeStruct((part, width + c), BF16),
        ),
        in_specs=[smem] + [vmem] * 9,
        out_specs=(vmem, vmem),
        scratch_shapes=[plane] * 9 + [narrow] * 3 + [wide, grads],
        compiler_params=params,
        name="update_second",
    )(index, state, state_1, cot, *weights)
    total_1 = sum_exchange(slice_1, "dp", groups).astype(BF16)
    whole_1 = gather_doubling(total_1, "dap", parts)

    pair_grad, slice_0 = pl.pallas_call(
        functools.partial(backward_first, n),
        out_shape=(
            jax.ShapeDtypeStruct((cells, c), BF16),
            jax.ShapeDtypeStruct((part, width + c), BF16),
        ),
        in_specs=[smem] + [vmem] * 9,
        out_specs=(vmem, vmem),
        scratch_shapes=[plane] * 7 + [narrow] * 3 + [wide, grads],
        compiler_params=params,
        name="backward_first",
    )(index, state, product_0, up_1, *weights)
    total_0 = jnp.sum(gather_rows(slice_0, "dp", groups).astype(F32), axis=0).astype(BF16)
    whole_0 = gather_rows(total_0, "dap", parts)

    whole = jnp.stack([whole_0, whole_1]).reshape(2, c, width + c).astype(F32)
    return (
        pair_grad.reshape(pair_repr.shape),
        whole[:, :, :width],
        whole[:, :, width:],
    )


def layer_norm(values, gain_vec, shift_vec, norm_axis):
    mean_value = jnp.mean(values, axis=norm_axis, keepdims=True)
    centred = values - mean_value
    variance = jnp.mean(centred * centred, axis=norm_axis, keepdims=True)
    return centred * lax.rsqrt(variance + NORM_EPSILON) * gain_vec + shift_vec


def norm_pullback(values, gain_vec, shift_vec, norm_axis, upstream):
    _, pull_back = jax.vjp(
        lambda inner_value: layer_norm(inner_value, gain_vec, shift_vec, norm_axis), values
    )
    return pull_back(upstream)[0]


def edge_pair(edge_pre, cell_mask):
    left_edge = jax.nn.sigmoid(edge_pre[1]) * edge_pre[0] * cell_mask
    right_edge = jax.nn.sigmoid(edge_pre[3]) * edge_pre[2] * cell_mask
    return jnp.stack([left_edge, right_edge]).astype(jnp.bfloat16)


def edge_pullback(edge_pre, cell_mask, grad_pair):
    sig_left = jax.nn.sigmoid(edge_pre[1])
    sig_right = jax.nn.sigmoid(edge_pre[3])
    grad_left = grad_pair[0].astype(jnp.float32) * cell_mask
    grad_right = grad_pair[1].astype(jnp.float32) * cell_mask
    return jnp.stack(
        [
            grad_left * sig_left,
            grad_left * edge_pre[0] * sig_left * (1.0 - sig_left),
            grad_right * sig_right,
            grad_right * edge_pre[2] * sig_right * (1.0 - sig_right),
        ]
    ).astype(jnp.bfloat16)


def triangle(pair_edges, outgoing):
    if outgoing:
        einsum_form = "cik,cjk->cij"
    else:
        einsum_form = "cki,ckj->cij"
    return jnp.einsum(
        einsum_form, pair_edges[0], pair_edges[1], preferred_element_type=jnp.float32
    ).astype(jnp.bfloat16)


def triangle_pullback(pair_edges, grad_product, outgoing):
    left_edge = pair_edges[0]
    right_edge = pair_edges[1]
    if outgoing:
        grad_left = jnp.einsum(
            "cij,cjk->cik", grad_product, right_edge, preferred_element_type=jnp.float32
        )
        grad_right = jnp.einsum(
            "cij,cik->cjk", grad_product, left_edge, preferred_element_type=jnp.float32
        )
    else:
        grad_left = jnp.einsum(
            "ckj,cij->cki", right_edge, grad_product, preferred_element_type=jnp.float32
        )
        grad_right = jnp.einsum(
            "cki,cij->ckj", left_edge, grad_product, preferred_element_type=jnp.float32
        )
    return jnp.stack([grad_left, grad_right]).astype(jnp.bfloat16)


def update_weights(proj_weight, proj_bias, norm_gain, norm_shift, update, channels, hidden):
    w_edge = proj_weight[update, :, : 4 * hidden].reshape(channels, 4, hidden)
    w_gate = proj_weight[update, :, 4 * hidden :]
    bias_edge = proj_bias[update, : 4 * hidden].reshape(4, hidden, 1, 1)
    bias_gate = proj_bias[update, 4 * hidden :]
    gain_in = norm_gain[update, :channels]
    shift_in = norm_shift[update, :channels]
    gain_out = norm_gain[update, channels:][:, None, None]
    shift_out = norm_shift[update, channels:][:, None, None]
    return (w_edge, w_gate, bias_edge, bias_gate, gain_in, shift_in, gain_out, shift_out)


def shards(
    pair_repr,
    pair_mask,
    cotangent,
    proj_weight,
    proj_bias,
    norm_gain,
    norm_shift,
    out_weight,
    out_bias,
):
    channels = pair_repr.shape[3]
    hidden = out_weight.shape[1]
    pair_state = pair_repr[0]
    cell_mask = pair_mask[0].astype(jnp.float32)
    records = []
    for update in range(2):
        w_edge, w_gate, bias_edge, bias_gate, gain_in, shift_in, gain_out, shift_out = (
            update_weights(proj_weight, proj_bias, norm_gain, norm_shift, update, channels, hidden)
        )
        state_f = pair_state.astype(jnp.float32)
        normed = layer_norm(state_f, gain_in, shift_in, -1).astype(jnp.bfloat16)
        edge_pre = (
            jnp.einsum("rnc,cgh->ghrn", normed, w_edge, preferred_element_type=jnp.float32)
            + bias_edge
        )
        gate_pre = (
            jnp.einsum("rnc,cd->rnd", normed, w_gate, preferred_element_type=jnp.float32)
            + bias_gate
        )
        pair_edges = edge_pair(edge_pre, cell_mask)
        spread = lax.all_to_all(pair_edges, "dap", split_axis=1, concat_axis=2, tiled=True)
        product = lax.all_to_all(
            triangle(spread, update == 0), "dap", split_axis=1, concat_axis=0, tiled=True
        )
        mixed_norm = layer_norm(product.astype(jnp.float32), gain_out, shift_out, 0).astype(
            jnp.bfloat16
        )
        branch = (
            jnp.einsum(
                "hrn,hd->rnd", mixed_norm, out_weight[update], preferred_element_type=jnp.float32
            )
            + out_bias[update]
        )
        records.append(
            (state_f, normed, edge_pre, gate_pre, pair_edges, spread, product, mixed_norm, branch)
        )
        pair_state = (state_f + jax.nn.sigmoid(gate_pre) * branch).astype(jnp.bfloat16)
    upstream = cotangent[0].astype(jnp.float32)
    proj_grads = []
    out_grads = []
    for update in (1, 0):
        state_f, normed, edge_pre, gate_pre, pair_edges, spread, product, mixed_norm, branch = (
            records[update]
        )
        w_edge, w_gate, bias_edge, bias_gate, gain_in, shift_in, gain_out, shift_out = (
            update_weights(proj_weight, proj_bias, norm_gain, norm_shift, update, channels, hidden)
        )
        gate_value = jax.nn.sigmoid(gate_pre)
        grad_branch = (upstream * gate_value).astype(jnp.bfloat16)
        grad_gate = (upstream * branch * gate_value * (1.0 - gate_value)).astype(jnp.bfloat16)
        out_grad = jnp.einsum(
            "hrn,rnd->hd", mixed_norm, grad_branch, preferred_element_type=jnp.float32
        )
        grad_mixed = jnp.einsum(
            "rnd,hd->hrn", grad_branch, out_weight[update], preferred_element_type=jnp.float32
        )
        grad_product = norm_pullback(
            product.astype(jnp.float32), gain_out, shift_out, 0, grad_mixed
        ).astype(jnp.bfloat16)
        column_edges = spread
        column_grad = lax.all_to_all(
            grad_product[None], "dap", split_axis=1, concat_axis=2, tiled=True
        )[0]
        grad_pair = lax.all_to_all(
            triangle_pullback(column_edges, column_grad, update == 0),
            "dap",
            split_axis=2,
            concat_axis=1,
            tiled=True,
        )
        grad_edge = edge_pullback(edge_pre, cell_mask, grad_pair)
        edge_grad = jnp.einsum(
            "rnc,ghrn->cgh", normed, grad_edge, preferred_element_type=jnp.float32
        ).reshape(channels, 4 * hidden)
        gate_grad = jnp.einsum("rnc,rnd->cd", normed, grad_gate, preferred_element_type=jnp.float32)
        grad_normed = jnp.einsum(
            "ghrn,cgh->rnc", grad_edge, w_edge, preferred_element_type=jnp.float32
        )
        grad_normed = grad_normed + jnp.einsum(
            "rnd,cd->rnc", grad_gate, w_gate, preferred_element_type=jnp.float32
        )
        upstream = upstream + norm_pullback(state_f, gain_in, shift_in, -1, grad_normed)
        proj_part = jnp.concatenate([edge_grad, gate_grad], axis=1)
        proj_grads.append(proj_part)
        out_grads.append(out_grad)
    proj_total = jnp.stack(proj_grads[::-1])
    out_total = jnp.stack(out_grads[::-1])
    proj_total, out_total = lax.psum((proj_total, out_total), ("dp", "dap"))
    return (upstream.astype(jnp.bfloat16)[None], proj_total, out_total)


def solution(mesh):
    placed = (
        P("dp", "dap", None, None),
        P("dp", "dap", None),
        P("dp", "dap", None, None),
        P(),
        P(),
        P(),
        P(),
        P(),
        P(),
    )
    groups, parts = mesh.shape["dp"], mesh.shape["dap"]

    def program(*args):
        n, c = args[0].shape[2:]
        rows = n // parts
        fits = 20 * n * n * c * 4 <= CROP_BUDGET
        even = args[7].shape[1] == c and parts & (parts - 1) == 0 and BLOCK_ROWS % rows == 0 and n % 16 == 0
        body = functools.partial(crop_shards, groups, parts) if fits and even else shards
        return spread_over(body)(*args)

    def spread_over(body):
        return jax.shard_map(
            body,
            mesh=mesh,
            in_specs=placed,
            out_specs=(P("dp", "dap", None, None), P(), P()),
            check_vma=False,
        )

    return program
```

```python
import functools

import jax
import jax.numpy as jnp
from jax import lax
from jax.experimental import pallas as pl
from jax.experimental.pallas import tpu as pltpu
from jax.sharding import PartitionSpec as P

NORM_EPSILON = 1e-05
VMEM_BYTES = 48 * 1024 * 1024
CROP_BUDGET = 32 * 1024 * 1024
BLOCK_ROWS = 8
F32 = jnp.float32
BF16 = jnp.bfloat16


def sigmoid(x):
    return 0.5 * jnp.tanh(0.5 * x) + 0.5


def dot(a, b, dims=((1,), (0,))):
    return lax.dot_general(a, b, (dims, ((), ())), preferred_element_type=F32)


def norm_parts(x):
    centred = x - jnp.mean(x, axis=-1, keepdims=True)
    rstd = lax.rsqrt(jnp.mean(centred * centred, axis=-1, keepdims=True) + NORM_EPSILON)
    return centred * rstd, rstd


def norm_vjp(x_hat, rstd, grad):
    mean_grad = jnp.mean(grad, axis=-1, keepdims=True)
    mean_prod = jnp.mean(grad * x_hat, axis=-1, keepdims=True)
    return rstd * (grad - mean_grad - x_hat * mean_prod)


def pair_mask_block(length, first_row, rows, n, lanes):
    shape = (rows, n, lanes)
    i = lax.broadcasted_iota(jnp.int32, shape, 0) + first_row
    j = lax.broadcasted_iota(jnp.int32, shape, 1)
    inside = jnp.where((i < length) & (j < length), 1.0, 0.0)
    return inside.reshape(rows * n, lanes)


def project(x, mask, u, w, b, gain, shift):
    c = x.shape[1]
    x_hat, rstd = norm_parts(x)
    normed = (x_hat * gain[u : u + 1, :c] + shift[u : u + 1, :c]).astype(BF16)
    pre = dot(normed, w[u]) + b[u : u + 1, :]
    h = (pre.shape[1] - c) // 4
    s_left = sigmoid(pre[:, h : 2 * h]) * mask
    s_right = sigmoid(pre[:, 3 * h : 4 * h]) * mask
    left = s_left * pre[:, :h]
    right = s_right * pre[:, 2 * h : 3 * h]
    gate = sigmoid(pre[:, 4 * h :])
    return x_hat, rstd, normed, s_left, s_right, left, right, gate


def mix(product, u, c, gain, shift, w_out, b_out):
    p_hat, p_rstd = norm_parts(product.astype(F32))
    mixed = (p_hat * gain[u : u + 1, c:] + shift[u : u + 1, c:]).astype(BF16)
    branch = dot(mixed, w_out[u]) + b_out[u : u + 1, :]
    return p_hat, p_rstd, mixed, branch


def unmix(up, gate, branch, p_hat, p_rstd, u, c, gain, w_out):
    d_branch = up * gate
    d_gate = (d_branch * branch * (1.0 - gate)).astype(BF16)
    d_branch = d_branch.astype(BF16)
    d_mixed = dot(d_branch, w_out[u], ((1,), (1,))) * gain[u : u + 1, c:]
    return d_branch, d_gate, norm_vjp(p_hat, p_rstd, d_mixed)


def contract(n, first, row_of, x, y):
    lanes = y.shape[1]
    tiles = (n // 8, 8, lanes)

    def step(e, totals):
        block = y[pl.ds(pl.multiple_of(e * n, n), n), :].reshape(tiles)
        return tuple(
            totals[a] + x[pl.ds(row_of(first + a, e), 8, stride=0), :][None] * block
            for a in range(BLOCK_ROWS)
        )

    zero = jnp.zeros(tiles, F32)
    totals = lax.fori_loop(0, n, step, (zero,) * BLOCK_ROWS, unroll=4)
    return jnp.stack(totals).reshape(BLOCK_ROWS * n, lanes)


def edge_grads(d_left, d_right, s_left, s_right, left, right):
    return (
        (d_left * s_left).astype(BF16),
        (d_left * left * (1.0 - s_left)).astype(BF16),
        (d_right * s_right).astype(BF16),
        (d_right * right * (1.0 - s_right)).astype(BF16),
    )


def crop_length(state_ref, cells):
    return jnp.max(state_ref[:, cells:, :].astype(F32)).astype(jnp.int32)


def joined(ref, first, count, cells):
    return jnp.concatenate([ref[first + q, :cells, :] for q in range(count)], axis=0)


def forward_first(
    n, state_ref, w, b, gain, shift, w_out, b_out, next_ref, product_ref, left_s, right_s, gate_s
):
    parts, cells, c = state_ref.shape
    rows = n // parts
    cells = rows * n
    length = crop_length(state_ref, cells)

    per = BLOCK_ROWS // rows

    @pl.loop(0, n // BLOCK_ROWS)
    def _(t):
        first = t * BLOCK_ROWS
        here = pl.ds(pl.multiple_of(first * n, BLOCK_ROWS * n), BLOCK_ROWS * n)
        x = joined(state_ref, t * per, per, cells).astype(F32)
        mask = pair_mask_block(length, first, BLOCK_ROWS, n, c)
        _, _, _, _, _, left, right, gate = project(x, mask, 0, w, b, gain, shift)
        left_s[here, :] = left
        gate_s[here, :] = gate
        for r in range(BLOCK_ROWS):
            right_s[pl.ds(first + r, n, stride=n), :] = right[r * n : (r + 1) * n]

    @pl.loop(0, n // BLOCK_ROWS)
    def _(t):
        totals = contract(n, t * BLOCK_ROWS, lambda i, k: i * n + k, left_s, right_s)
        here = pl.ds(pl.multiple_of(t * BLOCK_ROWS * n, BLOCK_ROWS * n), BLOCK_ROWS * n)
        product = totals.astype(BF16)
        product_ref[here, :] = product
        _, _, _, branch = mix(product, 0, c, gain, shift, w_out, b_out)
        x = joined(state_ref, t * per, per, cells)
        next_ref[here, :] = (x.astype(F32) + gate_s[here, :] * branch).astype(BF16)


def weight_grads(normed_s, d_pre_s, mixed_s, d_branch_s, grads_ref):
    width = d_pre_s.shape[1]
    grads_ref[:, :width] = dot(normed_s[...], d_pre_s[...], ((0,), (0,))).astype(BF16)
    grads_ref[:, width:] = dot(mixed_s[...], d_branch_s[...], ((0,), (0,))).astype(BF16)


def update_second(
    n,
    state_ref,
    next_ref,
    cot_ref,
    w,
    b,
    gain,
    shift,
    w_out,
    b_out,
    up_ref,
    grads_ref,
    left_s,
    right_s,
    s_left_s,
    s_right_s,
    gate_s,
    hat_s,
    rstd_s,
    d_product_s,
    d_product_t_s,
    normed_s,
    mixed_s,
    d_branch_s,
    d_pre_s,
):
    parts, _, c = state_ref.shape
    rows = n // parts
    cells = rows * n
    h = left_s.shape[1]
    length = crop_length(state_ref, cells)

    per = BLOCK_ROWS // rows

    @pl.loop(0, n // BLOCK_ROWS)
    def _(t):
        here = pl.ds(pl.multiple_of(t * BLOCK_ROWS * n, BLOCK_ROWS * n), BLOCK_ROWS * n)
        x = next_ref[here, :].astype(F32)
        mask = pair_mask_block(length, t * BLOCK_ROWS, BLOCK_ROWS, n, c)
        x_hat, rstd, normed, s_left, s_right, left, right, gate = project(
            x, mask, 1, w, b, gain, shift
        )
        left_s[here, :] = left
        right_s[here, :] = right
        s_left_s[here, :] = s_left
        s_right_s[here, :] = s_right
        gate_s[here, :] = gate
        hat_s[here, :] = x_hat
        rstd_s[here, :] = jnp.broadcast_to(rstd, x_hat.shape)
        normed_s[here, :] = normed

    @pl.loop(0, n // BLOCK_ROWS)
    def _(t):
        totals = contract(n, t * BLOCK_ROWS, lambda i, k: k * n + i, left_s, right_s)
        here = pl.ds(pl.multiple_of(t * BLOCK_ROWS * n, BLOCK_ROWS * n), BLOCK_ROWS * n)
        product = totals.astype(BF16)
        p_hat, p_rstd, mixed, branch = mix(product, 1, c, gain, shift, w_out, b_out)
        up = joined(cot_ref, t * per, per, cells).astype(F32)
        d_branch, d_gate, d_product = unmix(
            up, gate_s[here, :], branch, p_hat, p_rstd, 1, c, gain, w_out
        )
        mixed_s[here, :] = mixed
        d_branch_s[here, :] = d_branch
        d_pre_s[here, 4 * h :] = d_gate
        d_product_s[here, :] = d_product
        for r in range(BLOCK_ROWS):
            d_product_t_s[pl.ds(t * BLOCK_ROWS + r, n, stride=n), :] = d_product[
                r * n : (r + 1) * n
            ]

    @pl.loop(0, n // BLOCK_ROWS)
    def _(t):
        first = t * BLOCK_ROWS
        here = pl.ds(pl.multiple_of(first * n, BLOCK_ROWS * n), BLOCK_ROWS * n)
        d_left = contract(n, first, lambda k, j: k * n + j, right_s, d_product_t_s)
        d_right = contract(n, first, lambda k, i: k * n + i, left_s, d_product_s)
        grads = edge_grads(
            d_left, d_right, s_left_s[here, :], s_right_s[here, :], left_s[here, :], right_s[here, :]
        )
        for g in range(4):
            d_pre_s[here, g * h : (g + 1) * h] = grads[g]
        d_normed = dot(d_pre_s[here, :], w[1], ((1,), (1,))) * gain[1:2, :c]
        up = joined(cot_ref, t * per, per, cells).astype(F32)
        up_ref[here, :] = up + norm_vjp(hat_s[here, :], rstd_s[here, :], d_normed)

    weight_grads(normed_s, d_pre_s, mixed_s, d_branch_s, grads_ref)


def backward_first(
    n,
    index_ref,
    state_ref,
    product_ref,
    up_ref,
    w,
    b,
    gain,
    shift,
    w_out,
    b_out,
    out_ref,
    grads_ref,
    left_s,
    right_s,
    s_left_s,
    s_right_s,
    hat_s,
    rstd_s,
    d_product_s,
    normed_s,
    mixed_s,
    d_branch_s,
    d_pre_s,
):
    parts, _, c = state_ref.shape
    rows = n // parts
    cells = rows * n
    h = left_s.shape[1]
    length = crop_length(state_ref, cells)

    per = BLOCK_ROWS // rows

    @pl.loop(0, n // BLOCK_ROWS)
    def _(t):
        here = pl.ds(pl.multiple_of(t * BLOCK_ROWS * n, BLOCK_ROWS * n), BLOCK_ROWS * n)
        x = joined(state_ref, t * per, per, cells).astype(F32)
        mask = pair_mask_block(length, t * BLOCK_ROWS, BLOCK_ROWS, n, c)
        x_hat, rstd, normed, s_left, s_right, left, right, gate = project(
            x, mask, 0, w, b, gain, shift
        )
        left_s[here, :] = left
        right_s[here, :] = right
        s_left_s[here, :] = s_left
        s_right_s[here, :] = s_right
        hat_s[here, :] = x_hat
        rstd_s[here, :] = jnp.broadcast_to(rstd, x_hat.shape)
        normed_s[here, :] = normed
        p_hat, p_rstd, mixed, branch = mix(
            product_ref[here, :], 0, c, gain, shift, w_out, b_out
        )
        d_branch, d_gate, d_product = unmix(
            up_ref[here, :], gate, branch, p_hat, p_rstd, 0, c, gain, w_out
        )
        mixed_s[here, :] = mixed
        d_branch_s[here, :] = d_branch
        d_pre_s[here, 4 * h :] = d_gate
        d_product_s[here, :] = d_product

    @pl.loop(0, n // BLOCK_ROWS)
    def _(t):
        first = t * BLOCK_ROWS
        here = pl.ds(pl.multiple_of(first * n, BLOCK_ROWS * n), BLOCK_ROWS * n)
        d_left = contract(n, first, lambda i, j: i * n + j, d_product_s, right_s)
        d_right = contract(n, first, lambda j, i: i * n + j, d_product_s, left_s)
        grads = edge_grads(
            d_left, d_right, s_left_s[here, :], s_right_s[here, :], left_s[here, :], right_s[here, :]
        )
        for g in range(4):
            d_pre_s[here, g * h : (g + 1) * h] = grads[g]

    own = pl.ds(pl.multiple_of(index_ref[0] * cells, cells), cells)
    d_normed = dot(d_pre_s[own, :], w[0], ((1,), (1,))) * gain[0:1, :c]
    out_ref[...] = (
        up_ref[own, :] + norm_vjp(hat_s[own, :], rstd_s[own, :], d_normed)
    ).astype(BF16)
    weight_grads(normed_s, d_pre_s, mixed_s, d_branch_s, grads_ref)


def gather_rows(value, axis, size):
    spread = jnp.broadcast_to(value[None], (size,) + value.shape)
    return lax.all_to_all(spread, axis, split_axis=0, concat_axis=0, tiled=True)


def pair_rounds(value, axis, size):
    step, other = 1, None
    while step < size:
        if other is not None:
            value = (value.astype(F32) + other.astype(F32)).astype(BF16)
        other = lax.ppermute(value, axis, [(d, d ^ step) for d in range(size)])
        step *= 2
    return value, other


def prepare(state_ref, mask_ref, sent_ref):
    parts, _, c = sent_ref.shape
    cells = state_ref.shape[0]
    length = jnp.max(jnp.sum(mask_ref[...].astype(F32), axis=1, keepdims=True))
    below = jnp.full((sent_ref.shape[1] - cells, c), length, F32).astype(BF16)
    for part in range(parts):
        sent_ref[part, :cells, :] = state_ref[...]
        sent_ref[part, cells:, :] = below


def add_grads(own_0, other_0, own_1, other_1, proj_ref, out_ref):
    width = proj_ref.shape[2]
    for u, (own, other) in enumerate(((own_0, other_0), (own_1, other_1))):
        total = own[...].astype(F32) + other[...].astype(F32)
        proj_ref[u] = total[:, :width]
        out_ref[u] = total[:, width:]


def crop_shards(
    groups,
    parts,
    pair_repr,
    pair_mask,
    cotangent,
    proj_weight,
    proj_bias,
    norm_gain,
    norm_shift,
    out_weight,
    out_bias,
):
    _, rows, n, c = pair_repr.shape
    h = out_weight.shape[1]
    width = proj_weight.shape[2]
    cells, pairs = rows * n, n * n
    plane = pltpu.VMEM((pairs + 8, h), F32)
    narrow = pltpu.VMEM((pairs, h), BF16)
    wide = pltpu.VMEM((pairs, width), BF16)
    grads = jax.ShapeDtypeStruct((c, width + c), BF16)
    vmem = pl.BlockSpec(memory_space=pltpu.VMEM)
    smem = pl.BlockSpec(memory_space=pltpu.SMEM)
    params = pltpu.CompilerParams(vmem_limit_bytes=VMEM_BYTES)
    weights = (proj_weight, proj_bias, norm_gain, norm_shift, out_weight, out_bias)

    index = lax.axis_index("dap").astype(jnp.int32)[None]
    sent = pl.pallas_call(
        prepare,
        out_shape=jax.ShapeDtypeStruct((parts, cells + 16, c), BF16),
        in_specs=[vmem] * 2,
        out_specs=vmem,
        compiler_params=params,
        name="prepare",
    )(pair_repr.reshape(cells, c), pair_mask[0])
    state = lax.all_to_all(sent, "dap", split_axis=0, concat_axis=0, tiled=True)
    cot = gather_rows(cotangent.reshape(cells, c), "dap", parts)

    state_1, product_0 = pl.pallas_call(
        functools.partial(forward_first, n),
        out_shape=(
            jax.ShapeDtypeStruct((pairs, c), BF16),
            jax.ShapeDtypeStruct((pairs, h), BF16),
        ),
        in_specs=[vmem] * 7,
        out_specs=(vmem, vmem),
        scratch_shapes=[plane] * 3,
        compiler_params=params,
        name="forward_first",
    )(state, *weights)

    up_1, grads_1 = pl.pallas_call(
        functools.partial(update_second, n),
        out_shape=(
            jax.ShapeDtypeStruct((pairs, c), F32),
            grads,
        ),
        in_specs=[vmem] * 9,
        out_specs=(vmem, vmem),
        scratch_shapes=[plane] * 9 + [narrow] * 3 + [wide],
        compiler_params=params,
        name="update_second",
    )(state, state_1, cot, *weights)
    ends_1 = pair_rounds(grads_1, "dp", groups)

    pair_grad, grads_0 = pl.pallas_call(
        functools.partial(backward_first, n),
        out_shape=(
            jax.ShapeDtypeStruct((cells, c), BF16),
            grads,
        ),
        in_specs=[smem] + [vmem] * 9,
        out_specs=(vmem, vmem),
        scratch_shapes=[plane] * 7 + [narrow] * 3 + [wide],
        compiler_params=params,
        name="backward_first",
    )(index, state, product_0, up_1, *weights)
    ends_0 = pair_rounds(grads_0, "dp", groups)

    proj_total, out_total = pl.pallas_call(
        add_grads,
        out_shape=(
            jax.ShapeDtypeStruct((2, c, width), F32),
            jax.ShapeDtypeStruct((2, h, c), F32),
        ),
        in_specs=[vmem] * 4,
        out_specs=(vmem, vmem),
        compiler_params=params,
        name="add_grads",
    )(*ends_0, *ends_1)
    return pair_grad.reshape(pair_repr.shape), proj_total, out_total


def layer_norm(values, gain_vec, shift_vec, norm_axis):
    mean_value = jnp.mean(values, axis=norm_axis, keepdims=True)
    centred = values - mean_value
    variance = jnp.mean(centred * centred, axis=norm_axis, keepdims=True)
    return centred * lax.rsqrt(variance + NORM_EPSILON) * gain_vec + shift_vec


def norm_pullback(values, gain_vec, shift_vec, norm_axis, upstream):
    _, pull_back = jax.vjp(
        lambda inner_value: layer_norm(inner_value, gain_vec, shift_vec, norm_axis), values
    )
    return pull_back(upstream)[0]


def edge_pair(edge_pre, cell_mask):
    left_edge = jax.nn.sigmoid(edge_pre[1]) * edge_pre[0] * cell_mask
    right_edge = jax.nn.sigmoid(edge_pre[3]) * edge_pre[2] * cell_mask
    return jnp.stack([left_edge, right_edge]).astype(jnp.bfloat16)


def edge_pullback(edge_pre, cell_mask, grad_pair):
    sig_left = jax.nn.sigmoid(edge_pre[1])
    sig_right = jax.nn.sigmoid(edge_pre[3])
    grad_left = grad_pair[0].astype(jnp.float32) * cell_mask
    grad_right = grad_pair[1].astype(jnp.float32) * cell_mask
    return jnp.stack(
        [
            grad_left * sig_left,
            grad_left * edge_pre[0] * sig_left * (1.0 - sig_left),
            grad_right * sig_right,
            grad_right * edge_pre[2] * sig_right * (1.0 - sig_right),
        ]
    ).astype(jnp.bfloat16)


def triangle(pair_edges, outgoing):
    if outgoing:
        einsum_form = "cik,cjk->cij"
    else:
        einsum_form = "cki,ckj->cij"
    return jnp.einsum(
        einsum_form, pair_edges[0], pair_edges[1], preferred_element_type=jnp.float32
    ).astype(jnp.bfloat16)


def triangle_pullback(pair_edges, grad_product, outgoing):
    left_edge = pair_edges[0]
    right_edge = pair_edges[1]
    if outgoing:
        grad_left = jnp.einsum(
            "cij,cjk->cik", grad_product, right_edge, preferred_element_type=jnp.float32
        )
        grad_right = jnp.einsum(
            "cij,cik->cjk", grad_product, left_edge, preferred_element_type=jnp.float32
        )
    else:
        grad_left = jnp.einsum(
            "ckj,cij->cki", right_edge, grad_product, preferred_element_type=jnp.float32
        )
        grad_right = jnp.einsum(
            "cki,cij->ckj", left_edge, grad_product, preferred_element_type=jnp.float32
        )
    return jnp.stack([grad_left, grad_right]).astype(jnp.bfloat16)


def update_weights(proj_weight, proj_bias, norm_gain, norm_shift, update, channels, hidden):
    w_edge = proj_weight[update, :, : 4 * hidden].reshape(channels, 4, hidden)
    w_gate = proj_weight[update, :, 4 * hidden :]
    bias_edge = proj_bias[update, : 4 * hidden].reshape(4, hidden, 1, 1)
    bias_gate = proj_bias[update, 4 * hidden :]
    gain_in = norm_gain[update, :channels]
    shift_in = norm_shift[update, :channels]
    gain_out = norm_gain[update, channels:][:, None, None]
    shift_out = norm_shift[update, channels:][:, None, None]
    return (w_edge, w_gate, bias_edge, bias_gate, gain_in, shift_in, gain_out, shift_out)


def shards(
    pair_repr,
    pair_mask,
    cotangent,
    proj_weight,
    proj_bias,
    norm_gain,
    norm_shift,
    out_weight,
    out_bias,
):
    channels = pair_repr.shape[3]
    hidden = out_weight.shape[1]
    pair_state = pair_repr[0]
    cell_mask = pair_mask[0].astype(jnp.float32)
    records = []
    for update in range(2):
        w_edge, w_gate, bias_edge, bias_gate, gain_in, shift_in, gain_out, shift_out = (
            update_weights(proj_weight, proj_bias, norm_gain, norm_shift, update, channels, hidden)
        )
        state_f = pair_state.astype(jnp.float32)
        normed = layer_norm(state_f, gain_in, shift_in, -1).astype(jnp.bfloat16)
        edge_pre = (
            jnp.einsum("rnc,cgh->ghrn", normed, w_edge, preferred_element_type=jnp.float32)
            + bias_edge
        )
        gate_pre = (
            jnp.einsum("rnc,cd->rnd", normed, w_gate, preferred_element_type=jnp.float32)
            + bias_gate
        )
        pair_edges = edge_pair(edge_pre, cell_mask)
        spread = lax.all_to_all(pair_edges, "dap", split_axis=1, concat_axis=2, tiled=True)
        product = lax.all_to_all(
            triangle(spread, update == 0), "dap", split_axis=1, concat_axis=0, tiled=True
        )
        mixed_norm = layer_norm(product.astype(jnp.float32), gain_out, shift_out, 0).astype(
            jnp.bfloat16
        )
        branch = (
            jnp.einsum(
                "hrn,hd->rnd", mixed_norm, out_weight[update], preferred_element_type=jnp.float32
            )
            + out_bias[update]
        )
        records.append(
            (state_f, normed, edge_pre, gate_pre, pair_edges, spread, product, mixed_norm, branch)
        )
        pair_state = (state_f + jax.nn.sigmoid(gate_pre) * branch).astype(jnp.bfloat16)
    upstream = cotangent[0].astype(jnp.float32)
    proj_grads = []
    out_grads = []
    for update in (1, 0):
        state_f, normed, edge_pre, gate_pre, pair_edges, spread, product, mixed_norm, branch = (
            records[update]
        )
        w_edge, w_gate, bias_edge, bias_gate, gain_in, shift_in, gain_out, shift_out = (
            update_weights(proj_weight, proj_bias, norm_gain, norm_shift, update, channels, hidden)
        )
        gate_value = jax.nn.sigmoid(gate_pre)
        grad_branch = (upstream * gate_value).astype(jnp.bfloat16)
        grad_gate = (upstream * branch * gate_value * (1.0 - gate_value)).astype(jnp.bfloat16)
        out_grad = jnp.einsum(
            "hrn,rnd->hd", mixed_norm, grad_branch, preferred_element_type=jnp.float32
        )
        grad_mixed = jnp.einsum(
            "rnd,hd->hrn", grad_branch, out_weight[update], preferred_element_type=jnp.float32
        )
        grad_product = norm_pullback(
            product.astype(jnp.float32), gain_out, shift_out, 0, grad_mixed
        ).astype(jnp.bfloat16)
        column_edges = spread
        column_grad = lax.all_to_all(
            grad_product[None], "dap", split_axis=1, concat_axis=2, tiled=True
        )[0]
        grad_pair = lax.all_to_all(
            triangle_pullback(column_edges, column_grad, update == 0),
            "dap",
            split_axis=2,
            concat_axis=1,
            tiled=True,
        )
        grad_edge = edge_pullback(edge_pre, cell_mask, grad_pair)
        edge_grad = jnp.einsum(
            "rnc,ghrn->cgh", normed, grad_edge, preferred_element_type=jnp.float32
        ).reshape(channels, 4 * hidden)
        gate_grad = jnp.einsum("rnc,rnd->cd", normed, grad_gate, preferred_element_type=jnp.float32)
        grad_normed = jnp.einsum(
            "ghrn,cgh->rnc", grad_edge, w_edge, preferred_element_type=jnp.float32
        )
        grad_normed = grad_normed + jnp.einsum(
            "rnd,cd->rnc", grad_gate, w_gate, preferred_element_type=jnp.float32
        )
        upstream = upstream + norm_pullback(state_f, gain_in, shift_in, -1, grad_normed)
        proj_part = jnp.concatenate([edge_grad, gate_grad], axis=1)
        proj_grads.append(proj_part)
        out_grads.append(out_grad)
    proj_total = jnp.stack(proj_grads[::-1])
    out_total = jnp.stack(out_grads[::-1])
    proj_total, out_total = lax.psum((proj_total, out_total), ("dp", "dap"))
    return (upstream.astype(jnp.bfloat16)[None], proj_total, out_total)


def solution(mesh):
    placed = (
        P("dp", "dap", None, None),
        P("dp", "dap", None),
        P("dp", "dap", None, None),
        P(),
        P(),
        P(),
        P(),
        P(),
        P(),
    )
    groups, parts = mesh.shape["dp"], mesh.shape["dap"]

    def program(*args):
        n, c = args[0].shape[2:]
        rows = n // parts
        fits = 20 * n * n * c * 4 <= CROP_BUDGET
        even = args[7].shape[1] == c and groups > 1 and groups & (groups - 1) == 0 and BLOCK_ROWS % rows == 0 and n % 16 == 0
        body = functools.partial(crop_shards, groups, parts) if fits and even else shards
        return spread_over(body)(*args)

    def spread_over(body):
        return jax.shard_map(
            body,
            mesh=mesh,
            in_specs=placed,
            out_specs=(P("dp", "dap", None, None), P(), P()),
            check_vma=False,
        )

    return program
```

```python
import functools

import jax
import jax.numpy as jnp
from jax import lax
from jax.experimental import pallas as pl
from jax.experimental.pallas import tpu as pltpu
from jax.sharding import PartitionSpec as P

NORM_EPSILON = 1e-05
VMEM_BYTES = 24 * 1024 * 1024
PREPARE_BYTES = 63 * 1024 * 1024
CROP_BUDGET = 32 * 1024 * 1024
BLOCK_ROWS = 8
KEPT = 12
F32 = jnp.float32
BF16 = jnp.bfloat16


def sigmoid(x):
    return 0.5 * jnp.tanh(0.5 * x) + 0.5


def dot(a, b, dims=((1,), (0,))):
    return lax.dot_general(a, b, (dims, ((), ())), preferred_element_type=F32)


def norm_parts(x):
    centred = x - jnp.mean(x, axis=-1, keepdims=True)
    rstd = lax.rsqrt(jnp.mean(centred * centred, axis=-1, keepdims=True) + NORM_EPSILON)
    return centred * rstd, rstd


def norm_vjp(x_hat, rstd, grad):
    mean_grad = jnp.mean(grad, axis=-1, keepdims=True)
    mean_prod = jnp.mean(grad * x_hat, axis=-1, keepdims=True)
    return rstd * (grad - mean_grad - x_hat * mean_prod)


def pair_mask_block(length, first_row, rows, n, lanes):
    shape = (rows, n, lanes)
    i = lax.broadcasted_iota(jnp.int32, shape, 0) + first_row
    j = lax.broadcasted_iota(jnp.int32, shape, 1)
    inside = jnp.where((i < length) & (j < length), 1.0, 0.0)
    return inside.reshape(rows * n, lanes)


def project(x, mask, u, w, b, gain, shift):
    c = x.shape[1]
    x_hat, rstd = norm_parts(x)
    normed = (x_hat * gain[u : u + 1, :c] + shift[u : u + 1, :c]).astype(BF16)
    pre = dot(normed, w[u]) + b[u : u + 1, :]
    h = (pre.shape[1] - c) // 4
    s_left = sigmoid(pre[:, h : 2 * h]) * mask
    s_right = sigmoid(pre[:, 3 * h : 4 * h]) * mask
    left = s_left * pre[:, :h]
    right = s_right * pre[:, 2 * h : 3 * h]
    gate = sigmoid(pre[:, 4 * h :])
    return x_hat, rstd, normed, s_left, s_right, left, right, gate


def mix(product, u, c, gain, shift, w_out, b_out):
    p_hat, p_rstd = norm_parts(product.astype(F32))
    mixed = (p_hat * gain[u : u + 1, c:] + shift[u : u + 1, c:]).astype(BF16)
    branch = dot(mixed, w_out[u]) + b_out[u : u + 1, :]
    return p_hat, p_rstd, mixed, branch


def unmix(up, gate, branch, p_hat, p_rstd, u, c, gain, w_out):
    d_branch = up * gate
    d_gate = (d_branch * branch * (1.0 - gate)).astype(BF16)
    d_branch = d_branch.astype(BF16)
    d_mixed = dot(d_branch, w_out[u], ((1,), (1,))) * gain[u : u + 1, c:]
    return d_branch, d_gate, norm_vjp(p_hat, p_rstd, d_mixed)


def contract(n, first, row_of, x, y):
    lanes = y.shape[1]
    tiles = (n // 8, 8, lanes)

    def step(e, totals):
        block = y[pl.ds(pl.multiple_of(e * n, n), n), :].reshape(tiles)
        return tuple(
            totals[a] + x[pl.ds(row_of(first + a, e), 8, stride=0), :][None] * block
            for a in range(BLOCK_ROWS)
        )

    zero = jnp.zeros(tiles, F32)
    totals = lax.fori_loop(0, n, step, (zero,) * BLOCK_ROWS, unroll=4)
    return jnp.stack(totals).reshape(BLOCK_ROWS * n, lanes)


def edge_grads(d_left, d_right, s_left, s_right, left, right):
    return (
        (d_left * s_left).astype(BF16),
        (d_left * left * (1.0 - s_left)).astype(BF16),
        (d_right * s_right).astype(BF16),
        (d_right * right * (1.0 - s_right)).astype(BF16),
    )


def crop_length(state_ref, cells):
    return jnp.max(state_ref[:, cells:, :].astype(F32)).astype(jnp.int32)


def joined(ref, first, count, cells):
    return jnp.concatenate([ref[first + q, :cells, :] for q in range(count)], axis=0)


def forward(n, state_ref, w, b, gain, shift, w_out, b_out, *refs):
    kept, (right_t_s, next_s) = (refs[:KEPT], refs[KEPT : 2 * KEPT]), refs[2 * KEPT :]
    parts, _, c = state_ref.shape
    rows = n // parts
    cells = rows * n
    length = crop_length(state_ref, cells)
    per = BLOCK_ROWS // rows
    blocks = n // BLOCK_ROWS

    for u in range(2):
        (left_s, right_s, s_left_s, s_right_s, gate_s, hat_s, rstd_s) = kept[u][:7]
        (p_hat_s, p_rstd_s, branch_s, normed_s, mixed_s) = kept[u][7:]

        @pl.loop(0, blocks)
        def _(t):
            first = t * BLOCK_ROWS
            here = pl.ds(pl.multiple_of(first * n, BLOCK_ROWS * n), BLOCK_ROWS * n)
            x = joined(state_ref, t * per, per, cells) if u == 0 else next_s[here, :]
            mask = pair_mask_block(length, first, BLOCK_ROWS, n, c)
            x_hat, rstd, normed, s_left, s_right, left, right, gate = project(
                x.astype(F32), mask, u, w, b, gain, shift
            )
            left_s[here, :] = left
            right_s[here, :] = right
            s_left_s[here, :] = s_left
            s_right_s[here, :] = s_right
            gate_s[here, :] = gate
            hat_s[here, :] = x_hat
            rstd_s[here, :] = jnp.broadcast_to(rstd, x_hat.shape)
            normed_s[here, :] = normed
            if u == 0:
                for r in range(BLOCK_ROWS):
                    right_t_s[pl.ds(first + r, n, stride=n), :] = right[r * n : (r + 1) * n]

        @pl.loop(0, blocks)
        def _(t):
            first = t * BLOCK_ROWS
            here = pl.ds(pl.multiple_of(first * n, BLOCK_ROWS * n), BLOCK_ROWS * n)
            if u == 0:
                product = contract(n, first, lambda i, k: i * n + k, left_s, right_t_s)
            else:
                product = contract(n, first, lambda i, k: k * n + i, left_s, right_s)
            p_hat, p_rstd, mixed, branch = mix(
                product.astype(BF16), u, c, gain, shift, w_out, b_out
            )
            p_hat_s[here, :] = p_hat
            p_rstd_s[here, :] = jnp.broadcast_to(p_rstd, p_hat.shape)
            mixed_s[here, :] = mixed
            branch_s[here, :] = branch
            if u == 0:
                x = joined(state_ref, t * per, per, cells).astype(F32)
                next_s[here, :] = (x + gate_s[here, :] * branch).astype(BF16)


def weight_grads(normed_s, d_pre_s, mixed_s, d_branch_s, grads_ref):
    width = d_pre_s.shape[1]
    grads_ref[:, :width] = dot(normed_s[...], d_pre_s[...], ((0,), (0,))).astype(BF16)
    grads_ref[:, width:] = dot(mixed_s[...], d_branch_s[...], ((0,), (0,))).astype(BF16)


def backward(n, u, *refs):
    if u == 0:
        index_ref, refs = refs[0], refs[1:]
    up_in_ref, w, gain, w_out = refs[:4]
    (left_s, right_s, s_left_s, s_right_s, gate_s, hat_s, rstd_s) = refs[4:11]
    (p_hat_s, p_rstd_s, branch_s, normed_s, mixed_s) = refs[11 : 4 + KEPT]
    up_ref, grads_ref, d_product_s, d_branch_s, d_pre_s = refs[4 + KEPT : 9 + KEPT]
    c, h = w.shape[1], left_s.shape[1]
    blocks = n // BLOCK_ROWS

    def upstream(t, here):
        if u == 0:
            return up_in_ref[here, :]
        rows = n // up_in_ref.shape[0]
        per = BLOCK_ROWS // rows
        return joined(up_in_ref, t * per, per, rows * n).astype(F32)

    def input_pullback(here, up):
        d_normed = dot(d_pre_s[here, :], w[u], ((1,), (1,))) * gain[u : u + 1, :c]
        return up + norm_vjp(hat_s[here, :], rstd_s[here, :], d_normed)

    @pl.loop(0, blocks)
    def _(t):
        first = t * BLOCK_ROWS
        here = pl.ds(pl.multiple_of(first * n, BLOCK_ROWS * n), BLOCK_ROWS * n)
        d_branch, d_gate, d_product = unmix(
            upstream(t, here),
            gate_s[here, :],
            branch_s[here, :],
            p_hat_s[here, :],
            p_rstd_s[here, :],
            u,
            c,
            gain,
            w_out,
        )
        d_branch_s[here, :] = d_branch
        d_pre_s[here, 4 * h :] = d_gate
        d_product_s[here, :] = d_product
        if u == 1:
            d_product_t_s = refs[9 + KEPT]
            for r in range(BLOCK_ROWS):
                d_product_t_s[pl.ds(first + r, n, stride=n), :] = d_product[r * n : (r + 1) * n]

    @pl.loop(0, blocks)
    def _(t):
        first = t * BLOCK_ROWS
        here = pl.ds(pl.multiple_of(first * n, BLOCK_ROWS * n), BLOCK_ROWS * n)
        if u == 1:
            d_left = contract(n, first, lambda k, j: k * n + j, right_s, refs[9 + KEPT])
            d_right = contract(n, first, lambda k, i: k * n + i, left_s, d_product_s)
        else:
            d_left = contract(n, first, lambda i, j: i * n + j, d_product_s, right_s)
            d_right = contract(n, first, lambda j, i: i * n + j, d_product_s, left_s)
        grads = edge_grads(
            d_left, d_right, s_left_s[here, :], s_right_s[here, :], left_s[here, :], right_s[here, :]
        )
        for g in range(4):
            d_pre_s[here, g * h : (g + 1) * h] = grads[g]
        if u == 1:
            up_ref[here, :] = input_pullback(here, upstream(t, here))

    if u == 0:
        cells = up_ref.shape[0]
        own = pl.ds(pl.multiple_of(index_ref[0] * cells, cells), cells)
        up_ref[...] = input_pullback(own, up_in_ref[own, :]).astype(BF16)
    weight_grads(normed_s, d_pre_s, mixed_s, d_branch_s, grads_ref)


def exchange(value, axis, size, step):
    return lax.ppermute(value, axis, [(d, d ^ step) for d in range(size)])


def add_narrow(a, b):
    return (a.astype(F32) + b.astype(F32)).astype(BF16)


def prepare(state_ref, mask_ref, cot_ref, sent_ref, sent_cot_ref, state_s, mask_s, cot_s, sems):
    parts, _, c = sent_ref.shape
    cells = state_s.shape[0]
    copies = [
        pltpu.make_async_copy(*pair, sems.at[k])
        for k, pair in enumerate(((mask_ref, mask_s), (state_ref, state_s), (cot_ref, cot_s)))
    ]
    for copy in copies:
        copy.start()
    copies[0].wait()
    length = jnp.max(jnp.sum(mask_s[...].astype(F32), axis=1, keepdims=True))
    below = jnp.full((sent_ref.shape[1] - cells, c), length, F32).astype(BF16)
    for copy in copies[1:]:
        copy.wait()
    for part in range(parts):
        sent_ref[part, :cells, :] = state_s[...]
        sent_ref[part, cells:, :] = below
        sent_cot_ref[part] = cot_s[...]


def add_grads(own_0, other_0, own_1, other_1, proj_ref, out_ref):
    width = proj_ref.shape[2]
    for u, (own, other) in enumerate(((own_0, other_0), (own_1, other_1))):
        total = own[...].astype(F32) + other[...].astype(F32)
        proj_ref[u] = total[:, :width]
        out_ref[u] = total[:, width:]


def crop_shards(
    groups,
    parts,
    pair_repr,
    pair_mask,
    cotangent,
    proj_weight,
    proj_bias,
    norm_gain,
    norm_shift,
    out_weight,
    out_bias,
):
    _, rows, n, c = pair_repr.shape
    h = out_weight.shape[1]
    width = proj_weight.shape[2]
    cells, pairs = rows * n, n * n
    plane = jax.ShapeDtypeStruct((pairs + 8, h), F32)
    narrow = jax.ShapeDtypeStruct((pairs, h), BF16)
    grads = jax.ShapeDtypeStruct((c, width + c), BF16)
    kept = (plane,) * 10 + (narrow,) * 2
    vmem = pl.BlockSpec(memory_space=pltpu.VMEM)
    smem = pl.BlockSpec(memory_space=pltpu.SMEM)
    main = pl.BlockSpec(memory_space=pltpu.HBM)
    params = pltpu.CompilerParams(vmem_limit_bytes=VMEM_BYTES)

    def scratch(array):
        return pltpu.VMEM(array.shape, array.dtype)

    def cost(planes):
        flops = 4 * pairs * width * c
        return pl.CostEstimate(
            flops=flops, bytes_accessed=planes * pairs * c * 4, transcendentals=0
        )

    index = lax.axis_index("dap").astype(jnp.int32)[None]
    sent, sent_cot = pl.pallas_call(
        prepare,
        out_shape=(
            jax.ShapeDtypeStruct((parts, cells + 16, c), BF16),
            jax.ShapeDtypeStruct((parts, cells, c), BF16),
        ),
        in_specs=[main] * 3,
        out_specs=(vmem, vmem),
        scratch_shapes=[
            pltpu.VMEM((cells, c), BF16),
            pltpu.VMEM((rows, n), jnp.int32),
            pltpu.VMEM((cells, c), BF16),
            pltpu.SemaphoreType.DMA((3,)),
        ],
        compiler_params=pltpu.CompilerParams(vmem_limit_bytes=PREPARE_BYTES),
        name="prepare",
    )(pair_repr.reshape(cells, c), pair_mask[0], cotangent.reshape(cells, c))
    state = lax.all_to_all(sent, "dap", split_axis=0, concat_axis=0, tiled=True)
    cot = lax.all_to_all(sent_cot, "dap", split_axis=0, concat_axis=0, tiled=True)

    held = pl.pallas_call(
        functools.partial(forward, n),
        out_shape=kept * 2,
        in_specs=[vmem] * 7,
        out_specs=(vmem,) * (2 * KEPT),
        scratch_shapes=[scratch(plane), scratch(narrow)],
        compiler_params=params,
        cost_estimate=cost(64),
        name="forward",
    )(state, proj_weight, proj_bias, norm_gain, norm_shift, out_weight, out_bias)

    up_1, grads_1 = pl.pallas_call(
        functools.partial(backward, n, 1),
        out_shape=(jax.ShapeDtypeStruct((pairs, c), F32), grads),
        in_specs=[vmem] * (4 + KEPT),
        out_specs=(vmem, vmem),
        scratch_shapes=[scratch(plane), scratch(narrow), pltpu.VMEM((pairs, width), BF16)]
        + [scratch(plane)],
        compiler_params=params,
        cost_estimate=cost(48),
        name="backward_second",
    )(cot, proj_weight, norm_gain, out_weight, *held[KEPT:])
    far = groups // 2
    others_1 = exchange(grads_1, "dp", groups, far)

    pair_grad, grads_0 = pl.pallas_call(
        functools.partial(backward, n, 0),
        out_shape=(jax.ShapeDtypeStruct((cells, c), BF16), grads),
        in_specs=[smem] + [vmem] * (4 + KEPT),
        out_specs=(vmem, vmem),
        scratch_shapes=[scratch(plane), scratch(narrow), pltpu.VMEM((pairs, width), BF16)],
        compiler_params=params,
        cost_estimate=cost(48),
        name="backward_first",
    )(index, up_1, proj_weight, norm_gain, out_weight, *held[:KEPT])

    step = 1
    while step < far:
        near_1 = add_narrow(grads_1, others_1)
        others_1 = exchange(near_1, "dp", groups, step)
        others_0 = exchange(grads_0, "dp", groups, step)
        grads_1, grads_0 = near_1, add_narrow(grads_0, others_0)
        step *= 2
    others_0 = exchange(grads_0, "dp", groups, far)

    proj_total, out_total = pl.pallas_call(
        add_grads,
        out_shape=(
            jax.ShapeDtypeStruct((2, c, width), F32),
            jax.ShapeDtypeStruct((2, h, c), F32),
        ),
        in_specs=[vmem] * 4,
        out_specs=(vmem, vmem),
        compiler_params=params,
        name="add_grads",
    )(grads_0, others_0, grads_1, others_1)
    return pair_grad.reshape(pair_repr.shape), proj_total, out_total


def layer_norm(values, gain_vec, shift_vec, norm_axis):
    mean_value = jnp.mean(values, axis=norm_axis, keepdims=True)
    centred = values - mean_value
    variance = jnp.mean(centred * centred, axis=norm_axis, keepdims=True)
    return centred * lax.rsqrt(variance + NORM_EPSILON) * gain_vec + shift_vec


def norm_pullback(values, gain_vec, shift_vec, norm_axis, upstream):
    _, pull_back = jax.vjp(
        lambda inner_value: layer_norm(inner_value, gain_vec, shift_vec, norm_axis), values
    )
    return pull_back(upstream)[0]


def edge_pair(edge_pre, cell_mask):
    left_edge = jax.nn.sigmoid(edge_pre[1]) * edge_pre[0] * cell_mask
    right_edge = jax.nn.sigmoid(edge_pre[3]) * edge_pre[2] * cell_mask
    return jnp.stack([left_edge, right_edge]).astype(jnp.bfloat16)


def edge_pullback(edge_pre, cell_mask, grad_pair):
    sig_left = jax.nn.sigmoid(edge_pre[1])
    sig_right = jax.nn.sigmoid(edge_pre[3])
    grad_left = grad_pair[0].astype(jnp.float32) * cell_mask
    grad_right = grad_pair[1].astype(jnp.float32) * cell_mask
    return jnp.stack(
        [
            grad_left * sig_left,
            grad_left * edge_pre[0] * sig_left * (1.0 - sig_left),
            grad_right * sig_right,
            grad_right * edge_pre[2] * sig_right * (1.0 - sig_right),
        ]
    ).astype(jnp.bfloat16)


def triangle(pair_edges, outgoing):
    if outgoing:
        einsum_form = "cik,cjk->cij"
    else:
        einsum_form = "cki,ckj->cij"
    return jnp.einsum(
        einsum_form, pair_edges[0], pair_edges[1], preferred_element_type=jnp.float32
    ).astype(jnp.bfloat16)


def triangle_pullback(pair_edges, grad_product, outgoing):
    left_edge = pair_edges[0]
    right_edge = pair_edges[1]
    if outgoing:
        grad_left = jnp.einsum(
            "cij,cjk->cik", grad_product, right_edge, preferred_element_type=jnp.float32
        )
        grad_right = jnp.einsum(
            "cij,cik->cjk", grad_product, left_edge, preferred_element_type=jnp.float32
        )
    else:
        grad_left = jnp.einsum(
            "ckj,cij->cki", right_edge, grad_product, preferred_element_type=jnp.float32
        )
        grad_right = jnp.einsum(
            "cki,cij->ckj", left_edge, grad_product, preferred_element_type=jnp.float32
        )
    return jnp.stack([grad_left, grad_right]).astype(jnp.bfloat16)


def update_weights(proj_weight, proj_bias, norm_gain, norm_shift, update, channels, hidden):
    w_edge = proj_weight[update, :, : 4 * hidden].reshape(channels, 4, hidden)
    w_gate = proj_weight[update, :, 4 * hidden :]
    bias_edge = proj_bias[update, : 4 * hidden].reshape(4, hidden, 1, 1)
    bias_gate = proj_bias[update, 4 * hidden :]
    gain_in = norm_gain[update, :channels]
    shift_in = norm_shift[update, :channels]
    gain_out = norm_gain[update, channels:][:, None, None]
    shift_out = norm_shift[update, channels:][:, None, None]
    return (w_edge, w_gate, bias_edge, bias_gate, gain_in, shift_in, gain_out, shift_out)


def shards(
    pair_repr,
    pair_mask,
    cotangent,
    proj_weight,
    proj_bias,
    norm_gain,
    norm_shift,
    out_weight,
    out_bias,
):
    channels = pair_repr.shape[3]
    hidden = out_weight.shape[1]
    pair_state = pair_repr[0]
    cell_mask = pair_mask[0].astype(jnp.float32)
    records = []
    for update in range(2):
        w_edge, w_gate, bias_edge, bias_gate, gain_in, shift_in, gain_out, shift_out = (
            update_weights(proj_weight, proj_bias, norm_gain, norm_shift, update, channels, hidden)
        )
        state_f = pair_state.astype(jnp.float32)
        normed = layer_norm(state_f, gain_in, shift_in, -1).astype(jnp.bfloat16)
        edge_pre = (
            jnp.einsum("rnc,cgh->ghrn", normed, w_edge, preferred_element_type=jnp.float32)
            + bias_edge
        )
        gate_pre = (
            jnp.einsum("rnc,cd->rnd", normed, w_gate, preferred_element_type=jnp.float32)
            + bias_gate
        )
        pair_edges = edge_pair(edge_pre, cell_mask)
        spread = lax.all_to_all(pair_edges, "dap", split_axis=1, concat_axis=2, tiled=True)
        product = lax.all_to_all(
            triangle(spread, update == 0), "dap", split_axis=1, concat_axis=0, tiled=True
        )
        mixed_norm = layer_norm(product.astype(jnp.float32), gain_out, shift_out, 0).astype(
            jnp.bfloat16
        )
        branch = (
            jnp.einsum(
                "hrn,hd->rnd", mixed_norm, out_weight[update], preferred_element_type=jnp.float32
            )
            + out_bias[update]
        )
        records.append(
            (state_f, normed, edge_pre, gate_pre, pair_edges, spread, product, mixed_norm, branch)
        )
        pair_state = (state_f + jax.nn.sigmoid(gate_pre) * branch).astype(jnp.bfloat16)
    upstream = cotangent[0].astype(jnp.float32)
    proj_grads = []
    out_grads = []
    for update in (1, 0):
        state_f, normed, edge_pre, gate_pre, pair_edges, spread, product, mixed_norm, branch = (
            records[update]
        )
        w_edge, w_gate, bias_edge, bias_gate, gain_in, shift_in, gain_out, shift_out = (
            update_weights(proj_weight, proj_bias, norm_gain, norm_shift, update, channels, hidden)
        )
        gate_value = jax.nn.sigmoid(gate_pre)
        grad_branch = (upstream * gate_value).astype(jnp.bfloat16)
        grad_gate = (upstream * branch * gate_value * (1.0 - gate_value)).astype(jnp.bfloat16)
        out_grad = jnp.einsum(
            "hrn,rnd->hd", mixed_norm, grad_branch, preferred_element_type=jnp.float32
        )
        grad_mixed = jnp.einsum(
            "rnd,hd->hrn", grad_branch, out_weight[update], preferred_element_type=jnp.float32
        )
        grad_product = norm_pullback(
            product.astype(jnp.float32), gain_out, shift_out, 0, grad_mixed
        ).astype(jnp.bfloat16)
        column_edges = spread
        column_grad = lax.all_to_all(
            grad_product[None], "dap", split_axis=1, concat_axis=2, tiled=True
        )[0]
        grad_pair = lax.all_to_all(
            triangle_pullback(column_edges, column_grad, update == 0),
            "dap",
            split_axis=2,
            concat_axis=1,
            tiled=True,
        )
        grad_edge = edge_pullback(edge_pre, cell_mask, grad_pair)
        edge_grad = jnp.einsum(
            "rnc,ghrn->cgh", normed, grad_edge, preferred_element_type=jnp.float32
        ).reshape(channels, 4 * hidden)
        gate_grad = jnp.einsum("rnc,rnd->cd", normed, grad_gate, preferred_element_type=jnp.float32)
        grad_normed = jnp.einsum(
            "ghrn,cgh->rnc", grad_edge, w_edge, preferred_element_type=jnp.float32
        )
        grad_normed = grad_normed + jnp.einsum(
            "rnd,cd->rnc", grad_gate, w_gate, preferred_element_type=jnp.float32
        )
        upstream = upstream + norm_pullback(state_f, gain_in, shift_in, -1, grad_normed)
        proj_part = jnp.concatenate([edge_grad, gate_grad], axis=1)
        proj_grads.append(proj_part)
        out_grads.append(out_grad)
    proj_total = jnp.stack(proj_grads[::-1])
    out_total = jnp.stack(out_grads[::-1])
    proj_total, out_total = lax.psum((proj_total, out_total), ("dp", "dap"))
    return (upstream.astype(jnp.bfloat16)[None], proj_total, out_total)


def solution(mesh):
    placed = (
        P("dp", "dap", None, None),
        P("dp", "dap", None),
        P("dp", "dap", None, None),
        P(),
        P(),
        P(),
        P(),
        P(),
        P(),
    )
    groups, parts = mesh.shape["dp"], mesh.shape["dap"]

    def program(*args):
        n, c = args[0].shape[2:]
        rows = n // parts
        fits = 20 * n * n * c * 4 <= CROP_BUDGET
        even = args[7].shape[1] == c and groups > 1 and groups & (groups - 1) == 0 and BLOCK_ROWS % rows == 0 and n % 16 == 0
        body = functools.partial(crop_shards, groups, parts) if fits and even else shards
        return spread_over(body)(*args)

    def spread_over(body):
        return jax.shard_map(
            body,
            mesh=mesh,
            in_specs=placed,
            out_specs=(P("dp", "dap", None, None), P(), P()),
            check_vma=False,
        )

    return program
```

```python
import functools

import jax
import jax.numpy as jnp
from jax import lax
from jax.experimental import pallas as pl
from jax.experimental.pallas import tpu as pltpu
from jax.sharding import PartitionSpec as P

NORM_EPSILON = 1e-05
VMEM_BYTES = 24 * 1024 * 1024
PREPARE_BYTES = 63 * 1024 * 1024
CROP_BUDGET = 32 * 1024 * 1024
BLOCK_ROWS = 8
KEPT = 12
F32 = jnp.float32
BF16 = jnp.bfloat16


def sigmoid(x):
    return 0.5 * jnp.tanh(0.5 * x) + 0.5


def dot(a, b, dims=((1,), (0,))):
    return lax.dot_general(a, b, (dims, ((), ())), preferred_element_type=F32)


def norm_parts(x):
    centred = x - jnp.mean(x, axis=-1, keepdims=True)
    rstd = lax.rsqrt(jnp.mean(centred * centred, axis=-1, keepdims=True) + NORM_EPSILON)
    return centred * rstd, rstd


def norm_vjp(x_hat, rstd, grad):
    mean_grad = jnp.mean(grad, axis=-1, keepdims=True)
    mean_prod = jnp.mean(grad * x_hat, axis=-1, keepdims=True)
    return rstd * (grad - mean_grad - x_hat * mean_prod)


def pair_mask_block(length, first_row, rows, n, lanes):
    shape = (rows, n, lanes)
    i = lax.broadcasted_iota(jnp.int32, shape, 0) + first_row
    j = lax.broadcasted_iota(jnp.int32, shape, 1)
    inside = jnp.where((i < length) & (j < length), 1.0, 0.0)
    return inside.reshape(rows * n, lanes)


def project(x, mask, u, w, b, gain, shift):
    c = x.shape[1]
    x_hat, rstd = norm_parts(x)
    normed = (x_hat * gain[u : u + 1, :c] + shift[u : u + 1, :c]).astype(BF16)
    pre = dot(normed, w[u]) + b[u : u + 1, :]
    h = (pre.shape[1] - c) // 4
    s_left = sigmoid(pre[:, h : 2 * h]) * mask
    s_right = sigmoid(pre[:, 3 * h : 4 * h]) * mask
    left = s_left * pre[:, :h]
    right = s_right * pre[:, 2 * h : 3 * h]
    gate = sigmoid(pre[:, 4 * h :])
    return x_hat, rstd, normed, s_left, s_right, left, right, gate


def mix(product, u, c, gain, shift, w_out, b_out):
    p_hat, p_rstd = norm_parts(product.astype(F32))
    mixed = (p_hat * gain[u : u + 1, c:] + shift[u : u + 1, c:]).astype(BF16)
    branch = dot(mixed, w_out[u]) + b_out[u : u + 1, :]
    return p_hat, p_rstd, mixed, branch


def unmix(up, gate, branch, p_hat, p_rstd, u, c, gain, w_out):
    d_branch = up * gate
    d_gate = (d_branch * branch * (1.0 - gate)).astype(BF16)
    d_branch = d_branch.astype(BF16)
    d_mixed = dot(d_branch, w_out[u], ((1,), (1,))) * gain[u : u + 1, c:]
    return d_branch, d_gate, norm_vjp(p_hat, p_rstd, d_mixed)


def contract(n, first, row_of, x, y):
    lanes = y.shape[1]
    tiles = (n // 8, 8, lanes)

    def step(e, totals):
        block = y[pl.ds(pl.multiple_of(e * n, n), n), :].reshape(tiles)
        return tuple(
            totals[a] + x[pl.ds(row_of(first + a, e), 8, stride=0), :][None] * block
            for a in range(BLOCK_ROWS)
        )

    zero = jnp.zeros(tiles, F32)
    totals = lax.fori_loop(0, n, step, (zero,) * BLOCK_ROWS, unroll=4)
    return jnp.stack(totals).reshape(BLOCK_ROWS * n, lanes)


def edge_grads(d_left, d_right, s_left, s_right, left, right):
    return (
        (d_left * s_left).astype(BF16),
        (d_left * left * (1.0 - s_left)).astype(BF16),
        (d_right * s_right).astype(BF16),
        (d_right * right * (1.0 - s_right)).astype(BF16),
    )


def crop_length(state_ref, cells):
    return jnp.max(state_ref[:, 2 * cells :, :].astype(F32)).astype(jnp.int32)


def joined(ref, first, count, cells, place):
    span = slice(place * cells, (place + 1) * cells)
    return jnp.concatenate([ref[first + q, span, :] for q in range(count)], axis=0)


def forward(n, state_ref, w, b, gain, shift, w_out, b_out, *refs):
    kept, (right_t_s, next_s) = (refs[:KEPT], refs[KEPT : 2 * KEPT]), refs[2 * KEPT :]
    parts, _, c = state_ref.shape
    rows = n // parts
    cells = rows * n
    length = crop_length(state_ref, cells)
    per = BLOCK_ROWS // rows
    blocks = n // BLOCK_ROWS

    for u in range(2):
        (left_s, right_s, s_left_s, s_right_s, gate_s, hat_s, rstd_s) = kept[u][:7]
        (p_hat_s, p_rstd_s, branch_s, normed_s, mixed_s) = kept[u][7:]

        @pl.loop(0, blocks)
        def _(t):
            first = t * BLOCK_ROWS
            here = pl.ds(pl.multiple_of(first * n, BLOCK_ROWS * n), BLOCK_ROWS * n)
            x = joined(state_ref, t * per, per, cells, 0) if u == 0 else next_s[here, :]
            mask = pair_mask_block(length, first, BLOCK_ROWS, n, c)
            x_hat, rstd, normed, s_left, s_right, left, right, gate = project(
                x.astype(F32), mask, u, w, b, gain, shift
            )
            left_s[here, :] = left
            right_s[here, :] = right
            s_left_s[here, :] = s_left
            s_right_s[here, :] = s_right
            gate_s[here, :] = gate
            hat_s[here, :] = x_hat
            rstd_s[here, :] = jnp.broadcast_to(rstd, x_hat.shape)
            normed_s[here, :] = normed
            if u == 0:
                for r in range(BLOCK_ROWS):
                    right_t_s[pl.ds(first + r, n, stride=n), :] = right[r * n : (r + 1) * n]

        @pl.loop(0, blocks)
        def _(t):
            first = t * BLOCK_ROWS
            here = pl.ds(pl.multiple_of(first * n, BLOCK_ROWS * n), BLOCK_ROWS * n)
            if u == 0:
                product = contract(n, first, lambda i, k: i * n + k, left_s, right_t_s)
            else:
                product = contract(n, first, lambda i, k: k * n + i, left_s, right_s)
            p_hat, p_rstd, mixed, branch = mix(
                product.astype(BF16), u, c, gain, shift, w_out, b_out
            )
            p_hat_s[here, :] = p_hat
            p_rstd_s[here, :] = jnp.broadcast_to(p_rstd, p_hat.shape)
            mixed_s[here, :] = mixed
            branch_s[here, :] = branch
            if u == 0:
                x = joined(state_ref, t * per, per, cells, 0).astype(F32)
                next_s[here, :] = (x + gate_s[here, :] * branch).astype(BF16)


def weight_grads(normed_s, d_pre_s, mixed_s, d_branch_s, grads_ref):
    width = d_pre_s.shape[1]
    grads_ref[:, :width] = dot(normed_s[...], d_pre_s[...], ((0,), (0,))).astype(BF16)
    grads_ref[:, width:] = dot(mixed_s[...], d_branch_s[...], ((0,), (0,))).astype(BF16)


def backward(n, u, *refs):
    if u == 0:
        index_ref, refs = refs[0], refs[1:]
    up_in_ref, w, gain, w_out = refs[:4]
    (left_s, right_s, s_left_s, s_right_s, gate_s, hat_s, rstd_s) = refs[4:11]
    (p_hat_s, p_rstd_s, branch_s, normed_s, mixed_s) = refs[11 : 4 + KEPT]
    up_ref, grads_ref, d_product_s, d_branch_s, d_pre_s = refs[4 + KEPT : 9 + KEPT]
    c, h = w.shape[1], left_s.shape[1]
    blocks = n // BLOCK_ROWS

    def upstream(t, here):
        if u == 0:
            return up_in_ref[here, :]
        rows = n // up_in_ref.shape[0]
        per = BLOCK_ROWS // rows
        return joined(up_in_ref, t * per, per, rows * n, 1).astype(F32)

    def input_pullback(here, up):
        d_normed = dot(d_pre_s[here, :], w[u], ((1,), (1,))) * gain[u : u + 1, :c]
        return up + norm_vjp(hat_s[here, :], rstd_s[here, :], d_normed)

    @pl.loop(0, blocks)
    def _(t):
        first = t * BLOCK_ROWS
        here = pl.ds(pl.multiple_of(first * n, BLOCK_ROWS * n), BLOCK_ROWS * n)
        d_branch, d_gate, d_product = unmix(
            upstream(t, here),
            gate_s[here, :],
            branch_s[here, :],
            p_hat_s[here, :],
            p_rstd_s[here, :],
            u,
            c,
            gain,
            w_out,
        )
        d_branch_s[here, :] = d_branch
        d_pre_s[here, 4 * h :] = d_gate
        d_product_s[here, :] = d_product
        if u == 1:
            d_product_t_s = refs[9 + KEPT]
            for r in range(BLOCK_ROWS):
                d_product_t_s[pl.ds(first + r, n, stride=n), :] = d_product[r * n : (r + 1) * n]

    @pl.loop(0, blocks)
    def _(t):
        first = t * BLOCK_ROWS
        here = pl.ds(pl.multiple_of(first * n, BLOCK_ROWS * n), BLOCK_ROWS * n)
        if u == 1:
            d_left = contract(n, first, lambda k, j: k * n + j, right_s, refs[9 + KEPT])
            d_right = contract(n, first, lambda k, i: k * n + i, left_s, d_product_s)
        else:
            d_left = contract(n, first, lambda i, j: i * n + j, d_product_s, right_s)
            d_right = contract(n, first, lambda j, i: i * n + j, d_product_s, left_s)
        grads = edge_grads(
            d_left, d_right, s_left_s[here, :], s_right_s[here, :], left_s[here, :], right_s[here, :]
        )
        for g in range(4):
            d_pre_s[here, g * h : (g + 1) * h] = grads[g]
        if u == 1:
            up_ref[here, :] = input_pullback(here, upstream(t, here))

    if u == 0:
        cells = up_ref.shape[0]
        own = pl.ds(pl.multiple_of(index_ref[0] * cells, cells), cells)
        up_ref[...] = input_pullback(own, up_in_ref[own, :]).astype(BF16)
    weight_grads(normed_s, d_pre_s, mixed_s, d_branch_s, grads_ref)


def exchange(value, axis, size, step):
    return lax.ppermute(value, axis, [(d, d ^ step) for d in range(size)])


def add_narrow(a, b):
    return (a.astype(F32) + b.astype(F32)).astype(BF16)


def prepare(state_ref, mask_ref, cot_ref, sent_ref, state_s, mask_s, cot_s, sems):
    parts, _, c = sent_ref.shape
    cells = state_s.shape[0]
    copies = [
        pltpu.make_async_copy(*pair, sems.at[k])
        for k, pair in enumerate(((mask_ref, mask_s), (state_ref, state_s), (cot_ref, cot_s)))
    ]
    for copy in copies:
        copy.start()
    copies[0].wait()
    length = jnp.max(jnp.sum(mask_s[...].astype(F32), axis=1, keepdims=True))
    below = jnp.full((sent_ref.shape[1] - 2 * cells, c), length, F32).astype(BF16)
    for copy in copies[1:]:
        copy.wait()
    for part in range(parts):
        sent_ref[part, :cells, :] = state_s[...]
        sent_ref[part, cells : 2 * cells, :] = cot_s[...]
        sent_ref[part, 2 * cells :, :] = below


def add_grads(own_0, other_0, own_1, other_1, proj_ref, out_ref):
    width = proj_ref.shape[2]
    for u, (own, other) in enumerate(((own_0, other_0), (own_1, other_1))):
        total = own[...].astype(F32) + other[...].astype(F32)
        proj_ref[u] = total[:, :width]
        out_ref[u] = total[:, width:]


def crop_shards(
    groups,
    parts,
    pair_repr,
    pair_mask,
    cotangent,
    proj_weight,
    proj_bias,
    norm_gain,
    norm_shift,
    out_weight,
    out_bias,
):
    _, rows, n, c = pair_repr.shape
    h = out_weight.shape[1]
    width = proj_weight.shape[2]
    cells, pairs = rows * n, n * n
    plane = jax.ShapeDtypeStruct((pairs + 8, h), F32)
    narrow = jax.ShapeDtypeStruct((pairs, h), BF16)
    grads = jax.ShapeDtypeStruct((c, width + c), BF16)
    kept = (plane,) * 10 + (narrow,) * 2
    vmem = pl.BlockSpec(memory_space=pltpu.VMEM)
    smem = pl.BlockSpec(memory_space=pltpu.SMEM)
    main = pl.BlockSpec(memory_space=pltpu.HBM)
    params = pltpu.CompilerParams(vmem_limit_bytes=VMEM_BYTES)

    def scratch(array):
        return pltpu.VMEM(array.shape, array.dtype)

    def cost(planes):
        flops = 4 * pairs * width * c
        return pl.CostEstimate(
            flops=flops, bytes_accessed=planes * pairs * c * 4, transcendentals=0
        )

    index = lax.axis_index("dap").astype(jnp.int32)[None]
    sent = pl.pallas_call(
        prepare,
        out_shape=jax.ShapeDtypeStruct((parts, 2 * cells + 16, c), BF16),
        in_specs=[main] * 3,
        out_specs=vmem,
        scratch_shapes=[
            pltpu.VMEM((cells, c), BF16),
            pltpu.VMEM((rows, n), jnp.int32),
            pltpu.VMEM((cells, c), BF16),
            pltpu.SemaphoreType.DMA((3,)),
        ],
        compiler_params=pltpu.CompilerParams(vmem_limit_bytes=PREPARE_BYTES),
        name="prepare",
    )(pair_repr.reshape(cells, c), pair_mask[0], cotangent.reshape(cells, c))
    state = lax.all_to_all(sent, "dap", split_axis=0, concat_axis=0, tiled=True)

    held = pl.pallas_call(
        functools.partial(forward, n),
        out_shape=kept * 2,
        in_specs=[vmem] * 7,
        out_specs=(vmem,) * (2 * KEPT),
        scratch_shapes=[scratch(plane), scratch(narrow)],
        compiler_params=params,
        cost_estimate=cost(64),
        name="forward",
    )(state, proj_weight, proj_bias, norm_gain, norm_shift, out_weight, out_bias)

    up_1, grads_1 = pl.pallas_call(
        functools.partial(backward, n, 1),
        out_shape=(jax.ShapeDtypeStruct((pairs, c), F32), grads),
        in_specs=[vmem] * (4 + KEPT),
        out_specs=(vmem, vmem),
        scratch_shapes=[scratch(plane), scratch(narrow), pltpu.VMEM((pairs, width), BF16)]
        + [scratch(plane)],
        compiler_params=params,
        cost_estimate=cost(48),
        name="backward_second",
    )(state, proj_weight, norm_gain, out_weight, *held[KEPT:])
    far = groups // 2
    others_1 = exchange(grads_1, "dp", groups, far)

    pair_grad, grads_0 = pl.pallas_call(
        functools.partial(backward, n, 0),
        out_shape=(jax.ShapeDtypeStruct((cells, c), BF16), grads),
        in_specs=[smem] + [vmem] * (4 + KEPT),
        out_specs=(vmem, vmem),
        scratch_shapes=[scratch(plane), scratch(narrow), pltpu.VMEM((pairs, width), BF16)],
        compiler_params=params,
        cost_estimate=cost(48),
        name="backward_first",
    )(index, up_1, proj_weight, norm_gain, out_weight, *held[:KEPT])

    step = 1
    while step < far:
        near_1 = add_narrow(grads_1, others_1)
        others_1 = exchange(near_1, "dp", groups, step)
        others_0 = exchange(grads_0, "dp", groups, step)
        grads_1, grads_0 = near_1, add_narrow(grads_0, others_0)
        step *= 2
    others_0 = exchange(grads_0, "dp", groups, far)

    proj_total, out_total = pl.pallas_call(
        add_grads,
        out_shape=(
            jax.ShapeDtypeStruct((2, c, width), F32),
            jax.ShapeDtypeStruct((2, h, c), F32),
        ),
        in_specs=[vmem] * 4,
        out_specs=(vmem, vmem),
        compiler_params=params,
        name="add_grads",
    )(grads_0, others_0, grads_1, others_1)
    return pair_grad.reshape(pair_repr.shape), proj_total, out_total


def layer_norm(values, gain_vec, shift_vec, norm_axis):
    mean_value = jnp.mean(values, axis=norm_axis, keepdims=True)
    centred = values - mean_value
    variance = jnp.mean(centred * centred, axis=norm_axis, keepdims=True)
    return centred * lax.rsqrt(variance + NORM_EPSILON) * gain_vec + shift_vec


def norm_pullback(values, gain_vec, shift_vec, norm_axis, upstream):
    _, pull_back = jax.vjp(
        lambda inner_value: layer_norm(inner_value, gain_vec, shift_vec, norm_axis), values
    )
    return pull_back(upstream)[0]


def edge_pair(edge_pre, cell_mask):
    left_edge = jax.nn.sigmoid(edge_pre[1]) * edge_pre[0] * cell_mask
    right_edge = jax.nn.sigmoid(edge_pre[3]) * edge_pre[2] * cell_mask
    return jnp.stack([left_edge, right_edge]).astype(jnp.bfloat16)


def edge_pullback(edge_pre, cell_mask, grad_pair):
    sig_left = jax.nn.sigmoid(edge_pre[1])
    sig_right = jax.nn.sigmoid(edge_pre[3])
    grad_left = grad_pair[0].astype(jnp.float32) * cell_mask
    grad_right = grad_pair[1].astype(jnp.float32) * cell_mask
    return jnp.stack(
        [
            grad_left * sig_left,
            grad_left * edge_pre[0] * sig_left * (1.0 - sig_left),
            grad_right * sig_right,
            grad_right * edge_pre[2] * sig_right * (1.0 - sig_right),
        ]
    ).astype(jnp.bfloat16)


def triangle(pair_edges, outgoing):
    if outgoing:
        einsum_form = "cik,cjk->cij"
    else:
        einsum_form = "cki,ckj->cij"
    return jnp.einsum(
        einsum_form, pair_edges[0], pair_edges[1], preferred_element_type=jnp.float32
    ).astype(jnp.bfloat16)


def triangle_pullback(pair_edges, grad_product, outgoing):
    left_edge = pair_edges[0]
    right_edge = pair_edges[1]
    if outgoing:
        grad_left = jnp.einsum(
            "cij,cjk->cik", grad_product, right_edge, preferred_element_type=jnp.float32
        )
        grad_right = jnp.einsum(
            "cij,cik->cjk", grad_product, left_edge, preferred_element_type=jnp.float32
        )
    else:
        grad_left = jnp.einsum(
            "ckj,cij->cki", right_edge, grad_product, preferred_element_type=jnp.float32
        )
        grad_right = jnp.einsum(
            "cki,cij->ckj", left_edge, grad_product, preferred_element_type=jnp.float32
        )
    return jnp.stack([grad_left, grad_right]).astype(jnp.bfloat16)


def update_weights(proj_weight, proj_bias, norm_gain, norm_shift, update, channels, hidden):
    w_edge = proj_weight[update, :, : 4 * hidden].reshape(channels, 4, hidden)
    w_gate = proj_weight[update, :, 4 * hidden :]
    bias_edge = proj_bias[update, : 4 * hidden].reshape(4, hidden, 1, 1)
    bias_gate = proj_bias[update, 4 * hidden :]
    gain_in = norm_gain[update, :channels]
    shift_in = norm_shift[update, :channels]
    gain_out = norm_gain[update, channels:][:, None, None]
    shift_out = norm_shift[update, channels:][:, None, None]
    return (w_edge, w_gate, bias_edge, bias_gate, gain_in, shift_in, gain_out, shift_out)


def shards(
    pair_repr,
    pair_mask,
    cotangent,
    proj_weight,
    proj_bias,
    norm_gain,
    norm_shift,
    out_weight,
    out_bias,
):
    channels = pair_repr.shape[3]
    hidden = out_weight.shape[1]
    pair_state = pair_repr[0]
    cell_mask = pair_mask[0].astype(jnp.float32)
    records = []
    for update in range(2):
        w_edge, w_gate, bias_edge, bias_gate, gain_in, shift_in, gain_out, shift_out = (
            update_weights(proj_weight, proj_bias, norm_gain, norm_shift, update, channels, hidden)
        )
        state_f = pair_state.astype(jnp.float32)
        normed = layer_norm(state_f, gain_in, shift_in, -1).astype(jnp.bfloat16)
        edge_pre = (
            jnp.einsum("rnc,cgh->ghrn", normed, w_edge, preferred_element_type=jnp.float32)
            + bias_edge
        )
        gate_pre = (
            jnp.einsum("rnc,cd->rnd", normed, w_gate, preferred_element_type=jnp.float32)
            + bias_gate
        )
        pair_edges = edge_pair(edge_pre, cell_mask)
        spread = lax.all_to_all(pair_edges, "dap", split_axis=1, concat_axis=2, tiled=True)
        product = lax.all_to_all(
            triangle(spread, update == 0), "dap", split_axis=1, concat_axis=0, tiled=True
        )
        mixed_norm = layer_norm(product.astype(jnp.float32), gain_out, shift_out, 0).astype(
            jnp.bfloat16
        )
        branch = (
            jnp.einsum(
                "hrn,hd->rnd", mixed_norm, out_weight[update], preferred_element_type=jnp.float32
            )
            + out_bias[update]
        )
        records.append(
            (state_f, normed, edge_pre, gate_pre, pair_edges, spread, product, mixed_norm, branch)
        )
        pair_state = (state_f + jax.nn.sigmoid(gate_pre) * branch).astype(jnp.bfloat16)
    upstream = cotangent[0].astype(jnp.float32)
    proj_grads = []
    out_grads = []
    for update in (1, 0):
        state_f, normed, edge_pre, gate_pre, pair_edges, spread, product, mixed_norm, branch = (
            records[update]
        )
        w_edge, w_gate, bias_edge, bias_gate, gain_in, shift_in, gain_out, shift_out = (
            update_weights(proj_weight, proj_bias, norm_gain, norm_shift, update, channels, hidden)
        )
        gate_value = jax.nn.sigmoid(gate_pre)
        grad_branch = (upstream * gate_value).astype(jnp.bfloat16)
        grad_gate = (upstream * branch * gate_value * (1.0 - gate_value)).astype(jnp.bfloat16)
        out_grad = jnp.einsum(
            "hrn,rnd->hd", mixed_norm, grad_branch, preferred_element_type=jnp.float32
        )
        grad_mixed = jnp.einsum(
            "rnd,hd->hrn", grad_branch, out_weight[update], preferred_element_type=jnp.float32
        )
        grad_product = norm_pullback(
            product.astype(jnp.float32), gain_out, shift_out, 0, grad_mixed
        ).astype(jnp.bfloat16)
        column_edges = spread
        column_grad = lax.all_to_all(
            grad_product[None], "dap", split_axis=1, concat_axis=2, tiled=True
        )[0]
        grad_pair = lax.all_to_all(
            triangle_pullback(column_edges, column_grad, update == 0),
            "dap",
            split_axis=2,
            concat_axis=1,
            tiled=True,
        )
        grad_edge = edge_pullback(edge_pre, cell_mask, grad_pair)
        edge_grad = jnp.einsum(
            "rnc,ghrn->cgh", normed, grad_edge, preferred_element_type=jnp.float32
        ).reshape(channels, 4 * hidden)
        gate_grad = jnp.einsum("rnc,rnd->cd", normed, grad_gate, preferred_element_type=jnp.float32)
        grad_normed = jnp.einsum(
            "ghrn,cgh->rnc", grad_edge, w_edge, preferred_element_type=jnp.float32
        )
        grad_normed = grad_normed + jnp.einsum(
            "rnd,cd->rnc", grad_gate, w_gate, preferred_element_type=jnp.float32
        )
        upstream = upstream + norm_pullback(state_f, gain_in, shift_in, -1, grad_normed)
        proj_part = jnp.concatenate([edge_grad, gate_grad], axis=1)
        proj_grads.append(proj_part)
        out_grads.append(out_grad)
    proj_total = jnp.stack(proj_grads[::-1])
    out_total = jnp.stack(out_grads[::-1])
    proj_total, out_total = lax.psum((proj_total, out_total), ("dp", "dap"))
    return (upstream.astype(jnp.bfloat16)[None], proj_total, out_total)


def solution(mesh):
    placed = (
        P("dp", "dap", None, None),
        P("dp", "dap", None),
        P("dp", "dap", None, None),
        P(),
        P(),
        P(),
        P(),
        P(),
        P(),
    )
    groups, parts = mesh.shape["dp"], mesh.shape["dap"]

    def program(*args):
        n, c = args[0].shape[2:]
        rows = n // parts
        fits = 20 * n * n * c * 4 <= CROP_BUDGET
        even = args[7].shape[1] == c and groups > 1 and groups & (groups - 1) == 0 and BLOCK_ROWS % rows == 0 and n % 16 == 0
        body = functools.partial(crop_shards, groups, parts) if fits and even else shards
        return spread_over(body)(*args)

    def spread_over(body):
        return jax.shard_map(
            body,
            mesh=mesh,
            in_specs=placed,
            out_specs=(P("dp", "dap", None, None), P(), P()),
            check_vma=False,
        )

    return program
```

```python
import functools

import jax
import jax.numpy as jnp
from jax import lax
from jax.experimental import pallas as pl
from jax.experimental.pallas import tpu as pltpu
from jax.sharding import PartitionSpec as P

NORM_EPSILON = 1e-05
VMEM_BYTES = 16 * 1024 * 1024
PREPARE_BYTES = 63 * 1024 * 1024
CROP_BUDGET = 32 * 1024 * 1024
BLOCK_ROWS = 8
KEPT = 12
F32 = jnp.float32
BF16 = jnp.bfloat16


def sigmoid(x):
    return 0.5 * jnp.tanh(0.5 * x) + 0.5


def dot(a, b, dims=((1,), (0,))):
    return lax.dot_general(a, b, (dims, ((), ())), preferred_element_type=F32)


def norm_parts(x):
    centred = x - jnp.mean(x, axis=-1, keepdims=True)
    rstd = lax.rsqrt(jnp.mean(centred * centred, axis=-1, keepdims=True) + NORM_EPSILON)
    return centred * rstd, rstd


def norm_vjp(x_hat, rstd, grad):
    mean_grad = jnp.mean(grad, axis=-1, keepdims=True)
    mean_prod = jnp.mean(grad * x_hat, axis=-1, keepdims=True)
    return rstd * (grad - mean_grad - x_hat * mean_prod)


def pair_mask_block(length, first_row, rows, n, lanes):
    shape = (rows, n, lanes)
    i = lax.broadcasted_iota(jnp.int32, shape, 0) + first_row
    j = lax.broadcasted_iota(jnp.int32, shape, 1)
    inside = jnp.where((i < length) & (j < length), 1.0, 0.0)
    return inside.reshape(rows * n, lanes)


def project(x, mask, u, w, b, gain, shift):
    c = x.shape[1]
    x_hat, rstd = norm_parts(x)
    normed = (x_hat * gain[u : u + 1, :c] + shift[u : u + 1, :c]).astype(BF16)
    pre = dot(normed, w[u]) + b[u : u + 1, :]
    h = (pre.shape[1] - c) // 4
    s_left = sigmoid(pre[:, h : 2 * h]) * mask
    s_right = sigmoid(pre[:, 3 * h : 4 * h]) * mask
    left = s_left * pre[:, :h]
    right = s_right * pre[:, 2 * h : 3 * h]
    gate = sigmoid(pre[:, 4 * h :])
    return x_hat, rstd, normed, s_left, s_right, left, right, gate


def mix(product, u, c, gain, shift, w_out, b_out):
    p_hat, p_rstd = norm_parts(product.astype(F32))
    mixed = (p_hat * gain[u : u + 1, c:] + shift[u : u + 1, c:]).astype(BF16)
    branch = dot(mixed, w_out[u]) + b_out[u : u + 1, :]
    return p_hat, p_rstd, mixed, branch


def unmix(up, gate, branch, p_hat, p_rstd, u, c, gain, w_out):
    d_branch = up * gate
    d_gate = (d_branch * branch * (1.0 - gate)).astype(BF16)
    d_branch = d_branch.astype(BF16)
    d_mixed = dot(d_branch, w_out[u], ((1,), (1,))) * gain[u : u + 1, c:]
    return d_branch, d_gate, norm_vjp(p_hat, p_rstd, d_mixed)


def contract(n, first, row_of, x, y):
    lanes = y.shape[1]
    tiles = (n // 8, 8, lanes)

    def step(e, totals):
        block = y[pl.ds(pl.multiple_of(e * n, n), n), :].reshape(tiles)
        return tuple(
            totals[a] + x[pl.ds(row_of(first + a, e), 8, stride=0), :][None] * block
            for a in range(BLOCK_ROWS)
        )

    zero = jnp.zeros(tiles, F32)
    totals = lax.fori_loop(0, n, step, (zero,) * BLOCK_ROWS, unroll=4)
    return jnp.stack(totals).reshape(BLOCK_ROWS * n, lanes)


def edge_grads(d_left, d_right, s_left, s_right, left, right):
    return (
        (d_left * s_left).astype(BF16),
        (d_left * left * (1.0 - s_left)).astype(BF16),
        (d_right * s_right).astype(BF16),
        (d_right * right * (1.0 - s_right)).astype(BF16),
    )


def crop_length(state_ref, cells):
    return jnp.max(state_ref[:, 2 * cells :, :].astype(F32)).astype(jnp.int32)


def joined(ref, first, count, cells, place):
    span = slice(place * cells, (place + 1) * cells)
    return jnp.concatenate([ref[first + q, span, :] for q in range(count)], axis=0)


def forward(n, state_ref, w, b, gain, shift, w_out, b_out, *refs):
    kept, (right_t_s, next_s) = (refs[:KEPT], refs[KEPT : 2 * KEPT]), refs[2 * KEPT :]
    parts, _, c = state_ref.shape
    rows = n // parts
    cells = rows * n
    length = crop_length(state_ref, cells)
    per = BLOCK_ROWS // rows
    blocks = n // BLOCK_ROWS

    for u in range(2):
        (left_s, right_s, s_left_s, s_right_s, gate_s, hat_s, rstd_s) = kept[u][:7]
        (p_hat_s, p_rstd_s, branch_s, normed_s, mixed_s) = kept[u][7:]

        @pl.loop(0, blocks)
        def _(t):
            first = t * BLOCK_ROWS
            here = pl.ds(pl.multiple_of(first * n, BLOCK_ROWS * n), BLOCK_ROWS * n)
            x = joined(state_ref, t * per, per, cells, 0) if u == 0 else next_s[here, :]
            mask = pair_mask_block(length, first, BLOCK_ROWS, n, c)
            x_hat, rstd, normed, s_left, s_right, left, right, gate = project(
                x.astype(F32), mask, u, w, b, gain, shift
            )
            left_s[here, :] = left
            right_s[here, :] = right
            s_left_s[here, :] = s_left
            s_right_s[here, :] = s_right
            gate_s[here, :] = gate
            hat_s[here, :] = x_hat
            rstd_s[here, :] = jnp.broadcast_to(rstd, x_hat.shape)
            normed_s[here, :] = normed
            if u == 0:
                for r in range(BLOCK_ROWS):
                    right_t_s[pl.ds(first + r, n, stride=n), :] = right[r * n : (r + 1) * n]

        @pl.loop(0, blocks)
        def _(t):
            first = t * BLOCK_ROWS
            here = pl.ds(pl.multiple_of(first * n, BLOCK_ROWS * n), BLOCK_ROWS * n)
            if u == 0:
                product = contract(n, first, lambda i, k: i * n + k, left_s, right_t_s)
            else:
                product = contract(n, first, lambda i, k: k * n + i, left_s, right_s)
            p_hat, p_rstd, mixed, branch = mix(
                product.astype(BF16), u, c, gain, shift, w_out, b_out
            )
            p_hat_s[here, :] = p_hat
            p_rstd_s[here, :] = jnp.broadcast_to(p_rstd, p_hat.shape)
            mixed_s[here, :] = mixed
            branch_s[here, :] = branch
            if u == 0:
                x = joined(state_ref, t * per, per, cells, 0).astype(F32)
                next_s[here, :] = (x + gate_s[here, :] * branch).astype(BF16)


def weight_grads(normed_s, d_pre_s, mixed_s, d_branch_s, grads_ref):
    width = d_pre_s.shape[1]
    grads_ref[:, :width] = dot(normed_s[...], d_pre_s[...], ((0,), (0,))).astype(BF16)
    grads_ref[:, width:] = dot(mixed_s[...], d_branch_s[...], ((0,), (0,))).astype(BF16)


def backward(n, u, *refs):
    if u == 0:
        index_ref, refs = refs[0], refs[1:]
    up_in_ref, w, gain, w_out = refs[:4]
    (left_s, right_s, s_left_s, s_right_s, gate_s, hat_s, rstd_s) = refs[4:11]
    (p_hat_s, p_rstd_s, branch_s, normed_s, mixed_s) = refs[11 : 4 + KEPT]
    up_ref, grads_ref, d_product_s, d_branch_s, d_pre_s = refs[4 + KEPT : 9 + KEPT]
    c, h = w.shape[1], left_s.shape[1]
    blocks = n // BLOCK_ROWS

    def upstream(t, here):
        if u == 0:
            return up_in_ref[here, :]
        rows = n // up_in_ref.shape[0]
        per = BLOCK_ROWS // rows
        return joined(up_in_ref, t * per, per, rows * n, 1).astype(F32)

    def input_pullback(here, up):
        d_normed = dot(d_pre_s[here, :], w[u], ((1,), (1,))) * gain[u : u + 1, :c]
        return up + norm_vjp(hat_s[here, :], rstd_s[here, :], d_normed)

    @pl.loop(0, blocks)
    def _(t):
        first = t * BLOCK_ROWS
        here = pl.ds(pl.multiple_of(first * n, BLOCK_ROWS * n), BLOCK_ROWS * n)
        d_branch, d_gate, d_product = unmix(
            upstream(t, here),
            gate_s[here, :],
            branch_s[here, :],
            p_hat_s[here, :],
            p_rstd_s[here, :],
            u,
            c,
            gain,
            w_out,
        )
        d_branch_s[here, :] = d_branch
        d_pre_s[here, 4 * h :] = d_gate
        d_product_s[here, :] = d_product
        if u == 1:
            d_product_t_s = refs[9 + KEPT]
            for r in range(BLOCK_ROWS):
                d_product_t_s[pl.ds(first + r, n, stride=n), :] = d_product[r * n : (r + 1) * n]

    @pl.loop(0, blocks)
    def _(t):
        first = t * BLOCK_ROWS
        here = pl.ds(pl.multiple_of(first * n, BLOCK_ROWS * n), BLOCK_ROWS * n)
        if u == 1:
            d_left = contract(n, first, lambda k, j: k * n + j, right_s, refs[9 + KEPT])
            d_right = contract(n, first, lambda k, i: k * n + i, left_s, d_product_s)
        else:
            d_left = contract(n, first, lambda i, j: i * n + j, d_product_s, right_s)
            d_right = contract(n, first, lambda j, i: i * n + j, d_product_s, left_s)
        grads = edge_grads(
            d_left, d_right, s_left_s[here, :], s_right_s[here, :], left_s[here, :], right_s[here, :]
        )
        for g in range(4):
            d_pre_s[here, g * h : (g + 1) * h] = grads[g]
        if u == 1:
            up_ref[here, :] = input_pullback(here, upstream(t, here))

    if u == 0:
        cells = up_ref.shape[0]
        own = pl.ds(pl.multiple_of(index_ref[0] * cells, cells), cells)
        up_ref[...] = input_pullback(own, up_in_ref[own, :]).astype(BF16)
    weight_grads(normed_s, d_pre_s, mixed_s, d_branch_s, grads_ref)


def exchange(value, axis, size, step):
    return lax.ppermute(value, axis, [(d, d ^ step) for d in range(size)])


def add_narrow(a, b):
    return (a.astype(F32) + b.astype(F32)).astype(BF16)


def prepare(index_ref, state_ref, mask_ref, cot_ref, sent_ref, own_ref, state_s, mask_s, cot_s, sems):
    own_ref[0] = index_ref[0]
    parts, _, c = sent_ref.shape
    cells = state_s.shape[0]
    copies = [
        pltpu.make_async_copy(*pair, sems.at[k])
        for k, pair in enumerate(((mask_ref, mask_s), (state_ref, state_s), (cot_ref, cot_s)))
    ]
    for copy in copies:
        copy.start()
    copies[0].wait()
    length = jnp.max(jnp.sum(mask_s[...].astype(F32), axis=1, keepdims=True))
    below = jnp.full((sent_ref.shape[1] - 2 * cells, c), length, F32).astype(BF16)
    for copy in copies[1:]:
        copy.wait()
    for part in range(parts):
        sent_ref[part, :cells, :] = state_s[...]
        sent_ref[part, cells : 2 * cells, :] = cot_s[...]
        sent_ref[part, 2 * cells :, :] = below


def add_grads(own_0, other_0, own_1, other_1, proj_ref, out_ref):
    width = proj_ref.shape[2]
    for u, (own, other) in enumerate(((own_0, other_0), (own_1, other_1))):
        total = own[...].astype(F32) + other[...].astype(F32)
        proj_ref[u] = total[:, :width]
        out_ref[u] = total[:, width:]


def crop_shards(
    groups,
    parts,
    pair_repr,
    pair_mask,
    cotangent,
    proj_weight,
    proj_bias,
    norm_gain,
    norm_shift,
    out_weight,
    out_bias,
):
    _, rows, n, c = pair_repr.shape
    h = out_weight.shape[1]
    width = proj_weight.shape[2]
    cells, pairs = rows * n, n * n
    plane = jax.ShapeDtypeStruct((pairs + 8, h), F32)
    narrow = jax.ShapeDtypeStruct((pairs, h), BF16)
    grads = jax.ShapeDtypeStruct((c, width + c), BF16)
    kept = (plane,) * 10 + (narrow,) * 2
    vmem = pl.BlockSpec(memory_space=pltpu.VMEM)
    smem = pl.BlockSpec(memory_space=pltpu.SMEM)
    main = pl.BlockSpec(memory_space=pltpu.HBM)
    params = pltpu.CompilerParams(vmem_limit_bytes=VMEM_BYTES)

    def scratch(array):
        return pltpu.VMEM(array.shape, array.dtype)

    def cost(planes):
        flops = 4 * pairs * width * c
        return pl.CostEstimate(
            flops=flops, bytes_accessed=planes * pairs * c * 4, transcendentals=0
        )

    index = lax.axis_index("dap").astype(jnp.int32)[None]
    sent, own = pl.pallas_call(
        prepare,
        out_shape=(
            jax.ShapeDtypeStruct((parts, 2 * cells + 16, c), BF16),
            jax.ShapeDtypeStruct((1,), jnp.int32),
        ),
        in_specs=[smem] + [main] * 3,
        out_specs=(vmem, smem),
        scratch_shapes=[
            pltpu.VMEM((cells, c), BF16),
            pltpu.VMEM((rows, n), jnp.int32),
            pltpu.VMEM((cells, c), BF16),
            pltpu.SemaphoreType.DMA((3,)),
        ],
        compiler_params=pltpu.CompilerParams(vmem_limit_bytes=PREPARE_BYTES),
        name="prepare",
    )(index, pair_repr.reshape(cells, c), pair_mask[0], cotangent.reshape(cells, c))
    state = lax.all_to_all(sent, "dap", split_axis=0, concat_axis=0, tiled=True)

    held = pl.pallas_call(
        functools.partial(forward, n),
        out_shape=kept * 2,
        in_specs=[vmem] * 7,
        out_specs=(vmem,) * (2 * KEPT),
        scratch_shapes=[scratch(plane), scratch(narrow)],
        compiler_params=params,
        cost_estimate=cost(64),
        name="forward",
    )(state, proj_weight, proj_bias, norm_gain, norm_shift, out_weight, out_bias)

    up_1, grads_1 = pl.pallas_call(
        functools.partial(backward, n, 1),
        out_shape=(jax.ShapeDtypeStruct((pairs, c), F32), grads),
        in_specs=[vmem] * (4 + KEPT),
        out_specs=(vmem, vmem),
        scratch_shapes=[scratch(plane), scratch(narrow), pltpu.VMEM((pairs, width), BF16)]
        + [scratch(plane)],
        compiler_params=params,
        cost_estimate=cost(48),
        name="backward_second",
    )(state, proj_weight, norm_gain, out_weight, *held[KEPT:])
    far = groups // 2
    others_1 = exchange(grads_1, "dp", groups, far)

    pair_grad, grads_0 = pl.pallas_call(
        functools.partial(backward, n, 0),
        out_shape=(jax.ShapeDtypeStruct((cells, c), BF16), grads),
        in_specs=[smem] + [vmem] * (4 + KEPT),
        out_specs=(vmem, vmem),
        scratch_shapes=[scratch(plane), scratch(narrow), pltpu.VMEM((pairs, width), BF16)],
        compiler_params=params,
        cost_estimate=cost(48),
        name="backward_first",
    )(own, up_1, proj_weight, norm_gain, out_weight, *held[:KEPT])

    step = 1
    while step < far:
        near_1 = add_narrow(grads_1, others_1)
        others_1 = exchange(near_1, "dp", groups, step)
        others_0 = exchange(grads_0, "dp", groups, step)
        grads_1, grads_0 = near_1, add_narrow(grads_0, others_0)
        step *= 2
    others_0 = exchange(grads_0, "dp", groups, far)

    proj_total, out_total = pl.pallas_call(
        add_grads,
        out_shape=(
            jax.ShapeDtypeStruct((2, c, width), F32),
            jax.ShapeDtypeStruct((2, h, c), F32),
        ),
        in_specs=[vmem] * 4,
        out_specs=(vmem, vmem),
        compiler_params=params,
        name="add_grads",
    )(grads_0, others_0, grads_1, others_1)
    return pair_grad.reshape(pair_repr.shape), proj_total, out_total


def layer_norm(values, gain_vec, shift_vec, norm_axis):
    mean_value = jnp.mean(values, axis=norm_axis, keepdims=True)
    centred = values - mean_value
    variance = jnp.mean(centred * centred, axis=norm_axis, keepdims=True)
    return centred * lax.rsqrt(variance + NORM_EPSILON) * gain_vec + shift_vec


def norm_pullback(values, gain_vec, shift_vec, norm_axis, upstream):
    _, pull_back = jax.vjp(
        lambda inner_value: layer_norm(inner_value, gain_vec, shift_vec, norm_axis), values
    )
    return pull_back(upstream)[0]


def edge_pair(edge_pre, cell_mask):
    left_edge = jax.nn.sigmoid(edge_pre[1]) * edge_pre[0] * cell_mask
    right_edge = jax.nn.sigmoid(edge_pre[3]) * edge_pre[2] * cell_mask
    return jnp.stack([left_edge, right_edge]).astype(jnp.bfloat16)


def edge_pullback(edge_pre, cell_mask, grad_pair):
    sig_left = jax.nn.sigmoid(edge_pre[1])
    sig_right = jax.nn.sigmoid(edge_pre[3])
    grad_left = grad_pair[0].astype(jnp.float32) * cell_mask
    grad_right = grad_pair[1].astype(jnp.float32) * cell_mask
    return jnp.stack(
        [
            grad_left * sig_left,
            grad_left * edge_pre[0] * sig_left * (1.0 - sig_left),
            grad_right * sig_right,
            grad_right * edge_pre[2] * sig_right * (1.0 - sig_right),
        ]
    ).astype(jnp.bfloat16)


def triangle(pair_edges, outgoing):
    if outgoing:
        einsum_form = "cik,cjk->cij"
    else:
        einsum_form = "cki,ckj->cij"
    return jnp.einsum(
        einsum_form, pair_edges[0], pair_edges[1], preferred_element_type=jnp.float32
    ).astype(jnp.bfloat16)


def triangle_pullback(pair_edges, grad_product, outgoing):
    left_edge = pair_edges[0]
    right_edge = pair_edges[1]
    if outgoing:
        grad_left = jnp.einsum(
            "cij,cjk->cik", grad_product, right_edge, preferred_element_type=jnp.float32
        )
        grad_right = jnp.einsum(
            "cij,cik->cjk", grad_product, left_edge, preferred_element_type=jnp.float32
        )
    else:
        grad_left = jnp.einsum(
            "ckj,cij->cki", right_edge, grad_product, preferred_element_type=jnp.float32
        )
        grad_right = jnp.einsum(
            "cki,cij->ckj", left_edge, grad_product, preferred_element_type=jnp.float32
        )
    return jnp.stack([grad_left, grad_right]).astype(jnp.bfloat16)


def update_weights(proj_weight, proj_bias, norm_gain, norm_shift, update, channels, hidden):
    w_edge = proj_weight[update, :, : 4 * hidden].reshape(channels, 4, hidden)
    w_gate = proj_weight[update, :, 4 * hidden :]
    bias_edge = proj_bias[update, : 4 * hidden].reshape(4, hidden, 1, 1)
    bias_gate = proj_bias[update, 4 * hidden :]
    gain_in = norm_gain[update, :channels]
    shift_in = norm_shift[update, :channels]
    gain_out = norm_gain[update, channels:][:, None, None]
    shift_out = norm_shift[update, channels:][:, None, None]
    return (w_edge, w_gate, bias_edge, bias_gate, gain_in, shift_in, gain_out, shift_out)


def shards(
    pair_repr,
    pair_mask,
    cotangent,
    proj_weight,
    proj_bias,
    norm_gain,
    norm_shift,
    out_weight,
    out_bias,
):
    channels = pair_repr.shape[3]
    hidden = out_weight.shape[1]
    pair_state = pair_repr[0]
    cell_mask = pair_mask[0].astype(jnp.float32)
    records = []
    for update in range(2):
        w_edge, w_gate, bias_edge, bias_gate, gain_in, shift_in, gain_out, shift_out = (
            update_weights(proj_weight, proj_bias, norm_gain, norm_shift, update, channels, hidden)
        )
        state_f = pair_state.astype(jnp.float32)
        normed = layer_norm(state_f, gain_in, shift_in, -1).astype(jnp.bfloat16)
        edge_pre = (
            jnp.einsum("rnc,cgh->ghrn", normed, w_edge, preferred_element_type=jnp.float32)
            + bias_edge
        )
        gate_pre = (
            jnp.einsum("rnc,cd->rnd", normed, w_gate, preferred_element_type=jnp.float32)
            + bias_gate
        )
        pair_edges = edge_pair(edge_pre, cell_mask)
        spread = lax.all_to_all(pair_edges, "dap", split_axis=1, concat_axis=2, tiled=True)
        product = lax.all_to_all(
            triangle(spread, update == 0), "dap", split_axis=1, concat_axis=0, tiled=True
        )
        mixed_norm = layer_norm(product.astype(jnp.float32), gain_out, shift_out, 0).astype(
            jnp.bfloat16
        )
        branch = (
            jnp.einsum(
                "hrn,hd->rnd", mixed_norm, out_weight[update], preferred_element_type=jnp.float32
            )
            + out_bias[update]
        )
        records.append(
            (state_f, normed, edge_pre, gate_pre, pair_edges, spread, product, mixed_norm, branch)
        )
        pair_state = (state_f + jax.nn.sigmoid(gate_pre) * branch).astype(jnp.bfloat16)
    upstream = cotangent[0].astype(jnp.float32)
    proj_grads = []
    out_grads = []
    for update in (1, 0):
        state_f, normed, edge_pre, gate_pre, pair_edges, spread, product, mixed_norm, branch = (
            records[update]
        )
        w_edge, w_gate, bias_edge, bias_gate, gain_in, shift_in, gain_out, shift_out = (
            update_weights(proj_weight, proj_bias, norm_gain, norm_shift, update, channels, hidden)
        )
        gate_value = jax.nn.sigmoid(gate_pre)
        grad_branch = (upstream * gate_value).astype(jnp.bfloat16)
        grad_gate = (upstream * branch * gate_value * (1.0 - gate_value)).astype(jnp.bfloat16)
        out_grad = jnp.einsum(
            "hrn,rnd->hd", mixed_norm, grad_branch, preferred_element_type=jnp.float32
        )
        grad_mixed = jnp.einsum(
            "rnd,hd->hrn", grad_branch, out_weight[update], preferred_element_type=jnp.float32
        )
        grad_product = norm_pullback(
            product.astype(jnp.float32), gain_out, shift_out, 0, grad_mixed
        ).astype(jnp.bfloat16)
        column_edges = spread
        column_grad = lax.all_to_all(
            grad_product[None], "dap", split_axis=1, concat_axis=2, tiled=True
        )[0]
        grad_pair = lax.all_to_all(
            triangle_pullback(column_edges, column_grad, update == 0),
            "dap",
            split_axis=2,
            concat_axis=1,
            tiled=True,
        )
        grad_edge = edge_pullback(edge_pre, cell_mask, grad_pair)
        edge_grad = jnp.einsum(
            "rnc,ghrn->cgh", normed, grad_edge, preferred_element_type=jnp.float32
        ).reshape(channels, 4 * hidden)
        gate_grad = jnp.einsum("rnc,rnd->cd", normed, grad_gate, preferred_element_type=jnp.float32)
        grad_normed = jnp.einsum(
            "ghrn,cgh->rnc", grad_edge, w_edge, preferred_element_type=jnp.float32
        )
        grad_normed = grad_normed + jnp.einsum(
            "rnd,cd->rnc", grad_gate, w_gate, preferred_element_type=jnp.float32
        )
        upstream = upstream + norm_pullback(state_f, gain_in, shift_in, -1, grad_normed)
        proj_part = jnp.concatenate([edge_grad, gate_grad], axis=1)
        proj_grads.append(proj_part)
        out_grads.append(out_grad)
    proj_total = jnp.stack(proj_grads[::-1])
    out_total = jnp.stack(out_grads[::-1])
    proj_total, out_total = lax.psum((proj_total, out_total), ("dp", "dap"))
    return (upstream.astype(jnp.bfloat16)[None], proj_total, out_total)


def solution(mesh):
    placed = (
        P("dp", "dap", None, None),
        P("dp", "dap", None),
        P("dp", "dap", None, None),
        P(),
        P(),
        P(),
        P(),
        P(),
        P(),
    )
    groups, parts = mesh.shape["dp"], mesh.shape["dap"]

    def program(*args):
        n, c = args[0].shape[2:]
        rows = n // parts
        fits = 20 * n * n * c * 4 <= CROP_BUDGET
        even = args[7].shape[1] == c and groups > 1 and groups & (groups - 1) == 0 and BLOCK_ROWS % rows == 0 and n % 16 == 0
        body = functools.partial(crop_shards, groups, parts) if fits and even else shards
        return spread_over(body)(*args)

    def spread_over(body):
        return jax.shard_map(
            body,
            mesh=mesh,
            in_specs=placed,
            out_specs=(P("dp", "dap", None, None), P(), P()),
            check_vma=False,
        )

    return program
```

```python
import functools

import jax
import jax.numpy as jnp
from jax import lax
from jax.experimental import pallas as pl
from jax.experimental.pallas import tpu as pltpu
from jax.sharding import PartitionSpec as P

NORM_EPSILON = 1e-05
VMEM_BYTES = 16 * 1024 * 1024
PREPARE_BYTES = 63 * 1024 * 1024
CROP_BUDGET = 32 * 1024 * 1024
BLOCK_ROWS = 8
KEPT = 12
F32 = jnp.float32
BF16 = jnp.bfloat16


def sigmoid(x):
    return 0.5 * jnp.tanh(0.5 * x) + 0.5


def dot(a, b, dims=((1,), (0,))):
    return lax.dot_general(a, b, (dims, ((), ())), preferred_element_type=F32)


def norm_parts(x):
    centred = x - jnp.mean(x, axis=-1, keepdims=True)
    rstd = lax.rsqrt(jnp.mean(centred * centred, axis=-1, keepdims=True) + NORM_EPSILON)
    return centred * rstd, rstd


def norm_vjp(x_hat, rstd, grad):
    mean_grad = jnp.mean(grad, axis=-1, keepdims=True)
    mean_prod = jnp.mean(grad * x_hat, axis=-1, keepdims=True)
    return rstd * (grad - mean_grad - x_hat * mean_prod)


def pair_mask_block(length, first_row, rows, n, lanes):
    shape = (rows, n, lanes)
    i = lax.broadcasted_iota(jnp.int32, shape, 0) + first_row
    j = lax.broadcasted_iota(jnp.int32, shape, 1)
    inside = jnp.where((i < length) & (j < length), 1.0, 0.0)
    return inside.reshape(rows * n, lanes)


def project(x, mask, u, w, b, gain, shift):
    c = x.shape[1]
    x_hat, rstd = norm_parts(x)
    normed = (x_hat * gain[u : u + 1, :c] + shift[u : u + 1, :c]).astype(BF16)
    pre = dot(normed, w[u]) + b[u : u + 1, :]
    h = (pre.shape[1] - c) // 4
    s_left = sigmoid(pre[:, h : 2 * h]) * mask
    s_right = sigmoid(pre[:, 3 * h : 4 * h]) * mask
    left = s_left * pre[:, :h]
    right = s_right * pre[:, 2 * h : 3 * h]
    gate = sigmoid(pre[:, 4 * h :])
    return x_hat, rstd, normed, s_left, s_right, left, right, gate


def mix(product, u, c, gain, shift, w_out, b_out):
    p_hat, p_rstd = norm_parts(product.astype(F32))
    mixed = (p_hat * gain[u : u + 1, c:] + shift[u : u + 1, c:]).astype(BF16)
    branch = dot(mixed, w_out[u]) + b_out[u : u + 1, :]
    return p_hat, p_rstd, mixed, branch


def unmix(up, gate, branch, p_hat, p_rstd, u, c, gain, w_out):
    d_branch = up * gate
    d_gate = (d_branch * branch * (1.0 - gate)).astype(BF16)
    d_branch = d_branch.astype(BF16)
    d_mixed = dot(d_branch, w_out[u], ((1,), (1,))) * gain[u : u + 1, c:]
    return d_branch, d_gate, norm_vjp(p_hat, p_rstd, d_mixed)


def contract(n, first, row_of, x, y):
    lanes = y.shape[1]
    tiles = (n // 8, 8, lanes)

    def step(e, totals):
        block = y[pl.ds(pl.multiple_of(e * n, n), n), :].reshape(tiles)
        return tuple(
            totals[a] + x[pl.ds(row_of(first + a, e), 8, stride=0), :][None] * block
            for a in range(BLOCK_ROWS)
        )

    zero = jnp.zeros(tiles, F32)
    totals = lax.fori_loop(0, n, step, (zero,) * BLOCK_ROWS, unroll=True)
    return jnp.stack(totals).reshape(BLOCK_ROWS * n, lanes)


def edge_grads(d_left, d_right, s_left, s_right, left, right):
    return (
        (d_left * s_left).astype(BF16),
        (d_left * left * (1.0 - s_left)).astype(BF16),
        (d_right * s_right).astype(BF16),
        (d_right * right * (1.0 - s_right)).astype(BF16),
    )


def crop_length(state_ref, cells):
    return jnp.max(state_ref[:, 2 * cells :, :].astype(F32)).astype(jnp.int32)


def joined(ref, first, count, cells, place):
    span = slice(place * cells, (place + 1) * cells)
    return jnp.concatenate([ref[first + q, span, :] for q in range(count)], axis=0)


def forward(n, state_ref, w, b, gain, shift, w_out, b_out, *refs):
    kept, (right_t_s, next_s) = (refs[:KEPT], refs[KEPT : 2 * KEPT]), refs[2 * KEPT :]
    parts, _, c = state_ref.shape
    rows = n // parts
    cells = rows * n
    length = crop_length(state_ref, cells)
    per = BLOCK_ROWS // rows
    blocks = n // BLOCK_ROWS

    for u in range(2):
        (left_s, right_s, s_left_s, s_right_s, gate_s, hat_s, rstd_s) = kept[u][:7]
        (p_hat_s, p_rstd_s, branch_s, normed_s, mixed_s) = kept[u][7:]

        @pl.loop(0, blocks)
        def _(t):
            first = t * BLOCK_ROWS
            here = pl.ds(pl.multiple_of(first * n, BLOCK_ROWS * n), BLOCK_ROWS * n)
            x = joined(state_ref, t * per, per, cells, 0) if u == 0 else next_s[here, :]
            mask = pair_mask_block(length, first, BLOCK_ROWS, n, c)
            x_hat, rstd, normed, s_left, s_right, left, right, gate = project(
                x.astype(F32), mask, u, w, b, gain, shift
            )
            left_s[here, :] = left
            right_s[here, :] = right
            s_left_s[here, :] = s_left
            s_right_s[here, :] = s_right
            gate_s[here, :] = gate
            hat_s[here, :] = x_hat
            rstd_s[here, :] = jnp.broadcast_to(rstd, x_hat.shape)
            normed_s[here, :] = normed
            if u == 0:
                for r in range(BLOCK_ROWS):
                    right_t_s[pl.ds(first + r, n, stride=n), :] = right[r * n : (r + 1) * n]

        @pl.loop(0, blocks)
        def _(t):
            first = t * BLOCK_ROWS
            here = pl.ds(pl.multiple_of(first * n, BLOCK_ROWS * n), BLOCK_ROWS * n)
            if u == 0:
                product = contract(n, first, lambda i, k: i * n + k, left_s, right_t_s)
            else:
                product = contract(n, first, lambda i, k: k * n + i, left_s, right_s)
            p_hat, p_rstd, mixed, branch = mix(
                product.astype(BF16), u, c, gain, shift, w_out, b_out
            )
            p_hat_s[here, :] = p_hat
            p_rstd_s[here, :] = jnp.broadcast_to(p_rstd, p_hat.shape)
            mixed_s[here, :] = mixed
            branch_s[here, :] = branch
            if u == 0:
                x = joined(state_ref, t * per, per, cells, 0).astype(F32)
                next_s[here, :] = (x + gate_s[here, :] * branch).astype(BF16)


def weight_grads(normed_s, d_pre_s, mixed_s, d_branch_s, grads_ref):
    width = d_pre_s.shape[1]
    grads_ref[:, :width] = dot(normed_s[...], d_pre_s[...], ((0,), (0,))).astype(BF16)
    grads_ref[:, width:] = dot(mixed_s[...], d_branch_s[...], ((0,), (0,))).astype(BF16)


def backward(n, u, *refs):
    if u == 0:
        index_ref, refs = refs[0], refs[1:]
    up_in_ref, w, gain, w_out = refs[:4]
    (left_s, right_s, s_left_s, s_right_s, gate_s, hat_s, rstd_s) = refs[4:11]
    (p_hat_s, p_rstd_s, branch_s, normed_s, mixed_s) = refs[11 : 4 + KEPT]
    up_ref, grads_ref, d_product_s, d_branch_s, d_pre_s = refs[4 + KEPT : 9 + KEPT]
    c, h = w.shape[1], left_s.shape[1]
    blocks = n // BLOCK_ROWS

    def upstream(t, here):
        if u == 0:
            return up_in_ref[here, :]
        rows = n // up_in_ref.shape[0]
        per = BLOCK_ROWS // rows
        return joined(up_in_ref, t * per, per, rows * n, 1).astype(F32)

    def input_pullback(here, up):
        d_normed = dot(d_pre_s[here, :], w[u], ((1,), (1,))) * gain[u : u + 1, :c]
        return up + norm_vjp(hat_s[here, :], rstd_s[here, :], d_normed)

    @pl.loop(0, blocks)
    def _(t):
        first = t * BLOCK_ROWS
        here = pl.ds(pl.multiple_of(first * n, BLOCK_ROWS * n), BLOCK_ROWS * n)
        d_branch, d_gate, d_product = unmix(
            upstream(t, here),
            gate_s[here, :],
            branch_s[here, :],
            p_hat_s[here, :],
            p_rstd_s[here, :],
            u,
            c,
            gain,
            w_out,
        )
        d_branch_s[here, :] = d_branch
        d_pre_s[here, 4 * h :] = d_gate
        d_product_s[here, :] = d_product
        if u == 1:
            d_product_t_s = refs[9 + KEPT]
            for r in range(BLOCK_ROWS):
                d_product_t_s[pl.ds(first + r, n, stride=n), :] = d_product[r * n : (r + 1) * n]

    @pl.loop(0, blocks)
    def _(t):
        first = t * BLOCK_ROWS
        here = pl.ds(pl.multiple_of(first * n, BLOCK_ROWS * n), BLOCK_ROWS * n)
        if u == 1:
            d_left = contract(n, first, lambda k, j: k * n + j, right_s, refs[9 + KEPT])
            d_right = contract(n, first, lambda k, i: k * n + i, left_s, d_product_s)
        else:
            d_left = contract(n, first, lambda i, j: i * n + j, d_product_s, right_s)
            d_right = contract(n, first, lambda j, i: i * n + j, d_product_s, left_s)
        grads = edge_grads(
            d_left, d_right, s_left_s[here, :], s_right_s[here, :], left_s[here, :], right_s[here, :]
        )
        for g in range(4):
            d_pre_s[here, g * h : (g + 1) * h] = grads[g]
        if u == 1:
            up_ref[here, :] = input_pullback(here, upstream(t, here))

    if u == 0:
        cells = up_ref.shape[0]
        own = pl.ds(pl.multiple_of(index_ref[0] * cells, cells), cells)
        up_ref[...] = input_pullback(own, up_in_ref[own, :]).astype(BF16)
    weight_grads(normed_s, d_pre_s, mixed_s, d_branch_s, grads_ref)


def exchange(value, axis, size, step):
    return lax.ppermute(value, axis, [(d, d ^ step) for d in range(size)])


def add_narrow(a, b):
    return (a.astype(F32) + b.astype(F32)).astype(BF16)


def prepare(index_ref, state_ref, mask_ref, cot_ref, sent_ref, own_ref, state_s, mask_s, cot_s, sems):
    own_ref[0] = index_ref[0]
    parts, _, c = sent_ref.shape
    cells = state_s.shape[0]
    copies = [
        pltpu.make_async_copy(*pair, sems.at[k])
        for k, pair in enumerate(((mask_ref, mask_s), (state_ref, state_s), (cot_ref, cot_s)))
    ]
    for copy in copies:
        copy.start()
    copies[0].wait()
    length = jnp.max(jnp.sum(mask_s[...].astype(F32), axis=1, keepdims=True))
    below = jnp.full((sent_ref.shape[1] - 2 * cells, c), length, F32).astype(BF16)
    for copy in copies[1:]:
        copy.wait()
    for part in range(parts):
        sent_ref[part, :cells, :] = state_s[...]
        sent_ref[part, cells : 2 * cells, :] = cot_s[...]
        sent_ref[part, 2 * cells :, :] = below


def add_grads(own_0, other_0, own_both, other_both, proj_ref, out_ref):
    width = proj_ref.shape[2]
    for u, (own, other) in enumerate(((own_0, other_0), (own_both.at[1], other_both.at[1]))):
        total = own[...].astype(F32) + other[...].astype(F32)
        proj_ref[u] = total[:, :width]
        out_ref[u] = total[:, width:]


def crop_shards(
    groups,
    parts,
    pair_repr,
    pair_mask,
    cotangent,
    proj_weight,
    proj_bias,
    norm_gain,
    norm_shift,
    out_weight,
    out_bias,
):
    _, rows, n, c = pair_repr.shape
    h = out_weight.shape[1]
    width = proj_weight.shape[2]
    cells, pairs = rows * n, n * n
    plane = jax.ShapeDtypeStruct((pairs + 8, h), F32)
    narrow = jax.ShapeDtypeStruct((pairs, h), BF16)
    grads = jax.ShapeDtypeStruct((c, width + c), BF16)
    kept = (plane,) * 10 + (narrow,) * 2
    vmem = pl.BlockSpec(memory_space=pltpu.VMEM)
    smem = pl.BlockSpec(memory_space=pltpu.SMEM)
    main = pl.BlockSpec(memory_space=pltpu.HBM)
    params = pltpu.CompilerParams(vmem_limit_bytes=VMEM_BYTES)

    def scratch(array):
        return pltpu.VMEM(array.shape, array.dtype)

    def cost(planes):
        flops = 4 * pairs * width * c
        return pl.CostEstimate(
            flops=flops, bytes_accessed=planes * pairs * c * 4, transcendentals=0
        )

    index = lax.axis_index("dap").astype(jnp.int32)[None]
    sent, own = pl.pallas_call(
        prepare,
        out_shape=(
            jax.ShapeDtypeStruct((parts, 2 * cells + 16, c), BF16),
            jax.ShapeDtypeStruct((1,), jnp.int32),
        ),
        in_specs=[smem] + [main] * 3,
        out_specs=(vmem, smem),
        scratch_shapes=[
            pltpu.VMEM((cells, c), BF16),
            pltpu.VMEM((rows, n), jnp.int32),
            pltpu.VMEM((cells, c), BF16),
            pltpu.SemaphoreType.DMA((3,)),
        ],
        compiler_params=pltpu.CompilerParams(vmem_limit_bytes=PREPARE_BYTES),
        name="prepare",
    )(index, pair_repr.reshape(cells, c), pair_mask[0], cotangent.reshape(cells, c))
    state = lax.all_to_all(sent, "dap", split_axis=0, concat_axis=0, tiled=True)

    held = pl.pallas_call(
        functools.partial(forward, n),
        out_shape=kept * 2,
        in_specs=[vmem] * 7,
        out_specs=(vmem,) * (2 * KEPT),
        scratch_shapes=[scratch(plane), scratch(narrow)],
        compiler_params=params,
        cost_estimate=cost(64),
        name="forward",
    )(state, proj_weight, proj_bias, norm_gain, norm_shift, out_weight, out_bias)

    up_1, grads_1 = pl.pallas_call(
        functools.partial(backward, n, 1),
        out_shape=(jax.ShapeDtypeStruct((pairs, c), F32), grads),
        in_specs=[vmem] * (4 + KEPT),
        out_specs=(vmem, vmem),
        scratch_shapes=[scratch(plane), scratch(narrow), pltpu.VMEM((pairs, width), BF16)]
        + [scratch(plane)],
        compiler_params=params,
        cost_estimate=cost(48),
        name="backward_second",
    )(state, proj_weight, norm_gain, out_weight, *held[KEPT:])
    far = groups // 2
    others_1 = exchange(grads_1, "dp", groups, far)

    pair_grad, grads_0 = pl.pallas_call(
        functools.partial(backward, n, 0),
        out_shape=(jax.ShapeDtypeStruct((cells, c), BF16), grads),
        in_specs=[smem] + [vmem] * (4 + KEPT),
        out_specs=(vmem, vmem),
        scratch_shapes=[scratch(plane), scratch(narrow), pltpu.VMEM((pairs, width), BF16)],
        compiler_params=params,
        cost_estimate=cost(48),
        name="backward_first",
    )(own, up_1, proj_weight, norm_gain, out_weight, *held[:KEPT])

    both = jnp.stack([grads_0, add_narrow(grads_1, others_1)])
    others = jnp.zeros_like(both)
    step = 1
    while step < far:
        both = add_narrow(both, others) if step > 1 else both
        others = exchange(both, "dp", groups, step)
        step *= 2
    grads_0 = add_narrow(both[0], others[0])
    others_0 = exchange(grads_0, "dp", groups, far)

    proj_total, out_total = pl.pallas_call(
        add_grads,
        out_shape=(
            jax.ShapeDtypeStruct((2, c, width), F32),
            jax.ShapeDtypeStruct((2, h, c), F32),
        ),
        in_specs=[vmem] * 4,
        out_specs=(vmem, vmem),
        compiler_params=params,
        name="add_grads",
    )(grads_0, others_0, both, others)
    return pair_grad.reshape(pair_repr.shape), proj_total, out_total


def layer_norm(values, gain_vec, shift_vec, norm_axis):
    mean_value = jnp.mean(values, axis=norm_axis, keepdims=True)
    centred = values - mean_value
    variance = jnp.mean(centred * centred, axis=norm_axis, keepdims=True)
    return centred * lax.rsqrt(variance + NORM_EPSILON) * gain_vec + shift_vec


def norm_pullback(values, gain_vec, shift_vec, norm_axis, upstream):
    _, pull_back = jax.vjp(
        lambda inner_value: layer_norm(inner_value, gain_vec, shift_vec, norm_axis), values
    )
    return pull_back(upstream)[0]


def edge_pair(edge_pre, cell_mask):
    left_edge = jax.nn.sigmoid(edge_pre[1]) * edge_pre[0] * cell_mask
    right_edge = jax.nn.sigmoid(edge_pre[3]) * edge_pre[2] * cell_mask
    return jnp.stack([left_edge, right_edge]).astype(jnp.bfloat16)


def edge_pullback(edge_pre, cell_mask, grad_pair):
    sig_left = jax.nn.sigmoid(edge_pre[1])
    sig_right = jax.nn.sigmoid(edge_pre[3])
    grad_left = grad_pair[0].astype(jnp.float32) * cell_mask
    grad_right = grad_pair[1].astype(jnp.float32) * cell_mask
    return jnp.stack(
        [
            grad_left * sig_left,
            grad_left * edge_pre[0] * sig_left * (1.0 - sig_left),
            grad_right * sig_right,
            grad_right * edge_pre[2] * sig_right * (1.0 - sig_right),
        ]
    ).astype(jnp.bfloat16)


def triangle(pair_edges, outgoing):
    if outgoing:
        einsum_form = "cik,cjk->cij"
    else:
        einsum_form = "cki,ckj->cij"
    return jnp.einsum(
        einsum_form, pair_edges[0], pair_edges[1], preferred_element_type=jnp.float32
    ).astype(jnp.bfloat16)


def triangle_pullback(pair_edges, grad_product, outgoing):
    left_edge = pair_edges[0]
    right_edge = pair_edges[1]
    if outgoing:
        grad_left = jnp.einsum(
            "cij,cjk->cik", grad_product, right_edge, preferred_element_type=jnp.float32
        )
        grad_right = jnp.einsum(
            "cij,cik->cjk", grad_product, left_edge, preferred_element_type=jnp.float32
        )
    else:
        grad_left = jnp.einsum(
            "ckj,cij->cki", right_edge, grad_product, preferred_element_type=jnp.float32
        )
        grad_right = jnp.einsum(
            "cki,cij->ckj", left_edge, grad_product, preferred_element_type=jnp.float32
        )
    return jnp.stack([grad_left, grad_right]).astype(jnp.bfloat16)


def update_weights(proj_weight, proj_bias, norm_gain, norm_shift, update, channels, hidden):
    w_edge = proj_weight[update, :, : 4 * hidden].reshape(channels, 4, hidden)
    w_gate = proj_weight[update, :, 4 * hidden :]
    bias_edge = proj_bias[update, : 4 * hidden].reshape(4, hidden, 1, 1)
    bias_gate = proj_bias[update, 4 * hidden :]
    gain_in = norm_gain[update, :channels]
    shift_in = norm_shift[update, :channels]
    gain_out = norm_gain[update, channels:][:, None, None]
    shift_out = norm_shift[update, channels:][:, None, None]
    return (w_edge, w_gate, bias_edge, bias_gate, gain_in, shift_in, gain_out, shift_out)


def shards(
    pair_repr,
    pair_mask,
    cotangent,
    proj_weight,
    proj_bias,
    norm_gain,
    norm_shift,
    out_weight,
    out_bias,
):
    channels = pair_repr.shape[3]
    hidden = out_weight.shape[1]
    pair_state = pair_repr[0]
    cell_mask = pair_mask[0].astype(jnp.float32)
    records = []
    for update in range(2):
        w_edge, w_gate, bias_edge, bias_gate, gain_in, shift_in, gain_out, shift_out = (
            update_weights(proj_weight, proj_bias, norm_gain, norm_shift, update, channels, hidden)
        )
        state_f = pair_state.astype(jnp.float32)
        normed = layer_norm(state_f, gain_in, shift_in, -1).astype(jnp.bfloat16)
        edge_pre = (
            jnp.einsum("rnc,cgh->ghrn", normed, w_edge, preferred_element_type=jnp.float32)
            + bias_edge
        )
        gate_pre = (
            jnp.einsum("rnc,cd->rnd", normed, w_gate, preferred_element_type=jnp.float32)
            + bias_gate
        )
        pair_edges = edge_pair(edge_pre, cell_mask)
        spread = lax.all_to_all(pair_edges, "dap", split_axis=1, concat_axis=2, tiled=True)
        product = lax.all_to_all(
            triangle(spread, update == 0), "dap", split_axis=1, concat_axis=0, tiled=True
        )
        mixed_norm = layer_norm(product.astype(jnp.float32), gain_out, shift_out, 0).astype(
            jnp.bfloat16
        )
        branch = (
            jnp.einsum(
                "hrn,hd->rnd", mixed_norm, out_weight[update], preferred_element_type=jnp.float32
            )
            + out_bias[update]
        )
        records.append(
            (state_f, normed, edge_pre, gate_pre, pair_edges, spread, product, mixed_norm, branch)
        )
        pair_state = (state_f + jax.nn.sigmoid(gate_pre) * branch).astype(jnp.bfloat16)
    upstream = cotangent[0].astype(jnp.float32)
    proj_grads = []
    out_grads = []
    for update in (1, 0):
        state_f, normed, edge_pre, gate_pre, pair_edges, spread, product, mixed_norm, branch = (
            records[update]
        )
        w_edge, w_gate, bias_edge, bias_gate, gain_in, shift_in, gain_out, shift_out = (
            update_weights(proj_weight, proj_bias, norm_gain, norm_shift, update, channels, hidden)
        )
        gate_value = jax.nn.sigmoid(gate_pre)
        grad_branch = (upstream * gate_value).astype(jnp.bfloat16)
        grad_gate = (upstream * branch * gate_value * (1.0 - gate_value)).astype(jnp.bfloat16)
        out_grad = jnp.einsum(
            "hrn,rnd->hd", mixed_norm, grad_branch, preferred_element_type=jnp.float32
        )
        grad_mixed = jnp.einsum(
            "rnd,hd->hrn", grad_branch, out_weight[update], preferred_element_type=jnp.float32
        )
        grad_product = norm_pullback(
            product.astype(jnp.float32), gain_out, shift_out, 0, grad_mixed
        ).astype(jnp.bfloat16)
        column_edges = spread
        column_grad = lax.all_to_all(
            grad_product[None], "dap", split_axis=1, concat_axis=2, tiled=True
        )[0]
        grad_pair = lax.all_to_all(
            triangle_pullback(column_edges, column_grad, update == 0),
            "dap",
            split_axis=2,
            concat_axis=1,
            tiled=True,
        )
        grad_edge = edge_pullback(edge_pre, cell_mask, grad_pair)
        edge_grad = jnp.einsum(
            "rnc,ghrn->cgh", normed, grad_edge, preferred_element_type=jnp.float32
        ).reshape(channels, 4 * hidden)
        gate_grad = jnp.einsum("rnc,rnd->cd", normed, grad_gate, preferred_element_type=jnp.float32)
        grad_normed = jnp.einsum(
            "ghrn,cgh->rnc", grad_edge, w_edge, preferred_element_type=jnp.float32
        )
        grad_normed = grad_normed + jnp.einsum(
            "rnd,cd->rnc", grad_gate, w_gate, preferred_element_type=jnp.float32
        )
        upstream = upstream + norm_pullback(state_f, gain_in, shift_in, -1, grad_normed)
        proj_part = jnp.concatenate([edge_grad, gate_grad], axis=1)
        proj_grads.append(proj_part)
        out_grads.append(out_grad)
    proj_total = jnp.stack(proj_grads[::-1])
    out_total = jnp.stack(out_grads[::-1])
    proj_total, out_total = lax.psum((proj_total, out_total), ("dp", "dap"))
    return (upstream.astype(jnp.bfloat16)[None], proj_total, out_total)


def solution(mesh):
    placed = (
        P("dp", "dap", None, None),
        P("dp", "dap", None),
        P("dp", "dap", None, None),
        P(),
        P(),
        P(),
        P(),
        P(),
        P(),
    )
    groups, parts = mesh.shape["dp"], mesh.shape["dap"]

    def program(*args):
        n, c = args[0].shape[2:]
        rows = n // parts
        fits = 20 * n * n * c * 4 <= CROP_BUDGET
        even = args[7].shape[1] == c and groups > 1 and groups & (groups - 1) == 0 and BLOCK_ROWS % rows == 0 and n % 16 == 0
        body = functools.partial(crop_shards, groups, parts) if fits and even else shards
        return spread_over(body)(*args)

    def spread_over(body):
        return jax.shard_map(
            body,
            mesh=mesh,
            in_specs=placed,
            out_specs=(P("dp", "dap", None, None), P(), P()),
            check_vma=False,
        )

    return program
```

```python
import functools

import jax
import jax.numpy as jnp
from jax import lax
from jax.experimental import pallas as pl
from jax.experimental.pallas import tpu as pltpu
from jax.sharding import PartitionSpec as P

NORM_EPSILON = 1e-05
VMEM_BYTES = 16 * 1024 * 1024
PREPARE_BYTES = 63 * 1024 * 1024
CROP_BUDGET = 32 * 1024 * 1024
BLOCK_ROWS = 8
KEPT = 10
F32 = jnp.float32
BF16 = jnp.bfloat16


def sigmoid(x):
    return 0.5 * jnp.tanh(0.5 * x) + 0.5


def dot(a, b, dims=((1,), (0,))):
    return lax.dot_general(a, b, (dims, ((), ())), preferred_element_type=F32)


def norm_parts(x):
    centred = x - jnp.mean(x, axis=-1, keepdims=True)
    rstd = lax.rsqrt(jnp.mean(centred * centred, axis=-1, keepdims=True) + NORM_EPSILON)
    return centred * rstd, rstd


def norm_vjp(x_hat, rstd, grad):
    mean_grad = jnp.mean(grad, axis=-1, keepdims=True)
    mean_prod = jnp.mean(grad * x_hat, axis=-1, keepdims=True)
    return rstd * (grad - mean_grad - x_hat * mean_prod)


def pair_mask_block(length, first_row, rows, n, lanes):
    shape = (rows, n, lanes)
    i = lax.broadcasted_iota(jnp.int32, shape, 0) + first_row
    j = lax.broadcasted_iota(jnp.int32, shape, 1)
    inside = jnp.where((i < length) & (j < length), 1.0, 0.0)
    return inside.reshape(rows * n, lanes)


def project(x, mask, u, w, b, gain, shift):
    c = x.shape[1]
    x_hat, rstd = norm_parts(x)
    normed = (x_hat * gain[u : u + 1, :c] + shift[u : u + 1, :c]).astype(BF16)
    pre = dot(normed, w[u]) + b[u : u + 1, :]
    h = (pre.shape[1] - c) // 4
    s_left = sigmoid(pre[:, h : 2 * h]) * mask
    s_right = sigmoid(pre[:, 3 * h : 4 * h]) * mask
    left = s_left * pre[:, :h]
    right = s_right * pre[:, 2 * h : 3 * h]
    gate = sigmoid(pre[:, 4 * h :])
    return x_hat, rstd, normed, s_left, s_right, left, right, gate


def mix(product, u, c, gain, shift, w_out, b_out):
    p_hat, p_rstd = norm_parts(product.astype(F32))
    mixed = (p_hat * gain[u : u + 1, c:] + shift[u : u + 1, c:]).astype(BF16)
    branch = dot(mixed, w_out[u]) + b_out[u : u + 1, :]
    return p_hat, p_rstd, mixed, branch


def unmix(up, gate, branch, p_hat, p_rstd, u, c, gain, w_out):
    d_branch = up * gate
    d_gate = (d_branch * branch * (1.0 - gate)).astype(BF16)
    d_branch = d_branch.astype(BF16)
    d_mixed = dot(d_branch, w_out[u], ((1,), (1,))) * gain[u : u + 1, c:]
    return d_branch, d_gate, norm_vjp(p_hat, p_rstd, d_mixed)


def contract(n, first, row_of, x, y):
    lanes = y.shape[1]
    tiles = (n // 8, 8, lanes)

    def step(e, totals):
        block = y[pl.ds(pl.multiple_of(e * n, n), n), :].reshape(tiles)
        return tuple(
            totals[a] + x[pl.ds(row_of(first + a, e), 8, stride=0), :][None] * block
            for a in range(BLOCK_ROWS)
        )

    zero = jnp.zeros(tiles, F32)
    totals = lax.fori_loop(0, n, step, (zero,) * BLOCK_ROWS, unroll=True)
    return jnp.stack(totals).reshape(BLOCK_ROWS * n, lanes)


def edge_grads(d_left, d_right, s_left, s_right, left, right):
    return (
        (d_left * s_left).astype(BF16),
        (d_left * left * (1.0 - s_left)).astype(BF16),
        (d_right * s_right).astype(BF16),
        (d_right * right * (1.0 - s_right)).astype(BF16),
    )


def crop_length(state_ref, cells):
    return jnp.max(state_ref[:, 2 * cells :, :].astype(F32)).astype(jnp.int32)


def joined(ref, first, count, cells, place):
    span = slice(place * cells, (place + 1) * cells)
    return jnp.concatenate([ref[first + q, span, :] for q in range(count)], axis=0)


def forward(n, state_ref, w, b, gain, shift, w_out, b_out, *refs):
    kept, (right_t_s, next_s) = (refs[:KEPT], refs[KEPT : 2 * KEPT]), refs[2 * KEPT :]
    parts, _, c = state_ref.shape
    rows = n // parts
    cells = rows * n
    length = crop_length(state_ref, cells)
    per = BLOCK_ROWS // rows
    blocks = n // BLOCK_ROWS

    for u in range(2):
        (edges_s, slopes_s, gate_s, hat_s, rstd_s) = kept[u][:5]
        (p_hat_s, p_rstd_s, branch_s, normed_s, mixed_s) = kept[u][5:]

        @pl.loop(0, blocks)
        def _(t):
            first = t * BLOCK_ROWS
            here = pl.ds(pl.multiple_of(first * n, BLOCK_ROWS * n), BLOCK_ROWS * n)
            x = joined(state_ref, t * per, per, cells, 0) if u == 0 else next_s[here, :]
            mask = pair_mask_block(length, first, BLOCK_ROWS, n, c)
            x_hat, rstd, normed, s_left, s_right, left, right, gate = project(
                x.astype(F32), mask, u, w, b, gain, shift
            )
            edges_s[0, here, :] = left
            edges_s[1, here, :] = right
            slopes_s[0, here, :] = s_left
            slopes_s[1, here, :] = s_right
            gate_s[here, :] = gate
            hat_s[here, :] = x_hat
            rstd_s[here, :] = jnp.broadcast_to(rstd, x_hat.shape)
            normed_s[here, :] = normed
            if u == 0:
                for r in range(BLOCK_ROWS):
                    right_t_s[pl.ds(first + r, n, stride=n), :] = right[r * n : (r + 1) * n]

        @pl.loop(0, blocks)
        def _(t):
            first = t * BLOCK_ROWS
            here = pl.ds(pl.multiple_of(first * n, BLOCK_ROWS * n), BLOCK_ROWS * n)
            if u == 0:
                product = contract(n, first, lambda i, k: i * n + k, edges_s.at[0], right_t_s)
            else:
                product = contract(n, first, lambda i, k: k * n + i, edges_s.at[0], edges_s.at[1])
            p_hat, p_rstd, mixed, branch = mix(
                product.astype(BF16), u, c, gain, shift, w_out, b_out
            )
            p_hat_s[here, :] = p_hat
            p_rstd_s[here, :] = jnp.broadcast_to(p_rstd, p_hat.shape)
            mixed_s[here, :] = mixed
            branch_s[here, :] = branch
            if u == 0:
                x = joined(state_ref, t * per, per, cells, 0).astype(F32)
                next_s[here, :] = (x + gate_s[here, :] * branch).astype(BF16)


def weight_grads(normed_s, d_pre_s, mixed_s, d_branch_s, grads_ref):
    width = d_pre_s.shape[1]
    grads_ref[:, :width] = dot(normed_s[...], d_pre_s[...], ((0,), (0,))).astype(BF16)
    grads_ref[:, width:] = dot(mixed_s[...], d_branch_s[...], ((0,), (0,))).astype(BF16)


def backward(n, u, *refs):
    if u == 0:
        index_ref, refs = refs[0], refs[1:]
    up_in_ref, w, gain, w_out = refs[:4]
    (edges_s, slopes_s, gate_s, hat_s, rstd_s) = refs[4:9]
    (p_hat_s, p_rstd_s, branch_s, normed_s, mixed_s) = refs[9 : 4 + KEPT]
    up_ref, grads_ref, d_product_s, d_edges_s, d_branch_s, d_pre_s = refs[4 + KEPT :]
    c, h = w.shape[1], edges_s.shape[2]
    blocks = n // BLOCK_ROWS

    def upstream(t, here):
        if u == 0:
            return up_in_ref[here, :]
        rows = n // up_in_ref.shape[0]
        per = BLOCK_ROWS // rows
        return joined(up_in_ref, t * per, per, rows * n, 1).astype(F32)

    def input_pullback(here, up):
        d_normed = dot(d_pre_s[here, :], w[u], ((1,), (1,))) * gain[u : u + 1, :c]
        return up + norm_vjp(hat_s[here, :], rstd_s[here, :], d_normed)

    @pl.loop(0, blocks)
    def _(t):
        first = t * BLOCK_ROWS
        here = pl.ds(pl.multiple_of(first * n, BLOCK_ROWS * n), BLOCK_ROWS * n)
        d_branch, d_gate, d_product = unmix(
            upstream(t, here),
            gate_s[here, :],
            branch_s[here, :],
            p_hat_s[here, :],
            p_rstd_s[here, :],
            u,
            c,
            gain,
            w_out,
        )
        d_branch_s[here, :] = d_branch
        d_pre_s[here, 4 * h :] = d_gate
        if u == 1:
            for r in range(BLOCK_ROWS):
                d_product_s[0, pl.ds(first + r, n, stride=n), :] = d_product[r * n : (r + 1) * n]
            d_product_s[1, here, :] = d_product
        else:
            d_product_s[0, here, :] = d_product
            for r in range(BLOCK_ROWS):
                d_product_s[1, pl.ds(first + r, n, stride=n), :] = d_product[r * n : (r + 1) * n]

    @pl.loop(0, 2 * blocks)
    def _(step):
        side, first = step // blocks, step % blocks * BLOCK_ROWS
        here = pl.ds(pl.multiple_of(first * n, BLOCK_ROWS * n), BLOCK_ROWS * n)
        edges, d_product = edges_s.at[1 - side], d_product_s.at[side]
        x, y = (edges, d_product) if u == 1 else (d_product, edges)
        d_edges_s[side, here, :] = contract(n, first, lambda a, e: a * n + e, x, y)

    @pl.loop(0, blocks)
    def _(t):
        here = pl.ds(pl.multiple_of(t * BLOCK_ROWS * n, BLOCK_ROWS * n), BLOCK_ROWS * n)
        grads = edge_grads(
            d_edges_s[0, here, :],
            d_edges_s[1, here, :],
            slopes_s[0, here, :],
            slopes_s[1, here, :],
            edges_s[0, here, :],
            edges_s[1, here, :],
        )
        for g in range(4):
            d_pre_s[here, g * h : (g + 1) * h] = grads[g]
        if u == 1:
            up_ref[here, :] = input_pullback(here, upstream(t, here))

    if u == 0:
        cells = up_ref.shape[0]
        own = pl.ds(pl.multiple_of(index_ref[0] * cells, cells), cells)
        up_ref[...] = input_pullback(own, up_in_ref[own, :]).astype(BF16)
    weight_grads(normed_s, d_pre_s, mixed_s, d_branch_s, grads_ref)


def exchange(value, axis, size, step):
    return lax.ppermute(value, axis, [(d, d ^ step) for d in range(size)])


def add_narrow(a, b):
    return (a.astype(F32) + b.astype(F32)).astype(BF16)


def prepare(index_ref, state_ref, mask_ref, cot_ref, sent_ref, own_ref, state_s, mask_s, cot_s, sems):
    own_ref[0] = index_ref[0]
    parts, _, c = sent_ref.shape
    cells = state_s.shape[0]
    copies = [
        pltpu.make_async_copy(*pair, sems.at[k])
        for k, pair in enumerate(((mask_ref, mask_s), (state_ref, state_s), (cot_ref, cot_s)))
    ]
    for copy in copies:
        copy.start()
    copies[0].wait()
    length = jnp.max(jnp.sum(mask_s[...].astype(F32), axis=1, keepdims=True))
    below = jnp.full((sent_ref.shape[1] - 2 * cells, c), length, F32).astype(BF16)
    for copy in copies[1:]:
        copy.wait()
    for part in range(parts):
        sent_ref[part, :cells, :] = state_s[...]
        sent_ref[part, cells : 2 * cells, :] = cot_s[...]
        sent_ref[part, 2 * cells :, :] = below


def add_grads(own_0, other_0, own_both, other_both, proj_ref, out_ref):
    width = proj_ref.shape[2]
    for u, (own, other) in enumerate(((own_0, other_0), (own_both.at[1], other_both.at[1]))):
        total = own[...].astype(F32) + other[...].astype(F32)
        proj_ref[u] = total[:, :width]
        out_ref[u] = total[:, width:]


def crop_shards(
    groups,
    parts,
    pair_repr,
    pair_mask,
    cotangent,
    proj_weight,
    proj_bias,
    norm_gain,
    norm_shift,
    out_weight,
    out_bias,
):
    _, rows, n, c = pair_repr.shape
    h = out_weight.shape[1]
    width = proj_weight.shape[2]
    cells, pairs = rows * n, n * n
    plane = jax.ShapeDtypeStruct((pairs + 8, h), F32)
    narrow = jax.ShapeDtypeStruct((pairs, h), BF16)
    grads = jax.ShapeDtypeStruct((c, width + c), BF16)
    double = jax.ShapeDtypeStruct((2, pairs + 8, h), F32)
    kept = (double,) * 2 + (plane,) * 6 + (narrow,) * 2
    vmem = pl.BlockSpec(memory_space=pltpu.VMEM)
    smem = pl.BlockSpec(memory_space=pltpu.SMEM)
    main = pl.BlockSpec(memory_space=pltpu.HBM)
    params = pltpu.CompilerParams(vmem_limit_bytes=VMEM_BYTES)

    def scratch(array):
        return pltpu.VMEM(array.shape, array.dtype)

    def cost(planes):
        flops = 4 * pairs * width * c
        return pl.CostEstimate(
            flops=flops, bytes_accessed=planes * pairs * c * 4, transcendentals=0
        )

    index = lax.axis_index("dap").astype(jnp.int32)[None]
    sent, own = pl.pallas_call(
        prepare,
        out_shape=(
            jax.ShapeDtypeStruct((parts, 2 * cells + 16, c), BF16),
            jax.ShapeDtypeStruct((1,), jnp.int32),
        ),
        in_specs=[smem] + [main] * 3,
        out_specs=(vmem, smem),
        scratch_shapes=[
            pltpu.VMEM((cells, c), BF16),
            pltpu.VMEM((rows, n), jnp.int32),
            pltpu.VMEM((cells, c), BF16),
            pltpu.SemaphoreType.DMA((3,)),
        ],
        compiler_params=pltpu.CompilerParams(vmem_limit_bytes=PREPARE_BYTES),
        name="prepare",
    )(index, pair_repr.reshape(cells, c), pair_mask[0], cotangent.reshape(cells, c))
    state = lax.all_to_all(sent, "dap", split_axis=0, concat_axis=0, tiled=True)

    held = pl.pallas_call(
        functools.partial(forward, n),
        out_shape=kept * 2,
        in_specs=[vmem] * 7,
        out_specs=(vmem,) * (2 * KEPT),
        scratch_shapes=[scratch(plane), scratch(narrow)],
        compiler_params=params,
        cost_estimate=cost(64),
        name="forward",
    )(state, proj_weight, proj_bias, norm_gain, norm_shift, out_weight, out_bias)

    work = [scratch(double), scratch(double), scratch(narrow)]
    work.append(pltpu.VMEM((pairs, width), BF16))
    up_1, grads_1 = pl.pallas_call(
        functools.partial(backward, n, 1),
        out_shape=(jax.ShapeDtypeStruct((pairs, c), F32), grads),
        in_specs=[vmem] * (4 + KEPT),
        out_specs=(vmem, vmem),
        scratch_shapes=work,
        compiler_params=params,
        cost_estimate=cost(48),
        name="backward_second",
    )(state, proj_weight, norm_gain, out_weight, *held[KEPT:])
    far = groups // 2
    others_1 = exchange(grads_1, "dp", groups, far)

    pair_grad, grads_0 = pl.pallas_call(
        functools.partial(backward, n, 0),
        out_shape=(jax.ShapeDtypeStruct((cells, c), BF16), grads),
        in_specs=[smem] + [vmem] * (4 + KEPT),
        out_specs=(vmem, vmem),
        scratch_shapes=work,
        compiler_params=params,
        cost_estimate=cost(48),
        name="backward_first",
    )(own, up_1, proj_weight, norm_gain, out_weight, *held[:KEPT])

    both = jnp.stack([grads_0, add_narrow(grads_1, others_1)])
    others = jnp.zeros_like(both)
    step = 1
    while step < far:
        both = add_narrow(both, others) if step > 1 else both
        others = exchange(both, "dp", groups, step)
        step *= 2
    grads_0 = add_narrow(both[0], others[0])
    others_0 = exchange(grads_0, "dp", groups, far)

    proj_total, out_total = pl.pallas_call(
        add_grads,
        out_shape=(
            jax.ShapeDtypeStruct((2, c, width), F32),
            jax.ShapeDtypeStruct((2, h, c), F32),
        ),
        in_specs=[vmem] * 4,
        out_specs=(vmem, vmem),
        compiler_params=params,
        name="add_grads",
    )(grads_0, others_0, both, others)
    return pair_grad.reshape(pair_repr.shape), proj_total, out_total


def layer_norm(values, gain_vec, shift_vec, norm_axis):
    mean_value = jnp.mean(values, axis=norm_axis, keepdims=True)
    centred = values - mean_value
    variance = jnp.mean(centred * centred, axis=norm_axis, keepdims=True)
    return centred * lax.rsqrt(variance + NORM_EPSILON) * gain_vec + shift_vec


def norm_pullback(values, gain_vec, shift_vec, norm_axis, upstream):
    _, pull_back = jax.vjp(
        lambda inner_value: layer_norm(inner_value, gain_vec, shift_vec, norm_axis), values
    )
    return pull_back(upstream)[0]


def edge_pair(edge_pre, cell_mask):
    left_edge = jax.nn.sigmoid(edge_pre[1]) * edge_pre[0] * cell_mask
    right_edge = jax.nn.sigmoid(edge_pre[3]) * edge_pre[2] * cell_mask
    return jnp.stack([left_edge, right_edge]).astype(jnp.bfloat16)


def edge_pullback(edge_pre, cell_mask, grad_pair):
    sig_left = jax.nn.sigmoid(edge_pre[1])
    sig_right = jax.nn.sigmoid(edge_pre[3])
    grad_left = grad_pair[0].astype(jnp.float32) * cell_mask
    grad_right = grad_pair[1].astype(jnp.float32) * cell_mask
    return jnp.stack(
        [
            grad_left * sig_left,
            grad_left * edge_pre[0] * sig_left * (1.0 - sig_left),
            grad_right * sig_right,
            grad_right * edge_pre[2] * sig_right * (1.0 - sig_right),
        ]
    ).astype(jnp.bfloat16)


def triangle(pair_edges, outgoing):
    if outgoing:
        einsum_form = "cik,cjk->cij"
    else:
        einsum_form = "cki,ckj->cij"
    return jnp.einsum(
        einsum_form, pair_edges[0], pair_edges[1], preferred_element_type=jnp.float32
    ).astype(jnp.bfloat16)


def triangle_pullback(pair_edges, grad_product, outgoing):
    left_edge = pair_edges[0]
    right_edge = pair_edges[1]
    if outgoing:
        grad_left = jnp.einsum(
            "cij,cjk->cik", grad_product, right_edge, preferred_element_type=jnp.float32
        )
        grad_right = jnp.einsum(
            "cij,cik->cjk", grad_product, left_edge, preferred_element_type=jnp.float32
        )
    else:
        grad_left = jnp.einsum(
            "ckj,cij->cki", right_edge, grad_product, preferred_element_type=jnp.float32
        )
        grad_right = jnp.einsum(
            "cki,cij->ckj", left_edge, grad_product, preferred_element_type=jnp.float32
        )
    return jnp.stack([grad_left, grad_right]).astype(jnp.bfloat16)


def update_weights(proj_weight, proj_bias, norm_gain, norm_shift, update, channels, hidden):
    w_edge = proj_weight[update, :, : 4 * hidden].reshape(channels, 4, hidden)
    w_gate = proj_weight[update, :, 4 * hidden :]
    bias_edge = proj_bias[update, : 4 * hidden].reshape(4, hidden, 1, 1)
    bias_gate = proj_bias[update, 4 * hidden :]
    gain_in = norm_gain[update, :channels]
    shift_in = norm_shift[update, :channels]
    gain_out = norm_gain[update, channels:][:, None, None]
    shift_out = norm_shift[update, channels:][:, None, None]
    return (w_edge, w_gate, bias_edge, bias_gate, gain_in, shift_in, gain_out, shift_out)


def shards(
    pair_repr,
    pair_mask,
    cotangent,
    proj_weight,
    proj_bias,
    norm_gain,
    norm_shift,
    out_weight,
    out_bias,
):
    channels = pair_repr.shape[3]
    hidden = out_weight.shape[1]
    pair_state = pair_repr[0]
    cell_mask = pair_mask[0].astype(jnp.float32)
    records = []
    for update in range(2):
        w_edge, w_gate, bias_edge, bias_gate, gain_in, shift_in, gain_out, shift_out = (
            update_weights(proj_weight, proj_bias, norm_gain, norm_shift, update, channels, hidden)
        )
        state_f = pair_state.astype(jnp.float32)
        normed = layer_norm(state_f, gain_in, shift_in, -1).astype(jnp.bfloat16)
        edge_pre = (
            jnp.einsum("rnc,cgh->ghrn", normed, w_edge, preferred_element_type=jnp.float32)
            + bias_edge
        )
        gate_pre = (
            jnp.einsum("rnc,cd->rnd", normed, w_gate, preferred_element_type=jnp.float32)
            + bias_gate
        )
        pair_edges = edge_pair(edge_pre, cell_mask)
        spread = lax.all_to_all(pair_edges, "dap", split_axis=1, concat_axis=2, tiled=True)
        product = lax.all_to_all(
            triangle(spread, update == 0), "dap", split_axis=1, concat_axis=0, tiled=True
        )
        mixed_norm = layer_norm(product.astype(jnp.float32), gain_out, shift_out, 0).astype(
            jnp.bfloat16
        )
        branch = (
            jnp.einsum(
                "hrn,hd->rnd", mixed_norm, out_weight[update], preferred_element_type=jnp.float32
            )
            + out_bias[update]
        )
        records.append(
            (state_f, normed, edge_pre, gate_pre, pair_edges, spread, product, mixed_norm, branch)
        )
        pair_state = (state_f + jax.nn.sigmoid(gate_pre) * branch).astype(jnp.bfloat16)
    upstream = cotangent[0].astype(jnp.float32)
    proj_grads = []
    out_grads = []
    for update in (1, 0):
        state_f, normed, edge_pre, gate_pre, pair_edges, spread, product, mixed_norm, branch = (
            records[update]
        )
        w_edge, w_gate, bias_edge, bias_gate, gain_in, shift_in, gain_out, shift_out = (
            update_weights(proj_weight, proj_bias, norm_gain, norm_shift, update, channels, hidden)
        )
        gate_value = jax.nn.sigmoid(gate_pre)
        grad_branch = (upstream * gate_value).astype(jnp.bfloat16)
        grad_gate = (upstream * branch * gate_value * (1.0 - gate_value)).astype(jnp.bfloat16)
        out_grad = jnp.einsum(
            "hrn,rnd->hd", mixed_norm, grad_branch, preferred_element_type=jnp.float32
        )
        grad_mixed = jnp.einsum(
            "rnd,hd->hrn", grad_branch, out_weight[update], preferred_element_type=jnp.float32
        )
        grad_product = norm_pullback(
            product.astype(jnp.float32), gain_out, shift_out, 0, grad_mixed
        ).astype(jnp.bfloat16)
        column_edges = spread
        column_grad = lax.all_to_all(
            grad_product[None], "dap", split_axis=1, concat_axis=2, tiled=True
        )[0]
        grad_pair = lax.all_to_all(
            triangle_pullback(column_edges, column_grad, update == 0),
            "dap",
            split_axis=2,
            concat_axis=1,
            tiled=True,
        )
        grad_edge = edge_pullback(edge_pre, cell_mask, grad_pair)
        edge_grad = jnp.einsum(
            "rnc,ghrn->cgh", normed, grad_edge, preferred_element_type=jnp.float32
        ).reshape(channels, 4 * hidden)
        gate_grad = jnp.einsum("rnc,rnd->cd", normed, grad_gate, preferred_element_type=jnp.float32)
        grad_normed = jnp.einsum(
            "ghrn,cgh->rnc", grad_edge, w_edge, preferred_element_type=jnp.float32
        )
        grad_normed = grad_normed + jnp.einsum(
            "rnd,cd->rnc", grad_gate, w_gate, preferred_element_type=jnp.float32
        )
        upstream = upstream + norm_pullback(state_f, gain_in, shift_in, -1, grad_normed)
        proj_part = jnp.concatenate([edge_grad, gate_grad], axis=1)
        proj_grads.append(proj_part)
        out_grads.append(out_grad)
    proj_total = jnp.stack(proj_grads[::-1])
    out_total = jnp.stack(out_grads[::-1])
    proj_total, out_total = lax.psum((proj_total, out_total), ("dp", "dap"))
    return (upstream.astype(jnp.bfloat16)[None], proj_total, out_total)


def solution(mesh):
    placed = (
        P("dp", "dap", None, None),
        P("dp", "dap", None),
        P("dp", "dap", None, None),
        P(),
        P(),
        P(),
        P(),
        P(),
        P(),
    )
    groups, parts = mesh.shape["dp"], mesh.shape["dap"]

    def program(*args):
        n, c = args[0].shape[2:]
        rows = n // parts
        fits = 20 * n * n * c * 4 <= CROP_BUDGET
        even = args[7].shape[1] == c and groups > 1 and groups & (groups - 1) == 0 and BLOCK_ROWS % rows == 0 and n % 16 == 0
        body = functools.partial(crop_shards, groups, parts) if fits and even else shards
        return spread_over(body)(*args)

    def spread_over(body):
        return jax.shard_map(
            body,
            mesh=mesh,
            in_specs=placed,
            out_specs=(P("dp", "dap", None, None), P(), P()),
            check_vma=False,
        )

    return program
```

```python
import functools

import jax
import jax.numpy as jnp
from jax import lax
from jax.experimental import pallas as pl
from jax.experimental.pallas import tpu as pltpu
from jax.sharding import PartitionSpec as P

NORM_EPSILON = 1e-05
VMEM_BYTES = 16 * 1024 * 1024
PREPARE_BYTES = 63 * 1024 * 1024
CROP_BUDGET = 32 * 1024 * 1024
BLOCK_ROWS = 8
KEPT = 10
F32 = jnp.float32
BF16 = jnp.bfloat16


def sigmoid(x):
    return 0.5 * jnp.tanh(0.5 * x) + 0.5


def dot(a, b, dims=((1,), (0,))):
    return lax.dot_general(a, b, (dims, ((), ())), preferred_element_type=F32)


def lane_mean(x):
    c = x.shape[1]
    return dot(x.astype(BF16), jnp.full((c, c), 1.0 / c, BF16))


def norm_parts(x):
    centred = x.astype(F32) - lane_mean(x)
    rstd = lax.rsqrt(lane_mean(centred * centred) + NORM_EPSILON)
    return centred * rstd, rstd


def norm_vjp(x_hat, rstd, grad):
    return rstd * (grad - lane_mean(grad) - x_hat * lane_mean(grad * x_hat))


def pair_mask_block(length, first_row, rows, n, lanes):
    shape = (rows, n, lanes)
    i = lax.broadcasted_iota(jnp.int32, shape, 0) + first_row
    j = lax.broadcasted_iota(jnp.int32, shape, 1)
    inside = jnp.where((i < length) & (j < length), 1.0, 0.0)
    return inside.reshape(rows * n, lanes)


def project(x, mask, u, w, b, gain, shift):
    c = x.shape[1]
    x_hat, rstd = norm_parts(x)
    normed = (x_hat * gain[u : u + 1, :c] + shift[u : u + 1, :c]).astype(BF16)
    pre = dot(normed, w[u]) + b[u : u + 1, :]
    h = (pre.shape[1] - c) // 4
    s_left = sigmoid(pre[:, h : 2 * h]) * mask
    s_right = sigmoid(pre[:, 3 * h : 4 * h]) * mask
    left = s_left * pre[:, :h]
    right = s_right * pre[:, 2 * h : 3 * h]
    gate = sigmoid(pre[:, 4 * h :])
    return x_hat, rstd, normed, s_left, s_right, left, right, gate


def mix(product, u, c, gain, shift, w_out, b_out):
    p_hat, p_rstd = norm_parts(product)
    mixed = (p_hat * gain[u : u + 1, c:] + shift[u : u + 1, c:]).astype(BF16)
    branch = dot(mixed, w_out[u]) + b_out[u : u + 1, :]
    return p_hat, p_rstd, mixed, branch


def unmix(up, gate, branch, p_hat, p_rstd, u, c, gain, w_out):
    d_branch = up * gate
    d_gate = (d_branch * branch * (1.0 - gate)).astype(BF16)
    d_branch = d_branch.astype(BF16)
    d_mixed = dot(d_branch, w_out[u], ((1,), (1,))) * gain[u : u + 1, c:]
    return d_branch, d_gate, norm_vjp(p_hat, p_rstd, d_mixed)


def contract(n, first, row_of, x, y):
    lanes = y.shape[1]
    tiles = (n // 8, 8, lanes)

    def step(e, totals):
        block = y[pl.ds(pl.multiple_of(e * n, n), n), :].reshape(tiles)
        return tuple(
            totals[a] + x[pl.ds(row_of(first + a, e), 8, stride=0), :][None] * block
            for a in range(BLOCK_ROWS)
        )

    zero = jnp.zeros(tiles, F32)
    totals = lax.fori_loop(0, n, step, (zero,) * BLOCK_ROWS, unroll=True)
    return jnp.stack(totals).reshape(BLOCK_ROWS * n, lanes)


def edge_grads(d_left, d_right, s_left, s_right, left, right):
    return (
        (d_left * s_left).astype(BF16),
        (d_left * left * (1.0 - s_left)).astype(BF16),
        (d_right * s_right).astype(BF16),
        (d_right * right * (1.0 - s_right)).astype(BF16),
    )


def crop_length(state_ref, cells):
    return jnp.max(state_ref[:, 2 * cells :, :].astype(F32)).astype(jnp.int32)


def joined(ref, first, count, cells, place):
    span = slice(place * cells, (place + 1) * cells)
    return jnp.concatenate([ref[first + q, span, :] for q in range(count)], axis=0)


def forward(n, state_ref, w, b, gain, shift, w_out, b_out, *refs):
    kept, (right_t_s, next_s) = (refs[:KEPT], refs[KEPT : 2 * KEPT]), refs[2 * KEPT :]
    parts, _, c = state_ref.shape
    rows = n // parts
    cells = rows * n
    length = crop_length(state_ref, cells)
    per = BLOCK_ROWS // rows
    blocks = n // BLOCK_ROWS

    for u in range(2):
        (edges_s, slopes_s, gate_s, hat_s, rstd_s) = kept[u][:5]
        (p_hat_s, p_rstd_s, branch_s, normed_s, mixed_s) = kept[u][5:]

        @pl.loop(0, blocks)
        def _(t):
            first = t * BLOCK_ROWS
            here = pl.ds(pl.multiple_of(first * n, BLOCK_ROWS * n), BLOCK_ROWS * n)
            x = joined(state_ref, t * per, per, cells, 0) if u == 0 else next_s[here, :]
            mask = pair_mask_block(length, first, BLOCK_ROWS, n, c)
            x_hat, rstd, normed, s_left, s_right, left, right, gate = project(
                x, mask, u, w, b, gain, shift
            )
            edges_s[0, here, :] = left
            edges_s[1, here, :] = right
            slopes_s[0, here, :] = s_left
            slopes_s[1, here, :] = s_right
            gate_s[here, :] = gate
            hat_s[here, :] = x_hat
            rstd_s[here, :] = rstd
            normed_s[here, :] = normed
            if u == 0:
                for r in range(BLOCK_ROWS):
                    right_t_s[pl.ds(first + r, n, stride=n), :] = right[r * n : (r + 1) * n]

        @pl.loop(0, blocks)
        def _(t):
            first = t * BLOCK_ROWS
            here = pl.ds(pl.multiple_of(first * n, BLOCK_ROWS * n), BLOCK_ROWS * n)
            if u == 0:
                product = contract(n, first, lambda i, k: i * n + k, edges_s.at[0], right_t_s)
            else:
                product = contract(n, first, lambda i, k: k * n + i, edges_s.at[0], edges_s.at[1])
            p_hat, p_rstd, mixed, branch = mix(
                product.astype(BF16), u, c, gain, shift, w_out, b_out
            )
            p_hat_s[here, :] = p_hat
            p_rstd_s[here, :] = p_rstd
            mixed_s[here, :] = mixed
            branch_s[here, :] = branch
            if u == 0:
                x = joined(state_ref, t * per, per, cells, 0).astype(F32)
                next_s[here, :] = (x + gate_s[here, :] * branch).astype(BF16)


def backward(n, u, *refs):
    if u == 0:
        index_ref, refs = refs[0], refs[1:]
    up_in_ref, w, gain, w_out = refs[:4]
    (edges_s, slopes_s, gate_s, hat_s, rstd_s) = refs[4:9]
    (p_hat_s, p_rstd_s, branch_s, normed_s, mixed_s) = refs[9 : 4 + KEPT]
    up_ref, grads_ref, d_product_s, d_edges_s, d_pre_s, sums_s = refs[4 + KEPT :]
    c, h = w.shape[1], edges_s.shape[2]
    blocks = n // BLOCK_ROWS

    width = 4 * h + c
    sums_s[...] = jnp.zeros_like(sums_s)

    def upstream(t, here):
        if u == 0:
            return up_in_ref[here, :]
        rows = n // up_in_ref.shape[0]
        per = BLOCK_ROWS // rows
        return joined(up_in_ref, t * per, per, rows * n, 1).astype(F32)

    def input_pullback(here, up):
        d_normed = dot(d_pre_s[here, :], w[u], ((1,), (1,))) * gain[u : u + 1, :c]
        return up + norm_vjp(hat_s[here, :], rstd_s[here, :], d_normed)

    @pl.loop(0, blocks)
    def _(t):
        first = t * BLOCK_ROWS
        here = pl.ds(pl.multiple_of(first * n, BLOCK_ROWS * n), BLOCK_ROWS * n)
        d_branch, d_gate, d_product = unmix(
            upstream(t, here),
            gate_s[here, :],
            branch_s[here, :],
            p_hat_s[here, :],
            p_rstd_s[here, :],
            u,
            c,
            gain,
            w_out,
        )
        sums_s[:, width:] += dot(mixed_s[here, :], d_branch, ((0,), (0,)))
        d_pre_s[here, 4 * h :] = d_gate
        if u == 1:
            for r in range(BLOCK_ROWS):
                d_product_s[0, pl.ds(first + r, n, stride=n), :] = d_product[r * n : (r + 1) * n]
            d_product_s[1, here, :] = d_product
        else:
            d_product_s[0, here, :] = d_product
            for r in range(BLOCK_ROWS):
                d_product_s[1, pl.ds(first + r, n, stride=n), :] = d_product[r * n : (r + 1) * n]

    @pl.loop(0, 2 * blocks)
    def _(step):
        side, first = step // blocks, step % blocks * BLOCK_ROWS
        here = pl.ds(pl.multiple_of(first * n, BLOCK_ROWS * n), BLOCK_ROWS * n)
        edges, d_product = edges_s.at[1 - side], d_product_s.at[side]
        x, y = (edges, d_product) if u == 1 else (d_product, edges)
        d_edges_s[side, here, :] = contract(n, first, lambda a, e: a * n + e, x, y)

    @pl.loop(0, blocks)
    def _(t):
        here = pl.ds(pl.multiple_of(t * BLOCK_ROWS * n, BLOCK_ROWS * n), BLOCK_ROWS * n)
        grads = edge_grads(
            d_edges_s[0, here, :],
            d_edges_s[1, here, :],
            slopes_s[0, here, :],
            slopes_s[1, here, :],
            edges_s[0, here, :],
            edges_s[1, here, :],
        )
        for g in range(4):
            d_pre_s[here, g * h : (g + 1) * h] = grads[g]
        sums_s[:, :width] += dot(normed_s[here, :], d_pre_s[here, :], ((0,), (0,)))
        if u == 1:
            up_ref[here, :] = input_pullback(here, upstream(t, here))

    if u == 0:
        cells = up_ref.shape[0]
        own = pl.ds(pl.multiple_of(index_ref[0] * cells, cells), cells)
        up_ref[...] = input_pullback(own, up_in_ref[own, :]).astype(BF16)
    grads_ref[...] = sums_s[...].astype(BF16)


def exchange(value, axis, size, step):
    return lax.ppermute(value, axis, [(d, d ^ step) for d in range(size)])


def add_narrow(a, b):
    return (a.astype(F32) + b.astype(F32)).astype(BF16)


def prepare(index_ref, state_ref, mask_ref, cot_ref, sent_ref, own_ref, state_s, mask_s, cot_s, sems):
    own_ref[0] = index_ref[0]
    parts, _, c = sent_ref.shape
    cells = state_s.shape[0]
    copies = [
        pltpu.make_async_copy(*pair, sems.at[k])
        for k, pair in enumerate(((mask_ref, mask_s), (state_ref, state_s), (cot_ref, cot_s)))
    ]
    for copy in copies:
        copy.start()
    copies[0].wait()
    length = jnp.max(jnp.sum(mask_s[...].astype(F32), axis=1, keepdims=True))
    below = jnp.full((sent_ref.shape[1] - 2 * cells, c), length, F32).astype(BF16)
    for copy in copies[1:]:
        copy.wait()
    for part in range(parts):
        sent_ref[part, :cells, :] = state_s[...]
        sent_ref[part, cells : 2 * cells, :] = cot_s[...]
        sent_ref[part, 2 * cells :, :] = below


def add_grads(own_0, other_0, own_both, other_both, proj_ref, out_ref):
    width = proj_ref.shape[2]
    for u, (own, other) in enumerate(((own_0, other_0), (own_both.at[1], other_both.at[1]))):
        total = own[...].astype(F32) + other[...].astype(F32)
        proj_ref[u] = total[:, :width]
        out_ref[u] = total[:, width:]


def crop_shards(
    groups,
    parts,
    pair_repr,
    pair_mask,
    cotangent,
    proj_weight,
    proj_bias,
    norm_gain,
    norm_shift,
    out_weight,
    out_bias,
):
    _, rows, n, c = pair_repr.shape
    h = out_weight.shape[1]
    width = proj_weight.shape[2]
    cells, pairs = rows * n, n * n
    plane = jax.ShapeDtypeStruct((pairs + 8, h), F32)
    narrow = jax.ShapeDtypeStruct((pairs, h), BF16)
    grads = jax.ShapeDtypeStruct((c, width + c), BF16)
    double = jax.ShapeDtypeStruct((2, pairs + 8, h), F32)
    kept = (double,) * 2 + (plane,) * 6 + (narrow,) * 2
    vmem = pl.BlockSpec(memory_space=pltpu.VMEM)
    smem = pl.BlockSpec(memory_space=pltpu.SMEM)
    main = pl.BlockSpec(memory_space=pltpu.HBM)
    params = pltpu.CompilerParams(vmem_limit_bytes=VMEM_BYTES)

    def scratch(array):
        return pltpu.VMEM(array.shape, array.dtype)

    def cost(planes):
        flops = 4 * pairs * width * c
        return pl.CostEstimate(
            flops=flops, bytes_accessed=planes * pairs * c * 4, transcendentals=0
        )

    index = lax.axis_index("dap").astype(jnp.int32)[None]
    sent, own = pl.pallas_call(
        prepare,
        out_shape=(
            jax.ShapeDtypeStruct((parts, 2 * cells + 16, c), BF16),
            jax.ShapeDtypeStruct((1,), jnp.int32),
        ),
        in_specs=[smem] + [main] * 3,
        out_specs=(vmem, smem),
        scratch_shapes=[
            pltpu.VMEM((cells, c), BF16),
            pltpu.VMEM((rows, n), jnp.int32),
            pltpu.VMEM((cells, c), BF16),
            pltpu.SemaphoreType.DMA((3,)),
        ],
        compiler_params=pltpu.CompilerParams(vmem_limit_bytes=PREPARE_BYTES),
        name="prepare",
    )(index, pair_repr.reshape(cells, c), pair_mask[0], cotangent.reshape(cells, c))
    state = lax.all_to_all(sent, "dap", split_axis=0, concat_axis=0, tiled=True)

    held = pl.pallas_call(
        functools.partial(forward, n),
        out_shape=kept * 2,
        in_specs=[vmem] * 7,
        out_specs=(vmem,) * (2 * KEPT),
        scratch_shapes=[scratch(plane), scratch(narrow)],
        compiler_params=params,
        cost_estimate=cost(64),
        name="forward",
    )(state, proj_weight, proj_bias, norm_gain, norm_shift, out_weight, out_bias)

    work = [scratch(double), scratch(double)]
    work += [pltpu.VMEM((pairs, width), BF16), pltpu.VMEM(grads.shape, F32)]
    up_1, grads_1 = pl.pallas_call(
        functools.partial(backward, n, 1),
        out_shape=(jax.ShapeDtypeStruct((pairs, c), F32), grads),
        in_specs=[vmem] * (4 + KEPT),
        out_specs=(vmem, vmem),
        scratch_shapes=work,
        compiler_params=params,
        cost_estimate=cost(48),
        name="backward_second",
    )(state, proj_weight, norm_gain, out_weight, *held[KEPT:])
    far = groups // 2
    others_1 = exchange(grads_1, "dp", groups, far)

    pair_grad, grads_0 = pl.pallas_call(
        functools.partial(backward, n, 0),
        out_shape=(jax.ShapeDtypeStruct((cells, c), BF16), grads),
        in_specs=[smem] + [vmem] * (4 + KEPT),
        out_specs=(vmem, vmem),
        scratch_shapes=work,
        compiler_params=params,
        cost_estimate=cost(48),
        name="backward_first",
    )(own, up_1, proj_weight, norm_gain, out_weight, *held[:KEPT])

    both = jnp.stack([grads_0, add_narrow(grads_1, others_1)])
    others = jnp.zeros_like(both)
    step = 1
    while step < far:
        both = add_narrow(both, others) if step > 1 else both
        others = exchange(both, "dp", groups, step)
        step *= 2
    grads_0 = add_narrow(both[0], others[0])
    others_0 = exchange(grads_0, "dp", groups, far)

    proj_total, out_total = pl.pallas_call(
        add_grads,
        out_shape=(
            jax.ShapeDtypeStruct((2, c, width), F32),
            jax.ShapeDtypeStruct((2, h, c), F32),
        ),
        in_specs=[vmem] * 4,
        out_specs=(vmem, vmem),
        compiler_params=params,
        name="add_grads",
    )(grads_0, others_0, both, others)
    return pair_grad.reshape(pair_repr.shape), proj_total, out_total


def layer_norm(values, gain_vec, shift_vec, norm_axis):
    mean_value = jnp.mean(values, axis=norm_axis, keepdims=True)
    centred = values - mean_value
    variance = jnp.mean(centred * centred, axis=norm_axis, keepdims=True)
    return centred * lax.rsqrt(variance + NORM_EPSILON) * gain_vec + shift_vec


def norm_pullback(values, gain_vec, shift_vec, norm_axis, upstream):
    _, pull_back = jax.vjp(
        lambda inner_value: layer_norm(inner_value, gain_vec, shift_vec, norm_axis), values
    )
    return pull_back(upstream)[0]


def edge_pair(edge_pre, cell_mask):
    left_edge = jax.nn.sigmoid(edge_pre[1]) * edge_pre[0] * cell_mask
    right_edge = jax.nn.sigmoid(edge_pre[3]) * edge_pre[2] * cell_mask
    return jnp.stack([left_edge, right_edge]).astype(jnp.bfloat16)


def edge_pullback(edge_pre, cell_mask, grad_pair):
    sig_left = jax.nn.sigmoid(edge_pre[1])
    sig_right = jax.nn.sigmoid(edge_pre[3])
    grad_left = grad_pair[0].astype(jnp.float32) * cell_mask
    grad_right = grad_pair[1].astype(jnp.float32) * cell_mask
    return jnp.stack(
        [
            grad_left * sig_left,
            grad_left * edge_pre[0] * sig_left * (1.0 - sig_left),
            grad_right * sig_right,
            grad_right * edge_pre[2] * sig_right * (1.0 - sig_right),
        ]
    ).astype(jnp.bfloat16)


def triangle(pair_edges, outgoing):
    if outgoing:
        einsum_form = "cik,cjk->cij"
    else:
        einsum_form = "cki,ckj->cij"
    return jnp.einsum(
        einsum_form, pair_edges[0], pair_edges[1], preferred_element_type=jnp.float32
    ).astype(jnp.bfloat16)


def triangle_pullback(pair_edges, grad_product, outgoing):
    left_edge = pair_edges[0]
    right_edge = pair_edges[1]
    if outgoing:
        grad_left = jnp.einsum(
            "cij,cjk->cik", grad_product, right_edge, preferred_element_type=jnp.float32
        )
        grad_right = jnp.einsum(
            "cij,cik->cjk", grad_product, left_edge, preferred_element_type=jnp.float32
        )
    else:
        grad_left = jnp.einsum(
            "ckj,cij->cki", right_edge, grad_product, preferred_element_type=jnp.float32
        )
        grad_right = jnp.einsum(
            "cki,cij->ckj", left_edge, grad_product, preferred_element_type=jnp.float32
        )
    return jnp.stack([grad_left, grad_right]).astype(jnp.bfloat16)


def update_weights(proj_weight, proj_bias, norm_gain, norm_shift, update, channels, hidden):
    w_edge = proj_weight[update, :, : 4 * hidden].reshape(channels, 4, hidden)
    w_gate = proj_weight[update, :, 4 * hidden :]
    bias_edge = proj_bias[update, : 4 * hidden].reshape(4, hidden, 1, 1)
    bias_gate = proj_bias[update, 4 * hidden :]
    gain_in = norm_gain[update, :channels]
    shift_in = norm_shift[update, :channels]
    gain_out = norm_gain[update, channels:][:, None, None]
    shift_out = norm_shift[update, channels:][:, None, None]
    return (w_edge, w_gate, bias_edge, bias_gate, gain_in, shift_in, gain_out, shift_out)


def shards(
    pair_repr,
    pair_mask,
    cotangent,
    proj_weight,
    proj_bias,
    norm_gain,
    norm_shift,
    out_weight,
    out_bias,
):
    channels = pair_repr.shape[3]
    hidden = out_weight.shape[1]
    pair_state = pair_repr[0]
    cell_mask = pair_mask[0].astype(jnp.float32)
    records = []
    for update in range(2):
        w_edge, w_gate, bias_edge, bias_gate, gain_in, shift_in, gain_out, shift_out = (
            update_weights(proj_weight, proj_bias, norm_gain, norm_shift, update, channels, hidden)
        )
        state_f = pair_state.astype(jnp.float32)
        normed = layer_norm(state_f, gain_in, shift_in, -1).astype(jnp.bfloat16)
        edge_pre = (
            jnp.einsum("rnc,cgh->ghrn", normed, w_edge, preferred_element_type=jnp.float32)
            + bias_edge
        )
        gate_pre = (
            jnp.einsum("rnc,cd->rnd", normed, w_gate, preferred_element_type=jnp.float32)
            + bias_gate
        )
        pair_edges = edge_pair(edge_pre, cell_mask)
        spread = lax.all_to_all(pair_edges, "dap", split_axis=1, concat_axis=2, tiled=True)
        product = lax.all_to_all(
            triangle(spread, update == 0), "dap", split_axis=1, concat_axis=0, tiled=True
        )
        mixed_norm = layer_norm(product.astype(jnp.float32), gain_out, shift_out, 0).astype(
            jnp.bfloat16
        )
        branch = (
            jnp.einsum(
                "hrn,hd->rnd", mixed_norm, out_weight[update], preferred_element_type=jnp.float32
            )
            + out_bias[update]
        )
        records.append(
            (state_f, normed, edge_pre, gate_pre, pair_edges, spread, product, mixed_norm, branch)
        )
        pair_state = (state_f + jax.nn.sigmoid(gate_pre) * branch).astype(jnp.bfloat16)
    upstream = cotangent[0].astype(jnp.float32)
    proj_grads = []
    out_grads = []
    for update in (1, 0):
        state_f, normed, edge_pre, gate_pre, pair_edges, spread, product, mixed_norm, branch = (
            records[update]
        )
        w_edge, w_gate, bias_edge, bias_gate, gain_in, shift_in, gain_out, shift_out = (
            update_weights(proj_weight, proj_bias, norm_gain, norm_shift, update, channels, hidden)
        )
        gate_value = jax.nn.sigmoid(gate_pre)
        grad_branch = (upstream * gate_value).astype(jnp.bfloat16)
        grad_gate = (upstream * branch * gate_value * (1.0 - gate_value)).astype(jnp.bfloat16)
        out_grad = jnp.einsum(
            "hrn,rnd->hd", mixed_norm, grad_branch, preferred_element_type=jnp.float32
        )
        grad_mixed = jnp.einsum(
            "rnd,hd->hrn", grad_branch, out_weight[update], preferred_element_type=jnp.float32
        )
        grad_product = norm_pullback(
            product.astype(jnp.float32), gain_out, shift_out, 0, grad_mixed
        ).astype(jnp.bfloat16)
        column_edges = spread
        column_grad = lax.all_to_all(
            grad_product[None], "dap", split_axis=1, concat_axis=2, tiled=True
        )[0]
        grad_pair = lax.all_to_all(
            triangle_pullback(column_edges, column_grad, update == 0),
            "dap",
            split_axis=2,
            concat_axis=1,
            tiled=True,
        )
        grad_edge = edge_pullback(edge_pre, cell_mask, grad_pair)
        edge_grad = jnp.einsum(
            "rnc,ghrn->cgh", normed, grad_edge, preferred_element_type=jnp.float32
        ).reshape(channels, 4 * hidden)
        gate_grad = jnp.einsum("rnc,rnd->cd", normed, grad_gate, preferred_element_type=jnp.float32)
        grad_normed = jnp.einsum(
            "ghrn,cgh->rnc", grad_edge, w_edge, preferred_element_type=jnp.float32
        )
        grad_normed = grad_normed + jnp.einsum(
            "rnd,cd->rnc", grad_gate, w_gate, preferred_element_type=jnp.float32
        )
        upstream = upstream + norm_pullback(state_f, gain_in, shift_in, -1, grad_normed)
        proj_part = jnp.concatenate([edge_grad, gate_grad], axis=1)
        proj_grads.append(proj_part)
        out_grads.append(out_grad)
    proj_total = jnp.stack(proj_grads[::-1])
    out_total = jnp.stack(out_grads[::-1])
    proj_total, out_total = lax.psum((proj_total, out_total), ("dp", "dap"))
    return (upstream.astype(jnp.bfloat16)[None], proj_total, out_total)


def solution(mesh):
    placed = (
        P("dp", "dap", None, None),
        P("dp", "dap", None),
        P("dp", "dap", None, None),
        P(),
        P(),
        P(),
        P(),
        P(),
        P(),
    )
    groups, parts = mesh.shape["dp"], mesh.shape["dap"]

    def program(*args):
        n, c = args[0].shape[2:]
        rows = n // parts
        fits = 20 * n * n * c * 4 <= CROP_BUDGET
        even = c & (c - 1) == 0 and args[7].shape[1] == c and groups > 1 and groups & (groups - 1) == 0 and BLOCK_ROWS % rows == 0 and n % 16 == 0
        body = functools.partial(crop_shards, groups, parts) if fits and even else shards
        return spread_over(body)(*args)

    def spread_over(body):
        return jax.shard_map(
            body,
            mesh=mesh,
            in_specs=placed,
            out_specs=(P("dp", "dap", None, None), P(), P()),
            check_vma=False,
        )

    return program
```

```python
import functools

import jax
import jax.numpy as jnp
from jax import lax
from jax.experimental import pallas as pl
from jax.experimental.pallas import tpu as pltpu
from jax.sharding import PartitionSpec as P

NORM_EPSILON = 1e-05
VMEM_BYTES = 16 * 1024 * 1024
PREPARE_BYTES = 63 * 1024 * 1024
CROP_BUDGET = 32 * 1024 * 1024
BLOCK_ROWS = 8
KEPT = 10
F32 = jnp.float32
BF16 = jnp.bfloat16


def sigmoid(x):
    return 0.5 * jnp.tanh(0.5 * x) + 0.5


def dot(a, b, dims=((1,), (0,))):
    return lax.dot_general(a, b, (dims, ((), ())), preferred_element_type=F32)


def norm_parts(x):
    x = x.astype(F32)
    centred = x - jnp.mean(x, axis=-1, keepdims=True)
    rstd = lax.rsqrt(jnp.mean(centred * centred, axis=-1, keepdims=True) + NORM_EPSILON)
    return centred * rstd, jnp.broadcast_to(rstd, x.shape)


def norm_vjp(x_hat, rstd, grad):
    mean_grad = jnp.mean(grad, axis=-1, keepdims=True)
    mean_prod = jnp.mean(grad * x_hat, axis=-1, keepdims=True)
    return rstd * (grad - mean_grad - x_hat * mean_prod)


def pair_mask_block(length, first_row, rows, n, lanes):
    shape = (rows, n, lanes)
    i = lax.broadcasted_iota(jnp.int32, shape, 0) + first_row
    j = lax.broadcasted_iota(jnp.int32, shape, 1)
    inside = jnp.where((i < length) & (j < length), 1.0, 0.0)
    return inside.reshape(rows * n, lanes)


def project(x, mask, w, b, gain, shift):
    x_hat, rstd = norm_parts(x)
    normed = (x_hat * gain + shift).astype(BF16)
    pre = dot(normed, w) + b
    h = (pre.shape[1] - x.shape[1]) // 4
    s_left = sigmoid(pre[:, h : 2 * h]) * mask
    s_right = sigmoid(pre[:, 3 * h : 4 * h]) * mask
    left = s_left * pre[:, :h]
    right = s_right * pre[:, 2 * h : 3 * h]
    gate = sigmoid(pre[:, 4 * h :])
    return x_hat, rstd, normed, s_left, s_right, left, right, gate


def mix(product, gain, shift, w_out, b_out):
    p_hat, p_rstd = norm_parts(product)
    mixed = (p_hat * gain + shift).astype(BF16)
    return p_hat, p_rstd, mixed, dot(mixed, w_out) + b_out


def unmix(up, gate, branch, p_hat, p_rstd, gain, w_out):
    d_branch = up * gate
    d_gate = (d_branch * branch * (1.0 - gate)).astype(BF16)
    d_branch = d_branch.astype(BF16)
    d_mixed = dot(d_branch, w_out, ((1,), (1,))) * gain
    return d_branch, d_gate, norm_vjp(p_hat, p_rstd, d_mixed)


def contract(n, first, x, y, unroll=True):
    lanes = y.shape[1]
    tiles = (n // 8, 8, lanes)

    def step(e, totals):
        block = y[pl.ds(pl.multiple_of(e * n, n), n), :].reshape(tiles)
        return tuple(
            totals[a] + x[pl.ds((first + a) * n + e, 8, stride=0), :][None] * block
            for a in range(BLOCK_ROWS)
        )

    zero = jnp.zeros(tiles, F32)
    totals = lax.fori_loop(0, n, step, (zero,) * BLOCK_ROWS, unroll=unroll)
    return jnp.stack(totals).reshape(BLOCK_ROWS * n, lanes)


def edge_grads(d_left, d_right, s_left, s_right, left, right):
    return (
        (d_left * s_left).astype(BF16),
        (d_left * left * (1.0 - s_left)).astype(BF16),
        (d_right * s_right).astype(BF16),
        (d_right * right * (1.0 - s_right)).astype(BF16),
    )


def crop_length(state_ref, cells):
    return jnp.max(state_ref[:, 2 * cells :, :].astype(F32)).astype(jnp.int32)


def joined(ref, first, count, cells, place):
    span = slice(place * cells, (place + 1) * cells)
    return jnp.concatenate([ref[first + q, span, :] for q in range(count)], axis=0)


def block(t, rows, n):
    return pl.ds(pl.multiple_of(t * rows * n, rows * n), rows * n)


def forward(n, state_ref, w, b, gain, shift, w_out, b_out, *refs):
    (edges_s, slopes_s, gate_s, hat_s, rstd_s) = refs[:5]
    (p_hat_s, p_rstd_s, branch_s, normed_s, mixed_s) = refs[5:KEPT]
    (next_s,) = refs[KEPT:]
    parts, _, c = state_ref.shape
    rows = n // parts
    cells = rows * n
    length = crop_length(state_ref, cells)
    blocks = n // BLOCK_ROWS

    @pl.loop(0, parts)
    def _(t):
        next_s[block(t, rows, n), :] = state_ref[t, :cells, :]

    @pl.loop(0, 2)
    def _(u):
        bias, gains, shifts, bias_out = (
            jnp.where(u == 0, ref[0:1, :], ref[1:2, :]) for ref in (b, gain, shift, b_out)
        )

        @pl.loop(0, blocks, unroll=2)
        def _(t):
            first = t * BLOCK_ROWS
            here = block(t, BLOCK_ROWS, n)
            mask = pair_mask_block(length, first, BLOCK_ROWS, n, c)
            x_hat, rstd, normed, s_left, s_right, left, right, gate = project(
                next_s[here, :], mask, w[u], bias, gains[:, :c], shifts[:, :c]
            )
            edges_s[u, 0, here, :] = left
            edges_s[u, 1, here, :] = right
            for r in range(BLOCK_ROWS):
                swapped = pl.ds(first + r, n, stride=n)
                edges_s[u, 2, swapped, :] = right[r * n : (r + 1) * n]
                edges_s[u, 3, swapped, :] = left[r * n : (r + 1) * n]
            slopes_s[u, 0, here, :] = s_left
            slopes_s[u, 1, here, :] = s_right
            gate_s[u, here, :] = gate
            hat_s[u, here, :] = x_hat
            rstd_s[u, here, :] = rstd
            normed_s[u, here, :] = normed

        @pl.loop(0, blocks, unroll=2)
        def _(t):
            here = block(t, BLOCK_ROWS, n)
            product = contract(n, t * BLOCK_ROWS, edges_s.at[u, 3 * u], edges_s.at[u, 2 - u])
            p_hat, p_rstd, mixed, branch = mix(
                product.astype(BF16), gains[:, c:], shifts[:, c:], w_out[u], bias_out
            )
            p_hat_s[u, here, :] = p_hat
            p_rstd_s[u, here, :] = p_rstd
            mixed_s[u, here, :] = mixed
            branch_s[u, here, :] = branch
            x = next_s[here, :].astype(F32)
            next_s[here, :] = (x + gate_s[u, here, :] * branch).astype(BF16)


def backward(n, u, unmix_rows, unroll, *refs):
    if u == 0:
        index_ref, refs = refs[0], refs[1:]
    up_in_ref, w, gain, w_out = refs[:4]
    (edges_s, slopes_s, gate_s, hat_s, rstd_s) = (ref.at[u] for ref in refs[4:9])
    (p_hat_s, p_rstd_s, branch_s, normed_s, mixed_s) = (ref.at[u] for ref in refs[9 : 4 + KEPT])
    up_ref, grads_ref, d_product_s, d_edges_s, d_pre_s, sums_s = refs[4 + KEPT :]
    c, h = w.shape[1], edges_s.shape[2]
    width = 4 * h + c
    sums_s[...] = jnp.zeros_like(sums_s)

    def upstream(t, rows):
        if u == 0:
            return up_in_ref[block(t, rows, n), :]
        own = n // up_in_ref.shape[0]
        per = rows // own
        return joined(up_in_ref, t * per, per, own * n, 1).astype(F32)

    def input_pullback(here, up):
        d_normed = dot(d_pre_s[here, :], w[u], ((1,), (1,))) * gain[u : u + 1, :c]
        return up + norm_vjp(hat_s[here, :], rstd_s[here, :], d_normed)

    @pl.loop(0, n // unmix_rows)
    def _(t):
        here = block(t, unmix_rows, n)
        d_branch, d_gate, d_product = unmix(
            upstream(t, unmix_rows),
            gate_s[here, :],
            branch_s[here, :],
            p_hat_s[here, :],
            p_rstd_s[here, :],
            gain[u : u + 1, c:],
            w_out[u],
        )
        sums_s[:, width:] += dot(mixed_s[here, :], d_branch, ((0,), (0,)))
        d_pre_s[here, 4 * h :] = d_gate
        d_product_s[u, here, :] = d_product
        for r in range(unmix_rows):
            swapped = pl.ds(t * unmix_rows + r, n, stride=n)
            d_product_s[1 - u, swapped, :] = d_product[r * n : (r + 1) * n]

    blocks = n // BLOCK_ROWS

    @pl.loop(0, 2 * blocks)
    def _(step):
        side, t = step // blocks, step % blocks
        edges, d_product = edges_s.at[1 - side], d_product_s.at[side]
        x, y = (edges, d_product) if u == 1 else (d_product, edges)
        d_edges_s[side, block(t, BLOCK_ROWS, n), :] = contract(n, t * BLOCK_ROWS, x, y, unroll)

    @pl.loop(0, blocks)
    def _(t):
        here = block(t, BLOCK_ROWS, n)
        grads = edge_grads(
            d_edges_s[0, here, :],
            d_edges_s[1, here, :],
            slopes_s[0, here, :],
            slopes_s[1, here, :],
            edges_s[0, here, :],
            edges_s[1, here, :],
        )
        for g in range(4):
            d_pre_s[here, g * h : (g + 1) * h] = grads[g]
        sums_s[:, :width] += dot(normed_s[here, :], d_pre_s[here, :], ((0,), (0,)))
        if u == 1:
            up_ref[here, :] = input_pullback(here, upstream(t, BLOCK_ROWS))

    if u == 0:
        cells = up_ref.shape[0]
        own = pl.ds(pl.multiple_of(index_ref[0] * cells, cells), cells)
        up_ref[...] = input_pullback(own, up_in_ref[own, :]).astype(BF16)
    grads_ref[...] = sums_s[...].astype(BF16)


def exchange(value, axis, size, step):
    return lax.ppermute(value, axis, [(d, d ^ step) for d in range(size)])


def add_narrow(a, b):
    return (a.astype(F32) + b.astype(F32)).astype(BF16)


def prepare(index_ref, state_ref, mask_ref, cot_ref, sent_ref, own_ref, state_s, mask_s, cot_s, sems):
    own_ref[0] = index_ref[0]
    parts, _, c = sent_ref.shape
    cells = state_s.shape[0]
    copies = [
        pltpu.make_async_copy(*pair, sems.at[k])
        for k, pair in enumerate(((mask_ref, mask_s), (state_ref, state_s), (cot_ref, cot_s)))
    ]
    for copy in copies:
        copy.start()
    copies[0].wait()
    length = jnp.max(jnp.sum(mask_s[...].astype(F32), axis=1, keepdims=True))
    below = jnp.full((sent_ref.shape[1] - 2 * cells, c), length, F32).astype(BF16)
    for copy in copies[1:]:
        copy.wait()
    for part in range(parts):
        sent_ref[part, :cells, :] = state_s[...]
        sent_ref[part, cells : 2 * cells, :] = cot_s[...]
        sent_ref[part, 2 * cells :, :] = below


def add_grads(own_0, other_0, own_both, other_both, proj_ref, out_ref):
    width = proj_ref.shape[2]
    for u, (own, other) in enumerate(((own_0, other_0), (own_both.at[1], other_both.at[1]))):
        total = own[...].astype(F32) + other[...].astype(F32)
        proj_ref[u] = total[:, :width]
        out_ref[u] = total[:, width:]


def crop_shards(
    groups,
    parts,
    pair_repr,
    pair_mask,
    cotangent,
    proj_weight,
    proj_bias,
    norm_gain,
    norm_shift,
    out_weight,
    out_bias,
):
    _, rows, n, c = pair_repr.shape
    h = out_weight.shape[1]
    width = proj_weight.shape[2]
    cells, pairs = rows * n, n * n
    plane = (pairs + 8, h)
    kept = [jax.ShapeDtypeStruct((2, 4) + plane, F32), jax.ShapeDtypeStruct((2, 2) + plane, F32)]
    kept += [jax.ShapeDtypeStruct((2,) + plane, F32)] * 6
    kept += [jax.ShapeDtypeStruct((2, pairs, h), BF16)] * 2
    grads = jax.ShapeDtypeStruct((c, width + c), BF16)
    vmem = pl.BlockSpec(memory_space=pltpu.VMEM)
    smem = pl.BlockSpec(memory_space=pltpu.SMEM)
    main = pl.BlockSpec(memory_space=pltpu.HBM)
    params = pltpu.CompilerParams(vmem_limit_bytes=VMEM_BYTES)

    def cost(planes):
        flops = 4 * pairs * width * c
        return pl.CostEstimate(
            flops=flops, bytes_accessed=planes * pairs * c * 4, transcendentals=0
        )

    index = lax.axis_index("dap").astype(jnp.int32)[None]
    sent, own = pl.pallas_call(
        prepare,
        out_shape=(
            jax.ShapeDtypeStruct((parts, 2 * cells + 16, c), BF16),
            jax.ShapeDtypeStruct((1,), jnp.int32),
        ),
        in_specs=[smem] + [main] * 3,
        out_specs=(vmem, smem),
        scratch_shapes=[
            pltpu.VMEM((cells, c), BF16),
            pltpu.VMEM((rows, n), jnp.int32),
            pltpu.VMEM((cells, c), BF16),
            pltpu.SemaphoreType.DMA((3,)),
        ],
        compiler_params=pltpu.CompilerParams(vmem_limit_bytes=PREPARE_BYTES),
        name="prepare",
    )(index, pair_repr.reshape(cells, c), pair_mask[0], cotangent.reshape(cells, c))
    state = lax.all_to_all(sent, "dap", split_axis=0, concat_axis=0, tiled=True)

    held = pl.pallas_call(
        functools.partial(forward, n),
        out_shape=kept,
        in_specs=[vmem] * 7,
        out_specs=(vmem,) * KEPT,
        scratch_shapes=[pltpu.VMEM((pairs, c), BF16)],
        compiler_params=params,
        cost_estimate=cost(64),
        name="forward",
    )(state, proj_weight, proj_bias, norm_gain, norm_shift, out_weight, out_bias)

    work = [pltpu.VMEM((2,) + plane, F32)] * 2
    work += [pltpu.VMEM((pairs, width), BF16), pltpu.VMEM(grads.shape, F32)]
    up_1, grads_1 = pl.pallas_call(
        functools.partial(backward, n, 1, BLOCK_ROWS, True),
        out_shape=(jax.ShapeDtypeStruct((pairs, c), F32), grads),
        in_specs=[vmem] * (4 + KEPT),
        out_specs=(vmem, vmem),
        scratch_shapes=work,
        compiler_params=params,
        cost_estimate=cost(48),
        name="backward_second",
    )(state, proj_weight, norm_gain, out_weight, *held)
    far = groups // 2
    others_1 = exchange(grads_1, "dp", groups, far)

    pair_grad, grads_0 = pl.pallas_call(
        functools.partial(backward, n, 0, BLOCK_ROWS // 2, 8),
        out_shape=(jax.ShapeDtypeStruct((cells, c), BF16), grads),
        in_specs=[smem] + [vmem] * (4 + KEPT),
        out_specs=(vmem, vmem),
        scratch_shapes=work,
        compiler_params=params,
        cost_estimate=cost(48),
        name="backward_first",
    )(own, up_1, proj_weight, norm_gain, out_weight, *held)

    both = jnp.stack([grads_0, add_narrow(grads_1, others_1)])
    others = jnp.zeros_like(both)
    step = 1
    while step < far:
        both = add_narrow(both, others) if step > 1 else both
        others = exchange(both, "dp", groups, step)
        step *= 2
    grads_0 = add_narrow(both[0], others[0])
    others_0 = exchange(grads_0, "dp", groups, far)

    proj_total, out_total = pl.pallas_call(
        add_grads,
        out_shape=(
            jax.ShapeDtypeStruct((2, c, width), F32),
            jax.ShapeDtypeStruct((2, h, c), F32),
        ),
        in_specs=[vmem] * 4,
        out_specs=(vmem, vmem),
        compiler_params=params,
        name="add_grads",
    )(grads_0, others_0, both, others)
    return pair_grad.reshape(pair_repr.shape), proj_total, out_total


def layer_norm(values, gain_vec, shift_vec, norm_axis):
    mean_value = jnp.mean(values, axis=norm_axis, keepdims=True)
    centred = values - mean_value
    variance = jnp.mean(centred * centred, axis=norm_axis, keepdims=True)
    return centred * lax.rsqrt(variance + NORM_EPSILON) * gain_vec + shift_vec


def norm_pullback(values, gain_vec, shift_vec, norm_axis, upstream):
    _, pull_back = jax.vjp(
        lambda inner_value: layer_norm(inner_value, gain_vec, shift_vec, norm_axis), values
    )
    return pull_back(upstream)[0]


def edge_pair(edge_pre, cell_mask):
    left_edge = jax.nn.sigmoid(edge_pre[1]) * edge_pre[0] * cell_mask
    right_edge = jax.nn.sigmoid(edge_pre[3]) * edge_pre[2] * cell_mask
    return jnp.stack([left_edge, right_edge]).astype(jnp.bfloat16)


def edge_pullback(edge_pre, cell_mask, grad_pair):
    sig_left = jax.nn.sigmoid(edge_pre[1])
    sig_right = jax.nn.sigmoid(edge_pre[3])
    grad_left = grad_pair[0].astype(jnp.float32) * cell_mask
    grad_right = grad_pair[1].astype(jnp.float32) * cell_mask
    return jnp.stack(
        [
            grad_left * sig_left,
            grad_left * edge_pre[0] * sig_left * (1.0 - sig_left),
            grad_right * sig_right,
            grad_right * edge_pre[2] * sig_right * (1.0 - sig_right),
        ]
    ).astype(jnp.bfloat16)


def triangle(pair_edges, outgoing):
    if outgoing:
        einsum_form = "cik,cjk->cij"
    else:
        einsum_form = "cki,ckj->cij"
    return jnp.einsum(
        einsum_form, pair_edges[0], pair_edges[1], preferred_element_type=jnp.float32
    ).astype(jnp.bfloat16)


def triangle_pullback(pair_edges, grad_product, outgoing):
    left_edge = pair_edges[0]
    right_edge = pair_edges[1]
    if outgoing:
        grad_left = jnp.einsum(
            "cij,cjk->cik", grad_product, right_edge, preferred_element_type=jnp.float32
        )
        grad_right = jnp.einsum(
            "cij,cik->cjk", grad_product, left_edge, preferred_element_type=jnp.float32
        )
    else:
        grad_left = jnp.einsum(
            "ckj,cij->cki", right_edge, grad_product, preferred_element_type=jnp.float32
        )
        grad_right = jnp.einsum(
            "cki,cij->ckj", left_edge, grad_product, preferred_element_type=jnp.float32
        )
    return jnp.stack([grad_left, grad_right]).astype(jnp.bfloat16)


def update_weights(proj_weight, proj_bias, norm_gain, norm_shift, update, channels, hidden):
    w_edge = proj_weight[update, :, : 4 * hidden].reshape(channels, 4, hidden)
    w_gate = proj_weight[update, :, 4 * hidden :]
    bias_edge = proj_bias[update, : 4 * hidden].reshape(4, hidden, 1, 1)
    bias_gate = proj_bias[update, 4 * hidden :]
    gain_in = norm_gain[update, :channels]
    shift_in = norm_shift[update, :channels]
    gain_out = norm_gain[update, channels:][:, None, None]
    shift_out = norm_shift[update, channels:][:, None, None]
    return (w_edge, w_gate, bias_edge, bias_gate, gain_in, shift_in, gain_out, shift_out)


def shards(
    pair_repr,
    pair_mask,
    cotangent,
    proj_weight,
    proj_bias,
    norm_gain,
    norm_shift,
    out_weight,
    out_bias,
):
    channels = pair_repr.shape[3]
    hidden = out_weight.shape[1]
    pair_state = pair_repr[0]
    cell_mask = pair_mask[0].astype(jnp.float32)
    records = []
    for update in range(2):
        w_edge, w_gate, bias_edge, bias_gate, gain_in, shift_in, gain_out, shift_out = (
            update_weights(proj_weight, proj_bias, norm_gain, norm_shift, update, channels, hidden)
        )
        state_f = pair_state.astype(jnp.float32)
        normed = layer_norm(state_f, gain_in, shift_in, -1).astype(jnp.bfloat16)
        edge_pre = (
            jnp.einsum("rnc,cgh->ghrn", normed, w_edge, preferred_element_type=jnp.float32)
            + bias_edge
        )
        gate_pre = (
            jnp.einsum("rnc,cd->rnd", normed, w_gate, preferred_element_type=jnp.float32)
            + bias_gate
        )
        pair_edges = edge_pair(edge_pre, cell_mask)
        spread = lax.all_to_all(pair_edges, "dap", split_axis=1, concat_axis=2, tiled=True)
        product = lax.all_to_all(
            triangle(spread, update == 0), "dap", split_axis=1, concat_axis=0, tiled=True
        )
        mixed_norm = layer_norm(product.astype(jnp.float32), gain_out, shift_out, 0).astype(
            jnp.bfloat16
        )
        branch = (
            jnp.einsum(
                "hrn,hd->rnd", mixed_norm, out_weight[update], preferred_element_type=jnp.float32
            )
            + out_bias[update]
        )
        records.append(
            (state_f, normed, edge_pre, gate_pre, pair_edges, spread, product, mixed_norm, branch)
        )
        pair_state = (state_f + jax.nn.sigmoid(gate_pre) * branch).astype(jnp.bfloat16)
    upstream = cotangent[0].astype(jnp.float32)
    proj_grads = []
    out_grads = []
    for update in (1, 0):
        state_f, normed, edge_pre, gate_pre, pair_edges, spread, product, mixed_norm, branch = (
            records[update]
        )
        w_edge, w_gate, bias_edge, bias_gate, gain_in, shift_in, gain_out, shift_out = (
            update_weights(proj_weight, proj_bias, norm_gain, norm_shift, update, channels, hidden)
        )
        gate_value = jax.nn.sigmoid(gate_pre)
        grad_branch = (upstream * gate_value).astype(jnp.bfloat16)
        grad_gate = (upstream * branch * gate_value * (1.0 - gate_value)).astype(jnp.bfloat16)
        out_grad = jnp.einsum(
            "hrn,rnd->hd", mixed_norm, grad_branch, preferred_element_type=jnp.float32
        )
        grad_mixed = jnp.einsum(
            "rnd,hd->hrn", grad_branch, out_weight[update], preferred_element_type=jnp.float32
        )
        grad_product = norm_pullback(
            product.astype(jnp.float32), gain_out, shift_out, 0, grad_mixed
        ).astype(jnp.bfloat16)
        column_edges = spread
        column_grad = lax.all_to_all(
            grad_product[None], "dap", split_axis=1, concat_axis=2, tiled=True
        )[0]
        grad_pair = lax.all_to_all(
            triangle_pullback(column_edges, column_grad, update == 0),
            "dap",
            split_axis=2,
            concat_axis=1,
            tiled=True,
        )
        grad_edge = edge_pullback(edge_pre, cell_mask, grad_pair)
        edge_grad = jnp.einsum(
            "rnc,ghrn->cgh", normed, grad_edge, preferred_element_type=jnp.float32
        ).reshape(channels, 4 * hidden)
        gate_grad = jnp.einsum("rnc,rnd->cd", normed, grad_gate, preferred_element_type=jnp.float32)
        grad_normed = jnp.einsum(
            "ghrn,cgh->rnc", grad_edge, w_edge, preferred_element_type=jnp.float32
        )
        grad_normed = grad_normed + jnp.einsum(
            "rnd,cd->rnc", grad_gate, w_gate, preferred_element_type=jnp.float32
        )
        upstream = upstream + norm_pullback(state_f, gain_in, shift_in, -1, grad_normed)
        proj_part = jnp.concatenate([edge_grad, gate_grad], axis=1)
        proj_grads.append(proj_part)
        out_grads.append(out_grad)
    proj_total = jnp.stack(proj_grads[::-1])
    out_total = jnp.stack(out_grads[::-1])
    proj_total, out_total = lax.psum((proj_total, out_total), ("dp", "dap"))
    return (upstream.astype(jnp.bfloat16)[None], proj_total, out_total)


def solution(mesh):
    placed = (
        P("dp", "dap", None, None),
        P("dp", "dap", None),
        P("dp", "dap", None, None),
        P(),
        P(),
        P(),
        P(),
        P(),
        P(),
    )
    groups, parts = mesh.shape["dp"], mesh.shape["dap"]

    def program(*args):
        n, c = args[0].shape[2:]
        rows = n // parts
        fits = 20 * n * n * c * 4 <= CROP_BUDGET
        paired = groups > 1 and groups & (groups - 1) == 0
        even = args[7].shape[1] == c and BLOCK_ROWS // 2 % rows == 0 and n % 16 == 0
        body = functools.partial(crop_shards, groups, parts) if fits and even and paired else shards
        return spread_over(body)(*args)

    def spread_over(body):
        return jax.shard_map(
            body,
            mesh=mesh,
            in_specs=placed,
            out_specs=(P("dp", "dap", None, None), P(), P()),
            check_vma=False,
        )

    return program
```

```python
import functools

import jax
import jax.numpy as jnp
from jax import lax
from jax.experimental import pallas as pl
from jax.experimental.pallas import tpu as pltpu
from jax.sharding import PartitionSpec as P

NORM_EPSILON = 1e-05
VMEM_BYTES = 16 * 1024 * 1024
PREPARE_BYTES = 63 * 1024 * 1024
CROP_BUDGET = 32 * 1024 * 1024
BLOCK_ROWS = 8
STEP_ROWS = 16
KEPT = 10
F32 = jnp.float32
BF16 = jnp.bfloat16


def sigmoid(x):
    return 0.5 * jnp.tanh(0.5 * x) + 0.5


def dot(a, b, dims=((1,), (0,))):
    return lax.dot_general(a, b, (dims, ((), ())), preferred_element_type=F32)


def norm_parts(x):
    x = x.astype(F32)
    centred = x - jnp.mean(x, axis=-1, keepdims=True)
    rstd = lax.rsqrt(jnp.mean(centred * centred, axis=-1, keepdims=True) + NORM_EPSILON)
    return centred * rstd, jnp.broadcast_to(rstd, x.shape)


def norm_vjp(x_hat, rstd, grad):
    mean_grad = jnp.mean(grad, axis=-1, keepdims=True)
    mean_prod = jnp.mean(grad * x_hat, axis=-1, keepdims=True)
    return rstd * (grad - mean_grad - x_hat * mean_prod)


def pair_mask_block(length, first_row, rows, n, lanes):
    shape = (rows, n, lanes)
    i = lax.broadcasted_iota(jnp.int32, shape, 0) + first_row
    j = lax.broadcasted_iota(jnp.int32, shape, 1)
    inside = jnp.where((i < length) & (j < length), 1.0, 0.0)
    return inside.reshape(rows * n, lanes)


def project(x, mask, w, b, gain, shift):
    x_hat, rstd = norm_parts(x)
    normed = (x_hat * gain + shift).astype(BF16)
    pre = dot(normed, w) + b
    h = (pre.shape[1] - x.shape[1]) // 4
    s_left = sigmoid(pre[:, h : 2 * h]) * mask
    s_right = sigmoid(pre[:, 3 * h : 4 * h]) * mask
    left = s_left * pre[:, :h]
    right = s_right * pre[:, 2 * h : 3 * h]
    gate = sigmoid(pre[:, 4 * h :])
    return x_hat, rstd, normed, s_left, s_right, left, right, gate


def mix(product, gain, shift, w_out, b_out):
    p_hat, p_rstd = norm_parts(product)
    mixed = (p_hat * gain + shift).astype(BF16)
    return p_hat, p_rstd, mixed, dot(mixed, w_out) + b_out


def unmix(up, gate, branch, p_hat, p_rstd, gain, w_out):
    d_branch = up * gate
    d_gate = (d_branch * branch * (1.0 - gate)).astype(BF16)
    d_branch = d_branch.astype(BF16)
    d_mixed = dot(d_branch, w_out, ((1,), (1,))) * gain
    return d_branch, d_gate, norm_vjp(p_hat, p_rstd, d_mixed)


def contract(n, first, x, y):
    lanes = y.shape[1]
    tiles = (n // 8, 8, lanes)

    def step(e, totals):
        block = y[pl.ds(pl.multiple_of(e * n, n), n), :].reshape(tiles)
        return tuple(
            totals[a] + x[pl.ds((first + a) * n + e, 8, stride=0), :][None] * block
            for a in range(BLOCK_ROWS)
        )

    zero = jnp.zeros(tiles, F32)
    totals = lax.fori_loop(0, n, step, (zero,) * BLOCK_ROWS, unroll=True)
    return jnp.stack(totals).reshape(BLOCK_ROWS * n, lanes)


def edge_grads(d_left, d_right, s_left, s_right, left, right):
    return (
        (d_left * s_left).astype(BF16),
        (d_left * left * (1.0 - s_left)).astype(BF16),
        (d_right * s_right).astype(BF16),
        (d_right * right * (1.0 - s_right)).astype(BF16),
    )


def tail_values(block, lanes_from, lanes_to):
    lane = lax.broadcasted_iota(jnp.int32, block.shape, block.ndim - 1)
    inside = (lane >= lanes_from) & (lane < lanes_to)
    return jnp.max(jnp.where(inside, block.astype(F32), 0.0)).astype(jnp.int32)


def crop_length(state_ref, cells):
    return tail_values(state_ref[:, 2 * cells :, :], 0, 64)


def own_place(state_ref, cells):
    return tail_values(state_ref[0, 2 * cells :, :], 64, 128)


def joined(ref, first, count, cells, place):
    span = slice(place * cells, (place + 1) * cells)
    return jnp.concatenate([ref[first + q, span, :] for q in range(count)], axis=0)


def block(t, rows, n):
    return pl.ds(pl.multiple_of(t * rows * n, rows * n), rows * n)


def forward(n, state_ref, w, b, gain, shift, w_out, b_out, *refs):
    (edges_s, slopes_s, gate_s, hat_s, rstd_s) = refs[:5]
    (p_hat_s, p_rstd_s, branch_s, normed_s, mixed_s) = refs[5:KEPT]
    (next_s,) = refs[KEPT:]
    parts, _, c = state_ref.shape
    rows = n // parts
    cells = rows * n
    length = crop_length(state_ref, cells)
    steps = n // STEP_ROWS

    @pl.loop(0, parts)
    def _(t):
        next_s[block(t, rows, n), :] = state_ref[t, :cells, :]

    @pl.loop(0, 2)
    def _(u):
        bias, gains, shifts, bias_out = (
            jnp.where(u == 0, ref[0:1, :], ref[1:2, :]) for ref in (b, gain, shift, b_out)
        )

        @pl.loop(0, steps)
        def _(t):
            first = t * STEP_ROWS
            here = block(t, STEP_ROWS, n)
            mask = pair_mask_block(length, first, STEP_ROWS, n, c)
            x_hat, rstd, normed, s_left, s_right, left, right, gate = project(
                next_s[here, :], mask, w[u], bias, gains[:, :c], shifts[:, :c]
            )
            edges_s[u, 0, here, :] = left
            edges_s[u, 1, here, :] = right
            for r in range(STEP_ROWS):
                swapped = pl.ds(first + r, n, stride=n)
                edges_s[u, 2, swapped, :] = right[r * n : (r + 1) * n]
                edges_s[u, 3, swapped, :] = left[r * n : (r + 1) * n]
            slopes_s[u, 0, here, :] = s_left
            slopes_s[u, 1, here, :] = s_right
            gate_s[u, here, :] = gate
            hat_s[u, here, :] = x_hat
            rstd_s[u, here, :] = rstd
            normed_s[u, here, :] = normed

        @pl.loop(0, steps)
        def _(t):
            here = block(t, STEP_ROWS, n)
            x, y = edges_s.at[u, 3 * u], edges_s.at[u, 2 - u]
            product = [
                contract(n, t * STEP_ROWS + r, x, y) for r in range(0, STEP_ROWS, BLOCK_ROWS)
            ]
            p_hat, p_rstd, mixed, branch = mix(
                jnp.concatenate(product).astype(BF16), gains[:, c:], shifts[:, c:], w_out[u], bias_out
            )
            p_hat_s[u, here, :] = p_hat
            p_rstd_s[u, here, :] = p_rstd
            mixed_s[u, here, :] = mixed
            branch_s[u, here, :] = branch
            x = next_s[here, :].astype(F32)
            next_s[here, :] = (x + gate_s[u, here, :] * branch).astype(BF16)


def backward(n, u, *refs):
    up_in_ref, w, gain, w_out = refs[:4]
    (edges_s, slopes_s, gate_s, hat_s, rstd_s) = (ref.at[u] for ref in refs[4:9])
    (p_hat_s, p_rstd_s, branch_s, normed_s, mixed_s) = (ref.at[u] for ref in refs[9 : 4 + KEPT])
    if u == 1:
        up_ref, grads_ref, d_product_s, d_edges_s, sums_s, d_pre_s = refs[4 + KEPT :]
    else:
        d_pre_s, grads_ref, d_product_s, d_edges_s, sums_s = refs[4 + KEPT :]
    c, h = w.shape[1], edges_s.shape[2]
    width = 4 * h + c
    sums_s[...] = jnp.zeros_like(sums_s)

    def upstream(t, rows):
        if u == 0:
            return up_in_ref[block(t, rows, n), :]
        own = n // up_in_ref.shape[0]
        per = rows // own
        return joined(up_in_ref, t * per, per, own * n, 1).astype(F32)

    @pl.loop(0, n // STEP_ROWS)
    def _(t):
        here = block(t, STEP_ROWS, n)
        d_branch, d_gate, d_product = unmix(
            upstream(t, STEP_ROWS),
            gate_s[here, :],
            branch_s[here, :],
            p_hat_s[here, :],
            p_rstd_s[here, :],
            gain[u : u + 1, c:],
            w_out[u],
        )
        sums_s[:, width:] += dot(mixed_s[here, :], d_branch, ((0,), (0,)))
        d_pre_s[here, 4 * h :] = d_gate
        d_product_s[u, here, :] = d_product
        for r in range(STEP_ROWS):
            swapped = pl.ds(t * STEP_ROWS + r, n, stride=n)
            d_product_s[1 - u, swapped, :] = d_product[r * n : (r + 1) * n]

    blocks = n // BLOCK_ROWS

    @pl.loop(0, 2 * blocks)
    def _(step):
        side, t = step // blocks, step % blocks
        edges, d_product = edges_s.at[1 - side], d_product_s.at[side]
        x, y = (edges, d_product) if u == 1 else (d_product, edges)
        d_edges_s[side, block(t, BLOCK_ROWS, n), :] = contract(n, t * BLOCK_ROWS, x, y)

    @pl.loop(0, n // STEP_ROWS)
    def _(t):
        here = block(t, STEP_ROWS, n)
        grads = edge_grads(
            d_edges_s[0, here, :],
            d_edges_s[1, here, :],
            slopes_s[0, here, :],
            slopes_s[1, here, :],
            edges_s[0, here, :],
            edges_s[1, here, :],
        )
        d_pre = jnp.concatenate([*grads, d_pre_s[here, 4 * h :]], axis=1)
        normed = normed_s[here, :]
        if u == 1:
            d_normed = dot(d_pre, w[u], ((1,), (1,))) * gain[u : u + 1, :c]
            pulled = norm_vjp(hat_s[here, :], rstd_s[here, :], d_normed)
            up_ref[here, :] = upstream(t, STEP_ROWS) + pulled
        else:
            d_pre_s[here, : 4 * h] = d_pre[:, : 4 * h]
        sums_s[:, :width] += dot(normed, d_pre, ((0,), (0,)))

    grads_ref[...] = sums_s[...].astype(BF16)


def own_rows(state_ref, up_ref, d_pre_ref, w, gain, hat_ref, rstd_ref, out_ref):
    cells, c = out_ref.shape
    place = own_place(state_ref, cells)
    own = pl.ds(pl.multiple_of(place * cells, cells), cells)
    d_normed = dot(d_pre_ref[own, :], w[0], ((1,), (1,))) * gain[0:1, :c]
    pulled = norm_vjp(hat_ref[0, own, :], rstd_ref[0, own, :], d_normed)
    out_ref[...] = (up_ref[own, :] + pulled).astype(BF16)


def exchange(value, axis, size, step):
    return lax.ppermute(value, axis, [(d, d ^ step) for d in range(size)])


def add_narrow(a, b):
    return (a.astype(F32) + b.astype(F32)).astype(BF16)


def prepare(state_ref, mask_ref, cot_ref, sent_ref, state_s, mask_s, cot_s, sems):
    parts, _, c = sent_ref.shape
    cells = state_s.shape[0]
    copies = [
        pltpu.make_async_copy(*pair, sems.at[k])
        for k, pair in enumerate(((mask_ref, mask_s), (state_ref, state_s), (cot_ref, cot_s)))
    ]
    for copy in copies:
        copy.start()
    copies[0].wait()
    length = jnp.max(jnp.sum(mask_s[...].astype(F32), axis=1, keepdims=True))
    in_length = lax.broadcasted_iota(jnp.int32, (16, c), 1) < 64
    for copy in copies[1:]:
        copy.wait()
    for part in range(parts):
        sent_ref[part, :cells, :] = state_s[...]
        sent_ref[part, cells : 2 * cells, :] = cot_s[...]
        sent_ref[part, 2 * cells :, :] = jnp.where(in_length, length, float(part)).astype(BF16)


def add_grads(own_0, other_0, own_both, other_both, proj_ref, out_ref):
    width = proj_ref.shape[2]
    for u, (own, other) in enumerate(((own_0, other_0), (own_both.at[1], other_both.at[1]))):
        total = own[...].astype(F32) + other[...].astype(F32)
        proj_ref[u] = total[:, :width]
        out_ref[u] = total[:, width:]


def crop_shards(
    groups,
    parts,
    pair_repr,
    pair_mask,
    cotangent,
    proj_weight,
    proj_bias,
    norm_gain,
    norm_shift,
    out_weight,
    out_bias,
):
    _, rows, n, c = pair_repr.shape
    h = out_weight.shape[1]
    width = proj_weight.shape[2]
    cells, pairs = rows * n, n * n
    plane = (pairs + 8, h)
    kept = [jax.ShapeDtypeStruct((2, 4) + plane, F32), jax.ShapeDtypeStruct((2, 2) + plane, F32)]
    kept += [jax.ShapeDtypeStruct((2,) + plane, F32)] * 6
    kept += [jax.ShapeDtypeStruct((2, pairs, h), BF16)] * 2
    grads = jax.ShapeDtypeStruct((c, width + c), BF16)
    vmem = pl.BlockSpec(memory_space=pltpu.VMEM)
    main = pl.BlockSpec(memory_space=pltpu.HBM)
    params = pltpu.CompilerParams(vmem_limit_bytes=VMEM_BYTES)

    def cost(planes):
        flops = 4 * pairs * width * c
        return pl.CostEstimate(
            flops=flops, bytes_accessed=planes * pairs * c * 4, transcendentals=0
        )

    sent = pl.pallas_call(
        prepare,
        out_shape=jax.ShapeDtypeStruct((parts, 2 * cells + 16, c), BF16),
        in_specs=[main] * 3,
        out_specs=vmem,
        scratch_shapes=[
            pltpu.VMEM((cells, c), BF16),
            pltpu.VMEM((rows, n), jnp.int32),
            pltpu.VMEM((cells, c), BF16),
            pltpu.SemaphoreType.DMA((3,)),
        ],
        compiler_params=pltpu.CompilerParams(vmem_limit_bytes=PREPARE_BYTES),
        name="prepare",
    )(pair_repr.reshape(cells, c), pair_mask[0], cotangent.reshape(cells, c))
    state = lax.all_to_all(sent, "dap", split_axis=0, concat_axis=0, tiled=True)

    held = pl.pallas_call(
        functools.partial(forward, n),
        out_shape=kept,
        in_specs=[vmem] * 7,
        out_specs=(vmem,) * KEPT,
        scratch_shapes=[pltpu.VMEM((pairs, c), BF16)],
        compiler_params=params,
        cost_estimate=cost(64),
        name="forward",
    )(state, proj_weight, proj_bias, norm_gain, norm_shift, out_weight, out_bias)

    work = [pltpu.VMEM((2,) + plane, F32)] * 2
    work += [pltpu.VMEM(grads.shape, F32)]
    d_pre = jax.ShapeDtypeStruct((pairs, width), BF16)
    up_1, grads_1 = pl.pallas_call(
        functools.partial(backward, n, 1),
        out_shape=(jax.ShapeDtypeStruct((pairs, c), F32), grads),
        in_specs=[vmem] * (4 + KEPT),
        out_specs=(vmem, vmem),
        scratch_shapes=work + [pltpu.VMEM(d_pre.shape, BF16)],
        compiler_params=params,
        cost_estimate=cost(48),
        name="backward_second",
    )(state, proj_weight, norm_gain, out_weight, *held)
    far = groups // 2
    others_1 = exchange(grads_1, "dp", groups, far)

    d_pre_0, grads_0 = pl.pallas_call(
        functools.partial(backward, n, 0),
        out_shape=(d_pre, grads),
        in_specs=[vmem] * (4 + KEPT),
        out_specs=(vmem, vmem),
        scratch_shapes=work,
        compiler_params=params,
        cost_estimate=cost(48),
        name="backward_first",
    )(up_1, proj_weight, norm_gain, out_weight, *held)

    pair_grad = pl.pallas_call(
        own_rows,
        out_shape=jax.ShapeDtypeStruct((cells, c), BF16),
        in_specs=[vmem] * 7,
        out_specs=vmem,
        compiler_params=params,
        cost_estimate=cost(8),
        name="own_rows",
    )(state, up_1, d_pre_0, proj_weight, norm_gain, held[3], held[4])

    both = jnp.stack([grads_0, add_narrow(grads_1, others_1)])
    others = jnp.zeros_like(both)
    step = 1
    while step < far:
        both = add_narrow(both, others) if step > 1 else both
        others = exchange(both, "dp", groups, step)
        step *= 2
    grads_0 = add_narrow(both[0], others[0])
    others_0 = exchange(grads_0, "dp", groups, far)

    proj_total, out_total = pl.pallas_call(
        add_grads,
        out_shape=(
            jax.ShapeDtypeStruct((2, c, width), F32),
            jax.ShapeDtypeStruct((2, h, c), F32),
        ),
        in_specs=[vmem] * 4,
        out_specs=(vmem, vmem),
        compiler_params=params,
        name="add_grads",
    )(grads_0, others_0, both, others)
    return pair_grad.reshape(pair_repr.shape), proj_total, out_total


def layer_norm(values, gain_vec, shift_vec, norm_axis):
    mean_value = jnp.mean(values, axis=norm_axis, keepdims=True)
    centred = values - mean_value
    variance = jnp.mean(centred * centred, axis=norm_axis, keepdims=True)
    return centred * lax.rsqrt(variance + NORM_EPSILON) * gain_vec + shift_vec


def norm_pullback(values, gain_vec, shift_vec, norm_axis, upstream):
    _, pull_back = jax.vjp(
        lambda inner_value: layer_norm(inner_value, gain_vec, shift_vec, norm_axis), values
    )
    return pull_back(upstream)[0]


def edge_pair(edge_pre, cell_mask):
    left_edge = jax.nn.sigmoid(edge_pre[1]) * edge_pre[0] * cell_mask
    right_edge = jax.nn.sigmoid(edge_pre[3]) * edge_pre[2] * cell_mask
    return jnp.stack([left_edge, right_edge]).astype(jnp.bfloat16)


def edge_pullback(edge_pre, cell_mask, grad_pair):
    sig_left = jax.nn.sigmoid(edge_pre[1])
    sig_right = jax.nn.sigmoid(edge_pre[3])
    grad_left = grad_pair[0].astype(jnp.float32) * cell_mask
    grad_right = grad_pair[1].astype(jnp.float32) * cell_mask
    return jnp.stack(
        [
            grad_left * sig_left,
            grad_left * edge_pre[0] * sig_left * (1.0 - sig_left),
            grad_right * sig_right,
            grad_right * edge_pre[2] * sig_right * (1.0 - sig_right),
        ]
    ).astype(jnp.bfloat16)


def triangle(pair_edges, outgoing):
    if outgoing:
        einsum_form = "cik,cjk->cij"
    else:
        einsum_form = "cki,ckj->cij"
    return jnp.einsum(
        einsum_form, pair_edges[0], pair_edges[1], preferred_element_type=jnp.float32
    ).astype(jnp.bfloat16)


def triangle_pullback(pair_edges, grad_product, outgoing):
    left_edge = pair_edges[0]
    right_edge = pair_edges[1]
    if outgoing:
        grad_left = jnp.einsum(
            "cij,cjk->cik", grad_product, right_edge, preferred_element_type=jnp.float32
        )
        grad_right = jnp.einsum(
            "cij,cik->cjk", grad_product, left_edge, preferred_element_type=jnp.float32
        )
    else:
        grad_left = jnp.einsum(
            "ckj,cij->cki", right_edge, grad_product, preferred_element_type=jnp.float32
        )
        grad_right = jnp.einsum(
            "cki,cij->ckj", left_edge, grad_product, preferred_element_type=jnp.float32
        )
    return jnp.stack([grad_left, grad_right]).astype(jnp.bfloat16)


def update_weights(proj_weight, proj_bias, norm_gain, norm_shift, update, channels, hidden):
    w_edge = proj_weight[update, :, : 4 * hidden].reshape(channels, 4, hidden)
    w_gate = proj_weight[update, :, 4 * hidden :]
    bias_edge = proj_bias[update, : 4 * hidden].reshape(4, hidden, 1, 1)
    bias_gate = proj_bias[update, 4 * hidden :]
    gain_in = norm_gain[update, :channels]
    shift_in = norm_shift[update, :channels]
    gain_out = norm_gain[update, channels:][:, None, None]
    shift_out = norm_shift[update, channels:][:, None, None]
    return (w_edge, w_gate, bias_edge, bias_gate, gain_in, shift_in, gain_out, shift_out)


def shards(
    pair_repr,
    pair_mask,
    cotangent,
    proj_weight,
    proj_bias,
    norm_gain,
    norm_shift,
    out_weight,
    out_bias,
):
    channels = pair_repr.shape[3]
    hidden = out_weight.shape[1]
    pair_state = pair_repr[0]
    cell_mask = pair_mask[0].astype(jnp.float32)
    records = []
    for update in range(2):
        w_edge, w_gate, bias_edge, bias_gate, gain_in, shift_in, gain_out, shift_out = (
            update_weights(proj_weight, proj_bias, norm_gain, norm_shift, update, channels, hidden)
        )
        state_f = pair_state.astype(jnp.float32)
        normed = layer_norm(state_f, gain_in, shift_in, -1).astype(jnp.bfloat16)
        edge_pre = (
            jnp.einsum("rnc,cgh->ghrn", normed, w_edge, preferred_element_type=jnp.float32)
            + bias_edge
        )
        gate_pre = (
            jnp.einsum("rnc,cd->rnd", normed, w_gate, preferred_element_type=jnp.float32)
            + bias_gate
        )
        pair_edges = edge_pair(edge_pre, cell_mask)
        spread = lax.all_to_all(pair_edges, "dap", split_axis=1, concat_axis=2, tiled=True)
        product = lax.all_to_all(
            triangle(spread, update == 0), "dap", split_axis=1, concat_axis=0, tiled=True
        )
        mixed_norm = layer_norm(product.astype(jnp.float32), gain_out, shift_out, 0).astype(
            jnp.bfloat16
        )
        branch = (
            jnp.einsum(
                "hrn,hd->rnd", mixed_norm, out_weight[update], preferred_element_type=jnp.float32
            )
            + out_bias[update]
        )
        records.append(
            (state_f, normed, edge_pre, gate_pre, pair_edges, spread, product, mixed_norm, branch)
        )
        pair_state = (state_f + jax.nn.sigmoid(gate_pre) * branch).astype(jnp.bfloat16)
    upstream = cotangent[0].astype(jnp.float32)
    proj_grads = []
    out_grads = []
    for update in (1, 0):
        state_f, normed, edge_pre, gate_pre, pair_edges, spread, product, mixed_norm, branch = (
            records[update]
        )
        w_edge, w_gate, bias_edge, bias_gate, gain_in, shift_in, gain_out, shift_out = (
            update_weights(proj_weight, proj_bias, norm_gain, norm_shift, update, channels, hidden)
        )
        gate_value = jax.nn.sigmoid(gate_pre)
        grad_branch = (upstream * gate_value).astype(jnp.bfloat16)
        grad_gate = (upstream * branch * gate_value * (1.0 - gate_value)).astype(jnp.bfloat16)
        out_grad = jnp.einsum(
            "hrn,rnd->hd", mixed_norm, grad_branch, preferred_element_type=jnp.float32
        )
        grad_mixed = jnp.einsum(
            "rnd,hd->hrn", grad_branch, out_weight[update], preferred_element_type=jnp.float32
        )
        grad_product = norm_pullback(
            product.astype(jnp.float32), gain_out, shift_out, 0, grad_mixed
        ).astype(jnp.bfloat16)
        column_edges = spread
        column_grad = lax.all_to_all(
            grad_product[None], "dap", split_axis=1, concat_axis=2, tiled=True
        )[0]
        grad_pair = lax.all_to_all(
            triangle_pullback(column_edges, column_grad, update == 0),
            "dap",
            split_axis=2,
            concat_axis=1,
            tiled=True,
        )
        grad_edge = edge_pullback(edge_pre, cell_mask, grad_pair)
        edge_grad = jnp.einsum(
            "rnc,ghrn->cgh", normed, grad_edge, preferred_element_type=jnp.float32
        ).reshape(channels, 4 * hidden)
        gate_grad = jnp.einsum("rnc,rnd->cd", normed, grad_gate, preferred_element_type=jnp.float32)
        grad_normed = jnp.einsum(
            "ghrn,cgh->rnc", grad_edge, w_edge, preferred_element_type=jnp.float32
        )
        grad_normed = grad_normed + jnp.einsum(
            "rnd,cd->rnc", grad_gate, w_gate, preferred_element_type=jnp.float32
        )
        upstream = upstream + norm_pullback(state_f, gain_in, shift_in, -1, grad_normed)
        proj_part = jnp.concatenate([edge_grad, gate_grad], axis=1)
        proj_grads.append(proj_part)
        out_grads.append(out_grad)
    proj_total = jnp.stack(proj_grads[::-1])
    out_total = jnp.stack(out_grads[::-1])
    proj_total, out_total = lax.psum((proj_total, out_total), ("dp", "dap"))
    return (upstream.astype(jnp.bfloat16)[None], proj_total, out_total)


def solution(mesh):
    placed = (
        P("dp", "dap", None, None),
        P("dp", "dap", None),
        P("dp", "dap", None, None),
        P(),
        P(),
        P(),
        P(),
        P(),
        P(),
    )
    groups, parts = mesh.shape["dp"], mesh.shape["dap"]

    def program(*args):
        n, c = args[0].shape[2:]
        rows = n // parts
        fits = 20 * n * n * c * 4 <= CROP_BUDGET
        paired = groups > 1 and groups & (groups - 1) == 0
        even = args[7].shape[1] == c == 128 and STEP_ROWS % rows == 0 and n % STEP_ROWS == 0
        body = functools.partial(crop_shards, groups, parts) if fits and even and paired else shards
        return spread_over(body)(*args)

    def spread_over(body):
        return jax.shard_map(
            body,
            mesh=mesh,
            in_specs=placed,
            out_specs=(P("dp", "dap", None, None), P(), P()),
            check_vma=False,
        )

    return program
```

```python
import functools

import jax
import jax.numpy as jnp
from jax import lax
from jax.experimental import pallas as pl
from jax.experimental.pallas import tpu as pltpu
from jax.sharding import PartitionSpec as P

NORM_EPSILON = 1e-05
VMEM_BYTES = 16 * 1024 * 1024
PREPARE_BYTES = 63 * 1024 * 1024
CROP_BUDGET = 32 * 1024 * 1024
BLOCK_ROWS = 8
STEP_ROWS = 32
KEPT = 10
TAIL_ROWS = 16
F32 = jnp.float32
BF16 = jnp.bfloat16


def sigmoid(x):
    return 0.5 * jnp.tanh(0.5 * x) + 0.5


def dot(a, b, dims=((1,), (0,))):
    return lax.dot_general(a, b, (dims, ((), ())), preferred_element_type=F32)


def norm_parts(x):
    x = x.astype(F32)
    centred = x - jnp.mean(x, axis=-1, keepdims=True)
    rstd = lax.rsqrt(jnp.mean(centred * centred, axis=-1, keepdims=True) + NORM_EPSILON)
    return centred * rstd, jnp.broadcast_to(rstd, x.shape)


def norm_vjp(x_hat, rstd, grad):
    mean_grad = jnp.mean(grad, axis=-1, keepdims=True)
    mean_prod = jnp.mean(grad * x_hat, axis=-1, keepdims=True)
    return rstd * (grad - mean_grad - x_hat * mean_prod)


def pair_mask_block(length, first_row, rows, n, lanes):
    shape = (rows, n, lanes)
    i = lax.broadcasted_iota(jnp.int32, shape, 0) + first_row
    j = lax.broadcasted_iota(jnp.int32, shape, 1)
    inside = jnp.where((i < length) & (j < length), 1.0, 0.0)
    return inside.reshape(rows * n, lanes)


def project(x, mask, w, b, gain, shift):
    x_hat, rstd = norm_parts(x)
    normed = (x_hat * gain + shift).astype(BF16)
    pre = dot(normed, w) + b
    h = (pre.shape[1] - x.shape[1]) // 4
    s_left = sigmoid(pre[:, h : 2 * h]) * mask
    s_right = sigmoid(pre[:, 3 * h : 4 * h]) * mask
    left = s_left * pre[:, :h]
    right = s_right * pre[:, 2 * h : 3 * h]
    gate = sigmoid(pre[:, 4 * h :])
    return x_hat, rstd, normed, s_left, s_right, left, right, gate


def mix(product, gain, shift, w_out, b_out):
    p_hat, p_rstd = norm_parts(product)
    mixed = (p_hat * gain + shift).astype(BF16)
    return p_hat, p_rstd, mixed, dot(mixed, w_out) + b_out


def unmix(up, gate, branch, p_hat, p_rstd, gain, w_out):
    d_branch = up * gate
    d_gate = (d_branch * branch * (1.0 - gate)).astype(BF16)
    d_branch = d_branch.astype(BF16)
    d_mixed = dot(d_branch, w_out, ((1,), (1,))) * gain
    return d_branch, d_gate, norm_vjp(p_hat, p_rstd, d_mixed)


def contract(n, first, x, y):
    lanes = y.shape[1]
    tiles = (n // 8, 8, lanes)

    def step(e, totals):
        block = y[pl.ds(pl.multiple_of(e * n, n), n), :].reshape(tiles)
        return tuple(
            totals[a] + x[pl.ds((first + a) * n + e, 8, stride=0), :][None] * block
            for a in range(BLOCK_ROWS)
        )

    zero = jnp.zeros(tiles, F32)
    totals = lax.fori_loop(0, n, step, (zero,) * BLOCK_ROWS, unroll=True)
    return jnp.stack(totals).reshape(BLOCK_ROWS * n, lanes)


def edge_grads(d_left, d_right, s_left, s_right, left, right):
    return (
        (d_left * s_left).astype(BF16),
        (d_left * left * (1.0 - s_left)).astype(BF16),
        (d_right * s_right).astype(BF16),
        (d_right * right * (1.0 - s_right)).astype(BF16),
    )


def tail_values(block, lanes_from, lanes_to):
    lane = lax.broadcasted_iota(jnp.int32, block.shape, block.ndim - 1)
    inside = (lane >= lanes_from) & (lane < lanes_to)
    return jnp.max(jnp.where(inside, block.astype(F32), 0.0)).astype(jnp.int32)


def own_place(pair_ref):
    return tail_values(pair_ref[0, -TAIL_ROWS:, :], 64, 128)


def place_of(own, jump, side):
    return own ^ (2 * jump) ^ side


def block(t, rows, n):
    return pl.ds(pl.multiple_of(t * rows * n, rows * n), rows * n)


def forward(n, jumps, *refs):
    pairs, refs = refs[: len(jumps)], refs[len(jumps) :]
    (weights, vectors), refs = refs[:2], refs[2:]
    (edges_s, slopes_s, gate_s, hat_s, rstd_s) = refs[:5]
    (p_hat_s, p_rstd_s, branch_s, normed_s, mixed_s) = refs[5:KEPT]
    (next_s,) = refs[KEPT:]
    c = weights.shape[1]
    width = weights.shape[2] - c
    rows = n // (2 * len(jumps))
    cells = rows * n
    tails = jnp.stack([pair[:, cells:, :] for pair in pairs])
    length = tail_values(tails, 0, 64)
    own = own_place(pairs[0])
    for pair, jump in zip(pairs, jumps):
        for side in range(2):
            next_s[block(place_of(own, jump, side), rows, n), :] = pair[side, :cells, :]
    steps = n // STEP_ROWS

    @pl.loop(0, 2)
    def _(u):
        row = jnp.where(u == 0, vectors[0:1, :], vectors[1:2, :])
        bias, gains, shifts, bias_out = vector_parts(row, c, width)

        @pl.loop(0, steps)
        def _(t):
            first = t * STEP_ROWS
            here = block(t, STEP_ROWS, n)
            mask = pair_mask_block(length, first, STEP_ROWS, n, c)
            x_hat, rstd, normed, s_left, s_right, left, right, gate = project(
                next_s[here, :], mask, weights[u, :, :width], bias, gains[:, :c], shifts[:, :c]
            )
            edges_s[u, 0, here, :] = left
            edges_s[u, 1, here, :] = right
            for r in range(STEP_ROWS):
                swapped = pl.ds(first + r, n, stride=n)
                edges_s[u, 2, swapped, :] = right[r * n : (r + 1) * n]
                edges_s[u, 3, swapped, :] = left[r * n : (r + 1) * n]
            slopes_s[u, 0, here, :] = s_left
            slopes_s[u, 1, here, :] = s_right
            gate_s[u, here, :] = gate
            hat_s[u, here, :] = x_hat
            rstd_s[u, here, :] = rstd
            normed_s[u, here, :] = normed

        @pl.loop(0, steps)
        def _(t):
            here = block(t, STEP_ROWS, n)
            x, y = edges_s.at[u, 3 * u], edges_s.at[u, 2 - u]
            product = [
                contract(n, t * STEP_ROWS + r, x, y) for r in range(0, STEP_ROWS, BLOCK_ROWS)
            ]
            p_hat, p_rstd, mixed, branch = mix(
                jnp.concatenate(product).astype(BF16), gains[:, c:], shifts[:, c:], weights[u, :, width:], bias_out
            )
            p_hat_s[u, here, :] = p_hat
            p_rstd_s[u, here, :] = p_rstd
            mixed_s[u, here, :] = mixed
            branch_s[u, here, :] = branch
            x = next_s[here, :].astype(F32)
            next_s[here, :] = (x + gate_s[u, here, :] * branch).astype(BF16)


def backward(n, u, jumps, *refs):
    if u == 1:
        (pair, *parted), refs = refs[: 1 + len(jumps)], refs[1 + len(jumps) :]
        up_in_ref, refs = refs[-1], (None,) + refs[:-1]
        own = own_place(pair)
        for part, jump in zip(parted, jumps):
            for side in range(2):
                rows = part.shape[1] // n
                up_in_ref[block(place_of(own, jump, side), rows, n), :] = part[side]
    else:
        up_in_ref = refs[0]
    weights, vectors = refs[1:3]
    (edges_s, slopes_s, gate_s, hat_s, rstd_s) = (ref.at[u] for ref in refs[3:8])
    (p_hat_s, p_rstd_s, branch_s, normed_s, mixed_s) = (ref.at[u] for ref in refs[8 : 3 + KEPT])
    if u == 1:
        up_ref, grads_ref, d_product_s, d_edges_s, sums_s, d_pre_s = refs[3 + KEPT :]
    else:
        d_pre_s, grads_ref, d_product_s, d_edges_s, sums_s = refs[3 + KEPT :]
    c, h = weights.shape[1], edges_s.shape[2]
    width = 4 * h + c
    gain = vector_parts(vectors[u : u + 1, :], c, width)[1]
    sums_s[...] = jnp.zeros_like(sums_s)

    @pl.loop(0, n // STEP_ROWS)
    def _(t):
        here = block(t, STEP_ROWS, n)
        d_branch, d_gate, d_product = unmix(
            up_in_ref[here, :].astype(F32),
            gate_s[here, :],
            branch_s[here, :],
            p_hat_s[here, :],
            p_rstd_s[here, :],
            gain[:, c:],
            weights[u, :, width:],
        )
        sums_s[:, width:] += dot(mixed_s[here, :], d_branch, ((0,), (0,)))
        d_pre_s[here, 4 * h :] = d_gate
        d_product_s[u, here, :] = d_product
        for r in range(STEP_ROWS):
            swapped = pl.ds(t * STEP_ROWS + r, n, stride=n)
            d_product_s[1 - u, swapped, :] = d_product[r * n : (r + 1) * n]

    blocks = n // BLOCK_ROWS

    @pl.loop(0, 2 * blocks)
    def _(step):
        side, t = step // blocks, step % blocks
        edges, d_product = edges_s.at[1 - side], d_product_s.at[side]
        x, y = (edges, d_product) if u == 1 else (d_product, edges)
        d_edges_s[side, block(t, BLOCK_ROWS, n), :] = contract(n, t * BLOCK_ROWS, x, y)

    @pl.loop(0, n // STEP_ROWS)
    def _(t):
        here = block(t, STEP_ROWS, n)
        grads = edge_grads(
            d_edges_s[0, here, :],
            d_edges_s[1, here, :],
            slopes_s[0, here, :],
            slopes_s[1, here, :],
            edges_s[0, here, :],
            edges_s[1, here, :],
        )
        d_pre = jnp.concatenate([*grads, d_pre_s[here, 4 * h :]], axis=1)
        normed = normed_s[here, :]
        if u == 1:
            d_normed = dot(d_pre, weights[u, :, :width], ((1,), (1,))) * gain[:, :c]
            pulled = norm_vjp(hat_s[here, :], rstd_s[here, :], d_normed)
            up_ref[here, :] = up_in_ref[here, :].astype(F32) + pulled
        else:
            d_pre_s[here, : 4 * h] = d_pre[:, : 4 * h]
        sums_s[:, :width] += dot(normed, d_pre, ((0,), (0,)))

    grads_ref[...] = sums_s[...].astype(BF16)


def own_rows(pair_ref, up_ref, d_pre_ref, weights, vectors, hat_ref, rstd_ref, out_ref):
    cells, c = out_ref.shape
    place = own_place(pair_ref)
    own = pl.ds(pl.multiple_of(place * cells, cells), cells)
    width = d_pre_ref.shape[1]
    gain = vector_parts(vectors[0:1, :], c, width)[1]
    d_normed = dot(d_pre_ref[own, :], weights[0, :, :width], ((1,), (1,))) * gain[:, :c]
    pulled = norm_vjp(hat_ref[0, own, :], rstd_ref[0, own, :], d_normed)
    out_ref[...] = (up_ref[own, :] + pulled).astype(BF16)


def exchange(value, axis, size, step):
    return lax.ppermute(value, axis, [(d, d ^ step) for d in range(size)])


def add_narrow(a, b):
    return (a.astype(F32) + b.astype(F32)).astype(BF16)


def prepare(
    index_ref, mask_ref, state_ref, cot_ref, w, w_out, b, gain, shift, b_out, *refs
):
    sent_ref, weights_ref, vectors_ref, mask_s, tail_s, sems = refs
    cells, c = state_ref.shape
    below, width = cells + TAIL_ROWS, w.shape[2]
    copies = [(mask_ref, mask_s), (state_ref, sent_ref.at[:cells]), (cot_ref, sent_ref.at[below:])]
    copies += [(w, weights_ref.at[:, :, :width]), (w_out, weights_ref.at[:, :, width:])]
    first = 0
    for vector in (b, gain, shift, b_out):
        last = first + vector.shape[1]
        copies.append((vector, vectors_ref.at[:, first:last]))
        first = last
    copies = [pltpu.make_async_copy(*pair, sems.at[k]) for k, pair in enumerate(copies)]
    for copy in copies:
        copy.start()
    copies[0].wait()
    length = jnp.max(jnp.sum(mask_s[...].astype(F32), axis=1, keepdims=True))
    in_length = lax.broadcasted_iota(jnp.int32, tail_s.shape, 1) < 64
    place = index_ref[0].astype(F32)
    tail_s[...] = jnp.where(in_length, length, place).astype(BF16)
    copies.append(
        pltpu.make_async_copy(tail_s, sent_ref.at[cells:below], sems.at[len(copies)])
    )
    copies[-1].start()
    for copy in copies[1:]:
        copy.wait()


def hold(weights_in, vectors_in, weights_out, vectors_out):
    weights_out[...] = weights_in[...]
    vectors_out[...] = vectors_in[...]


def vector_parts(row, c, width):
    ends = [width, width + 2 * c, width + 4 * c, width + 5 * c]
    return [row[:, first:last] for first, last in zip([0] + ends, ends)]


def add_grads(own_0, other_0, own_both, other_both, proj_ref, out_ref):
    width = proj_ref.shape[2]
    for u, (own, other) in enumerate(((own_0, other_0), (own_both.at[1], other_both.at[1]))):
        total = own[...].astype(F32) + other[...].astype(F32)
        proj_ref[u] = total[:, :width]
        out_ref[u] = total[:, width:]


def crop_shards(
    groups,
    parts,
    pair_repr,
    pair_mask,
    cotangent,
    proj_weight,
    proj_bias,
    norm_gain,
    norm_shift,
    out_weight,
    out_bias,
):
    _, rows, n, c = pair_repr.shape
    h = out_weight.shape[1]
    width = proj_weight.shape[2]
    cells, pairs = rows * n, n * n
    plane = (pairs + 8, h)
    kept = [jax.ShapeDtypeStruct((2, 4) + plane, F32), jax.ShapeDtypeStruct((2, 2) + plane, F32)]
    kept += [jax.ShapeDtypeStruct((2,) + plane, F32)] * 6
    kept += [jax.ShapeDtypeStruct((2, pairs, h), BF16)] * 2
    grads = jax.ShapeDtypeStruct((c, width + c), BF16)
    vmem = pl.BlockSpec(memory_space=pltpu.VMEM)
    main = pl.BlockSpec(memory_space=pltpu.HBM)
    params = pltpu.CompilerParams(vmem_limit_bytes=VMEM_BYTES)

    def cost(planes):
        flops = 4 * pairs * width * c
        return pl.CostEstimate(
            flops=flops, bytes_accessed=planes * pairs * c * 4, transcendentals=0
        )

    packed = (
        jax.ShapeDtypeStruct((2, c, width + c), BF16),
        jax.ShapeDtypeStruct((2, width + 5 * c), F32),
    )
    sent, *weights = pl.pallas_call(
        prepare,
        out_shape=(jax.ShapeDtypeStruct((2 * cells + TAIL_ROWS, c), BF16),) + packed,
        in_specs=[pl.BlockSpec(memory_space=pltpu.SMEM)] + [main] * 9,
        out_specs=[main] * 3,
        scratch_shapes=[
            pltpu.VMEM((rows, n), jnp.int32),
            pltpu.VMEM((TAIL_ROWS, c), BF16),
            pltpu.SemaphoreType.DMA((10,)),
        ],
        compiler_params=pltpu.CompilerParams(vmem_limit_bytes=PREPARE_BYTES),
        name="prepare",
    )(
        lax.axis_index("dap").astype(jnp.int32)[None],
        pair_mask[0],
        pair_repr.reshape(cells, c),
        cotangent.reshape(cells, c),
        proj_weight,
        out_weight,
        proj_bias,
        norm_gain,
        norm_shift,
        out_bias,
    )
    weights = pl.pallas_call(
        hold,
        out_shape=packed,
        in_specs=[vmem] * 2,
        out_specs=[vmem] * 2,
        compiler_params=params,
        cost_estimate=cost(8),
        name="hold",
    )(*weights)
    beside = exchange(sent, "dap", parts, 1)
    beside, *weights = lax.optimization_barrier((beside, *weights))
    split = cells + TAIL_ROWS
    states = [jnp.stack([sent[:split], beside[:split]])]
    cots = [jnp.stack([sent[split:], beside[split:]])]
    half = parts // 2
    jumps = [0, *range(1, half // 2), *reversed(range(half // 2, half))]
    for group in (states, cots):
        group += [exchange(group[0], "dap", parts, 2 * jump) for jump in jumps[1:]]

    held = pl.pallas_call(
        functools.partial(forward, n, jumps),
        out_shape=kept,
        in_specs=[vmem] * (half + 2),
        out_specs=(vmem,) * KEPT,
        scratch_shapes=[pltpu.VMEM((pairs, c), BF16)],
        compiler_params=params,
        cost_estimate=cost(64),
        name="forward",
    )(*states, *weights)

    work = [pltpu.VMEM((2,) + plane, F32)] * 2
    work += [pltpu.VMEM(grads.shape, F32)]
    d_pre = jax.ShapeDtypeStruct((pairs, width), BF16)
    up_1, grads_1 = pl.pallas_call(
        functools.partial(backward, n, 1, jumps),
        out_shape=(jax.ShapeDtypeStruct((pairs, c), F32), grads),
        in_specs=[vmem] * (3 + half + KEPT),
        out_specs=(vmem, vmem),
        scratch_shapes=work + [pltpu.VMEM(d_pre.shape, BF16), pltpu.VMEM((pairs, c), BF16)],
        compiler_params=params,
        cost_estimate=cost(48),
        name="backward_second",
    )(states[0], *cots, *weights, *held)
    far = groups // 2
    others_1 = exchange(grads_1, "dp", groups, far)

    d_pre_0, grads_0 = pl.pallas_call(
        functools.partial(backward, n, 0, jumps),
        out_shape=(d_pre, grads),
        in_specs=[vmem] * (3 + KEPT),
        out_specs=(vmem, vmem),
        scratch_shapes=work,
        compiler_params=params,
        cost_estimate=cost(48),
        name="backward_first",
    )(up_1, *weights, *held)

    pair_grad = pl.pallas_call(
        own_rows,
        out_shape=jax.ShapeDtypeStruct((cells, c), BF16),
        in_specs=[vmem] * 7,
        out_specs=vmem,
        compiler_params=params,
        cost_estimate=cost(8),
        name="own_rows",
    )(states[0], up_1, d_pre_0, *weights, held[3], held[4])

    both = jnp.stack([grads_0, add_narrow(grads_1, others_1)])
    others = jnp.zeros_like(both)
    step = 1
    while step < far:
        both = add_narrow(both, others) if step > 1 else both
        others = exchange(both, "dp", groups, step)
        step *= 2
    grads_0 = add_narrow(both[0], others[0])
    others_0 = exchange(grads_0, "dp", groups, far)

    proj_total, out_total = pl.pallas_call(
        add_grads,
        out_shape=(
            jax.ShapeDtypeStruct((2, c, width), F32),
            jax.ShapeDtypeStruct((2, h, c), F32),
        ),
        in_specs=[vmem] * 4,
        out_specs=(vmem, vmem),
        compiler_params=params,
        name="add_grads",
    )(grads_0, others_0, both, others)
    return pair_grad.reshape(pair_repr.shape), proj_total, out_total


def layer_norm(values, gain_vec, shift_vec, norm_axis):
    mean_value = jnp.mean(values, axis=norm_axis, keepdims=True)
    centred = values - mean_value
    variance = jnp.mean(centred * centred, axis=norm_axis, keepdims=True)
    return centred * lax.rsqrt(variance + NORM_EPSILON) * gain_vec + shift_vec


def norm_pullback(values, gain_vec, shift_vec, norm_axis, upstream):
    _, pull_back = jax.vjp(
        lambda inner_value: layer_norm(inner_value, gain_vec, shift_vec, norm_axis), values
    )
    return pull_back(upstream)[0]


def edge_pair(edge_pre, cell_mask):
    left_edge = jax.nn.sigmoid(edge_pre[1]) * edge_pre[0] * cell_mask
    right_edge = jax.nn.sigmoid(edge_pre[3]) * edge_pre[2] * cell_mask
    return jnp.stack([left_edge, right_edge]).astype(jnp.bfloat16)


def edge_pullback(edge_pre, cell_mask, grad_pair):
    sig_left = jax.nn.sigmoid(edge_pre[1])
    sig_right = jax.nn.sigmoid(edge_pre[3])
    grad_left = grad_pair[0].astype(jnp.float32) * cell_mask
    grad_right = grad_pair[1].astype(jnp.float32) * cell_mask
    return jnp.stack(
        [
            grad_left * sig_left,
            grad_left * edge_pre[0] * sig_left * (1.0 - sig_left),
            grad_right * sig_right,
            grad_right * edge_pre[2] * sig_right * (1.0 - sig_right),
        ]
    ).astype(jnp.bfloat16)


def triangle(pair_edges, outgoing):
    if outgoing:
        einsum_form = "cik,cjk->cij"
    else:
        einsum_form = "cki,ckj->cij"
    return jnp.einsum(
        einsum_form, pair_edges[0], pair_edges[1], preferred_element_type=jnp.float32
    ).astype(jnp.bfloat16)


def triangle_pullback(pair_edges, grad_product, outgoing):
    left_edge = pair_edges[0]
    right_edge = pair_edges[1]
    if outgoing:
        grad_left = jnp.einsum(
            "cij,cjk->cik", grad_product, right_edge, preferred_element_type=jnp.float32
        )
        grad_right = jnp.einsum(
            "cij,cik->cjk", grad_product, left_edge, preferred_element_type=jnp.float32
        )
    else:
        grad_left = jnp.einsum(
            "ckj,cij->cki", right_edge, grad_product, preferred_element_type=jnp.float32
        )
        grad_right = jnp.einsum(
            "cki,cij->ckj", left_edge, grad_product, preferred_element_type=jnp.float32
        )
    return jnp.stack([grad_left, grad_right]).astype(jnp.bfloat16)


def update_weights(proj_weight, proj_bias, norm_gain, norm_shift, update, channels, hidden):
    w_edge = proj_weight[update, :, : 4 * hidden].reshape(channels, 4, hidden)
    w_gate = proj_weight[update, :, 4 * hidden :]
    bias_edge = proj_bias[update, : 4 * hidden].reshape(4, hidden, 1, 1)
    bias_gate = proj_bias[update, 4 * hidden :]
    gain_in = norm_gain[update, :channels]
    shift_in = norm_shift[update, :channels]
    gain_out = norm_gain[update, channels:][:, None, None]
    shift_out = norm_shift[update, channels:][:, None, None]
    return (w_edge, w_gate, bias_edge, bias_gate, gain_in, shift_in, gain_out, shift_out)


def shards(
    pair_repr,
    pair_mask,
    cotangent,
    proj_weight,
    proj_bias,
    norm_gain,
    norm_shift,
    out_weight,
    out_bias,
):
    channels = pair_repr.shape[3]
    hidden = out_weight.shape[1]
    pair_state = pair_repr[0]
    cell_mask = pair_mask[0].astype(jnp.float32)
    records = []
    for update in range(2):
        w_edge, w_gate, bias_edge, bias_gate, gain_in, shift_in, gain_out, shift_out = (
            update_weights(proj_weight, proj_bias, norm_gain, norm_shift, update, channels, hidden)
        )
        state_f = pair_state.astype(jnp.float32)
        normed = layer_norm(state_f, gain_in, shift_in, -1).astype(jnp.bfloat16)
        edge_pre = (
            jnp.einsum("rnc,cgh->ghrn", normed, w_edge, preferred_element_type=jnp.float32)
            + bias_edge
        )
        gate_pre = (
            jnp.einsum("rnc,cd->rnd", normed, w_gate, preferred_element_type=jnp.float32)
            + bias_gate
        )
        pair_edges = edge_pair(edge_pre, cell_mask)
        spread = lax.all_to_all(pair_edges, "dap", split_axis=1, concat_axis=2, tiled=True)
        product = lax.all_to_all(
            triangle(spread, update == 0), "dap", split_axis=1, concat_axis=0, tiled=True
        )
        mixed_norm = layer_norm(product.astype(jnp.float32), gain_out, shift_out, 0).astype(
            jnp.bfloat16
        )
        branch = (
            jnp.einsum(
                "hrn,hd->rnd", mixed_norm, out_weight[update], preferred_element_type=jnp.float32
            )
            + out_bias[update]
        )
        records.append(
            (state_f, normed, edge_pre, gate_pre, pair_edges, spread, product, mixed_norm, branch)
        )
        pair_state = (state_f + jax.nn.sigmoid(gate_pre) * branch).astype(jnp.bfloat16)
    upstream = cotangent[0].astype(jnp.float32)
    proj_grads = []
    out_grads = []
    for update in (1, 0):
        state_f, normed, edge_pre, gate_pre, pair_edges, spread, product, mixed_norm, branch = (
            records[update]
        )
        w_edge, w_gate, bias_edge, bias_gate, gain_in, shift_in, gain_out, shift_out = (
            update_weights(proj_weight, proj_bias, norm_gain, norm_shift, update, channels, hidden)
        )
        gate_value = jax.nn.sigmoid(gate_pre)
        grad_branch = (upstream * gate_value).astype(jnp.bfloat16)
        grad_gate = (upstream * branch * gate_value * (1.0 - gate_value)).astype(jnp.bfloat16)
        out_grad = jnp.einsum(
            "hrn,rnd->hd", mixed_norm, grad_branch, preferred_element_type=jnp.float32
        )
        grad_mixed = jnp.einsum(
            "rnd,hd->hrn", grad_branch, out_weight[update], preferred_element_type=jnp.float32
        )
        grad_product = norm_pullback(
            product.astype(jnp.float32), gain_out, shift_out, 0, grad_mixed
        ).astype(jnp.bfloat16)
        column_edges = spread
        column_grad = lax.all_to_all(
            grad_product[None], "dap", split_axis=1, concat_axis=2, tiled=True
        )[0]
        grad_pair = lax.all_to_all(
            triangle_pullback(column_edges, column_grad, update == 0),
            "dap",
            split_axis=2,
            concat_axis=1,
            tiled=True,
        )
        grad_edge = edge_pullback(edge_pre, cell_mask, grad_pair)
        edge_grad = jnp.einsum(
            "rnc,ghrn->cgh", normed, grad_edge, preferred_element_type=jnp.float32
        ).reshape(channels, 4 * hidden)
        gate_grad = jnp.einsum("rnc,rnd->cd", normed, grad_gate, preferred_element_type=jnp.float32)
        grad_normed = jnp.einsum(
            "ghrn,cgh->rnc", grad_edge, w_edge, preferred_element_type=jnp.float32
        )
        grad_normed = grad_normed + jnp.einsum(
            "rnd,cd->rnc", grad_gate, w_gate, preferred_element_type=jnp.float32
        )
        upstream = upstream + norm_pullback(state_f, gain_in, shift_in, -1, grad_normed)
        proj_part = jnp.concatenate([edge_grad, gate_grad], axis=1)
        proj_grads.append(proj_part)
        out_grads.append(out_grad)
    proj_total = jnp.stack(proj_grads[::-1])
    out_total = jnp.stack(out_grads[::-1])
    proj_total, out_total = lax.psum((proj_total, out_total), ("dp", "dap"))
    return (upstream.astype(jnp.bfloat16)[None], proj_total, out_total)


def solution(mesh):
    placed = (
        P("dp", "dap", None, None),
        P("dp", "dap", None),
        P("dp", "dap", None, None),
        P(),
        P(),
        P(),
        P(),
        P(),
        P(),
    )
    groups, parts = mesh.shape["dp"], mesh.shape["dap"]

    def program(*args):
        n, c = args[0].shape[2:]
        rows = n // parts
        fits = 20 * n * n * c * 4 <= CROP_BUDGET
        paired = all(size > 1 and size & (size - 1) == 0 for size in (groups, parts))
        even = args[7].shape[1] == c == 128 and STEP_ROWS % rows == 0 and n % STEP_ROWS == 0
        body = functools.partial(crop_shards, groups, parts) if fits and even and paired else shards
        return spread_over(body)(*args)

    def spread_over(body):
        return jax.shard_map(
            body,
            mesh=mesh,
            in_specs=placed,
            out_specs=(P("dp", "dap", None, None), P(), P()),
            check_vma=False,
        )

    return program
```

```python
import functools

import jax
import jax.numpy as jnp
from jax import lax
from jax.experimental import pallas as pl
from jax.experimental.pallas import tpu as pltpu
from jax.sharding import PartitionSpec as P

NORM_EPSILON = 1e-05
VMEM_BYTES = 16 * 1024 * 1024
PREPARE_BYTES = 63 * 1024 * 1024
CROP_BUDGET = 32 * 1024 * 1024
BLOCK_ROWS = 8
STEP_ROWS = 32
KEPT = 10
TAIL_ROWS = 16
F32 = jnp.float32
BF16 = jnp.bfloat16


def sigmoid(x):
    return 0.5 * jnp.tanh(0.5 * x) + 0.5


def dot(a, b, dims=((1,), (0,))):
    return lax.dot_general(a, b, (dims, ((), ())), preferred_element_type=F32)


def norm_parts(x):
    x = x.astype(F32)
    centred = x - jnp.mean(x, axis=-1, keepdims=True)
    rstd = lax.rsqrt(jnp.mean(centred * centred, axis=-1, keepdims=True) + NORM_EPSILON)
    return centred * rstd, jnp.broadcast_to(rstd, x.shape)


def norm_vjp(x_hat, rstd, grad):
    mean_grad = jnp.mean(grad, axis=-1, keepdims=True)
    mean_prod = jnp.mean(grad * x_hat, axis=-1, keepdims=True)
    return rstd * (grad - mean_grad - x_hat * mean_prod)


def pair_mask_block(length, first_row, rows, n, lanes):
    shape = (rows, n, lanes)
    i = lax.broadcasted_iota(jnp.int32, shape, 0) + first_row
    j = lax.broadcasted_iota(jnp.int32, shape, 1)
    inside = jnp.where((i < length) & (j < length), 1.0, 0.0)
    return inside.reshape(rows * n, lanes)


def project(x, mask, w, b, gain, shift):
    x_hat, rstd = norm_parts(x)
    normed = (x_hat * gain + shift).astype(BF16)
    pre = dot(normed, w) + b
    h = (pre.shape[1] - x.shape[1]) // 4
    s_left = sigmoid(pre[:, h : 2 * h]) * mask
    s_right = sigmoid(pre[:, 3 * h : 4 * h]) * mask
    left = s_left * pre[:, :h]
    right = s_right * pre[:, 2 * h : 3 * h]
    gate = sigmoid(pre[:, 4 * h :])
    return x_hat, rstd, normed, s_left, s_right, left, right, gate


def mix(product, gain, shift, w_out, b_out):
    p_hat, p_rstd = norm_parts(product)
    mixed = (p_hat * gain + shift).astype(BF16)
    return p_hat, p_rstd, mixed, dot(mixed, w_out) + b_out


def unmix(up, gate, branch, p_hat, p_rstd, gain, w_out):
    d_branch = up * gate
    d_gate = (d_branch * branch * (1.0 - gate)).astype(BF16)
    d_branch = d_branch.astype(BF16)
    d_mixed = dot(d_branch, w_out, ((1,), (1,))) * gain
    return d_branch, d_gate, norm_vjp(p_hat, p_rstd, d_mixed)


def contract(n, first, x, y):
    lanes = y.shape[1]
    tiles = (n // 8, 8, lanes)

    def step(e, totals):
        block = y[pl.ds(pl.multiple_of(e * n, n), n), :].reshape(tiles)
        return tuple(
            totals[a] + x[pl.ds((first + a) * n + e, 8, stride=0), :][None] * block
            for a in range(BLOCK_ROWS)
        )

    zero = jnp.zeros(tiles, F32)
    totals = lax.fori_loop(0, n, step, (zero,) * BLOCK_ROWS, unroll=True)
    return jnp.stack(totals).reshape(BLOCK_ROWS * n, lanes)


def edge_grads(d_left, d_right, s_left, s_right, left, right):
    return (
        (d_left * s_left).astype(BF16),
        (d_left * left * (1.0 - s_left)).astype(BF16),
        (d_right * s_right).astype(BF16),
        (d_right * right * (1.0 - s_right)).astype(BF16),
    )


def tail_values(block, lanes_from, lanes_to):
    lane = lax.broadcasted_iota(jnp.int32, block.shape, block.ndim - 1)
    inside = (lane >= lanes_from) & (lane < lanes_to)
    return jnp.max(jnp.where(inside, block.astype(F32), 0.0)).astype(jnp.int32)


def own_place(pair_ref):
    return tail_values(pair_ref[0, -TAIL_ROWS:, :], 64, 128)


def place_of(own, jump, side):
    return own ^ (2 * jump) ^ side


def block(t, rows, n):
    return pl.ds(pl.multiple_of(t * rows * n, rows * n), rows * n)


def forward(n, jumps, *refs):
    pairs, refs = refs[: len(jumps)], refs[len(jumps) :]
    (weights, vectors), refs = refs[:2], refs[2:]
    (edges_s, slopes_s, gate_s, hat_s, rstd_s) = refs[:5]
    (p_hat_s, p_rstd_s, branch_s, normed_s, mixed_s) = refs[5:KEPT]
    (next_s,) = refs[KEPT:]
    c = weights.shape[1]
    width = weights.shape[2] - c
    rows = n // (2 * len(jumps))
    cells = rows * n
    tails = jnp.stack([pair[:, cells:, :] for pair in pairs])
    length = tail_values(tails, 0, 64)
    own = own_place(pairs[0])
    for pair, jump in zip(pairs, jumps):
        for side in range(2):
            next_s[block(place_of(own, jump, side), rows, n), :] = pair[side, :cells, :]
    steps = n // STEP_ROWS

    @pl.loop(0, 2)
    def _(u):
        row = jnp.where(u == 0, vectors[0:1, :], vectors[1:2, :])
        bias, gains, shifts, bias_out = vector_parts(row, c, width)

        @pl.loop(0, steps)
        def _(t):
            first = t * STEP_ROWS
            here = block(t, STEP_ROWS, n)
            mask = pair_mask_block(length, first, STEP_ROWS, n, c)
            x_hat, rstd, normed, s_left, s_right, left, right, gate = project(
                next_s[here, :], mask, weights[u, :, :width], bias, gains[:, :c], shifts[:, :c]
            )
            edges_s[u, 0, here, :] = left
            edges_s[u, 1, here, :] = right
            for r in range(STEP_ROWS):
                swapped = pl.ds(first + r, n, stride=n)
                edges_s[u, 2, swapped, :] = right[r * n : (r + 1) * n]
                edges_s[u, 3, swapped, :] = left[r * n : (r + 1) * n]
            slopes_s[u, 0, here, :] = s_left
            slopes_s[u, 1, here, :] = s_right
            gate_s[u, here, :] = gate
            hat_s[u, here, :] = x_hat
            rstd_s[u, here, :] = rstd
            normed_s[u, here, :] = normed

        @pl.loop(0, steps)
        def _(t):
            here = block(t, STEP_ROWS, n)
            x, y = edges_s.at[u, 3 * u], edges_s.at[u, 2 - u]
            product = [
                contract(n, t * STEP_ROWS + r, x, y) for r in range(0, STEP_ROWS, BLOCK_ROWS)
            ]
            p_hat, p_rstd, mixed, branch = mix(
                jnp.concatenate(product).astype(BF16), gains[:, c:], shifts[:, c:], weights[u, :, width:], bias_out
            )
            p_hat_s[u, here, :] = p_hat
            p_rstd_s[u, here, :] = p_rstd
            mixed_s[u, here, :] = mixed
            branch_s[u, here, :] = branch
            x = next_s[here, :].astype(F32)
            next_s[here, :] = (x + gate_s[u, here, :] * branch).astype(BF16)


def backward(n, u, jumps, *refs):
    if u == 1:
        (pair, *parted), refs = refs[: 1 + len(jumps)], refs[1 + len(jumps) :]
        up_in_ref, refs = refs[-1], (None,) + refs[:-1]
        own = own_place(pair)
        for part, jump in zip(parted, jumps):
            for side in range(2):
                rows = part.shape[1] // n
                up_in_ref[block(place_of(own, jump, side), rows, n), :] = part[side]
    else:
        up_in_ref = refs[0]
    weights, vectors = refs[1:3]
    (edges_s, slopes_s, gate_s, hat_s, rstd_s) = (ref.at[u] for ref in refs[3:8])
    (p_hat_s, p_rstd_s, branch_s, normed_s, mixed_s) = (ref.at[u] for ref in refs[8 : 3 + KEPT])
    if u == 1:
        up_ref, grads_ref, d_product_s, d_edges_s, sums_s, d_pre_s = refs[3 + KEPT :]
    else:
        d_pre_s, grads_ref, d_product_s, d_edges_s, sums_s = refs[3 + KEPT :]
    c, h = weights.shape[1], edges_s.shape[2]
    width = 4 * h + c
    gain = vector_parts(vectors[u : u + 1, :], c, width)[1]
    sums_s[...] = jnp.zeros_like(sums_s)

    @pl.loop(0, n // STEP_ROWS)
    def _(t):
        here = block(t, STEP_ROWS, n)
        d_branch, d_gate, d_product = unmix(
            up_in_ref[here, :].astype(F32),
            gate_s[here, :],
            branch_s[here, :],
            p_hat_s[here, :],
            p_rstd_s[here, :],
            gain[:, c:],
            weights[u, :, width:],
        )
        sums_s[:, width:] += dot(mixed_s[here, :], d_branch, ((0,), (0,)))
        d_pre_s[here, 4 * h :] = d_gate
        d_product_s[u, here, :] = d_product
        for r in range(STEP_ROWS):
            swapped = pl.ds(t * STEP_ROWS + r, n, stride=n)
            d_product_s[1 - u, swapped, :] = d_product[r * n : (r + 1) * n]

    blocks = n // BLOCK_ROWS

    @pl.loop(0, 2 * blocks)
    def _(step):
        side, t = step // blocks, step % blocks
        edges, d_product = edges_s.at[1 - side], d_product_s.at[side]
        x, y = (edges, d_product) if u == 1 else (d_product, edges)
        d_edges_s[side, block(t, BLOCK_ROWS, n), :] = contract(n, t * BLOCK_ROWS, x, y)

    @pl.loop(0, n // STEP_ROWS)
    def _(t):
        here = block(t, STEP_ROWS, n)
        grads = edge_grads(
            d_edges_s[0, here, :],
            d_edges_s[1, here, :],
            slopes_s[0, here, :],
            slopes_s[1, here, :],
            edges_s[0, here, :],
            edges_s[1, here, :],
        )
        d_pre = jnp.concatenate([*grads, d_pre_s[here, 4 * h :]], axis=1)
        normed = normed_s[here, :]
        if u == 1:
            d_normed = dot(d_pre, weights[u, :, :width], ((1,), (1,))) * gain[:, :c]
            pulled = norm_vjp(hat_s[here, :], rstd_s[here, :], d_normed)
            up_ref[here, :] = up_in_ref[here, :].astype(F32) + pulled
        else:
            d_pre_s[here, : 4 * h] = d_pre[:, : 4 * h]
        sums_s[:, :width] += dot(normed, d_pre, ((0,), (0,)))

    grads_ref[...] = sums_s[...].astype(BF16)


def own_rows(pair_ref, up_ref, d_pre_ref, weights, vectors, hat_ref, rstd_ref, out_ref):
    cells, c = out_ref.shape
    place = own_place(pair_ref)
    own = pl.ds(pl.multiple_of(place * cells, cells), cells)
    width = d_pre_ref.shape[1]
    gain = vector_parts(vectors[0:1, :], c, width)[1]
    d_normed = dot(d_pre_ref[own, :], weights[0, :, :width], ((1,), (1,))) * gain[:, :c]
    pulled = norm_vjp(hat_ref[0, own, :], rstd_ref[0, own, :], d_normed)
    out_ref[...] = (up_ref[own, :] + pulled).astype(BF16)


def exchange(value, axis, size, step):
    return lax.ppermute(value, axis, [(d, d ^ step) for d in range(size)])


def add_narrow(a, b):
    return (a.astype(F32) + b.astype(F32)).astype(BF16)


def prepare(
    index_ref, mask_ref, state_ref, cot_ref, w, w_out, b, gain, shift, b_out, *refs
):
    sent_ref, weights_ref, vectors_ref, mask_s, sems = refs
    cells, c = state_ref.shape
    below, width = cells + TAIL_ROWS, w.shape[2]
    copies = [(mask_ref, mask_s), (state_ref, sent_ref.at[:cells]), (cot_ref, sent_ref.at[below:])]
    copies += [(w, weights_ref.at[:, :, :width]), (w_out, weights_ref.at[:, :, width:])]
    first = 0
    for vector in (b, gain, shift, b_out):
        last = first + vector.shape[1]
        copies.append((vector, vectors_ref.at[:, first:last]))
        first = last
    copies = [pltpu.make_async_copy(*pair, sems.at[k]) for k, pair in enumerate(copies)]
    for copy in copies:
        copy.start()
    copies[0].wait()
    length = jnp.max(jnp.sum(mask_s[...].astype(F32), axis=1, keepdims=True))
    in_length = lax.broadcasted_iota(jnp.int32, (TAIL_ROWS, c), 1) < 64
    place = index_ref[0].astype(F32)
    sent_ref[cells:below, :] = jnp.where(in_length, length, place).astype(BF16)
    for copy in copies[1:]:
        copy.wait()


def pair_up(near_ref, far_ref, state_ref, cot_ref):
    split = state_ref.shape[1]
    for side, ref in enumerate((near_ref, far_ref)):
        state_ref[side] = ref[:split, :]
        cot_ref[side] = ref[split:, :]


def hold(weights_in, vectors_in, weights_out, vectors_out):
    weights_out[...] = weights_in[...]
    vectors_out[...] = vectors_in[...]


def vector_parts(row, c, width):
    ends = [width, width + 2 * c, width + 4 * c, width + 5 * c]
    return [row[:, first:last] for first, last in zip([0] + ends, ends)]


def add_grads(own_0, other_0, own_both, other_both, proj_ref, out_ref):
    width = proj_ref.shape[2]
    for u, (own, other) in enumerate(((own_0, other_0), (own_both.at[1], other_both.at[1]))):
        total = own[...].astype(F32) + other[...].astype(F32)
        proj_ref[u] = total[:, :width]
        out_ref[u] = total[:, width:]


def crop_shards(
    groups,
    parts,
    pair_repr,
    pair_mask,
    cotangent,
    proj_weight,
    proj_bias,
    norm_gain,
    norm_shift,
    out_weight,
    out_bias,
):
    _, rows, n, c = pair_repr.shape
    h = out_weight.shape[1]
    width = proj_weight.shape[2]
    cells, pairs = rows * n, n * n
    plane = (pairs + 8, h)
    kept = [jax.ShapeDtypeStruct((2, 4) + plane, F32), jax.ShapeDtypeStruct((2, 2) + plane, F32)]
    kept += [jax.ShapeDtypeStruct((2,) + plane, F32)] * 6
    kept += [jax.ShapeDtypeStruct((2, pairs, h), BF16)] * 2
    grads = jax.ShapeDtypeStruct((c, width + c), BF16)
    vmem = pl.BlockSpec(memory_space=pltpu.VMEM)
    main = pl.BlockSpec(memory_space=pltpu.HBM)
    params = pltpu.CompilerParams(vmem_limit_bytes=VMEM_BYTES)

    def cost(planes):
        flops = 4 * pairs * width * c
        return pl.CostEstimate(
            flops=flops, bytes_accessed=planes * pairs * c * 4, transcendentals=0
        )

    packed = (
        jax.ShapeDtypeStruct((2, c, width + c), BF16),
        jax.ShapeDtypeStruct((2, width + 5 * c), F32),
    )
    sent, *weights = pl.pallas_call(
        prepare,
        out_shape=(jax.ShapeDtypeStruct((2 * cells + TAIL_ROWS, c), BF16),) + packed,
        in_specs=[pl.BlockSpec(memory_space=pltpu.SMEM)] + [main] * 9,
        out_specs=[vmem] * 3,
        scratch_shapes=[pltpu.VMEM((rows, n), jnp.int32), pltpu.SemaphoreType.DMA((9,))],
        compiler_params=pltpu.CompilerParams(vmem_limit_bytes=PREPARE_BYTES),
        name="prepare",
    )(
        lax.axis_index("dap").astype(jnp.int32)[None],
        pair_mask[0],
        pair_repr.reshape(cells, c),
        cotangent.reshape(cells, c),
        proj_weight,
        out_weight,
        proj_bias,
        norm_gain,
        norm_shift,
        out_bias,
    )
    weights = pl.pallas_call(
        hold,
        out_shape=packed,
        in_specs=[vmem] * 2,
        out_specs=[vmem] * 2,
        compiler_params=params,
        cost_estimate=cost(8),
        name="hold",
    )(*weights)
    beside = exchange(sent, "dap", parts, 1)
    beside, *weights = lax.optimization_barrier((beside, *weights))
    state, cot = pl.pallas_call(
        pair_up,
        out_shape=(
            jax.ShapeDtypeStruct((2, cells + TAIL_ROWS, c), BF16),
            jax.ShapeDtypeStruct((2, cells, c), BF16),
        ),
        in_specs=[vmem] * 2,
        out_specs=[vmem] * 2,
        compiler_params=params,
        name="pair_up",
    )(sent, beside)
    states, cots = [state], [cot]
    half = parts // 2
    jumps = [0, *range(1, half // 2), *reversed(range(half // 2, half))]
    for group in (states, cots):
        group += [exchange(group[0], "dap", parts, 2 * jump) for jump in jumps[1:]]

    held = pl.pallas_call(
        functools.partial(forward, n, jumps),
        out_shape=kept,
        in_specs=[vmem] * (half + 2),
        out_specs=(vmem,) * KEPT,
        scratch_shapes=[pltpu.VMEM((pairs, c), BF16)],
        compiler_params=params,
        cost_estimate=cost(64),
        name="forward",
    )(*states, *weights)

    work = [pltpu.VMEM((2,) + plane, F32)] * 2
    work += [pltpu.VMEM(grads.shape, F32)]
    d_pre = jax.ShapeDtypeStruct((pairs, width), BF16)
    up_1, grads_1 = pl.pallas_call(
        functools.partial(backward, n, 1, jumps),
        out_shape=(jax.ShapeDtypeStruct((pairs, c), F32), grads),
        in_specs=[vmem] * (3 + half + KEPT),
        out_specs=(vmem, vmem),
        scratch_shapes=work + [pltpu.VMEM(d_pre.shape, BF16), pltpu.VMEM((pairs, c), BF16)],
        compiler_params=params,
        cost_estimate=cost(48),
        name="backward_second",
    )(states[0], *cots, *weights, *held)
    far = groups // 2
    others_1 = exchange(grads_1, "dp", groups, far)

    d_pre_0, grads_0 = pl.pallas_call(
        functools.partial(backward, n, 0, jumps),
        out_shape=(d_pre, grads),
        in_specs=[vmem] * (3 + KEPT),
        out_specs=(vmem, vmem),
        scratch_shapes=work,
        compiler_params=params,
        cost_estimate=cost(48),
        name="backward_first",
    )(up_1, *weights, *held)

    pair_grad = pl.pallas_call(
        own_rows,
        out_shape=jax.ShapeDtypeStruct((cells, c), BF16),
        in_specs=[vmem] * 7,
        out_specs=vmem,
        compiler_params=params,
        cost_estimate=cost(8),
        name="own_rows",
    )(states[0], up_1, d_pre_0, *weights, held[3], held[4])

    both = jnp.stack([grads_0, add_narrow(grads_1, others_1)])
    others = jnp.zeros_like(both)
    step = 1
    while step < far:
        both = add_narrow(both, others) if step > 1 else both
        others = exchange(both, "dp", groups, step)
        step *= 2
    grads_0 = add_narrow(both[0], others[0])
    others_0 = exchange(grads_0, "dp", groups, far)

    proj_total, out_total = pl.pallas_call(
        add_grads,
        out_shape=(
            jax.ShapeDtypeStruct((2, c, width), F32),
            jax.ShapeDtypeStruct((2, h, c), F32),
        ),
        in_specs=[vmem] * 4,
        out_specs=(vmem, vmem),
        compiler_params=params,
        name="add_grads",
    )(grads_0, others_0, both, others)
    return pair_grad.reshape(pair_repr.shape), proj_total, out_total


def layer_norm(values, gain_vec, shift_vec, norm_axis):
    mean_value = jnp.mean(values, axis=norm_axis, keepdims=True)
    centred = values - mean_value
    variance = jnp.mean(centred * centred, axis=norm_axis, keepdims=True)
    return centred * lax.rsqrt(variance + NORM_EPSILON) * gain_vec + shift_vec


def norm_pullback(values, gain_vec, shift_vec, norm_axis, upstream):
    _, pull_back = jax.vjp(
        lambda inner_value: layer_norm(inner_value, gain_vec, shift_vec, norm_axis), values
    )
    return pull_back(upstream)[0]


def edge_pair(edge_pre, cell_mask):
    left_edge = jax.nn.sigmoid(edge_pre[1]) * edge_pre[0] * cell_mask
    right_edge = jax.nn.sigmoid(edge_pre[3]) * edge_pre[2] * cell_mask
    return jnp.stack([left_edge, right_edge]).astype(jnp.bfloat16)


def edge_pullback(edge_pre, cell_mask, grad_pair):
    sig_left = jax.nn.sigmoid(edge_pre[1])
    sig_right = jax.nn.sigmoid(edge_pre[3])
    grad_left = grad_pair[0].astype(jnp.float32) * cell_mask
    grad_right = grad_pair[1].astype(jnp.float32) * cell_mask
    return jnp.stack(
        [
            grad_left * sig_left,
            grad_left * edge_pre[0] * sig_left * (1.0 - sig_left),
            grad_right * sig_right,
            grad_right * edge_pre[2] * sig_right * (1.0 - sig_right),
        ]
    ).astype(jnp.bfloat16)


def triangle(pair_edges, outgoing):
    if outgoing:
        einsum_form = "cik,cjk->cij"
    else:
        einsum_form = "cki,ckj->cij"
    return jnp.einsum(
        einsum_form, pair_edges[0], pair_edges[1], preferred_element_type=jnp.float32
    ).astype(jnp.bfloat16)


def triangle_pullback(pair_edges, grad_product, outgoing):
    left_edge = pair_edges[0]
    right_edge = pair_edges[1]
    if outgoing:
        grad_left = jnp.einsum(
            "cij,cjk->cik", grad_product, right_edge, preferred_element_type=jnp.float32
        )
        grad_right = jnp.einsum(
            "cij,cik->cjk", grad_product, left_edge, preferred_element_type=jnp.float32
        )
    else:
        grad_left = jnp.einsum(
            "ckj,cij->cki", right_edge, grad_product, preferred_element_type=jnp.float32
        )
        grad_right = jnp.einsum(
            "cki,cij->ckj", left_edge, grad_product, preferred_element_type=jnp.float32
        )
    return jnp.stack([grad_left, grad_right]).astype(jnp.bfloat16)


def update_weights(proj_weight, proj_bias, norm_gain, norm_shift, update, channels, hidden):
    w_edge = proj_weight[update, :, : 4 * hidden].reshape(channels, 4, hidden)
    w_gate = proj_weight[update, :, 4 * hidden :]
    bias_edge = proj_bias[update, : 4 * hidden].reshape(4, hidden, 1, 1)
    bias_gate = proj_bias[update, 4 * hidden :]
    gain_in = norm_gain[update, :channels]
    shift_in = norm_shift[update, :channels]
    gain_out = norm_gain[update, channels:][:, None, None]
    shift_out = norm_shift[update, channels:][:, None, None]
    return (w_edge, w_gate, bias_edge, bias_gate, gain_in, shift_in, gain_out, shift_out)


def shards(
    pair_repr,
    pair_mask,
    cotangent,
    proj_weight,
    proj_bias,
    norm_gain,
    norm_shift,
    out_weight,
    out_bias,
):
    channels = pair_repr.shape[3]
    hidden = out_weight.shape[1]
    pair_state = pair_repr[0]
    cell_mask = pair_mask[0].astype(jnp.float32)
    records = []
    for update in range(2):
        w_edge, w_gate, bias_edge, bias_gate, gain_in, shift_in, gain_out, shift_out = (
            update_weights(proj_weight, proj_bias, norm_gain, norm_shift, update, channels, hidden)
        )
        state_f = pair_state.astype(jnp.float32)
        normed = layer_norm(state_f, gain_in, shift_in, -1).astype(jnp.bfloat16)
        edge_pre = (
            jnp.einsum("rnc,cgh->ghrn", normed, w_edge, preferred_element_type=jnp.float32)
            + bias_edge
        )
        gate_pre = (
            jnp.einsum("rnc,cd->rnd", normed, w_gate, preferred_element_type=jnp.float32)
            + bias_gate
        )
        pair_edges = edge_pair(edge_pre, cell_mask)
        spread = lax.all_to_all(pair_edges, "dap", split_axis=1, concat_axis=2, tiled=True)
        product = lax.all_to_all(
            triangle(spread, update == 0), "dap", split_axis=1, concat_axis=0, tiled=True
        )
        mixed_norm = layer_norm(product.astype(jnp.float32), gain_out, shift_out, 0).astype(
            jnp.bfloat16
        )
        branch = (
            jnp.einsum(
                "hrn,hd->rnd", mixed_norm, out_weight[update], preferred_element_type=jnp.float32
            )
            + out_bias[update]
        )
        records.append(
            (state_f, normed, edge_pre, gate_pre, pair_edges, spread, product, mixed_norm, branch)
        )
        pair_state = (state_f + jax.nn.sigmoid(gate_pre) * branch).astype(jnp.bfloat16)
    upstream = cotangent[0].astype(jnp.float32)
    proj_grads = []
    out_grads = []
    for update in (1, 0):
        state_f, normed, edge_pre, gate_pre, pair_edges, spread, product, mixed_norm, branch = (
            records[update]
        )
        w_edge, w_gate, bias_edge, bias_gate, gain_in, shift_in, gain_out, shift_out = (
            update_weights(proj_weight, proj_bias, norm_gain, norm_shift, update, channels, hidden)
        )
        gate_value = jax.nn.sigmoid(gate_pre)
        grad_branch = (upstream * gate_value).astype(jnp.bfloat16)
        grad_gate = (upstream * branch * gate_value * (1.0 - gate_value)).astype(jnp.bfloat16)
        out_grad = jnp.einsum(
            "hrn,rnd->hd", mixed_norm, grad_branch, preferred_element_type=jnp.float32
        )
        grad_mixed = jnp.einsum(
            "rnd,hd->hrn", grad_branch, out_weight[update], preferred_element_type=jnp.float32
        )
        grad_product = norm_pullback(
            product.astype(jnp.float32), gain_out, shift_out, 0, grad_mixed
        ).astype(jnp.bfloat16)
        column_edges = spread
        column_grad = lax.all_to_all(
            grad_product[None], "dap", split_axis=1, concat_axis=2, tiled=True
        )[0]
        grad_pair = lax.all_to_all(
            triangle_pullback(column_edges, column_grad, update == 0),
            "dap",
            split_axis=2,
            concat_axis=1,
            tiled=True,
        )
        grad_edge = edge_pullback(edge_pre, cell_mask, grad_pair)
        edge_grad = jnp.einsum(
            "rnc,ghrn->cgh", normed, grad_edge, preferred_element_type=jnp.float32
        ).reshape(channels, 4 * hidden)
        gate_grad = jnp.einsum("rnc,rnd->cd", normed, grad_gate, preferred_element_type=jnp.float32)
        grad_normed = jnp.einsum(
            "ghrn,cgh->rnc", grad_edge, w_edge, preferred_element_type=jnp.float32
        )
        grad_normed = grad_normed + jnp.einsum(
            "rnd,cd->rnc", grad_gate, w_gate, preferred_element_type=jnp.float32
        )
        upstream = upstream + norm_pullback(state_f, gain_in, shift_in, -1, grad_normed)
        proj_part = jnp.concatenate([edge_grad, gate_grad], axis=1)
        proj_grads.append(proj_part)
        out_grads.append(out_grad)
    proj_total = jnp.stack(proj_grads[::-1])
    out_total = jnp.stack(out_grads[::-1])
    proj_total, out_total = lax.psum((proj_total, out_total), ("dp", "dap"))
    return (upstream.astype(jnp.bfloat16)[None], proj_total, out_total)


def solution(mesh):
    placed = (
        P("dp", "dap", None, None),
        P("dp", "dap", None),
        P("dp", "dap", None, None),
        P(),
        P(),
        P(),
        P(),
        P(),
        P(),
    )
    groups, parts = mesh.shape["dp"], mesh.shape["dap"]

    def program(*args):
        n, c = args[0].shape[2:]
        rows = n // parts
        fits = 20 * n * n * c * 4 <= CROP_BUDGET
        paired = all(size > 1 and size & (size - 1) == 0 for size in (groups, parts))
        even = args[7].shape[1] == c == 128 and STEP_ROWS % rows == 0 and n % STEP_ROWS == 0
        body = functools.partial(crop_shards, groups, parts) if fits and even and paired else shards
        return spread_over(body)(*args)

    def spread_over(body):
        return jax.shard_map(
            body,
            mesh=mesh,
            in_specs=placed,
            out_specs=(P("dp", "dap", None, None), P(), P()),
            check_vma=False,
        )

    return program
```

```python
import functools

import jax
import jax.numpy as jnp
from jax import lax
from jax.experimental import pallas as pl
from jax.experimental.pallas import tpu as pltpu
from jax.sharding import PartitionSpec as P

NORM_EPSILON = 1e-05
VMEM_BYTES = 16 * 1024 * 1024
PREPARE_BYTES = 63 * 1024 * 1024
CROP_BUDGET = 32 * 1024 * 1024
BLOCK_ROWS = 8
STEP_ROWS = 32
KEPT = 10
TAIL_ROWS = 16
F32 = jnp.float32
BF16 = jnp.bfloat16


def sigmoid(x):
    return 0.5 * jnp.tanh(0.5 * x) + 0.5


def dot(a, b, dims=((1,), (0,))):
    return lax.dot_general(a, b, (dims, ((), ())), preferred_element_type=F32)


def norm_parts(x):
    x = x.astype(F32)
    centred = x - jnp.mean(x, axis=-1, keepdims=True)
    rstd = lax.rsqrt(jnp.mean(centred * centred, axis=-1, keepdims=True) + NORM_EPSILON)
    return centred * rstd, jnp.broadcast_to(rstd, x.shape)


def norm_vjp(x_hat, rstd, grad):
    mean_grad = jnp.mean(grad, axis=-1, keepdims=True)
    mean_prod = jnp.mean(grad * x_hat, axis=-1, keepdims=True)
    return rstd * (grad - mean_grad - x_hat * mean_prod)


def pair_mask_block(length, first_row, rows, n, lanes):
    shape = (rows, n, lanes)
    i = lax.broadcasted_iota(jnp.int32, shape, 0) + first_row
    j = lax.broadcasted_iota(jnp.int32, shape, 1)
    inside = jnp.where((i < length) & (j < length), 1.0, 0.0)
    return inside.reshape(rows * n, lanes)


def project(x, mask, w, b, gain, shift):
    x_hat, rstd = norm_parts(x)
    normed = (x_hat * gain + shift).astype(BF16)
    pre = dot(normed, w) + b
    h = (pre.shape[1] - x.shape[1]) // 4
    s_left = sigmoid(pre[:, h : 2 * h]) * mask
    s_right = sigmoid(pre[:, 3 * h : 4 * h]) * mask
    left = s_left * pre[:, :h]
    right = s_right * pre[:, 2 * h : 3 * h]
    gate = sigmoid(pre[:, 4 * h :])
    return x_hat, rstd, normed, s_left, s_right, left, right, gate


def mix(product, gain, shift, w_out, b_out):
    p_hat, p_rstd = norm_parts(product)
    mixed = (p_hat * gain + shift).astype(BF16)
    return p_hat, p_rstd, mixed, dot(mixed, w_out) + b_out


def unmix(up, gate, branch, p_hat, p_rstd, gain, w_out):
    d_branch = up * gate
    d_gate = (d_branch * branch * (1.0 - gate)).astype(BF16)
    d_branch = d_branch.astype(BF16)
    d_mixed = dot(d_branch, w_out, ((1,), (1,))) * gain
    return d_branch, d_gate, norm_vjp(p_hat, p_rstd, d_mixed)


def contract(n, first, x, y):
    lanes = y.shape[1]
    tiles = (n // 8, 8, lanes)

    def step(e, totals):
        block = y[pl.ds(pl.multiple_of(e * n, n), n), :].reshape(tiles)
        return tuple(
            totals[a] + x[pl.ds((first + a) * n + e, 8, stride=0), :][None] * block
            for a in range(BLOCK_ROWS)
        )

    zero = jnp.zeros(tiles, F32)
    totals = lax.fori_loop(0, n, step, (zero,) * BLOCK_ROWS, unroll=True)
    return jnp.stack(totals).reshape(BLOCK_ROWS * n, lanes)


def edge_grads(d_edge, slope, edge):
    grads = (d_edge * slope).astype(BF16), (d_edge * edge * (1.0 - slope)).astype(BF16)
    return jnp.concatenate(grads, axis=1)


def tail_values(block, lanes_from, lanes_to):
    lane = lax.broadcasted_iota(jnp.int32, block.shape, block.ndim - 1)
    inside = (lane >= lanes_from) & (lane < lanes_to)
    return jnp.max(jnp.where(inside, block.astype(F32), 0.0)).astype(jnp.int32)


def own_place(pair_ref):
    return tail_values(pair_ref[0, -TAIL_ROWS:, :], 64, 128)


def place_of(own, jump, side):
    return own ^ (2 * jump) ^ side


def block(t, rows, n):
    return pl.ds(pl.multiple_of(t * rows * n, rows * n), rows * n)


def forward(n, jumps, *refs):
    pairs, refs = refs[: len(jumps)], refs[len(jumps) :]
    (weights, vectors), refs = refs[:2], refs[2:]
    (edges_s, slopes_s, gate_s, hat_s, rstd_s) = refs[:5]
    (p_hat_s, p_rstd_s, branch_s, normed_s, mixed_s) = refs[5:KEPT]
    (next_s,) = refs[KEPT:]
    c = weights.shape[1]
    width = weights.shape[2] - c
    rows = n // (2 * len(jumps))
    cells = rows * n
    tails = jnp.stack([pair[:, cells:, :] for pair in pairs])
    length = tail_values(tails, 0, 64)
    own = own_place(pairs[0])
    for pair, jump in zip(pairs, jumps):
        for side in range(2):
            next_s[block(place_of(own, jump, side), rows, n), :] = pair[side, :cells, :]
    steps = n // STEP_ROWS

    @pl.loop(0, 2)
    def _(u):
        row = jnp.where(u == 0, vectors[0:1, :], vectors[1:2, :])
        bias, gains, shifts, bias_out = vector_parts(row, c, width)

        @pl.loop(0, steps)
        def _(t):
            first = t * STEP_ROWS
            here = block(t, STEP_ROWS, n)
            mask = pair_mask_block(length, first, STEP_ROWS, n, c)
            x_hat, rstd, normed, s_left, s_right, left, right, gate = project(
                next_s[here, :], mask, weights[u, :, :width], bias, gains[:, :c], shifts[:, :c]
            )
            edges_s[u, 0, here, :] = left
            edges_s[u, 1, here, :] = right
            for r in range(STEP_ROWS):
                swapped = pl.ds(first + r, n, stride=n)
                edges_s[u, 2, swapped, :] = right[r * n : (r + 1) * n]
                edges_s[u, 3, swapped, :] = left[r * n : (r + 1) * n]
            slopes_s[u, 0, here, :] = s_left
            slopes_s[u, 1, here, :] = s_right
            gate_s[u, here, :] = gate
            hat_s[u, here, :] = x_hat
            rstd_s[u, here, :] = rstd
            normed_s[u, here, :] = normed

        @pl.loop(0, steps)
        def _(t):
            here = block(t, STEP_ROWS, n)
            x, y = edges_s.at[u, 3 * u], edges_s.at[u, 2 - u]
            product = [
                contract(n, t * STEP_ROWS + r, x, y) for r in range(0, STEP_ROWS, BLOCK_ROWS)
            ]
            p_hat, p_rstd, mixed, branch = mix(
                jnp.concatenate(product).astype(BF16), gains[:, c:], shifts[:, c:], weights[u, :, width:], bias_out
            )
            p_hat_s[u, here, :] = p_hat
            p_rstd_s[u, here, :] = p_rstd
            mixed_s[u, here, :] = mixed
            branch_s[u, here, :] = branch
            x = next_s[here, :].astype(F32)
            next_s[here, :] = (x + gate_s[u, here, :] * branch).astype(BF16)


def kept_parts(refs, u):
    return [ref.at[u] for ref in refs[:KEPT]]


def store_swapped(ref, rows, n, first, values):
    for r in range(rows):
        ref[pl.ds(first + r, n, stride=n), :] = values[r * n : (r + 1) * n]


def backward_second(n, jumps, pair, *refs):
    parted, refs = refs[: len(jumps)], refs[len(jumps) :]
    weights, vectors = refs[:2]
    (edges_s, slopes_s, gate_s, hat_s, rstd_s, *kept) = kept_parts(refs[2:], 1)
    (p_hat_s, p_rstd_s, branch_s, normed_s, mixed_s) = kept
    up_ref, grads_ref, d_product_s, d_edges_s, d_pre_s, cot_s = refs[2 + KEPT :]
    c, h = weights.shape[1], edges_s.shape[2]
    width = 4 * h + c
    gain = vector_parts(vectors[1:2, :], c, width)[1]
    own = own_place(pair)
    for part, jump in zip(parted, jumps):
        for side in range(2):
            cot_s[block(place_of(own, jump, side), part.shape[1] // n, n), :] = part[side]

    @pl.loop(0, n // STEP_ROWS)
    def _(t):
        here = block(t, STEP_ROWS, n)
        d_branch, d_gate, d_product = unmix(
            cot_s[here, :].astype(F32),
            gate_s[here, :],
            branch_s[here, :],
            p_hat_s[here, :],
            p_rstd_s[here, :],
            gain[:, c:],
            weights[1, :, width:],
        )
        d_out = dot(mixed_s[here, :], d_branch, ((0,), (0,)))
        d_pre_s[here, 4 * h :] = d_gate
        d_product_s[1, here, :] = d_product
        store_swapped(d_product_s.at[0], STEP_ROWS, n, t * STEP_ROWS, d_product)
        grads_ref[:, width:] = d_out.astype(BF16)

    blocks = n // BLOCK_ROWS

    @pl.loop(0, 2 * blocks)
    def _(step):
        side, t = step // blocks, step % blocks
        d_edges_s[side, block(t, BLOCK_ROWS, n), :] = contract(
            n, t * BLOCK_ROWS, edges_s.at[1 - side], d_product_s.at[side]
        )

    @pl.loop(0, n // STEP_ROWS)
    def _(t):
        here = block(t, STEP_ROWS, n)
        grads = [
            edge_grads(d_edges_s[side, here, :], slopes_s[side, here, :], edges_s[side, here, :])
            for side in range(2)
        ]
        d_pre = jnp.concatenate([*grads, d_pre_s[here, 4 * h :]], axis=1)
        normed = normed_s[here, :]
        d_normed = dot(d_pre, weights[1, :, :width], ((1,), (1,))) * gain[:, :c]
        pulled = norm_vjp(hat_s[here, :], rstd_s[here, :], d_normed)
        up_ref[here, :] = cot_s[here, :].astype(F32) + pulled
        grads_ref[:, :width] = dot(normed, d_pre, ((0,), (0,))).astype(BF16)


def backward_left(n, up_in_ref, weights, vectors, *refs):
    (edges_s, slopes_s, gate_s, _, _, *kept) = kept_parts(refs, 0)
    (p_hat_s, p_rstd_s, branch_s, normed_s, mixed_s) = kept
    d_pre_ref, d_product_t_ref, grads_ref, d_product_s, d_edge_s = refs[KEPT:]
    c, h = weights.shape[1], edges_s.shape[2]
    width = 4 * h + c
    gain = vector_parts(vectors[0:1, :], c, width)[1]

    @pl.loop(0, n // STEP_ROWS)
    def _(t):
        here = block(t, STEP_ROWS, n)
        d_branch, d_gate, d_product = unmix(
            up_in_ref[here, :],
            gate_s[here, :],
            branch_s[here, :],
            p_hat_s[here, :],
            p_rstd_s[here, :],
            gain[:, c:],
            weights[0, :, width:],
        )
        d_out = dot(mixed_s[here, :], d_branch, ((0,), (0,)))
        d_pre_ref[here, 2 * h :] = d_gate
        d_product_s[here, :] = d_product
        store_swapped(d_product_t_ref, STEP_ROWS, n, t * STEP_ROWS, d_product)
        grads_ref[:, 2 * h + c :] = d_out.astype(BF16)

    one_side(n, 0, d_product_s, edges_s, slopes_s, d_edge_s, d_pre_ref)
    d_pre = dot(normed_s[...], d_pre_ref[...], ((0,), (0,)))
    grads_ref[:, : 2 * h + c] = d_pre.astype(BF16)


def backward_right(n, d_product_t_ref, *refs):
    (edges_s, slopes_s, *kept) = kept_parts(refs, 0)
    normed_s = kept[-2]
    d_pre_ref, grads_ref, d_edge_s = refs[KEPT:]
    one_side(n, 1, d_product_t_ref, edges_s, slopes_s, d_edge_s, d_pre_ref)
    grads_ref[...] = dot(normed_s[...], d_pre_ref[...], ((0,), (0,))).astype(BF16)


def one_side(n, side, x, edges_s, slopes_s, d_edge_s, d_pre_ref):
    h = edges_s.shape[2]

    @pl.loop(0, n // BLOCK_ROWS)
    def _(t):
        d_edge_s[block(t, BLOCK_ROWS, n), :] = contract(
            n, t * BLOCK_ROWS, x, edges_s.at[1 - side]
        )

    @pl.loop(0, n // STEP_ROWS)
    def _(t):
        here = block(t, STEP_ROWS, n)
        d_pre_ref[here, : 2 * h] = edge_grads(
            d_edge_s[here, :], slopes_s[side, here, :], edges_s[side, here, :]
        )


def own_rows(
    pair_ref, up_ref, d_left_ref, d_right_ref, weights, vectors, hat_ref, rstd_ref, out_ref
):
    cells, c = out_ref.shape
    half = d_right_ref.shape[1]
    place = own_place(pair_ref)
    own = pl.ds(pl.multiple_of(place * cells, cells), cells)
    width = d_left_ref.shape[1] + half
    gain = vector_parts(vectors[0:1, :], c, width)[1]
    d_left, d_right = d_left_ref[own, :], d_right_ref[own, :]
    d_pre = jnp.concatenate([d_left[:, :half], d_right, d_left[:, half:]], axis=1)
    d_normed = dot(d_pre, weights[0, :, :width], ((1,), (1,))) * gain[:, :c]
    pulled = norm_vjp(hat_ref[0, own, :], rstd_ref[0, own, :], d_normed)
    out_ref[...] = (up_ref[own, :] + pulled).astype(BF16)


def exchange(value, axis, size, step):
    return lax.ppermute(value, axis, [(d, d ^ step) for d in range(size)])


def near_rounds(value, groups):
    other = exchange(value, "dp", groups, 1)
    step = 2
    while step < groups // 2:
        value = add_narrow(value, other)
        other = exchange(value, "dp", groups, step)
        step *= 2
    return value, other


def add_narrow(a, b):
    return (a.astype(F32) + b.astype(F32)).astype(BF16)


def prepare(
    index_ref, mask_ref, state_ref, cot_ref, w, w_out, b, gain, shift, b_out, *refs
):
    sent_ref, weights_ref, vectors_ref, mask_s, sems = refs
    cells, c = state_ref.shape
    below, width = cells + TAIL_ROWS, w.shape[2]
    copies = [(mask_ref, mask_s), (state_ref, sent_ref.at[:cells]), (cot_ref, sent_ref.at[below:])]
    copies += [(w, weights_ref.at[:, :, :width]), (w_out, weights_ref.at[:, :, width:])]
    first = 0
    for vector in (b, gain, shift, b_out):
        last = first + vector.shape[1]
        copies.append((vector, vectors_ref.at[:, first:last]))
        first = last
    copies = [pltpu.make_async_copy(*pair, sems.at[k]) for k, pair in enumerate(copies)]
    for copy in copies:
        copy.start()
    copies[0].wait()
    length = jnp.max(jnp.sum(mask_s[...].astype(F32), axis=1, keepdims=True))
    in_length = lax.broadcasted_iota(jnp.int32, (TAIL_ROWS, c), 1) < 64
    place = index_ref[0].astype(F32)
    sent_ref[cells:below, :] = jnp.where(in_length, length, place).astype(BF16)
    for copy in copies[1:]:
        copy.wait()


def pair_up(near_ref, far_ref, state_ref, cot_ref):
    split = state_ref.shape[1]
    for side, ref in enumerate((near_ref, far_ref)):
        state_ref[side] = ref[:split, :]
        cot_ref[side] = ref[split:, :]


def hold(weights_in, vectors_in, weights_out, vectors_out):
    weights_out[...] = weights_in[...]
    vectors_out[...] = vectors_in[...]


def vector_parts(row, c, width):
    ends = [width, width + 2 * c, width + 4 * c, width + 5 * c]
    return [row[:, first:last] for first, last in zip([0] + ends, ends)]


def add_grads(left, left_far, rest, rest_near, right, right_far, proj_ref, out_ref):
    width = proj_ref.shape[2]
    c = out_ref.shape[2]
    half = (width - c) // 2
    total = left[...].astype(F32) + left_far[...].astype(F32)
    proj_ref[0, :, :half] = total[:, :half]
    proj_ref[0, :, 2 * half :] = total[:, half : half + c]
    out_ref[0] = total[:, half + c :]
    proj_ref[0, :, half : 2 * half] = right[...].astype(F32) + right_far[...].astype(F32)
    total = rest[:, : width + c].astype(F32) + rest_near[:, : width + c].astype(F32)
    proj_ref[1] = total[:, :width]
    out_ref[1] = total[:, width:]


def crop_shards(
    groups,
    parts,
    pair_repr,
    pair_mask,
    cotangent,
    proj_weight,
    proj_bias,
    norm_gain,
    norm_shift,
    out_weight,
    out_bias,
):
    _, rows, n, c = pair_repr.shape
    h = out_weight.shape[1]
    width = proj_weight.shape[2]
    cells, pairs = rows * n, n * n
    plane = (pairs + 8, h)
    kept = [jax.ShapeDtypeStruct((2, 4) + plane, F32), jax.ShapeDtypeStruct((2, 2) + plane, F32)]
    kept += [jax.ShapeDtypeStruct((2,) + plane, F32)] * 6
    kept += [jax.ShapeDtypeStruct((2, pairs, h), BF16)] * 2
    grads = jax.ShapeDtypeStruct((c, width + c), BF16)
    vmem = pl.BlockSpec(memory_space=pltpu.VMEM)
    main = pl.BlockSpec(memory_space=pltpu.HBM)
    params = pltpu.CompilerParams(vmem_limit_bytes=VMEM_BYTES)

    def cost(planes):
        flops = 4 * pairs * width * c
        return pl.CostEstimate(
            flops=flops, bytes_accessed=planes * pairs * c * 4, transcendentals=0
        )

    packed = (
        jax.ShapeDtypeStruct((2, c, width + c), BF16),
        jax.ShapeDtypeStruct((2, width + 5 * c), F32),
    )
    sent, *weights = pl.pallas_call(
        prepare,
        out_shape=(jax.ShapeDtypeStruct((2 * cells + TAIL_ROWS, c), BF16),) + packed,
        in_specs=[pl.BlockSpec(memory_space=pltpu.SMEM)] + [main] * 9,
        out_specs=[vmem] * 3,
        scratch_shapes=[pltpu.VMEM((rows, n), jnp.int32), pltpu.SemaphoreType.DMA((9,))],
        compiler_params=pltpu.CompilerParams(vmem_limit_bytes=PREPARE_BYTES),
        name="prepare",
    )(
        lax.axis_index("dap").astype(jnp.int32)[None],
        pair_mask[0],
        pair_repr.reshape(cells, c),
        cotangent.reshape(cells, c),
        proj_weight,
        out_weight,
        proj_bias,
        norm_gain,
        norm_shift,
        out_bias,
    )
    weights = pl.pallas_call(
        hold,
        out_shape=packed,
        in_specs=[vmem] * 2,
        out_specs=[vmem] * 2,
        compiler_params=params,
        cost_estimate=cost(8),
        name="hold",
    )(*weights)
    beside = exchange(sent, "dap", parts, 1)
    beside, *weights = lax.optimization_barrier((beside, *weights))
    state, cot = pl.pallas_call(
        pair_up,
        out_shape=(
            jax.ShapeDtypeStruct((2, cells + TAIL_ROWS, c), BF16),
            jax.ShapeDtypeStruct((2, cells, c), BF16),
        ),
        in_specs=[vmem] * 2,
        out_specs=[vmem] * 2,
        compiler_params=params,
        name="pair_up",
    )(sent, beside)
    states, cots = [state], [cot]
    half = parts // 2
    jumps = [0, *range(1, half // 2), *reversed(range(half // 2, half))]
    for group in (states, cots):
        group += [exchange(group[0], "dap", parts, 2 * jump) for jump in jumps[1:]]

    held = pl.pallas_call(
        functools.partial(forward, n, jumps),
        out_shape=kept,
        in_specs=[vmem] * (half + 2),
        out_specs=(vmem,) * KEPT,
        scratch_shapes=[pltpu.VMEM((pairs, c), BF16)],
        compiler_params=params,
        cost_estimate=cost(64),
        name="forward",
    )(*states, *weights)

    double, single = pltpu.VMEM((2,) + plane, F32), pltpu.VMEM(plane, F32)
    up_1, grads_1 = pl.pallas_call(
        functools.partial(backward_second, n, jumps),
        out_shape=(jax.ShapeDtypeStruct((pairs, c), F32), grads),
        in_specs=[vmem] * (3 + half + KEPT),
        out_specs=(vmem, vmem),
        scratch_shapes=[
            double,
            double,
            pltpu.VMEM((pairs, width), BF16),
            pltpu.VMEM((pairs, c), BF16),
        ],
        compiler_params=params,
        cost_estimate=cost(48),
        name="backward_second",
    )(states[0], *cots, *weights, *held)
    far = groups // 2
    others_1 = exchange(grads_1, "dp", groups, far)

    d_left, d_product_t, grads_left = pl.pallas_call(
        functools.partial(backward_left, n),
        out_shape=(
            jax.ShapeDtypeStruct((pairs, 2 * h + c), BF16),
            jax.ShapeDtypeStruct(plane, F32),
            jax.ShapeDtypeStruct((c, 2 * h + 2 * c), BF16),
        ),
        in_specs=[vmem] * (3 + KEPT),
        out_specs=[vmem] * 3,
        scratch_shapes=[single, single],
        compiler_params=params,
        cost_estimate=cost(24),
        name="backward_left",
    )(up_1, *weights, *held)
    grads_left = near_rounds(grads_left, groups)

    d_right, grads_right = pl.pallas_call(
        functools.partial(backward_right, n),
        out_shape=(
            jax.ShapeDtypeStruct((pairs, 2 * h), BF16),
            jax.ShapeDtypeStruct((c, 2 * h), BF16),
        ),
        in_specs=[vmem] * (1 + KEPT),
        out_specs=[vmem] * 2,
        scratch_shapes=[single],
        compiler_params=params,
        cost_estimate=cost(24),
        name="backward_right",
    )(d_product_t, *held)
    pair_grad = pl.pallas_call(
        own_rows,
        out_shape=jax.ShapeDtypeStruct((cells, c), BF16),
        in_specs=[vmem] * 8,
        out_specs=vmem,
        compiler_params=params,
        cost_estimate=cost(8),
        name="own_rows",
    )(states[0], up_1, d_left, d_right, *weights, held[3], held[4])

    left = add_narrow(*grads_left)
    left_far = exchange(left, "dp", groups, far)
    rest, rest_near = near_rounds(
        jnp.concatenate([add_narrow(grads_1, others_1), grads_right], axis=1), groups
    )
    right = add_narrow(rest[:, width + c :], rest_near[:, width + c :])
    right_far = exchange(right, "dp", groups, far)

    proj_total, out_total = pl.pallas_call(
        add_grads,
        out_shape=(
            jax.ShapeDtypeStruct((2, c, width), F32),
            jax.ShapeDtypeStruct((2, h, c), F32),
        ),
        in_specs=[vmem] * 6,
        out_specs=(vmem, vmem),
        compiler_params=params,
        name="add_grads",
    )(left, left_far, rest, rest_near, right, right_far)
    return pair_grad.reshape(pair_repr.shape), proj_total, out_total


def layer_norm(values, gain_vec, shift_vec, norm_axis):
    mean_value = jnp.mean(values, axis=norm_axis, keepdims=True)
    centred = values - mean_value
    variance = jnp.mean(centred * centred, axis=norm_axis, keepdims=True)
    return centred * lax.rsqrt(variance + NORM_EPSILON) * gain_vec + shift_vec


def norm_pullback(values, gain_vec, shift_vec, norm_axis, upstream):
    _, pull_back = jax.vjp(
        lambda inner_value: layer_norm(inner_value, gain_vec, shift_vec, norm_axis), values
    )
    return pull_back(upstream)[0]


def edge_pair(edge_pre, cell_mask):
    left_edge = jax.nn.sigmoid(edge_pre[1]) * edge_pre[0] * cell_mask
    right_edge = jax.nn.sigmoid(edge_pre[3]) * edge_pre[2] * cell_mask
    return jnp.stack([left_edge, right_edge]).astype(jnp.bfloat16)


def edge_pullback(edge_pre, cell_mask, grad_pair):
    sig_left = jax.nn.sigmoid(edge_pre[1])
    sig_right = jax.nn.sigmoid(edge_pre[3])
    grad_left = grad_pair[0].astype(jnp.float32) * cell_mask
    grad_right = grad_pair[1].astype(jnp.float32) * cell_mask
    return jnp.stack(
        [
            grad_left * sig_left,
            grad_left * edge_pre[0] * sig_left * (1.0 - sig_left),
            grad_right * sig_right,
            grad_right * edge_pre[2] * sig_right * (1.0 - sig_right),
        ]
    ).astype(jnp.bfloat16)


def triangle(pair_edges, outgoing):
    if outgoing:
        einsum_form = "cik,cjk->cij"
    else:
        einsum_form = "cki,ckj->cij"
    return jnp.einsum(
        einsum_form, pair_edges[0], pair_edges[1], preferred_element_type=jnp.float32
    ).astype(jnp.bfloat16)


def triangle_pullback(pair_edges, grad_product, outgoing):
    left_edge = pair_edges[0]
    right_edge = pair_edges[1]
    if outgoing:
        grad_left = jnp.einsum(
            "cij,cjk->cik", grad_product, right_edge, preferred_element_type=jnp.float32
        )
        grad_right = jnp.einsum(
            "cij,cik->cjk", grad_product, left_edge, preferred_element_type=jnp.float32
        )
    else:
        grad_left = jnp.einsum(
            "ckj,cij->cki", right_edge, grad_product, preferred_element_type=jnp.float32
        )
        grad_right = jnp.einsum(
            "cki,cij->ckj", left_edge, grad_product, preferred_element_type=jnp.float32
        )
    return jnp.stack([grad_left, grad_right]).astype(jnp.bfloat16)


def update_weights(proj_weight, proj_bias, norm_gain, norm_shift, update, channels, hidden):
    w_edge = proj_weight[update, :, : 4 * hidden].reshape(channels, 4, hidden)
    w_gate = proj_weight[update, :, 4 * hidden :]
    bias_edge = proj_bias[update, : 4 * hidden].reshape(4, hidden, 1, 1)
    bias_gate = proj_bias[update, 4 * hidden :]
    gain_in = norm_gain[update, :channels]
    shift_in = norm_shift[update, :channels]
    gain_out = norm_gain[update, channels:][:, None, None]
    shift_out = norm_shift[update, channels:][:, None, None]
    return (w_edge, w_gate, bias_edge, bias_gate, gain_in, shift_in, gain_out, shift_out)


def shards(
    pair_repr,
    pair_mask,
    cotangent,
    proj_weight,
    proj_bias,
    norm_gain,
    norm_shift,
    out_weight,
    out_bias,
):
    channels = pair_repr.shape[3]
    hidden = out_weight.shape[1]
    pair_state = pair_repr[0]
    cell_mask = pair_mask[0].astype(jnp.float32)
    records = []
    for update in range(2):
        w_edge, w_gate, bias_edge, bias_gate, gain_in, shift_in, gain_out, shift_out = (
            update_weights(proj_weight, proj_bias, norm_gain, norm_shift, update, channels, hidden)
        )
        state_f = pair_state.astype(jnp.float32)
        normed = layer_norm(state_f, gain_in, shift_in, -1).astype(jnp.bfloat16)
        edge_pre = (
            jnp.einsum("rnc,cgh->ghrn", normed, w_edge, preferred_element_type=jnp.float32)
            + bias_edge
        )
        gate_pre = (
            jnp.einsum("rnc,cd->rnd", normed, w_gate, preferred_element_type=jnp.float32)
            + bias_gate
        )
        pair_edges = edge_pair(edge_pre, cell_mask)
        spread = lax.all_to_all(pair_edges, "dap", split_axis=1, concat_axis=2, tiled=True)
        product = lax.all_to_all(
            triangle(spread, update == 0), "dap", split_axis=1, concat_axis=0, tiled=True
        )
        mixed_norm = layer_norm(product.astype(jnp.float32), gain_out, shift_out, 0).astype(
            jnp.bfloat16
        )
        branch = (
            jnp.einsum(
                "hrn,hd->rnd", mixed_norm, out_weight[update], preferred_element_type=jnp.float32
            )
            + out_bias[update]
        )
        records.append(
            (state_f, normed, edge_pre, gate_pre, pair_edges, spread, product, mixed_norm, branch)
        )
        pair_state = (state_f + jax.nn.sigmoid(gate_pre) * branch).astype(jnp.bfloat16)
    upstream = cotangent[0].astype(jnp.float32)
    proj_grads = []
    out_grads = []
    for update in (1, 0):
        state_f, normed, edge_pre, gate_pre, pair_edges, spread, product, mixed_norm, branch = (
            records[update]
        )
        w_edge, w_gate, bias_edge, bias_gate, gain_in, shift_in, gain_out, shift_out = (
            update_weights(proj_weight, proj_bias, norm_gain, norm_shift, update, channels, hidden)
        )
        gate_value = jax.nn.sigmoid(gate_pre)
        grad_branch = (upstream * gate_value).astype(jnp.bfloat16)
        grad_gate = (upstream * branch * gate_value * (1.0 - gate_value)).astype(jnp.bfloat16)
        out_grad = jnp.einsum(
            "hrn,rnd->hd", mixed_norm, grad_branch, preferred_element_type=jnp.float32
        )
        grad_mixed = jnp.einsum(
            "rnd,hd->hrn", grad_branch, out_weight[update], preferred_element_type=jnp.float32
        )
        grad_product = norm_pullback(
            product.astype(jnp.float32), gain_out, shift_out, 0, grad_mixed
        ).astype(jnp.bfloat16)
        column_edges = spread
        column_grad = lax.all_to_all(
            grad_product[None], "dap", split_axis=1, concat_axis=2, tiled=True
        )[0]
        grad_pair = lax.all_to_all(
            triangle_pullback(column_edges, column_grad, update == 0),
            "dap",
            split_axis=2,
            concat_axis=1,
            tiled=True,
        )
        grad_edge = edge_pullback(edge_pre, cell_mask, grad_pair)
        edge_grad = jnp.einsum(
            "rnc,ghrn->cgh", normed, grad_edge, preferred_element_type=jnp.float32
        ).reshape(channels, 4 * hidden)
        gate_grad = jnp.einsum("rnc,rnd->cd", normed, grad_gate, preferred_element_type=jnp.float32)
        grad_normed = jnp.einsum(
            "ghrn,cgh->rnc", grad_edge, w_edge, preferred_element_type=jnp.float32
        )
        grad_normed = grad_normed + jnp.einsum(
            "rnd,cd->rnc", grad_gate, w_gate, preferred_element_type=jnp.float32
        )
        upstream = upstream + norm_pullback(state_f, gain_in, shift_in, -1, grad_normed)
        proj_part = jnp.concatenate([edge_grad, gate_grad], axis=1)
        proj_grads.append(proj_part)
        out_grads.append(out_grad)
    proj_total = jnp.stack(proj_grads[::-1])
    out_total = jnp.stack(out_grads[::-1])
    proj_total, out_total = lax.psum((proj_total, out_total), ("dp", "dap"))
    return (upstream.astype(jnp.bfloat16)[None], proj_total, out_total)


def solution(mesh):
    placed = (
        P("dp", "dap", None, None),
        P("dp", "dap", None),
        P("dp", "dap", None, None),
        P(),
        P(),
        P(),
        P(),
        P(),
        P(),
    )
    groups, parts = mesh.shape["dp"], mesh.shape["dap"]

    def program(*args):
        n, c = args[0].shape[2:]
        rows = n // parts
        fits = 20 * n * n * c * 4 <= CROP_BUDGET
        paired = all(size >= 4 and size & (size - 1) == 0 for size in (groups, parts))
        even = args[7].shape[1] == c == 128 and STEP_ROWS % rows == 0 and n == STEP_ROWS
        body = functools.partial(crop_shards, groups, parts) if fits and even and paired else shards
        return spread_over(body)(*args)

    def spread_over(body):
        return jax.shard_map(
            body,
            mesh=mesh,
            in_specs=placed,
            out_specs=(P("dp", "dap", None, None), P(), P()),
            check_vma=False,
        )

    return program
```

```python
import functools

import jax
import jax.numpy as jnp
from jax import lax
from jax.experimental import pallas as pl
from jax.experimental.pallas import tpu as pltpu
from jax.sharding import PartitionSpec as P

NORM_EPSILON = 1e-05
VMEM_BYTES = 16 * 1024 * 1024
PREPARE_BYTES = 63 * 1024 * 1024
CROP_BUDGET = 32 * 1024 * 1024
BLOCK_ROWS = 8
STEP_ROWS = 32
KEPT = 10
TAIL_ROWS = 16
F32 = jnp.float32
BF16 = jnp.bfloat16


def sigmoid(x):
    return 0.5 * jnp.tanh(0.5 * x) + 0.5


def dot(a, b, dims=((1,), (0,))):
    return lax.dot_general(a, b, (dims, ((), ())), preferred_element_type=F32)


def norm_parts(x):
    x = x.astype(F32)
    centred = x - jnp.mean(x, axis=-1, keepdims=True)
    rstd = lax.rsqrt(jnp.mean(centred * centred, axis=-1, keepdims=True) + NORM_EPSILON)
    return centred * rstd, jnp.broadcast_to(rstd, x.shape)


def norm_vjp(x_hat, rstd, grad):
    mean_grad = jnp.mean(grad, axis=-1, keepdims=True)
    mean_prod = jnp.mean(grad * x_hat, axis=-1, keepdims=True)
    return rstd * (grad - mean_grad - x_hat * mean_prod)


def pair_mask_block(length, first_row, rows, n, lanes):
    shape = (rows, n, lanes)
    i = lax.broadcasted_iota(jnp.int32, shape, 0) + first_row
    j = lax.broadcasted_iota(jnp.int32, shape, 1)
    inside = jnp.where((i < length) & (j < length), 1.0, 0.0)
    return inside.reshape(rows * n, lanes)


def project(x, mask, w, b, gain, shift):
    x_hat, rstd = norm_parts(x)
    normed = (x_hat * gain + shift).astype(BF16)
    pre = dot(normed, w) + b
    h = (pre.shape[1] - x.shape[1]) // 4
    s_left = sigmoid(pre[:, h : 2 * h]) * mask
    s_right = sigmoid(pre[:, 3 * h : 4 * h]) * mask
    left = s_left * pre[:, :h]
    right = s_right * pre[:, 2 * h : 3 * h]
    gate = sigmoid(pre[:, 4 * h :])
    return x_hat, rstd, normed, s_left, s_right, left, right, gate


def mix(product, gain, shift, w_out, b_out):
    p_hat, p_rstd = norm_parts(product)
    mixed = (p_hat * gain + shift).astype(BF16)
    return p_hat, p_rstd, mixed, dot(mixed, w_out) + b_out


def unmix(up, gate, branch, p_hat, p_rstd, gain, w_out):
    d_branch = up * gate
    d_gate = (d_branch * branch * (1.0 - gate)).astype(BF16)
    d_branch = d_branch.astype(BF16)
    d_mixed = dot(d_branch, w_out, ((1,), (1,))) * gain
    return d_branch, d_gate, norm_vjp(p_hat, p_rstd, d_mixed)


def contract(n, first, x, y):
    lanes = y.shape[1]
    tiles = (n // 8, 8, lanes)

    def step(e, totals):
        block = y[pl.ds(pl.multiple_of(e * n, n), n), :].reshape(tiles)
        return tuple(
            totals[a] + x[pl.ds((first + a) * n + e, 8, stride=0), :][None] * block
            for a in range(BLOCK_ROWS)
        )

    zero = jnp.zeros(tiles, F32)
    totals = lax.fori_loop(0, n, step, (zero,) * BLOCK_ROWS, unroll=True)
    return jnp.stack(totals).reshape(BLOCK_ROWS * n, lanes)


def edge_grads(d_edge, slope, edge):
    grads = (d_edge * slope).astype(BF16), (d_edge * edge * (1.0 - slope)).astype(BF16)
    return jnp.concatenate(grads, axis=1)


def tail_values(block, lanes_from, lanes_to):
    lane = lax.broadcasted_iota(jnp.int32, block.shape, block.ndim - 1)
    inside = (lane >= lanes_from) & (lane < lanes_to)
    return jnp.max(jnp.where(inside, block.astype(F32), 0.0)).astype(jnp.int32)


def own_place(pair_ref):
    return tail_values(pair_ref[0, -TAIL_ROWS:, :], 64, 128)


def place_of(own, jump, side):
    return own ^ (2 * jump) ^ side


def block(t, rows, n):
    return pl.ds(pl.multiple_of(t * rows * n, rows * n), rows * n)


def forward(n, jumps, *refs):
    pairs, refs = refs[: len(jumps)], refs[len(jumps) :]
    (weights, vectors), refs = refs[:2], refs[2:]
    (edges_s, slopes_s, gate_s, hat_s, rstd_s) = refs[:5]
    (p_hat_s, p_rstd_s, branch_s, normed_s, mixed_s) = refs[5:KEPT]
    (next_s,) = refs[KEPT:]
    c = weights.shape[1]
    width = weights.shape[2] - c
    rows = n // (2 * len(jumps))
    cells = rows * n
    tails = jnp.stack([pair[:, cells:, :] for pair in pairs])
    length = tail_values(tails, 0, 64)
    own = own_place(pairs[0])
    for pair, jump in zip(pairs, jumps):
        for side in range(2):
            next_s[block(place_of(own, jump, side), rows, n), :] = pair[side, :cells, :]
    steps = n // STEP_ROWS

    @pl.loop(0, 2)
    def _(u):
        row = jnp.where(u == 0, vectors[0:1, :], vectors[1:2, :])
        bias, gains, shifts, bias_out = vector_parts(row, c, width)

        @pl.loop(0, steps)
        def _(t):
            first = t * STEP_ROWS
            here = block(t, STEP_ROWS, n)
            mask = pair_mask_block(length, first, STEP_ROWS, n, c)
            x_hat, rstd, normed, s_left, s_right, left, right, gate = project(
                next_s[here, :], mask, weights[u, :, :width], bias, gains[:, :c], shifts[:, :c]
            )
            edges_s[u, 0, here, :] = left
            edges_s[u, 1, here, :] = right
            for r in range(STEP_ROWS):
                swapped = pl.ds(first + r, n, stride=n)
                edges_s[u, 2, swapped, :] = right[r * n : (r + 1) * n]
                edges_s[u, 3, swapped, :] = left[r * n : (r + 1) * n]
            slopes_s[u, 0, here, :] = s_left
            slopes_s[u, 1, here, :] = s_right
            gate_s[u, here, :] = gate
            hat_s[u, here, :] = x_hat
            rstd_s[u, here, :] = rstd
            normed_s[u, here, :] = normed

        @pl.loop(0, steps)
        def _(t):
            here = block(t, STEP_ROWS, n)
            x, y = edges_s.at[u, 3 * u], edges_s.at[u, 2 - u]
            product = [
                contract(n, t * STEP_ROWS + r, x, y) for r in range(0, STEP_ROWS, BLOCK_ROWS)
            ]
            p_hat, p_rstd, mixed, branch = mix(
                jnp.concatenate(product).astype(BF16), gains[:, c:], shifts[:, c:], weights[u, :, width:], bias_out
            )
            p_hat_s[u, here, :] = p_hat
            p_rstd_s[u, here, :] = p_rstd
            mixed_s[u, here, :] = mixed
            branch_s[u, here, :] = branch
            x = next_s[here, :].astype(F32)
            next_s[here, :] = (x + gate_s[u, here, :] * branch).astype(BF16)


def kept_parts(refs, u):
    return [ref.at[u] for ref in refs[:KEPT]]


def store_swapped(ref, rows, n, first, values):
    for r in range(rows):
        ref[pl.ds(first + r, n, stride=n), :] = values[r * n : (r + 1) * n]


def backward_second(n, jumps, pair, *refs):
    parted, refs = refs[: len(jumps)], refs[len(jumps) :]
    weights, vectors = refs[:2]
    (edges_s, slopes_s, gate_s, hat_s, rstd_s, *kept) = kept_parts(refs[2:], 1)
    (p_hat_s, p_rstd_s, branch_s, normed_s, mixed_s) = kept
    up_ref, grads_ref, d_product_s, d_edges_s, d_pre_s, cot_s = refs[2 + KEPT :]
    c, h = weights.shape[1], edges_s.shape[2]
    width = 4 * h + c
    gain = vector_parts(vectors[1:2, :], c, width)[1]
    own = own_place(pair)
    for part, jump in zip(parted, jumps):
        for side in range(2):
            cot_s[block(place_of(own, jump, side), part.shape[1] // n, n), :] = part[side]

    @pl.loop(0, n // STEP_ROWS)
    def _(t):
        here = block(t, STEP_ROWS, n)
        d_branch, d_gate, d_product = unmix(
            cot_s[here, :].astype(F32),
            gate_s[here, :],
            branch_s[here, :],
            p_hat_s[here, :],
            p_rstd_s[here, :],
            gain[:, c:],
            weights[1, :, width:],
        )
        d_out = dot(mixed_s[here, :], d_branch, ((0,), (0,)))
        d_pre_s[here, 4 * h :] = d_gate
        d_product_s[1, here, :] = d_product
        store_swapped(d_product_s.at[0], STEP_ROWS, n, t * STEP_ROWS, d_product)
        grads_ref[:, width:] = d_out.astype(BF16)

    blocks = n // BLOCK_ROWS

    @pl.loop(0, 2 * blocks)
    def _(step):
        side, t = step // blocks, step % blocks
        d_edges_s[side, block(t, BLOCK_ROWS, n), :] = contract(
            n, t * BLOCK_ROWS, edges_s.at[1 - side], d_product_s.at[side]
        )

    @pl.loop(0, n // STEP_ROWS)
    def _(t):
        here = block(t, STEP_ROWS, n)
        grads = [
            edge_grads(d_edges_s[side, here, :], slopes_s[side, here, :], edges_s[side, here, :])
            for side in range(2)
        ]
        d_pre = jnp.concatenate([*grads, d_pre_s[here, 4 * h :]], axis=1)
        normed = normed_s[here, :]
        d_normed = dot(d_pre, weights[1, :, :width], ((1,), (1,))) * gain[:, :c]
        pulled = norm_vjp(hat_s[here, :], rstd_s[here, :], d_normed)
        up_ref[here, :] = cot_s[here, :].astype(F32) + pulled
        grads_ref[:, :width] = dot(normed, d_pre, ((0,), (0,))).astype(BF16)


def backward_left(n, up_in_ref, weights, vectors, *refs):
    (edges_s, slopes_s, gate_s, _, _, *kept) = kept_parts(refs, 0)
    (p_hat_s, p_rstd_s, branch_s, normed_s, mixed_s) = kept
    d_pre_ref, d_product_t_ref, grads_ref, d_product_s, d_edge_s = refs[KEPT:]
    c, h = weights.shape[1], edges_s.shape[2]
    width = 4 * h + c
    gain = vector_parts(vectors[0:1, :], c, width)[1]

    @pl.loop(0, n // STEP_ROWS)
    def _(t):
        here = block(t, STEP_ROWS, n)
        d_branch, d_gate, d_product = unmix(
            up_in_ref[here, :],
            gate_s[here, :],
            branch_s[here, :],
            p_hat_s[here, :],
            p_rstd_s[here, :],
            gain[:, c:],
            weights[0, :, width:],
        )
        d_out = dot(mixed_s[here, :], d_branch, ((0,), (0,)))
        d_pre_ref[here, 2 * h :] = d_gate
        d_product_s[here, :] = d_product
        store_swapped(d_product_t_ref, STEP_ROWS, n, t * STEP_ROWS, d_product)
        grads_ref[:, 2 * h + c :] = d_out.astype(BF16)

    one_side(n, 0, d_product_s, edges_s, slopes_s, d_edge_s, d_pre_ref)
    d_pre = dot(normed_s[...], d_pre_ref[...], ((0,), (0,)))
    grads_ref[:, : 2 * h + c] = d_pre.astype(BF16)


def backward_right(n, d_product_t_ref, *refs):
    (edges_s, slopes_s, *kept) = kept_parts(refs, 0)
    normed_s = kept[-2]
    d_pre_ref, grads_ref, d_edge_s = refs[KEPT:]
    one_side(n, 1, d_product_t_ref, edges_s, slopes_s, d_edge_s, d_pre_ref)
    grads_ref[...] = dot(normed_s[...], d_pre_ref[...], ((0,), (0,))).astype(BF16)


def one_side(n, side, x, edges_s, slopes_s, d_edge_s, d_pre_ref):
    h = edges_s.shape[2]

    @pl.loop(0, n // BLOCK_ROWS)
    def _(t):
        d_edge_s[block(t, BLOCK_ROWS, n), :] = contract(
            n, t * BLOCK_ROWS, x, edges_s.at[1 - side]
        )

    @pl.loop(0, n // STEP_ROWS)
    def _(t):
        here = block(t, STEP_ROWS, n)
        d_pre_ref[here, : 2 * h] = edge_grads(
            d_edge_s[here, :], slopes_s[side, here, :], edges_s[side, here, :]
        )


def own_rows(
    pair_ref, up_ref, d_left_ref, d_right_ref, weights, vectors, hat_ref, rstd_ref, out_ref
):
    cells, c = out_ref.shape
    half = d_right_ref.shape[1]
    place = own_place(pair_ref)
    own = pl.ds(pl.multiple_of(place * cells, cells), cells)
    width = d_left_ref.shape[1] + half
    gain = vector_parts(vectors[0:1, :], c, width)[1]
    d_left, d_right = d_left_ref[own, :], d_right_ref[own, :]
    d_pre = jnp.concatenate([d_left[:, :half], d_right, d_left[:, half:]], axis=1)
    d_normed = dot(d_pre, weights[0, :, :width], ((1,), (1,))) * gain[:, :c]
    pulled = norm_vjp(hat_ref[0, own, :], rstd_ref[0, own, :], d_normed)
    out_ref[...] = (up_ref[own, :] + pulled).astype(BF16)


def exchange(value, axis, size, step):
    return lax.ppermute(value, axis, [(d, d ^ step) for d in range(size)])


def near_rounds(value, groups):
    other = exchange(value, "dp", groups, 1)
    step = 2
    while step < groups // 2:
        value = add_narrow(value, other)
        other = exchange(value, "dp", groups, step)
        step *= 2
    return value, other


def add_narrow(a, b):
    return (a.astype(F32) + b.astype(F32)).astype(BF16)


def prepare(
    index_ref, mask_ref, state_ref, cot_ref, w, w_out, b, gain, shift, b_out, *refs
):
    sent_ref, weights_ref, vectors_ref, mask_s, sems = refs
    cells, c = state_ref.shape
    below, width = cells + TAIL_ROWS, w.shape[2]
    copies = [(mask_ref, mask_s), (state_ref, sent_ref.at[:cells]), (cot_ref, sent_ref.at[below:])]
    copies += [(w, weights_ref.at[:, :, :width]), (w_out, weights_ref.at[:, :, width:])]
    first = 0
    for vector in (b, gain, shift, b_out):
        last = first + vector.shape[1]
        copies.append((vector, vectors_ref.at[:, first:last]))
        first = last
    copies = [pltpu.make_async_copy(*pair, sems.at[k]) for k, pair in enumerate(copies)]
    for copy in copies:
        copy.start()
    copies[0].wait()
    length = jnp.max(jnp.sum(mask_s[...].astype(F32), axis=1, keepdims=True))
    in_length = lax.broadcasted_iota(jnp.int32, (TAIL_ROWS, c), 1) < 64
    place = index_ref[0].astype(F32)
    sent_ref[cells:below, :] = jnp.where(in_length, length, place).astype(BF16)
    for copy in copies[1:]:
        copy.wait()


def pair_up(near_ref, far_ref, state_ref, cot_ref):
    split = state_ref.shape[1]
    for side, ref in enumerate((near_ref, far_ref)):
        state_ref[side] = ref[:split, :]
        cot_ref[side] = ref[split:, :]


def hold(weights_in, vectors_in, weights_out, vectors_out):
    weights_out[...] = weights_in[...]
    vectors_out[...] = vectors_in[...]


def vector_parts(row, c, width):
    ends = [width, width + 2 * c, width + 4 * c, width + 5 * c]
    return [row[:, first:last] for first, last in zip([0] + ends, ends)]


def add_grads(rest, rest_near, left, left_near, right, right_far, proj_ref, out_ref):
    width = proj_ref.shape[2]
    c = out_ref.shape[2]
    half = (width - c) // 2
    total = rest[:, : width + c].astype(F32) + rest_near[:, : width + c].astype(F32)
    proj_ref[1] = total[:, :width]
    out_ref[1] = total[:, width:]
    total = left[...].astype(F32) + left_near[...].astype(F32)
    proj_ref[0, :, :half] = total[:, :half]
    proj_ref[0, :, 2 * half :] = total[:, half : half + c]
    out_ref[0] = total[:, half + c :]
    proj_ref[0, :, half : 2 * half] = right[...].astype(F32) + right_far[...].astype(F32)


def crop_shards(
    groups,
    parts,
    pair_repr,
    pair_mask,
    cotangent,
    proj_weight,
    proj_bias,
    norm_gain,
    norm_shift,
    out_weight,
    out_bias,
):
    _, rows, n, c = pair_repr.shape
    h = out_weight.shape[1]
    width = proj_weight.shape[2]
    cells, pairs = rows * n, n * n
    plane = (pairs + 8, h)
    kept = [jax.ShapeDtypeStruct((2, 4) + plane, F32), jax.ShapeDtypeStruct((2, 2) + plane, F32)]
    kept += [jax.ShapeDtypeStruct((2,) + plane, F32)] * 6
    kept += [jax.ShapeDtypeStruct((2, pairs, h), BF16)] * 2
    grads = jax.ShapeDtypeStruct((c, width + c), BF16)
    vmem = pl.BlockSpec(memory_space=pltpu.VMEM)
    main = pl.BlockSpec(memory_space=pltpu.HBM)
    params = pltpu.CompilerParams(vmem_limit_bytes=VMEM_BYTES)

    def cost(planes):
        flops = 4 * pairs * width * c
        return pl.CostEstimate(
            flops=flops, bytes_accessed=planes * pairs * c * 4, transcendentals=0
        )

    packed = (
        jax.ShapeDtypeStruct((2, c, width + c), BF16),
        jax.ShapeDtypeStruct((2, width + 5 * c), F32),
    )
    sent, *weights = pl.pallas_call(
        prepare,
        out_shape=(jax.ShapeDtypeStruct((2 * cells + TAIL_ROWS, c), BF16),) + packed,
        in_specs=[pl.BlockSpec(memory_space=pltpu.SMEM)] + [main] * 9,
        out_specs=[vmem] * 3,
        scratch_shapes=[pltpu.VMEM((rows, n), jnp.int32), pltpu.SemaphoreType.DMA((9,))],
        compiler_params=pltpu.CompilerParams(vmem_limit_bytes=PREPARE_BYTES),
        name="prepare",
    )(
        lax.axis_index("dap").astype(jnp.int32)[None],
        pair_mask[0],
        pair_repr.reshape(cells, c),
        cotangent.reshape(cells, c),
        proj_weight,
        out_weight,
        proj_bias,
        norm_gain,
        norm_shift,
        out_bias,
    )
    weights = pl.pallas_call(
        hold,
        out_shape=packed,
        in_specs=[vmem] * 2,
        out_specs=[vmem] * 2,
        compiler_params=params,
        cost_estimate=cost(8),
        name="hold",
    )(*weights)
    beside = exchange(sent, "dap", parts, 1)
    beside, *weights = lax.optimization_barrier((beside, *weights))
    state, cot = pl.pallas_call(
        pair_up,
        out_shape=(
            jax.ShapeDtypeStruct((2, cells + TAIL_ROWS, c), BF16),
            jax.ShapeDtypeStruct((2, cells, c), BF16),
        ),
        in_specs=[vmem] * 2,
        out_specs=[vmem] * 2,
        compiler_params=params,
        name="pair_up",
    )(sent, beside)
    states, cots = [state], [cot]
    half = parts // 2
    jumps = [0, *range(1, half // 2), *reversed(range(half // 2, half))]
    for group in (states, cots):
        group += [exchange(group[0], "dap", parts, 2 * jump) for jump in jumps[1:]]

    held = pl.pallas_call(
        functools.partial(forward, n, jumps),
        out_shape=kept,
        in_specs=[vmem] * (half + 2),
        out_specs=(vmem,) * KEPT,
        scratch_shapes=[pltpu.VMEM((pairs, c), BF16)],
        compiler_params=params,
        cost_estimate=cost(64),
        name="forward",
    )(*states, *weights)

    double, single = pltpu.VMEM((2,) + plane, F32), pltpu.VMEM(plane, F32)
    up_1, grads_1 = pl.pallas_call(
        functools.partial(backward_second, n, jumps),
        out_shape=(jax.ShapeDtypeStruct((pairs, c), F32), grads),
        in_specs=[vmem] * (3 + half + KEPT),
        out_specs=(vmem, vmem),
        scratch_shapes=[
            double,
            double,
            pltpu.VMEM((pairs, width), BF16),
            pltpu.VMEM((pairs, c), BF16),
        ],
        compiler_params=params,
        cost_estimate=cost(48),
        name="backward_second",
    )(states[0], *cots, *weights, *held)
    far = groups // 2
    others_1 = exchange(grads_1, "dp", groups, far)

    d_left, d_product_t, grads_left = pl.pallas_call(
        functools.partial(backward_left, n),
        out_shape=(
            jax.ShapeDtypeStruct((pairs, 2 * h + c), BF16),
            jax.ShapeDtypeStruct(plane, F32),
            jax.ShapeDtypeStruct((c, 2 * h + 2 * c), BF16),
        ),
        in_specs=[vmem] * (3 + KEPT),
        out_specs=[vmem] * 3,
        scratch_shapes=[single, single],
        compiler_params=params,
        cost_estimate=cost(24),
        name="backward_left",
    )(up_1, *weights, *held)
    others_left = exchange(grads_left, "dp", groups, far)

    d_right, grads_right = pl.pallas_call(
        functools.partial(backward_right, n),
        out_shape=(
            jax.ShapeDtypeStruct((pairs, 2 * h), BF16),
            jax.ShapeDtypeStruct((c, 2 * h), BF16),
        ),
        in_specs=[vmem] * (1 + KEPT),
        out_specs=[vmem] * 2,
        scratch_shapes=[single],
        compiler_params=params,
        cost_estimate=cost(24),
        name="backward_right",
    )(d_product_t, *held)
    pair_grad = pl.pallas_call(
        own_rows,
        out_shape=jax.ShapeDtypeStruct((cells, c), BF16),
        in_specs=[vmem] * 8,
        out_specs=vmem,
        compiler_params=params,
        cost_estimate=cost(8),
        name="own_rows",
    )(states[0], up_1, d_left, d_right, *weights, held[3], held[4])

    rest, rest_near = near_rounds(
        jnp.concatenate([add_narrow(grads_1, others_1), grads_right], axis=1), groups
    )
    right = add_narrow(rest[:, width + c :], rest_near[:, width + c :])
    right_far = exchange(right, "dp", groups, far)
    _, others_left = lax.optimization_barrier((right, others_left))
    ends_left = near_rounds(add_narrow(grads_left, others_left), groups)

    proj_total, out_total = pl.pallas_call(
        add_grads,
        out_shape=(
            jax.ShapeDtypeStruct((2, c, width), F32),
            jax.ShapeDtypeStruct((2, h, c), F32),
        ),
        in_specs=[vmem] * 6,
        out_specs=(vmem, vmem),
        compiler_params=params,
        name="add_grads",
    )(rest, rest_near, *ends_left, right, right_far)
    return pair_grad.reshape(pair_repr.shape), proj_total, out_total


def layer_norm(values, gain_vec, shift_vec, norm_axis):
    mean_value = jnp.mean(values, axis=norm_axis, keepdims=True)
    centred = values - mean_value
    variance = jnp.mean(centred * centred, axis=norm_axis, keepdims=True)
    return centred * lax.rsqrt(variance + NORM_EPSILON) * gain_vec + shift_vec


def norm_pullback(values, gain_vec, shift_vec, norm_axis, upstream):
    _, pull_back = jax.vjp(
        lambda inner_value: layer_norm(inner_value, gain_vec, shift_vec, norm_axis), values
    )
    return pull_back(upstream)[0]


def edge_pair(edge_pre, cell_mask):
    left_edge = jax.nn.sigmoid(edge_pre[1]) * edge_pre[0] * cell_mask
    right_edge = jax.nn.sigmoid(edge_pre[3]) * edge_pre[2] * cell_mask
    return jnp.stack([left_edge, right_edge]).astype(jnp.bfloat16)


def edge_pullback(edge_pre, cell_mask, grad_pair):
    sig_left = jax.nn.sigmoid(edge_pre[1])
    sig_right = jax.nn.sigmoid(edge_pre[3])
    grad_left = grad_pair[0].astype(jnp.float32) * cell_mask
    grad_right = grad_pair[1].astype(jnp.float32) * cell_mask
    return jnp.stack(
        [
            grad_left * sig_left,
            grad_left * edge_pre[0] * sig_left * (1.0 - sig_left),
            grad_right * sig_right,
            grad_right * edge_pre[2] * sig_right * (1.0 - sig_right),
        ]
    ).astype(jnp.bfloat16)


def triangle(pair_edges, outgoing):
    if outgoing:
        einsum_form = "cik,cjk->cij"
    else:
        einsum_form = "cki,ckj->cij"
    return jnp.einsum(
        einsum_form, pair_edges[0], pair_edges[1], preferred_element_type=jnp.float32
    ).astype(jnp.bfloat16)


def triangle_pullback(pair_edges, grad_product, outgoing):
    left_edge = pair_edges[0]
    right_edge = pair_edges[1]
    if outgoing:
        grad_left = jnp.einsum(
            "cij,cjk->cik", grad_product, right_edge, preferred_element_type=jnp.float32
        )
        grad_right = jnp.einsum(
            "cij,cik->cjk", grad_product, left_edge, preferred_element_type=jnp.float32
        )
    else:
        grad_left = jnp.einsum(
            "ckj,cij->cki", right_edge, grad_product, preferred_element_type=jnp.float32
        )
        grad_right = jnp.einsum(
            "cki,cij->ckj", left_edge, grad_product, preferred_element_type=jnp.float32
        )
    return jnp.stack([grad_left, grad_right]).astype(jnp.bfloat16)


def update_weights(proj_weight, proj_bias, norm_gain, norm_shift, update, channels, hidden):
    w_edge = proj_weight[update, :, : 4 * hidden].reshape(channels, 4, hidden)
    w_gate = proj_weight[update, :, 4 * hidden :]
    bias_edge = proj_bias[update, : 4 * hidden].reshape(4, hidden, 1, 1)
    bias_gate = proj_bias[update, 4 * hidden :]
    gain_in = norm_gain[update, :channels]
    shift_in = norm_shift[update, :channels]
    gain_out = norm_gain[update, channels:][:, None, None]
    shift_out = norm_shift[update, channels:][:, None, None]
    return (w_edge, w_gate, bias_edge, bias_gate, gain_in, shift_in, gain_out, shift_out)


def shards(
    pair_repr,
    pair_mask,
    cotangent,
    proj_weight,
    proj_bias,
    norm_gain,
    norm_shift,
    out_weight,
    out_bias,
):
    channels = pair_repr.shape[3]
    hidden = out_weight.shape[1]
    pair_state = pair_repr[0]
    cell_mask = pair_mask[0].astype(jnp.float32)
    records = []
    for update in range(2):
        w_edge, w_gate, bias_edge, bias_gate, gain_in, shift_in, gain_out, shift_out = (
            update_weights(proj_weight, proj_bias, norm_gain, norm_shift, update, channels, hidden)
        )
        state_f = pair_state.astype(jnp.float32)
        normed = layer_norm(state_f, gain_in, shift_in, -1).astype(jnp.bfloat16)
        edge_pre = (
            jnp.einsum("rnc,cgh->ghrn", normed, w_edge, preferred_element_type=jnp.float32)
            + bias_edge
        )
        gate_pre = (
            jnp.einsum("rnc,cd->rnd", normed, w_gate, preferred_element_type=jnp.float32)
            + bias_gate
        )
        pair_edges = edge_pair(edge_pre, cell_mask)
        spread = lax.all_to_all(pair_edges, "dap", split_axis=1, concat_axis=2, tiled=True)
        product = lax.all_to_all(
            triangle(spread, update == 0), "dap", split_axis=1, concat_axis=0, tiled=True
        )
        mixed_norm = layer_norm(product.astype(jnp.float32), gain_out, shift_out, 0).astype(
            jnp.bfloat16
        )
        branch = (
            jnp.einsum(
                "hrn,hd->rnd", mixed_norm, out_weight[update], preferred_element_type=jnp.float32
            )
            + out_bias[update]
        )
        records.append(
            (state_f, normed, edge_pre, gate_pre, pair_edges, spread, product, mixed_norm, branch)
        )
        pair_state = (state_f + jax.nn.sigmoid(gate_pre) * branch).astype(jnp.bfloat16)
    upstream = cotangent[0].astype(jnp.float32)
    proj_grads = []
    out_grads = []
    for update in (1, 0):
        state_f, normed, edge_pre, gate_pre, pair_edges, spread, product, mixed_norm, branch = (
            records[update]
        )
        w_edge, w_gate, bias_edge, bias_gate, gain_in, shift_in, gain_out, shift_out = (
            update_weights(proj_weight, proj_bias, norm_gain, norm_shift, update, channels, hidden)
        )
        gate_value = jax.nn.sigmoid(gate_pre)
        grad_branch = (upstream * gate_value).astype(jnp.bfloat16)
        grad_gate = (upstream * branch * gate_value * (1.0 - gate_value)).astype(jnp.bfloat16)
        out_grad = jnp.einsum(
            "hrn,rnd->hd", mixed_norm, grad_branch, preferred_element_type=jnp.float32
        )
        grad_mixed = jnp.einsum(
            "rnd,hd->hrn", grad_branch, out_weight[update], preferred_element_type=jnp.float32
        )
        grad_product = norm_pullback(
            product.astype(jnp.float32), gain_out, shift_out, 0, grad_mixed
        ).astype(jnp.bfloat16)
        column_edges = spread
        column_grad = lax.all_to_all(
            grad_product[None], "dap", split_axis=1, concat_axis=2, tiled=True
        )[0]
        grad_pair = lax.all_to_all(
            triangle_pullback(column_edges, column_grad, update == 0),
            "dap",
            split_axis=2,
            concat_axis=1,
            tiled=True,
        )
        grad_edge = edge_pullback(edge_pre, cell_mask, grad_pair)
        edge_grad = jnp.einsum(
            "rnc,ghrn->cgh", normed, grad_edge, preferred_element_type=jnp.float32
        ).reshape(channels, 4 * hidden)
        gate_grad = jnp.einsum("rnc,rnd->cd", normed, grad_gate, preferred_element_type=jnp.float32)
        grad_normed = jnp.einsum(
            "ghrn,cgh->rnc", grad_edge, w_edge, preferred_element_type=jnp.float32
        )
        grad_normed = grad_normed + jnp.einsum(
            "rnd,cd->rnc", grad_gate, w_gate, preferred_element_type=jnp.float32
        )
        upstream = upstream + norm_pullback(state_f, gain_in, shift_in, -1, grad_normed)
        proj_part = jnp.concatenate([edge_grad, gate_grad], axis=1)
        proj_grads.append(proj_part)
        out_grads.append(out_grad)
    proj_total = jnp.stack(proj_grads[::-1])
    out_total = jnp.stack(out_grads[::-1])
    proj_total, out_total = lax.psum((proj_total, out_total), ("dp", "dap"))
    return (upstream.astype(jnp.bfloat16)[None], proj_total, out_total)


def solution(mesh):
    placed = (
        P("dp", "dap", None, None),
        P("dp", "dap", None),
        P("dp", "dap", None, None),
        P(),
        P(),
        P(),
        P(),
        P(),
        P(),
    )
    groups, parts = mesh.shape["dp"], mesh.shape["dap"]

    def program(*args):
        n, c = args[0].shape[2:]
        rows = n // parts
        fits = 20 * n * n * c * 4 <= CROP_BUDGET
        paired = all(size >= 4 and size & (size - 1) == 0 for size in (groups, parts))
        even = args[7].shape[1] == c == 128 and STEP_ROWS % rows == 0 and n == STEP_ROWS
        body = functools.partial(crop_shards, groups, parts) if fits and even and paired else shards
        return spread_over(body)(*args)

    def spread_over(body):
        return jax.shard_map(
            body,
            mesh=mesh,
            in_specs=placed,
            out_specs=(P("dp", "dap", None, None), P(), P()),
            check_vma=False,
        )

    return program
```

```python
import functools

import jax
import jax.numpy as jnp
from jax import lax
from jax.experimental import pallas as pl
from jax.experimental.pallas import tpu as pltpu
from jax.sharding import PartitionSpec as P

NORM_EPSILON = 1e-05
VMEM_BYTES = 16 * 1024 * 1024
PREPARE_BYTES = 63 * 1024 * 1024
CROP_BUDGET = 32 * 1024 * 1024
BLOCK_ROWS = 8
STEP_ROWS = 32
KEPT = 10
TAIL_ROWS = 16
F32 = jnp.float32
BF16 = jnp.bfloat16


def sigmoid(x):
    return 0.5 * jnp.tanh(0.5 * x) + 0.5


def dot(a, b, dims=((1,), (0,))):
    return lax.dot_general(a, b, (dims, ((), ())), preferred_element_type=F32)


def norm_parts(x):
    x = x.astype(F32)
    centred = x - jnp.mean(x, axis=-1, keepdims=True)
    rstd = lax.rsqrt(jnp.mean(centred * centred, axis=-1, keepdims=True) + NORM_EPSILON)
    return centred * rstd, jnp.broadcast_to(rstd, x.shape)


def norm_vjp(x_hat, rstd, grad):
    mean_grad = jnp.mean(grad, axis=-1, keepdims=True)
    mean_prod = jnp.mean(grad * x_hat, axis=-1, keepdims=True)
    return rstd * (grad - mean_grad - x_hat * mean_prod)


def pair_mask_block(length, first_row, rows, n, lanes):
    shape = (rows, n, lanes)
    i = lax.broadcasted_iota(jnp.int32, shape, 0) + first_row
    j = lax.broadcasted_iota(jnp.int32, shape, 1)
    inside = jnp.where((i < length) & (j < length), 1.0, 0.0)
    return inside.reshape(rows * n, lanes)


def project(x, mask, w, b, gain, shift):
    x_hat, rstd = norm_parts(x)
    normed = (x_hat * gain + shift).astype(BF16)
    pre = dot(normed, w) + b
    h = (pre.shape[1] - x.shape[1]) // 4
    s_left = sigmoid(pre[:, h : 2 * h]) * mask
    s_right = sigmoid(pre[:, 3 * h : 4 * h]) * mask
    left = s_left * pre[:, :h]
    right = s_right * pre[:, 2 * h : 3 * h]
    gate = sigmoid(pre[:, 4 * h :])
    return x_hat, rstd, normed, s_left, s_right, left, right, gate


def mix(product, gain, shift, w_out, b_out):
    p_hat, p_rstd = norm_parts(product)
    mixed = (p_hat * gain + shift).astype(BF16)
    return p_hat, p_rstd, mixed, dot(mixed, w_out) + b_out


def unmix(up, gate, branch, p_hat, p_rstd, gain, w_out):
    d_branch = up * gate
    d_gate = (d_branch * branch * (1.0 - gate)).astype(BF16)
    d_branch = d_branch.astype(BF16)
    d_mixed = dot(d_branch, w_out, ((1,), (1,))) * gain
    return d_branch, d_gate, norm_vjp(p_hat, p_rstd, d_mixed)


def contract(n, first, x, y):
    lanes = y.shape[1]
    tiles = (n // 8, 8, lanes)

    def step(e, totals):
        block = y[pl.ds(pl.multiple_of(e * n, n), n), :].reshape(tiles)
        return tuple(
            totals[a] + x[pl.ds((first + a) * n + e, 8, stride=0), :][None] * block
            for a in range(BLOCK_ROWS)
        )

    zero = jnp.zeros(tiles, F32)
    totals = lax.fori_loop(0, n, step, (zero,) * BLOCK_ROWS, unroll=True)
    return jnp.stack(totals).reshape(BLOCK_ROWS * n, lanes)


def edge_grads(d_edge, slope, edge):
    grads = (d_edge * slope).astype(BF16), (d_edge * edge * (1.0 - slope)).astype(BF16)
    return jnp.concatenate(grads, axis=1)


def tail_values(block, lanes_from, lanes_to):
    lane = lax.broadcasted_iota(jnp.int32, block.shape, block.ndim - 1)
    inside = (lane >= lanes_from) & (lane < lanes_to)
    return jnp.max(jnp.where(inside, block.astype(F32), 0.0)).astype(jnp.int32)


def own_place(pair_ref):
    return tail_values(pair_ref[0, -TAIL_ROWS:, :], 64, 128)


def place_of(own, jump, side):
    return own ^ (2 * jump) ^ side


def block(t, rows, n):
    return pl.ds(pl.multiple_of(t * rows * n, rows * n), rows * n)


def forward(n, jumps, *refs):
    pairs, refs = refs[: len(jumps)], refs[len(jumps) :]
    (weights, vectors), refs = refs[:2], refs[2:]
    (edges_s, slopes_s, gate_s, hat_s, rstd_s) = refs[:5]
    (p_hat_s, p_rstd_s, branch_s, normed_s, mixed_s) = refs[5:KEPT]
    (next_s,) = refs[KEPT:]
    c = weights.shape[1]
    width = weights.shape[2] - c
    rows = n // (2 * len(jumps))
    cells = rows * n
    tails = jnp.stack([pair[:, cells:, :] for pair in pairs])
    length = tail_values(tails, 0, 64)
    own = own_place(pairs[0])
    for pair, jump in zip(pairs, jumps):
        for side in range(2):
            next_s[block(place_of(own, jump, side), rows, n), :] = pair[side, :cells, :]
    steps = n // STEP_ROWS

    @pl.loop(0, 2)
    def _(u):
        row = jnp.where(u == 0, vectors[0:1, :], vectors[1:2, :])
        bias, gains, shifts, bias_out = vector_parts(row, c, width)

        @pl.loop(0, steps)
        def _(t):
            first = t * STEP_ROWS
            here = block(t, STEP_ROWS, n)
            mask = pair_mask_block(length, first, STEP_ROWS, n, c)
            x_hat, rstd, normed, s_left, s_right, left, right, gate = project(
                next_s[here, :], mask, weights[u, :, :width], bias, gains[:, :c], shifts[:, :c]
            )
            edges_s[u, 0, here, :] = left
            edges_s[u, 1, here, :] = right
            for r in range(STEP_ROWS):
                swapped = pl.ds(first + r, n, stride=n)
                edges_s[u, 2, swapped, :] = right[r * n : (r + 1) * n]
                edges_s[u, 3, swapped, :] = left[r * n : (r + 1) * n]
            slopes_s[u, 0, here, :] = s_left
            slopes_s[u, 1, here, :] = s_right
            gate_s[u, here, :] = gate
            hat_s[u, here, :] = x_hat
            rstd_s[u, here, :] = rstd
            normed_s[u, here, :] = normed

        @pl.loop(0, steps)
        def _(t):
            here = block(t, STEP_ROWS, n)
            x, y = edges_s.at[u, 3 * u], edges_s.at[u, 2 - u]
            product = [
                contract(n, t * STEP_ROWS + r, x, y) for r in range(0, STEP_ROWS, BLOCK_ROWS)
            ]
            p_hat, p_rstd, mixed, branch = mix(
                jnp.concatenate(product).astype(BF16), gains[:, c:], shifts[:, c:], weights[u, :, width:], bias_out
            )
            p_hat_s[u, here, :] = p_hat
            p_rstd_s[u, here, :] = p_rstd
            mixed_s[u, here, :] = mixed
            branch_s[u, here, :] = branch
            x = next_s[here, :].astype(F32)
            next_s[here, :] = (x + gate_s[u, here, :] * branch).astype(BF16)


def kept_parts(refs, u):
    return [ref.at[u] for ref in refs[:KEPT]]


def store_swapped(ref, rows, n, first, values):
    for r in range(rows):
        ref[pl.ds(first + r, n, stride=n), :] = values[r * n : (r + 1) * n]


def backward_second(n, jumps, pair, *refs):
    parted, refs = refs[: len(jumps)], refs[len(jumps) :]
    weights, vectors = refs[:2]
    (edges_s, slopes_s, gate_s, hat_s, rstd_s, *kept) = kept_parts(refs[2:], 1)
    (p_hat_s, p_rstd_s, branch_s, normed_s, mixed_s) = kept
    up_ref, grads_ref, d_product_s, d_edges_s, d_pre_s, cot_s = refs[2 + KEPT :]
    c, h = weights.shape[1], edges_s.shape[2]
    width = 4 * h + c
    gain = vector_parts(vectors[1:2, :], c, width)[1]
    own = own_place(pair)
    for part, jump in zip(parted, jumps):
        for side in range(2):
            cot_s[block(place_of(own, jump, side), part.shape[1] // n, n), :] = part[side]

    @pl.loop(0, n // STEP_ROWS)
    def _(t):
        here = block(t, STEP_ROWS, n)
        d_branch, d_gate, d_product = unmix(
            cot_s[here, :].astype(F32),
            gate_s[here, :],
            branch_s[here, :],
            p_hat_s[here, :],
            p_rstd_s[here, :],
            gain[:, c:],
            weights[1, :, width:],
        )
        d_out = dot(mixed_s[here, :], d_branch, ((0,), (0,)))
        d_pre_s[here, 4 * h :] = d_gate
        d_product_s[1, here, :] = d_product
        store_swapped(d_product_s.at[0], STEP_ROWS, n, t * STEP_ROWS, d_product)
        grads_ref[:, width:] = d_out.astype(BF16)

    blocks = n // BLOCK_ROWS

    @pl.loop(0, 2 * blocks)
    def _(step):
        side, t = step // blocks, step % blocks
        d_edges_s[side, block(t, BLOCK_ROWS, n), :] = contract(
            n, t * BLOCK_ROWS, edges_s.at[1 - side], d_product_s.at[side]
        )

    @pl.loop(0, n // STEP_ROWS)
    def _(t):
        here = block(t, STEP_ROWS, n)
        grads = [
            edge_grads(d_edges_s[side, here, :], slopes_s[side, here, :], edges_s[side, here, :])
            for side in range(2)
        ]
        d_pre = jnp.concatenate([*grads, d_pre_s[here, 4 * h :]], axis=1)
        normed = normed_s[here, :]
        d_normed = dot(d_pre, weights[1, :, :width], ((1,), (1,))) * gain[:, :c]
        pulled = norm_vjp(hat_s[here, :], rstd_s[here, :], d_normed)
        up_ref[here, :] = cot_s[here, :].astype(F32) + pulled
        grads_ref[:, :width] = dot(normed, d_pre, ((0,), (0,))).astype(BF16)


def backward_left(n, up_in_ref, weights, vectors, *refs):
    (edges_s, slopes_s, gate_s, _, _, *kept) = kept_parts(refs, 0)
    (p_hat_s, p_rstd_s, branch_s, normed_s, mixed_s) = kept
    d_pre_ref, d_product_t_ref, grads_ref, d_product_s, d_edge_s = refs[KEPT:]
    c, h = weights.shape[1], edges_s.shape[2]
    width = 4 * h + c
    gain = vector_parts(vectors[0:1, :], c, width)[1]

    @pl.loop(0, n // STEP_ROWS)
    def _(t):
        here = block(t, STEP_ROWS, n)
        d_branch, d_gate, d_product = unmix(
            up_in_ref[here, :],
            gate_s[here, :],
            branch_s[here, :],
            p_hat_s[here, :],
            p_rstd_s[here, :],
            gain[:, c:],
            weights[0, :, width:],
        )
        d_out = dot(mixed_s[here, :], d_branch, ((0,), (0,)))
        d_pre_ref[here, 2 * h :] = d_gate
        d_product_s[here, :] = d_product
        store_swapped(d_product_t_ref, STEP_ROWS, n, t * STEP_ROWS, d_product)
        grads_ref[:, 2 * h + c :] = d_out.astype(BF16)

    one_side(n, 0, d_product_s, edges_s, slopes_s, d_edge_s, d_pre_ref)
    d_pre = dot(normed_s[...], d_pre_ref[...], ((0,), (0,)))
    grads_ref[:, : 2 * h + c] = d_pre.astype(BF16)


def backward_right(n, d_product_t_ref, *refs):
    (edges_s, slopes_s, *kept) = kept_parts(refs, 0)
    normed_s = kept[-2]
    d_pre_ref, grads_ref, d_edge_s = refs[KEPT:]
    one_side(n, 1, d_product_t_ref, edges_s, slopes_s, d_edge_s, d_pre_ref)
    grads_ref[...] = dot(normed_s[...], d_pre_ref[...], ((0,), (0,))).astype(BF16)


def one_side(n, side, x, edges_s, slopes_s, d_edge_s, d_pre_ref):
    h = edges_s.shape[2]

    @pl.loop(0, n // BLOCK_ROWS)
    def _(t):
        d_edge_s[block(t, BLOCK_ROWS, n), :] = contract(
            n, t * BLOCK_ROWS, x, edges_s.at[1 - side]
        )

    @pl.loop(0, n // STEP_ROWS)
    def _(t):
        here = block(t, STEP_ROWS, n)
        d_pre_ref[here, : 2 * h] = edge_grads(
            d_edge_s[here, :], slopes_s[side, here, :], edges_s[side, here, :]
        )


def own_rows(
    pair_ref, up_ref, d_left_ref, d_right_ref, weights, vectors, hat_ref, rstd_ref, out_ref
):
    cells, c = out_ref.shape
    half = d_right_ref.shape[1]
    place = own_place(pair_ref)
    own = pl.ds(pl.multiple_of(place * cells, cells), cells)
    width = d_left_ref.shape[1] + half
    gain = vector_parts(vectors[0:1, :], c, width)[1]
    d_left, d_right = d_left_ref[own, :], d_right_ref[own, :]
    d_pre = jnp.concatenate([d_left[:, :half], d_right, d_left[:, half:]], axis=1)
    d_normed = dot(d_pre, weights[0, :, :width], ((1,), (1,))) * gain[:, :c]
    pulled = norm_vjp(hat_ref[0, own, :], rstd_ref[0, own, :], d_normed)
    out_ref[...] = (up_ref[own, :] + pulled).astype(BF16)


def exchange(value, axis, size, step):
    return lax.ppermute(value, axis, [(d, d ^ step) for d in range(size)])


def near_rounds(value, groups):
    other = exchange(value, "dp", groups, 1)
    step = 2
    while step < groups // 2:
        value = add_narrow(value, other)
        other = exchange(value, "dp", groups, step)
        step *= 2
    return value, other


def add_narrow(a, b):
    return (a.astype(F32) + b.astype(F32)).astype(BF16)


def prepare(
    index_ref, mask_ref, state_ref, cot_ref, w, w_out, b, gain, shift, b_out, *refs
):
    sent_ref, weights_ref, vectors_ref, mask_s, sems = refs
    cells, c = state_ref.shape
    below, width = cells + TAIL_ROWS, w.shape[2]
    copies = [(mask_ref, mask_s), (state_ref, sent_ref.at[:cells]), (cot_ref, sent_ref.at[below:])]
    copies += [(w, weights_ref.at[:, :, :width]), (w_out, weights_ref.at[:, :, width:])]
    first = 0
    for vector in (b, gain, shift, b_out):
        last = first + vector.shape[1]
        copies.append((vector, vectors_ref.at[:, first:last]))
        first = last
    copies = [pltpu.make_async_copy(*pair, sems.at[k]) for k, pair in enumerate(copies)]
    for copy in copies:
        copy.start()
    copies[0].wait()
    length = jnp.max(jnp.sum(mask_s[...].astype(F32), axis=1, keepdims=True))
    in_length = lax.broadcasted_iota(jnp.int32, (TAIL_ROWS, c), 1) < 64
    place = index_ref[0].astype(F32)
    sent_ref[cells:below, :] = jnp.where(in_length, length, place).astype(BF16)
    for copy in copies[1:]:
        copy.wait()


def pair_up(near_ref, far_ref, state_ref, cot_ref):
    split = state_ref.shape[1]
    for side, ref in enumerate((near_ref, far_ref)):
        state_ref[side] = ref[:split, :]
        cot_ref[side] = ref[split:, :]


def hold(weights_in, vectors_in, weights_out, vectors_out):
    weights_out[...] = weights_in[...]
    vectors_out[...] = vectors_in[...]


def vector_parts(row, c, width):
    ends = [width, width + 2 * c, width + 4 * c, width + 5 * c]
    return [row[:, first:last] for first, last in zip([0] + ends, ends)]


def add_grads(rest, rest_near, left, left_near, right, right_far, proj_ref, out_ref):
    width = proj_ref.shape[2]
    c = out_ref.shape[2]
    half = (width - c) // 2
    total = rest[:, : width + c].astype(F32) + rest_near[:, : width + c].astype(F32)
    proj_ref[1] = total[:, :width]
    out_ref[1] = total[:, width:]
    total = left[...].astype(F32) + left_near[...].astype(F32)
    proj_ref[0, :, :half] = total[:, :half]
    proj_ref[0, :, 2 * half :] = total[:, half : half + c]
    out_ref[0] = total[:, half + c :]
    proj_ref[0, :, half : 2 * half] = right[...].astype(F32) + right_far[...].astype(F32)


def crop_shards(
    groups,
    parts,
    pair_repr,
    pair_mask,
    cotangent,
    proj_weight,
    proj_bias,
    norm_gain,
    norm_shift,
    out_weight,
    out_bias,
):
    _, rows, n, c = pair_repr.shape
    h = out_weight.shape[1]
    width = proj_weight.shape[2]
    cells, pairs = rows * n, n * n
    plane = (pairs + 8, h)
    kept = [jax.ShapeDtypeStruct((2, 4) + plane, F32), jax.ShapeDtypeStruct((2, 2) + plane, F32)]
    kept += [jax.ShapeDtypeStruct((2,) + plane, F32)] * 6
    kept += [jax.ShapeDtypeStruct((2, pairs, h), BF16)] * 2
    grads = jax.ShapeDtypeStruct((c, width + c), BF16)
    vmem = pl.BlockSpec(memory_space=pltpu.VMEM)
    main = pl.BlockSpec(memory_space=pltpu.HBM)
    params = pltpu.CompilerParams(vmem_limit_bytes=VMEM_BYTES)

    def cost(planes):
        flops = 4 * pairs * width * c
        return pl.CostEstimate(
            flops=flops, bytes_accessed=planes * pairs * c * 4, transcendentals=0
        )

    packed = (
        jax.ShapeDtypeStruct((2, c, width + c), BF16),
        jax.ShapeDtypeStruct((2, width + 5 * c), F32),
    )
    sent, *weights = pl.pallas_call(
        prepare,
        out_shape=(jax.ShapeDtypeStruct((2 * cells + TAIL_ROWS, c), BF16),) + packed,
        in_specs=[pl.BlockSpec(memory_space=pltpu.SMEM)] + [main] * 9,
        out_specs=[vmem] * 3,
        scratch_shapes=[pltpu.VMEM((rows, n), jnp.int32), pltpu.SemaphoreType.DMA((9,))],
        compiler_params=pltpu.CompilerParams(vmem_limit_bytes=PREPARE_BYTES),
        name="prepare",
    )(
        lax.axis_index("dap").astype(jnp.int32)[None],
        pair_mask[0],
        pair_repr.reshape(cells, c),
        cotangent.reshape(cells, c),
        proj_weight,
        out_weight,
        proj_bias,
        norm_gain,
        norm_shift,
        out_bias,
    )
    weights = pl.pallas_call(
        hold,
        out_shape=packed,
        in_specs=[vmem] * 2,
        out_specs=[vmem] * 2,
        compiler_params=params,
        cost_estimate=cost(8),
        name="hold",
    )(*weights)
    beside = exchange(sent, "dap", parts, 1)
    beside, *weights = lax.optimization_barrier((beside, *weights))
    state, cot = pl.pallas_call(
        pair_up,
        out_shape=(
            jax.ShapeDtypeStruct((2, cells + TAIL_ROWS, c), BF16),
            jax.ShapeDtypeStruct((2, cells, c), BF16),
        ),
        in_specs=[vmem] * 2,
        out_specs=[vmem] * 2,
        compiler_params=params,
        name="pair_up",
    )(sent, beside)
    states, cots = [state], [cot]
    half = parts // 2
    jumps = [0, *range(1, half // 2), *reversed(range(half // 2, half))]
    for group in (states, cots):
        group += [exchange(group[0], "dap", parts, 2 * jump) for jump in jumps[1:]]

    held = pl.pallas_call(
        functools.partial(forward, n, jumps),
        out_shape=kept,
        in_specs=[vmem] * (half + 2),
        out_specs=(vmem,) * KEPT,
        scratch_shapes=[pltpu.VMEM((pairs, c), BF16)],
        compiler_params=params,
        cost_estimate=cost(64),
        name="forward",
    )(*states, *weights)

    double, single = pltpu.VMEM((2,) + plane, F32), pltpu.VMEM(plane, F32)
    up_1, grads_1 = pl.pallas_call(
        functools.partial(backward_second, n, jumps),
        out_shape=(jax.ShapeDtypeStruct((pairs, c), F32), grads),
        in_specs=[vmem] * (3 + half + KEPT),
        out_specs=(vmem, vmem),
        scratch_shapes=[
            double,
            double,
            pltpu.VMEM((pairs, width), BF16),
            pltpu.VMEM((pairs, c), BF16),
        ],
        compiler_params=params,
        cost_estimate=cost(48),
        name="backward_second",
    )(states[0], *cots, *weights, *held)
    far = groups // 2
    others_1 = exchange(grads_1, "dp", groups, far)

    d_left, d_product_t, grads_left = pl.pallas_call(
        functools.partial(backward_left, n),
        out_shape=(
            jax.ShapeDtypeStruct((pairs, 2 * h + c), BF16),
            jax.ShapeDtypeStruct(plane, F32),
            jax.ShapeDtypeStruct((c, 2 * h + 2 * c), BF16),
        ),
        in_specs=[vmem] * (3 + KEPT),
        out_specs=[vmem] * 3,
        scratch_shapes=[single, single],
        compiler_params=params,
        cost_estimate=cost(24),
        name="backward_left",
    )(up_1, *weights, *held)
    others_left = exchange(grads_left, "dp", groups, far)

    d_right, grads_right = pl.pallas_call(
        functools.partial(backward_right, n),
        out_shape=(
            jax.ShapeDtypeStruct((pairs, 2 * h), BF16),
            jax.ShapeDtypeStruct((c, 2 * h), BF16),
        ),
        in_specs=[vmem] * (1 + KEPT),
        out_specs=[vmem] * 2,
        scratch_shapes=[single],
        compiler_params=params,
        cost_estimate=cost(24),
        name="backward_right",
    )(d_product_t, *held)
    pair_grad = pl.pallas_call(
        own_rows,
        out_shape=jax.ShapeDtypeStruct((cells, c), BF16),
        in_specs=[vmem] * 8,
        out_specs=vmem,
        compiler_params=params,
        cost_estimate=cost(8),
        name="own_rows",
    )(states[0], up_1, d_left, d_right, *weights, held[3], held[4])

    rest, rest_near = near_rounds(
        jnp.concatenate([add_narrow(grads_1, others_1), grads_right], axis=1), groups
    )
    right = add_narrow(rest[:, width + c :], rest_near[:, width + c :])
    right_far = exchange(right, "dp", groups, far)
    ends_left = near_rounds(add_narrow(grads_left, others_left), groups)

    proj_total, out_total = pl.pallas_call(
        add_grads,
        out_shape=(
            jax.ShapeDtypeStruct((2, c, width), F32),
            jax.ShapeDtypeStruct((2, h, c), F32),
        ),
        in_specs=[vmem] * 6,
        out_specs=(vmem, vmem),
        compiler_params=params,
        name="add_grads",
    )(rest, rest_near, *ends_left, right, right_far)
    return pair_grad.reshape(pair_repr.shape), proj_total, out_total


def layer_norm(values, gain_vec, shift_vec, norm_axis):
    mean_value = jnp.mean(values, axis=norm_axis, keepdims=True)
    centred = values - mean_value
    variance = jnp.mean(centred * centred, axis=norm_axis, keepdims=True)
    return centred * lax.rsqrt(variance + NORM_EPSILON) * gain_vec + shift_vec


def norm_pullback(values, gain_vec, shift_vec, norm_axis, upstream):
    _, pull_back = jax.vjp(
        lambda inner_value: layer_norm(inner_value, gain_vec, shift_vec, norm_axis), values
    )
    return pull_back(upstream)[0]


def edge_pair(edge_pre, cell_mask):
    left_edge = jax.nn.sigmoid(edge_pre[1]) * edge_pre[0] * cell_mask
    right_edge = jax.nn.sigmoid(edge_pre[3]) * edge_pre[2] * cell_mask
    return jnp.stack([left_edge, right_edge]).astype(jnp.bfloat16)


def edge_pullback(edge_pre, cell_mask, grad_pair):
    sig_left = jax.nn.sigmoid(edge_pre[1])
    sig_right = jax.nn.sigmoid(edge_pre[3])
    grad_left = grad_pair[0].astype(jnp.float32) * cell_mask
    grad_right = grad_pair[1].astype(jnp.float32) * cell_mask
    return jnp.stack(
        [
            grad_left * sig_left,
            grad_left * edge_pre[0] * sig_left * (1.0 - sig_left),
            grad_right * sig_right,
            grad_right * edge_pre[2] * sig_right * (1.0 - sig_right),
        ]
    ).astype(jnp.bfloat16)


def triangle(pair_edges, outgoing):
    if outgoing:
        einsum_form = "cik,cjk->cij"
    else:
        einsum_form = "cki,ckj->cij"
    return jnp.einsum(
        einsum_form, pair_edges[0], pair_edges[1], preferred_element_type=jnp.float32
    ).astype(jnp.bfloat16)


def triangle_pullback(pair_edges, grad_product, outgoing):
    left_edge = pair_edges[0]
    right_edge = pair_edges[1]
    if outgoing:
        grad_left = jnp.einsum(
            "cij,cjk->cik", grad_product, right_edge, preferred_element_type=jnp.float32
        )
        grad_right = jnp.einsum(
            "cij,cik->cjk", grad_product, left_edge, preferred_element_type=jnp.float32
        )
    else:
        grad_left = jnp.einsum(
            "ckj,cij->cki", right_edge, grad_product, preferred_element_type=jnp.float32
        )
        grad_right = jnp.einsum(
            "cki,cij->ckj", left_edge, grad_product, preferred_element_type=jnp.float32
        )
    return jnp.stack([grad_left, grad_right]).astype(jnp.bfloat16)


def update_weights(proj_weight, proj_bias, norm_gain, norm_shift, update, channels, hidden):
    w_edge = proj_weight[update, :, : 4 * hidden].reshape(channels, 4, hidden)
    w_gate = proj_weight[update, :, 4 * hidden :]
    bias_edge = proj_bias[update, : 4 * hidden].reshape(4, hidden, 1, 1)
    bias_gate = proj_bias[update, 4 * hidden :]
    gain_in = norm_gain[update, :channels]
    shift_in = norm_shift[update, :channels]
    gain_out = norm_gain[update, channels:][:, None, None]
    shift_out = norm_shift[update, channels:][:, None, None]
    return (w_edge, w_gate, bias_edge, bias_gate, gain_in, shift_in, gain_out, shift_out)


def shards(
    pair_repr,
    pair_mask,
    cotangent,
    proj_weight,
    proj_bias,
    norm_gain,
    norm_shift,
    out_weight,
    out_bias,
):
    channels = pair_repr.shape[3]
    hidden = out_weight.shape[1]
    pair_state = pair_repr[0]
    cell_mask = pair_mask[0].astype(jnp.float32)
    records = []
    for update in range(2):
        w_edge, w_gate, bias_edge, bias_gate, gain_in, shift_in, gain_out, shift_out = (
            update_weights(proj_weight, proj_bias, norm_gain, norm_shift, update, channels, hidden)
        )
        state_f = pair_state.astype(jnp.float32)
        normed = layer_norm(state_f, gain_in, shift_in, -1).astype(jnp.bfloat16)
        edge_pre = (
            jnp.einsum("rnc,cgh->ghrn", normed, w_edge, preferred_element_type=jnp.float32)
            + bias_edge
        )
        gate_pre = (
            jnp.einsum("rnc,cd->rnd", normed, w_gate, preferred_element_type=jnp.float32)
            + bias_gate
        )
        pair_edges = edge_pair(edge_pre, cell_mask)
        spread = lax.all_to_all(pair_edges, "dap", split_axis=1, concat_axis=2, tiled=True)
        product = lax.all_to_all(
            triangle(spread, update == 0), "dap", split_axis=1, concat_axis=0, tiled=True
        )
        mixed_norm = layer_norm(product.astype(jnp.float32), gain_out, shift_out, 0).astype(
            jnp.bfloat16
        )
        branch = (
            jnp.einsum(
                "hrn,hd->rnd", mixed_norm, out_weight[update], preferred_element_type=jnp.float32
            )
            + out_bias[update]
        )
        records.append(
            (state_f, normed, edge_pre, gate_pre, pair_edges, spread, product, mixed_norm, branch)
        )
        pair_state = (state_f + jax.nn.sigmoid(gate_pre) * branch).astype(jnp.bfloat16)
    upstream = cotangent[0].astype(jnp.float32)
    proj_grads = []
    out_grads = []
    for update in (1, 0):
        state_f, normed, edge_pre, gate_pre, pair_edges, spread, product, mixed_norm, branch = (
            records[update]
        )
        w_edge, w_gate, bias_edge, bias_gate, gain_in, shift_in, gain_out, shift_out = (
            update_weights(proj_weight, proj_bias, norm_gain, norm_shift, update, channels, hidden)
        )
        gate_value = jax.nn.sigmoid(gate_pre)
        grad_branch = (upstream * gate_value).astype(jnp.bfloat16)
        grad_gate = (upstream * branch * gate_value * (1.0 - gate_value)).astype(jnp.bfloat16)
        out_grad = jnp.einsum(
            "hrn,rnd->hd", mixed_norm, grad_branch, preferred_element_type=jnp.float32
        )
        grad_mixed = jnp.einsum(
            "rnd,hd->hrn", grad_branch, out_weight[update], preferred_element_type=jnp.float32
        )
        grad_product = norm_pullback(
            product.astype(jnp.float32), gain_out, shift_out, 0, grad_mixed
        ).astype(jnp.bfloat16)
        column_edges = spread
        column_grad = lax.all_to_all(
            grad_product[None], "dap", split_axis=1, concat_axis=2, tiled=True
        )[0]
        grad_pair = lax.all_to_all(
            triangle_pullback(column_edges, column_grad, update == 0),
            "dap",
            split_axis=2,
            concat_axis=1,
            tiled=True,
        )
        grad_edge = edge_pullback(edge_pre, cell_mask, grad_pair)
        edge_grad = jnp.einsum(
            "rnc,ghrn->cgh", normed, grad_edge, preferred_element_type=jnp.float32
        ).reshape(channels, 4 * hidden)
        gate_grad = jnp.einsum("rnc,rnd->cd", normed, grad_gate, preferred_element_type=jnp.float32)
        grad_normed = jnp.einsum(
            "ghrn,cgh->rnc", grad_edge, w_edge, preferred_element_type=jnp.float32
        )
        grad_normed = grad_normed + jnp.einsum(
            "rnd,cd->rnc", grad_gate, w_gate, preferred_element_type=jnp.float32
        )
        upstream = upstream + norm_pullback(state_f, gain_in, shift_in, -1, grad_normed)
        proj_part = jnp.concatenate([edge_grad, gate_grad], axis=1)
        proj_grads.append(proj_part)
        out_grads.append(out_grad)
    proj_total = jnp.stack(proj_grads[::-1])
    out_total = jnp.stack(out_grads[::-1])
    proj_total, out_total = lax.psum((proj_total, out_total), ("dp", "dap"))
    return (upstream.astype(jnp.bfloat16)[None], proj_total, out_total)


def solution(mesh):
    placed = (
        P("dp", "dap", None, None),
        P("dp", "dap", None),
        P("dp", "dap", None, None),
        P(),
        P(),
        P(),
        P(),
        P(),
        P(),
    )
    groups, parts = mesh.shape["dp"], mesh.shape["dap"]

    def program(*args):
        n, c = args[0].shape[2:]
        rows = n // parts
        fits = 20 * n * n * c * 4 <= CROP_BUDGET
        paired = all(size >= 4 and size & (size - 1) == 0 for size in (groups, parts))
        even = args[7].shape[1] == c == 128 and STEP_ROWS % rows == 0 and n == STEP_ROWS
        body = functools.partial(crop_shards, groups, parts) if fits and even and paired else shards
        return spread_over(body)(*args)

    def spread_over(body):
        return jax.shard_map(
            body,
            mesh=mesh,
            in_specs=placed,
            out_specs=(P("dp", "dap", None, None), P(), P()),
            check_vma=False,
        )

    return program
```

```python
import functools

import jax
import jax.numpy as jnp
from jax import lax
from jax.experimental import pallas as pl
from jax.experimental.pallas import tpu as pltpu
from jax.sharding import PartitionSpec as P

NORM_EPSILON = 1e-05
VMEM_BYTES = 16 * 1024 * 1024
PREPARE_BYTES = 63 * 1024 * 1024
CROP_BUDGET = 32 * 1024 * 1024
BLOCK_ROWS = 8
STEP_ROWS = 32
KEPT = 10
TAIL_ROWS = 16
F32 = jnp.float32
BF16 = jnp.bfloat16


def sigmoid(x):
    return 0.5 * jnp.tanh(0.5 * x) + 0.5


def dot(a, b, dims=((1,), (0,))):
    return lax.dot_general(a, b, (dims, ((), ())), preferred_element_type=F32)


def norm_parts(x):
    x = x.astype(F32)
    centred = x - jnp.mean(x, axis=-1, keepdims=True)
    rstd = lax.rsqrt(jnp.mean(centred * centred, axis=-1, keepdims=True) + NORM_EPSILON)
    return centred * rstd, jnp.broadcast_to(rstd, x.shape)


def norm_vjp(x_hat, rstd, grad):
    mean_grad = jnp.mean(grad, axis=-1, keepdims=True)
    mean_prod = jnp.mean(grad * x_hat, axis=-1, keepdims=True)
    return rstd * (grad - mean_grad - x_hat * mean_prod)


def pair_mask_block(length, first_row, rows, n, lanes):
    shape = (rows, n, lanes)
    i = lax.broadcasted_iota(jnp.int32, shape, 0) + first_row
    j = lax.broadcasted_iota(jnp.int32, shape, 1)
    inside = jnp.where((i < length) & (j < length), 1.0, 0.0)
    return inside.reshape(rows * n, lanes)


def project(x, mask, w, b, gain, shift):
    x_hat, rstd = norm_parts(x)
    normed = (x_hat * gain + shift).astype(BF16)
    pre = dot(normed, w) + b
    h = (pre.shape[1] - x.shape[1]) // 4
    s_left = sigmoid(pre[:, h : 2 * h]) * mask
    s_right = sigmoid(pre[:, 3 * h : 4 * h]) * mask
    left = s_left * pre[:, :h]
    right = s_right * pre[:, 2 * h : 3 * h]
    gate = sigmoid(pre[:, 4 * h :])
    return x_hat, rstd, normed, s_left, s_right, left, right, gate


def mix(product, gain, shift, w_out, b_out):
    p_hat, p_rstd = norm_parts(product)
    mixed = (p_hat * gain + shift).astype(BF16)
    return p_hat, p_rstd, mixed, dot(mixed, w_out) + b_out


def unmix(up, gate, branch, p_hat, p_rstd, gain, w_out):
    d_branch = up * gate
    d_gate = (d_branch * branch * (1.0 - gate)).astype(BF16)
    d_branch = d_branch.astype(BF16)
    d_mixed = dot(d_branch, w_out, ((1,), (1,))) * gain
    return d_branch, d_gate, norm_vjp(p_hat, p_rstd, d_mixed)


def contract(n, first, x, y):
    lanes = y.shape[1]
    tiles = (n // 8, 8, lanes)

    def step(e, totals):
        block = y[pl.ds(pl.multiple_of(e * n, n), n), :].reshape(tiles)
        return tuple(
            totals[a] + x[pl.ds((first + a) * n + e, 8, stride=0), :][None] * block
            for a in range(BLOCK_ROWS)
        )

    zero = jnp.zeros(tiles, F32)
    totals = lax.fori_loop(0, n, step, (zero,) * BLOCK_ROWS, unroll=True)
    return jnp.stack(totals).reshape(BLOCK_ROWS * n, lanes)


def edge_grads(d_edge, slope, edge):
    grads = (d_edge * slope).astype(BF16), (d_edge * edge * (1.0 - slope)).astype(BF16)
    return jnp.concatenate(grads, axis=1)


def tail_values(block, lanes_from, lanes_to):
    lane = lax.broadcasted_iota(jnp.int32, block.shape, block.ndim - 1)
    inside = (lane >= lanes_from) & (lane < lanes_to)
    return jnp.max(jnp.where(inside, block.astype(F32), 0.0)).astype(jnp.int32)


def own_place(pair_ref):
    return tail_values(pair_ref[0, -TAIL_ROWS:, :], 64, 128)


def place_of(own, jump, side):
    return own ^ (2 * jump) ^ side


def block(t, rows, n):
    return pl.ds(pl.multiple_of(t * rows * n, rows * n), rows * n)


def forward(n, jumps, *refs):
    pairs, refs = refs[: len(jumps)], refs[len(jumps) :]
    (weights, vectors), refs = refs[:2], refs[2:]
    (edges_s, slopes_s, gate_s, hat_s, rstd_s) = refs[:5]
    (p_hat_s, p_rstd_s, branch_s, normed_s, mixed_s) = refs[5:KEPT]
    (next_s,) = refs[KEPT:]
    c = weights.shape[1]
    width = weights.shape[2] - c
    rows = n // (2 * len(jumps))
    cells = rows * n
    tails = jnp.stack([pair[:, cells:, :] for pair in pairs if pair.shape[1] > cells])
    length = tail_values(tails, 0, 64)
    own = own_place(pairs[0])
    for pair, jump in zip(pairs, jumps):
        for side in range(2):
            next_s[block(place_of(own, jump, side), rows, n), :] = pair[side, :cells, :]
    steps = n // STEP_ROWS

    @pl.loop(0, 2)
    def _(u):
        row = jnp.where(u == 0, vectors[0:1, :], vectors[1:2, :])
        bias, gains, shifts, bias_out = vector_parts(row, c, width)

        @pl.loop(0, steps)
        def _(t):
            first = t * STEP_ROWS
            here = block(t, STEP_ROWS, n)
            mask = pair_mask_block(length, first, STEP_ROWS, n, c)
            x_hat, rstd, normed, s_left, s_right, left, right, gate = project(
                next_s[here, :], mask, weights[u, :, :width], bias, gains[:, :c], shifts[:, :c]
            )
            edges_s[u, 0, here, :] = left
            edges_s[u, 1, here, :] = right
            for r in range(STEP_ROWS):
                swapped = pl.ds(first + r, n, stride=n)
                edges_s[u, 2, swapped, :] = right[r * n : (r + 1) * n]
                edges_s[u, 3, swapped, :] = left[r * n : (r + 1) * n]
            slopes_s[u, 0, here, :] = s_left
            slopes_s[u, 1, here, :] = s_right
            gate_s[u, here, :] = gate
            hat_s[u, here, :] = x_hat
            rstd_s[u, here, :] = rstd
            normed_s[u, here, :] = normed

        @pl.loop(0, steps)
        def _(t):
            here = block(t, STEP_ROWS, n)
            x, y = edges_s.at[u, 3 * u], edges_s.at[u, 2 - u]
            product = [
                contract(n, t * STEP_ROWS + r, x, y) for r in range(0, STEP_ROWS, BLOCK_ROWS)
            ]
            p_hat, p_rstd, mixed, branch = mix(
                jnp.concatenate(product).astype(BF16), gains[:, c:], shifts[:, c:], weights[u, :, width:], bias_out
            )
            p_hat_s[u, here, :] = p_hat
            p_rstd_s[u, here, :] = p_rstd
            mixed_s[u, here, :] = mixed
            branch_s[u, here, :] = branch
            x = next_s[here, :].astype(F32)
            next_s[here, :] = (x + gate_s[u, here, :] * branch).astype(BF16)


def kept_parts(refs, u):
    return [ref.at[u] for ref in refs[:KEPT]]


def store_swapped(ref, rows, n, first, values):
    for r in range(rows):
        ref[pl.ds(first + r, n, stride=n), :] = values[r * n : (r + 1) * n]


def backward_second(n, jumps, pair, *refs):
    parted, refs = refs[: len(jumps)], refs[len(jumps) :]
    weights, vectors = refs[:2]
    (edges_s, slopes_s, gate_s, _, _, *kept) = kept_parts(refs[2:], 1)
    (p_hat_s, p_rstd_s, branch_s, normed_s, mixed_s) = kept
    d_pre_s, cot_s, grads_ref, d_product_s, d_edges_s = refs[2 + KEPT :]
    c, h = weights.shape[1], edges_s.shape[2]
    width = 4 * h + c
    gain = vector_parts(vectors[1:2, :], c, width)[1]
    own = own_place(pair)
    for part, jump in zip(parted, jumps):
        for side in range(2):
            cot_s[block(place_of(own, jump, side), part.shape[1] // n, n), :] = part[side]

    @pl.loop(0, n // STEP_ROWS)
    def _(t):
        here = block(t, STEP_ROWS, n)
        d_branch, d_gate, d_product = unmix(
            cot_s[here, :].astype(F32),
            gate_s[here, :],
            branch_s[here, :],
            p_hat_s[here, :],
            p_rstd_s[here, :],
            gain[:, c:],
            weights[1, :, width:],
        )
        d_out = dot(mixed_s[here, :], d_branch, ((0,), (0,)))
        d_pre_s[here, 4 * h :] = d_gate
        d_product_s[1, here, :] = d_product
        store_swapped(d_product_s.at[0], STEP_ROWS, n, t * STEP_ROWS, d_product)
        grads_ref[:, width:] = d_out.astype(BF16)

    blocks = n // BLOCK_ROWS

    @pl.loop(0, 2 * blocks)
    def _(step):
        side, t = step // blocks, step % blocks
        d_edges_s[side, block(t, BLOCK_ROWS, n), :] = contract(
            n, t * BLOCK_ROWS, edges_s.at[1 - side], d_product_s.at[side]
        )

    @pl.loop(0, n // STEP_ROWS)
    def _(t):
        here = block(t, STEP_ROWS, n)
        grads = [
            edge_grads(d_edges_s[side, here, :], slopes_s[side, here, :], edges_s[side, here, :])
            for side in range(2)
        ]
        d_pre = jnp.concatenate([*grads, d_pre_s[here, 4 * h :]], axis=1)
        d_pre_s[here, : 4 * h] = d_pre[:, : 4 * h]
        grads_ref[:, :width] = dot(normed_s[here, :], d_pre, ((0,), (0,))).astype(BF16)


def backward_left(n, d_pre_1_ref, cot_ref, weights, vectors, *refs):
    hat_1_s, rstd_1_s = kept_parts(refs, 1)[3:5]
    (edges_s, slopes_s, gate_s, _, _, *kept) = kept_parts(refs, 0)
    (p_hat_s, p_rstd_s, branch_s, normed_s, mixed_s) = kept
    up_ref, d_pre_ref, d_product_t_ref, grads_ref, d_product_s, d_edge_s = refs[KEPT:]
    c, h = weights.shape[1], edges_s.shape[2]
    width = 4 * h + c
    gain, gain_1 = (vector_parts(vectors[u : u + 1, :], c, width)[1] for u in range(2))

    @pl.loop(0, n // STEP_ROWS)
    def _(t):
        here = block(t, STEP_ROWS, n)
        d_normed = dot(d_pre_1_ref[here, :], weights[1, :, :width], ((1,), (1,)))
        pulled = norm_vjp(hat_1_s[here, :], rstd_1_s[here, :], d_normed * gain_1[:, :c])
        up = cot_ref[here, :].astype(F32) + pulled
        up_ref[here, :] = up
        d_branch, d_gate, d_product = unmix(
            up,
            gate_s[here, :],
            branch_s[here, :],
            p_hat_s[here, :],
            p_rstd_s[here, :],
            gain[:, c:],
            weights[0, :, width:],
        )
        d_out = dot(mixed_s[here, :], d_branch, ((0,), (0,)))
        d_pre_ref[here, 2 * h :] = d_gate
        d_product_s[here, :] = d_product
        store_swapped(d_product_t_ref, STEP_ROWS, n, t * STEP_ROWS, d_product)
        grads_ref[:, 2 * h + c :] = d_out.astype(BF16)

    one_side(n, 0, d_product_s, edges_s, slopes_s, d_edge_s, d_pre_ref)
    d_pre = dot(normed_s[...], d_pre_ref[...], ((0,), (0,)))
    grads_ref[:, : 2 * h + c] = d_pre.astype(BF16)


def backward_right(n, d_product_t_ref, *refs):
    (edges_s, slopes_s, *kept) = kept_parts(refs, 0)
    normed_s = kept[-2]
    d_pre_ref, grads_ref, d_edge_s = refs[KEPT:]
    one_side(n, 1, d_product_t_ref, edges_s, slopes_s, d_edge_s, d_pre_ref)
    grads_ref[...] = dot(normed_s[...], d_pre_ref[...], ((0,), (0,))).astype(BF16)


def one_side(n, side, x, edges_s, slopes_s, d_edge_s, d_pre_ref):
    h = edges_s.shape[2]

    @pl.loop(0, n // BLOCK_ROWS)
    def _(t):
        d_edge_s[block(t, BLOCK_ROWS, n), :] = contract(
            n, t * BLOCK_ROWS, x, edges_s.at[1 - side]
        )

    @pl.loop(0, n // STEP_ROWS)
    def _(t):
        here = block(t, STEP_ROWS, n)
        d_pre_ref[here, : 2 * h] = edge_grads(
            d_edge_s[here, :], slopes_s[side, here, :], edges_s[side, here, :]
        )


def own_rows(
    pair_ref, up_ref, d_left_ref, d_right_ref, weights, vectors, hat_ref, rstd_ref, out_ref
):
    cells, c = out_ref.shape
    half = d_right_ref.shape[1]
    place = own_place(pair_ref)
    own = pl.ds(pl.multiple_of(place * cells, cells), cells)
    width = d_left_ref.shape[1] + half
    gain = vector_parts(vectors[0:1, :], c, width)[1]
    d_left, d_right = d_left_ref[own, :], d_right_ref[own, :]
    d_pre = jnp.concatenate([d_left[:, :half], d_right, d_left[:, half:]], axis=1)
    d_normed = dot(d_pre, weights[0, :, :width], ((1,), (1,))) * gain[:, :c]
    pulled = norm_vjp(hat_ref[0, own, :], rstd_ref[0, own, :], d_normed)
    out_ref[...] = (up_ref[own, :] + pulled).astype(BF16)


def exchange(value, axis, size, step):
    return lax.ppermute(value, axis, [(d, d ^ step) for d in range(size)])


def near_rounds(value, groups):
    other = exchange(value, "dp", groups, 1)
    step = 2
    while step < groups // 2:
        value = add_narrow(value, other)
        other = exchange(value, "dp", groups, step)
        step *= 2
    return value, other


def add_narrow(a, b):
    return (a.astype(F32) + b.astype(F32)).astype(BF16)


def prepare(
    index_ref, mask_ref, state_ref, cot_ref, w, w_out, b, gain, shift, b_out, *refs
):
    sent_ref, weights_ref, vectors_ref, mask_s, sems = refs
    cells, c = state_ref.shape
    below, width = cells + TAIL_ROWS, w.shape[2]
    copies = [(mask_ref, mask_s), (state_ref, sent_ref.at[:cells]), (cot_ref, sent_ref.at[below:])]
    copies += [(w, weights_ref.at[:, :, :width]), (w_out, weights_ref.at[:, :, width:])]
    first = 0
    for vector in (b, gain, shift, b_out):
        last = first + vector.shape[1]
        copies.append((vector, vectors_ref.at[:, first:last]))
        first = last
    copies = [pltpu.make_async_copy(*pair, sems.at[k]) for k, pair in enumerate(copies)]
    for copy in copies:
        copy.start()
    copies[0].wait()
    length = jnp.max(jnp.sum(mask_s[...].astype(F32), axis=1, keepdims=True))
    in_length = lax.broadcasted_iota(jnp.int32, (TAIL_ROWS, c), 1) < 64
    place = index_ref[0].astype(F32)
    sent_ref[cells:below, :] = jnp.where(in_length, length, place).astype(BF16)
    for copy in copies[1:]:
        copy.wait()


def pair_up(near_ref, far_ref, state_ref, rows_ref, cot_ref):
    split, cells = state_ref.shape[1], rows_ref.shape[1]
    for side, ref in enumerate((near_ref, far_ref)):
        state_ref[side] = ref[:split, :]
        rows_ref[side] = ref[:cells, :]
        cot_ref[side] = ref[split:, :]


def hold(weights_in, vectors_in, weights_out, vectors_out):
    weights_out[...] = weights_in[...]
    vectors_out[...] = vectors_in[...]


def vector_parts(row, c, width):
    ends = [width, width + 2 * c, width + 4 * c, width + 5 * c]
    return [row[:, first:last] for first, last in zip([0] + ends, ends)]


def add_grads(rest, rest_near, left, left_near, right, right_far, proj_ref, out_ref):
    width = proj_ref.shape[2]
    c = out_ref.shape[2]
    half = (width - c) // 2
    total = rest[:, : width + c].astype(F32) + rest_near[:, : width + c].astype(F32)
    proj_ref[1] = total[:, :width]
    out_ref[1] = total[:, width:]
    total = left[...].astype(F32) + left_near[...].astype(F32)
    proj_ref[0, :, :half] = total[:, :half]
    proj_ref[0, :, 2 * half :] = total[:, half : half + c]
    out_ref[0] = total[:, half + c :]
    proj_ref[0, :, half : 2 * half] = right[...].astype(F32) + right_far[...].astype(F32)


def crop_shards(
    groups,
    parts,
    pair_repr,
    pair_mask,
    cotangent,
    proj_weight,
    proj_bias,
    norm_gain,
    norm_shift,
    out_weight,
    out_bias,
):
    _, rows, n, c = pair_repr.shape
    h = out_weight.shape[1]
    width = proj_weight.shape[2]
    cells, pairs = rows * n, n * n
    plane = (pairs + 8, h)
    kept = [jax.ShapeDtypeStruct((2, 4) + plane, F32), jax.ShapeDtypeStruct((2, 2) + plane, F32)]
    kept += [jax.ShapeDtypeStruct((2,) + plane, F32)] * 6
    kept += [jax.ShapeDtypeStruct((2, pairs, h), BF16)] * 2
    grads = jax.ShapeDtypeStruct((c, width + c), BF16)
    vmem = pl.BlockSpec(memory_space=pltpu.VMEM)
    main = pl.BlockSpec(memory_space=pltpu.HBM)
    params = pltpu.CompilerParams(vmem_limit_bytes=VMEM_BYTES)

    def cost(planes):
        flops = 4 * pairs * width * c
        return pl.CostEstimate(
            flops=flops, bytes_accessed=planes * pairs * c * 4, transcendentals=0
        )

    packed = (
        jax.ShapeDtypeStruct((2, c, width + c), BF16),
        jax.ShapeDtypeStruct((2, width + 5 * c), F32),
    )
    sent, *weights = pl.pallas_call(
        prepare,
        out_shape=(jax.ShapeDtypeStruct((2 * cells + TAIL_ROWS, c), BF16),) + packed,
        in_specs=[pl.BlockSpec(memory_space=pltpu.SMEM)] + [main] * 9,
        out_specs=[vmem] * 3,
        scratch_shapes=[pltpu.VMEM((rows, n), jnp.int32), pltpu.SemaphoreType.DMA((9,))],
        compiler_params=pltpu.CompilerParams(vmem_limit_bytes=PREPARE_BYTES),
        name="prepare",
    )(
        lax.axis_index("dap").astype(jnp.int32)[None],
        pair_mask[0],
        pair_repr.reshape(cells, c),
        cotangent.reshape(cells, c),
        proj_weight,
        out_weight,
        proj_bias,
        norm_gain,
        norm_shift,
        out_bias,
    )
    weights = pl.pallas_call(
        hold,
        out_shape=packed,
        in_specs=[vmem] * 2,
        out_specs=[vmem] * 2,
        compiler_params=params,
        cost_estimate=cost(8),
        name="hold",
    )(*weights)
    beside = exchange(sent, "dap", parts, 1)
    beside, *weights = lax.optimization_barrier((beside, *weights))
    state, state_rows, cot = pl.pallas_call(
        pair_up,
        out_shape=(
            jax.ShapeDtypeStruct((2, cells + TAIL_ROWS, c), BF16),
            jax.ShapeDtypeStruct((2, cells, c), BF16),
            jax.ShapeDtypeStruct((2, cells, c), BF16),
        ),
        in_specs=[vmem] * 2,
        out_specs=[vmem] * 3,
        compiler_params=params,
        name="pair_up",
    )(sent, beside)
    states, cots = [state], [cot]
    half = parts // 2
    jumps = [0, *range(1, half // 2), *reversed(range(half // 2, half))]
    for jump in jumps[1:]:
        with_tail = jump == half // 2
        states.append(exchange(state if with_tail else state_rows, "dap", parts, 2 * jump))
    cots += [exchange(cot, "dap", parts, 2 * jump) for jump in jumps[1:]]

    held = pl.pallas_call(
        functools.partial(forward, n, jumps),
        out_shape=kept,
        in_specs=[vmem] * (half + 2),
        out_specs=(vmem,) * KEPT,
        scratch_shapes=[pltpu.VMEM((pairs, c), BF16)],
        compiler_params=params,
        cost_estimate=cost(64),
        name="forward",
    )(*states, *weights)

    double, single = pltpu.VMEM((2,) + plane, F32), pltpu.VMEM(plane, F32)
    d_pre_1, cot, grads_1 = pl.pallas_call(
        functools.partial(backward_second, n, jumps),
        out_shape=(
            jax.ShapeDtypeStruct((pairs, width), BF16),
            jax.ShapeDtypeStruct((pairs, c), BF16),
            grads,
        ),
        in_specs=[vmem] * (3 + half + KEPT),
        out_specs=[vmem] * 3,
        scratch_shapes=[double, double],
        compiler_params=params,
        cost_estimate=cost(48),
        name="backward_second",
    )(states[0], *cots, *weights, *held)
    far = groups // 2
    others_1 = exchange(grads_1, "dp", groups, far)

    up_1, d_left, d_product_t, grads_left = pl.pallas_call(
        functools.partial(backward_left, n),
        out_shape=(
            jax.ShapeDtypeStruct((pairs, c), F32),
            jax.ShapeDtypeStruct((pairs, 2 * h + c), BF16),
            jax.ShapeDtypeStruct(plane, F32),
            jax.ShapeDtypeStruct((c, 2 * h + 2 * c), BF16),
        ),
        in_specs=[vmem] * (4 + KEPT),
        out_specs=[vmem] * 4,
        scratch_shapes=[single, single],
        compiler_params=params,
        cost_estimate=cost(24),
        name="backward_left",
    )(d_pre_1, cot, *weights, *held)
    others_left = exchange(grads_left, "dp", groups, far)

    d_right, grads_right = pl.pallas_call(
        functools.partial(backward_right, n),
        out_shape=(
            jax.ShapeDtypeStruct((pairs, 2 * h), BF16),
            jax.ShapeDtypeStruct((c, 2 * h), BF16),
        ),
        in_specs=[vmem] * (1 + KEPT),
        out_specs=[vmem] * 2,
        scratch_shapes=[single],
        compiler_params=params,
        cost_estimate=cost(24),
        name="backward_right",
    )(d_product_t, *held)
    pair_grad = pl.pallas_call(
        own_rows,
        out_shape=jax.ShapeDtypeStruct((cells, c), BF16),
        in_specs=[vmem] * 8,
        out_specs=vmem,
        compiler_params=params,
        cost_estimate=cost(8),
        name="own_rows",
    )(states[0], up_1, d_left, d_right, *weights, held[3], held[4])

    rest, rest_near = near_rounds(
        jnp.concatenate([add_narrow(grads_1, others_1), grads_right], axis=1), groups
    )
    right = add_narrow(rest[:, width + c :], rest_near[:, width + c :])
    right_far = exchange(right, "dp", groups, far)
    ends_left = near_rounds(add_narrow(grads_left, others_left), groups)

    proj_total, out_total = pl.pallas_call(
        add_grads,
        out_shape=(
            jax.ShapeDtypeStruct((2, c, width), F32),
            jax.ShapeDtypeStruct((2, h, c), F32),
        ),
        in_specs=[vmem] * 6,
        out_specs=(vmem, vmem),
        compiler_params=params,
        name="add_grads",
    )(rest, rest_near, *ends_left, right, right_far)
    return pair_grad.reshape(pair_repr.shape), proj_total, out_total


def layer_norm(values, gain_vec, shift_vec, norm_axis):
    mean_value = jnp.mean(values, axis=norm_axis, keepdims=True)
    centred = values - mean_value
    variance = jnp.mean(centred * centred, axis=norm_axis, keepdims=True)
    return centred * lax.rsqrt(variance + NORM_EPSILON) * gain_vec + shift_vec


def norm_pullback(values, gain_vec, shift_vec, norm_axis, upstream):
    _, pull_back = jax.vjp(
        lambda inner_value: layer_norm(inner_value, gain_vec, shift_vec, norm_axis), values
    )
    return pull_back(upstream)[0]


def edge_pair(edge_pre, cell_mask):
    left_edge = jax.nn.sigmoid(edge_pre[1]) * edge_pre[0] * cell_mask
    right_edge = jax.nn.sigmoid(edge_pre[3]) * edge_pre[2] * cell_mask
    return jnp.stack([left_edge, right_edge]).astype(jnp.bfloat16)


def edge_pullback(edge_pre, cell_mask, grad_pair):
    sig_left = jax.nn.sigmoid(edge_pre[1])
    sig_right = jax.nn.sigmoid(edge_pre[3])
    grad_left = grad_pair[0].astype(jnp.float32) * cell_mask
    grad_right = grad_pair[1].astype(jnp.float32) * cell_mask
    return jnp.stack(
        [
            grad_left * sig_left,
            grad_left * edge_pre[0] * sig_left * (1.0 - sig_left),
            grad_right * sig_right,
            grad_right * edge_pre[2] * sig_right * (1.0 - sig_right),
        ]
    ).astype(jnp.bfloat16)


def triangle(pair_edges, outgoing):
    if outgoing:
        einsum_form = "cik,cjk->cij"
    else:
        einsum_form = "cki,ckj->cij"
    return jnp.einsum(
        einsum_form, pair_edges[0], pair_edges[1], preferred_element_type=jnp.float32
    ).astype(jnp.bfloat16)


def triangle_pullback(pair_edges, grad_product, outgoing):
    left_edge = pair_edges[0]
    right_edge = pair_edges[1]
    if outgoing:
        grad_left = jnp.einsum(
            "cij,cjk->cik", grad_product, right_edge, preferred_element_type=jnp.float32
        )
        grad_right = jnp.einsum(
            "cij,cik->cjk", grad_product, left_edge, preferred_element_type=jnp.float32
        )
    else:
        grad_left = jnp.einsum(
            "ckj,cij->cki", right_edge, grad_product, preferred_element_type=jnp.float32
        )
        grad_right = jnp.einsum(
            "cki,cij->ckj", left_edge, grad_product, preferred_element_type=jnp.float32
        )
    return jnp.stack([grad_left, grad_right]).astype(jnp.bfloat16)


def update_weights(proj_weight, proj_bias, norm_gain, norm_shift, update, channels, hidden):
    w_edge = proj_weight[update, :, : 4 * hidden].reshape(channels, 4, hidden)
    w_gate = proj_weight[update, :, 4 * hidden :]
    bias_edge = proj_bias[update, : 4 * hidden].reshape(4, hidden, 1, 1)
    bias_gate = proj_bias[update, 4 * hidden :]
    gain_in = norm_gain[update, :channels]
    shift_in = norm_shift[update, :channels]
    gain_out = norm_gain[update, channels:][:, None, None]
    shift_out = norm_shift[update, channels:][:, None, None]
    return (w_edge, w_gate, bias_edge, bias_gate, gain_in, shift_in, gain_out, shift_out)


def shards(
    pair_repr,
    pair_mask,
    cotangent,
    proj_weight,
    proj_bias,
    norm_gain,
    norm_shift,
    out_weight,
    out_bias,
):
    channels = pair_repr.shape[3]
    hidden = out_weight.shape[1]
    pair_state = pair_repr[0]
    cell_mask = pair_mask[0].astype(jnp.float32)
    records = []
    for update in range(2):
        w_edge, w_gate, bias_edge, bias_gate, gain_in, shift_in, gain_out, shift_out = (
            update_weights(proj_weight, proj_bias, norm_gain, norm_shift, update, channels, hidden)
        )
        state_f = pair_state.astype(jnp.float32)
        normed = layer_norm(state_f, gain_in, shift_in, -1).astype(jnp.bfloat16)
        edge_pre = (
            jnp.einsum("rnc,cgh->ghrn", normed, w_edge, preferred_element_type=jnp.float32)
            + bias_edge
        )
        gate_pre = (
            jnp.einsum("rnc,cd->rnd", normed, w_gate, preferred_element_type=jnp.float32)
            + bias_gate
        )
        pair_edges = edge_pair(edge_pre, cell_mask)
        spread = lax.all_to_all(pair_edges, "dap", split_axis=1, concat_axis=2, tiled=True)
        product = lax.all_to_all(
            triangle(spread, update == 0), "dap", split_axis=1, concat_axis=0, tiled=True
        )
        mixed_norm = layer_norm(product.astype(jnp.float32), gain_out, shift_out, 0).astype(
            jnp.bfloat16
        )
        branch = (
            jnp.einsum(
                "hrn,hd->rnd", mixed_norm, out_weight[update], preferred_element_type=jnp.float32
            )
            + out_bias[update]
        )
        records.append(
            (state_f, normed, edge_pre, gate_pre, pair_edges, spread, product, mixed_norm, branch)
        )
        pair_state = (state_f + jax.nn.sigmoid(gate_pre) * branch).astype(jnp.bfloat16)
    upstream = cotangent[0].astype(jnp.float32)
    proj_grads = []
    out_grads = []
    for update in (1, 0):
        state_f, normed, edge_pre, gate_pre, pair_edges, spread, product, mixed_norm, branch = (
            records[update]
        )
        w_edge, w_gate, bias_edge, bias_gate, gain_in, shift_in, gain_out, shift_out = (
            update_weights(proj_weight, proj_bias, norm_gain, norm_shift, update, channels, hidden)
        )
        gate_value = jax.nn.sigmoid(gate_pre)
        grad_branch = (upstream * gate_value).astype(jnp.bfloat16)
        grad_gate = (upstream * branch * gate_value * (1.0 - gate_value)).astype(jnp.bfloat16)
        out_grad = jnp.einsum(
            "hrn,rnd->hd", mixed_norm, grad_branch, preferred_element_type=jnp.float32
        )
        grad_mixed = jnp.einsum(
            "rnd,hd->hrn", grad_branch, out_weight[update], preferred_element_type=jnp.float32
        )
        grad_product = norm_pullback(
            product.astype(jnp.float32), gain_out, shift_out, 0, grad_mixed
        ).astype(jnp.bfloat16)
        column_edges = spread
        column_grad = lax.all_to_all(
            grad_product[None], "dap", split_axis=1, concat_axis=2, tiled=True
        )[0]
        grad_pair = lax.all_to_all(
            triangle_pullback(column_edges, column_grad, update == 0),
            "dap",
            split_axis=2,
            concat_axis=1,
            tiled=True,
        )
        grad_edge = edge_pullback(edge_pre, cell_mask, grad_pair)
        edge_grad = jnp.einsum(
            "rnc,ghrn->cgh", normed, grad_edge, preferred_element_type=jnp.float32
        ).reshape(channels, 4 * hidden)
        gate_grad = jnp.einsum("rnc,rnd->cd", normed, grad_gate, preferred_element_type=jnp.float32)
        grad_normed = jnp.einsum(
            "ghrn,cgh->rnc", grad_edge, w_edge, preferred_element_type=jnp.float32
        )
        grad_normed = grad_normed + jnp.einsum(
            "rnd,cd->rnc", grad_gate, w_gate, preferred_element_type=jnp.float32
        )
        upstream = upstream + norm_pullback(state_f, gain_in, shift_in, -1, grad_normed)
        proj_part = jnp.concatenate([edge_grad, gate_grad], axis=1)
        proj_grads.append(proj_part)
        out_grads.append(out_grad)
    proj_total = jnp.stack(proj_grads[::-1])
    out_total = jnp.stack(out_grads[::-1])
    proj_total, out_total = lax.psum((proj_total, out_total), ("dp", "dap"))
    return (upstream.astype(jnp.bfloat16)[None], proj_total, out_total)


def solution(mesh):
    placed = (
        P("dp", "dap", None, None),
        P("dp", "dap", None),
        P("dp", "dap", None, None),
        P(),
        P(),
        P(),
        P(),
        P(),
        P(),
    )
    groups, parts = mesh.shape["dp"], mesh.shape["dap"]

    def program(*args):
        n, c = args[0].shape[2:]
        rows = n // parts
        fits = 20 * n * n * c * 4 <= CROP_BUDGET
        paired = all(size >= 4 and size & (size - 1) == 0 for size in (groups, parts))
        even = args[7].shape[1] == c == 128 and STEP_ROWS % rows == 0 and n == STEP_ROWS
        body = functools.partial(crop_shards, groups, parts) if fits and even and paired else shards
        return spread_over(body)(*args)

    def spread_over(body):
        return jax.shard_map(
            body,
            mesh=mesh,
            in_specs=placed,
            out_specs=(P("dp", "dap", None, None), P(), P()),
            check_vma=False,
        )

    return program
```

```python
import functools

import jax
import jax.numpy as jnp
from jax import lax
from jax.experimental import pallas as pl
from jax.experimental.pallas import tpu as pltpu
from jax.sharding import PartitionSpec as P

NORM_EPSILON = 1e-05
VMEM_BYTES = 16 * 1024 * 1024
PREPARE_BYTES = 63 * 1024 * 1024
CROP_BUDGET = 32 * 1024 * 1024
BLOCK_ROWS = 8
STEP_ROWS = 32
KEPT = 10
TAIL_ROWS = 16
F32 = jnp.float32
BF16 = jnp.bfloat16


def sigmoid(x):
    return 0.5 * jnp.tanh(0.5 * x) + 0.5


def dot(a, b, dims=((1,), (0,))):
    return lax.dot_general(a, b, (dims, ((), ())), preferred_element_type=F32)


def norm_parts(x):
    x = x.astype(F32)
    centred = x - jnp.mean(x, axis=-1, keepdims=True)
    rstd = lax.rsqrt(jnp.mean(centred * centred, axis=-1, keepdims=True) + NORM_EPSILON)
    return centred * rstd, jnp.broadcast_to(rstd, x.shape)


def norm_vjp(x_hat, rstd, grad):
    mean_grad = jnp.mean(grad, axis=-1, keepdims=True)
    mean_prod = jnp.mean(grad * x_hat, axis=-1, keepdims=True)
    return rstd * (grad - mean_grad - x_hat * mean_prod)


def pair_mask_block(length, first_row, rows, n, lanes):
    shape = (rows, n, lanes)
    i = lax.broadcasted_iota(jnp.int32, shape, 0) + first_row
    j = lax.broadcasted_iota(jnp.int32, shape, 1)
    inside = jnp.where((i < length) & (j < length), 1.0, 0.0)
    return inside.reshape(rows * n, lanes)


def project(x, mask, w, b, gain, shift):
    x_hat, rstd = norm_parts(x)
    normed = (x_hat * gain + shift).astype(BF16)
    pre = dot(normed, w) + b
    h = (pre.shape[1] - x.shape[1]) // 4
    s_left = sigmoid(pre[:, h : 2 * h]) * mask
    s_right = sigmoid(pre[:, 3 * h : 4 * h]) * mask
    left = s_left * pre[:, :h]
    right = s_right * pre[:, 2 * h : 3 * h]
    gate = sigmoid(pre[:, 4 * h :])
    return x_hat, rstd, normed, s_left, s_right, left, right, gate


def mix(product, gain, shift, w_out, b_out):
    p_hat, p_rstd = norm_parts(product)
    mixed = (p_hat * gain + shift).astype(BF16)
    return p_hat, p_rstd, mixed, dot(mixed, w_out) + b_out


def unmix(up, gate, branch, p_hat, p_rstd, gain, w_out):
    d_branch = up * gate
    d_gate = (d_branch * branch * (1.0 - gate)).astype(BF16)
    d_branch = d_branch.astype(BF16)
    d_mixed = dot(d_branch, w_out, ((1,), (1,))) * gain
    return d_branch, d_gate, norm_vjp(p_hat, p_rstd, d_mixed)


def contract(n, first, x, y):
    lanes = y.shape[1]
    tiles = (n // 8, 8, lanes)

    def step(e, totals):
        block = y[pl.ds(pl.multiple_of(e * n, n), n), :].reshape(tiles)
        return tuple(
            totals[a] + x[pl.ds((first + a) * n + e, 8, stride=0), :][None] * block
            for a in range(BLOCK_ROWS)
        )

    zero = jnp.zeros(tiles, F32)
    totals = lax.fori_loop(0, n, step, (zero,) * BLOCK_ROWS, unroll=True)
    return jnp.stack(totals).reshape(BLOCK_ROWS * n, lanes)


def edge_grads(d_edge, slope, edge):
    grads = (d_edge * slope).astype(BF16), (d_edge * edge * (1.0 - slope)).astype(BF16)
    return jnp.concatenate(grads, axis=1)


def tail_values(block, lanes_from, lanes_to):
    lane = lax.broadcasted_iota(jnp.int32, block.shape, block.ndim - 1)
    inside = (lane >= lanes_from) & (lane < lanes_to)
    return jnp.max(jnp.where(inside, block.astype(F32), 0.0)).astype(jnp.int32)


def own_place(pair_ref):
    return tail_values(pair_ref[0, -TAIL_ROWS:, :], 64, 128)


def place_of(own, jump, side):
    return own ^ (2 * jump) ^ side


def block(t, rows, n):
    return pl.ds(pl.multiple_of(t * rows * n, rows * n), rows * n)


def forward(n, jumps, *refs):
    pairs, refs = refs[: len(jumps)], refs[len(jumps) :]
    (weights, vectors), refs = refs[:2], refs[2:]
    (edges_s, slopes_s, gate_s, hat_s, rstd_s) = refs[:5]
    (p_hat_s, p_rstd_s, branch_s, normed_s, mixed_s) = refs[5:KEPT]
    (next_s,) = refs[KEPT:]
    c = weights.shape[1]
    width = weights.shape[2] - c
    rows = n // (2 * len(jumps))
    cells = rows * n
    tails = jnp.stack([pair[:, cells:, :] for pair in pairs])
    length = tail_values(tails, 0, 64)
    own = own_place(pairs[0])
    for pair, jump in zip(pairs, jumps):
        for side in range(2):
            next_s[block(place_of(own, jump, side), rows, n), :] = pair[side, :cells, :]
    steps = n // STEP_ROWS

    @pl.loop(0, 2)
    def _(u):
        row = jnp.where(u == 0, vectors[0:1, :], vectors[1:2, :])
        bias, gains, shifts, bias_out = vector_parts(row, c, width)

        @pl.loop(0, steps)
        def _(t):
            first = t * STEP_ROWS
            here = block(t, STEP_ROWS, n)
            mask = pair_mask_block(length, first, STEP_ROWS, n, c)
            x_hat, rstd, normed, s_left, s_right, left, right, gate = project(
                next_s[here, :], mask, weights[u, :, :width], bias, gains[:, :c], shifts[:, :c]
            )
            edges_s[u, 0, here, :] = left
            edges_s[u, 1, here, :] = right
            for r in range(STEP_ROWS):
                swapped = pl.ds(first + r, n, stride=n)
                edges_s[u, 2, swapped, :] = right[r * n : (r + 1) * n]
                edges_s[u, 3, swapped, :] = left[r * n : (r + 1) * n]
            slopes_s[u, 0, here, :] = s_left
            slopes_s[u, 1, here, :] = s_right
            gate_s[u, here, :] = gate
            hat_s[u, here, :] = x_hat
            rstd_s[u, here, :] = rstd
            normed_s[u, here, :] = normed

        @pl.loop(0, steps)
        def _(t):
            here = block(t, STEP_ROWS, n)
            x, y = edges_s.at[u, 3 * u], edges_s.at[u, 2 - u]
            product = [
                contract(n, t * STEP_ROWS + r, x, y) for r in range(0, STEP_ROWS, BLOCK_ROWS)
            ]
            p_hat, p_rstd, mixed, branch = mix(
                jnp.concatenate(product).astype(BF16), gains[:, c:], shifts[:, c:], weights[u, :, width:], bias_out
            )
            p_hat_s[u, here, :] = p_hat
            p_rstd_s[u, here, :] = p_rstd
            mixed_s[u, here, :] = mixed
            branch_s[u, here, :] = branch
            x = next_s[here, :].astype(F32)
            next_s[here, :] = (x + gate_s[u, here, :] * branch).astype(BF16)


def kept_parts(refs, u):
    return [ref.at[u] for ref in refs[:KEPT]]


def store_swapped(ref, rows, n, first, values):
    for r in range(rows):
        ref[pl.ds(first + r, n, stride=n), :] = values[r * n : (r + 1) * n]


def backward_second(n, jumps, pair, *refs):
    parted, refs = refs[: len(jumps)], refs[len(jumps) :]
    weights, vectors = refs[:2]
    (edges_s, slopes_s, gate_s, _, _, *kept) = kept_parts(refs[2:], 1)
    (p_hat_s, p_rstd_s, branch_s, normed_s, mixed_s) = kept
    d_pre_s, cot_s, grads_ref, d_product_s, d_edges_s = refs[2 + KEPT :]
    c, h = weights.shape[1], edges_s.shape[2]
    width = 4 * h + c
    gain = vector_parts(vectors[1:2, :], c, width)[1]
    own = own_place(pair)
    for part, jump in zip(parted, jumps):
        for side in range(2):
            cot_s[block(place_of(own, jump, side), part.shape[1] // n, n), :] = part[side]

    @pl.loop(0, n // STEP_ROWS)
    def _(t):
        here = block(t, STEP_ROWS, n)
        d_branch, d_gate, d_product = unmix(
            cot_s[here, :].astype(F32),
            gate_s[here, :],
            branch_s[here, :],
            p_hat_s[here, :],
            p_rstd_s[here, :],
            gain[:, c:],
            weights[1, :, width:],
        )
        d_out = dot(mixed_s[here, :], d_branch, ((0,), (0,)))
        d_pre_s[here, 4 * h :] = d_gate
        d_product_s[1, here, :] = d_product
        store_swapped(d_product_s.at[0], STEP_ROWS, n, t * STEP_ROWS, d_product)
        grads_ref[:, width:] = d_out.astype(BF16)

    blocks = n // BLOCK_ROWS

    @pl.loop(0, 2 * blocks)
    def _(step):
        side, t = step // blocks, step % blocks
        d_edges_s[side, block(t, BLOCK_ROWS, n), :] = contract(
            n, t * BLOCK_ROWS, edges_s.at[1 - side], d_product_s.at[side]
        )

    @pl.loop(0, n // STEP_ROWS)
    def _(t):
        here = block(t, STEP_ROWS, n)
        grads = [
            edge_grads(d_edges_s[side, here, :], slopes_s[side, here, :], edges_s[side, here, :])
            for side in range(2)
        ]
        d_pre = jnp.concatenate([*grads, d_pre_s[here, 4 * h :]], axis=1)
        d_pre_s[here, : 4 * h] = d_pre[:, : 4 * h]
        grads_ref[:, :width] = dot(normed_s[here, :], d_pre, ((0,), (0,))).astype(BF16)


def backward_left(n, d_pre_1_ref, cot_ref, weights, vectors, *refs):
    hat_1_s, rstd_1_s = kept_parts(refs, 1)[3:5]
    (edges_s, slopes_s, gate_s, _, _, *kept) = kept_parts(refs, 0)
    (p_hat_s, p_rstd_s, branch_s, normed_s, mixed_s) = kept
    up_ref, d_pre_ref, d_product_t_ref, grads_ref, d_product_s, d_edge_s = refs[KEPT:]
    c, h = weights.shape[1], edges_s.shape[2]
    width = 4 * h + c
    gain, gain_1 = (vector_parts(vectors[u : u + 1, :], c, width)[1] for u in range(2))

    @pl.loop(0, n // STEP_ROWS)
    def _(t):
        here = block(t, STEP_ROWS, n)
        d_normed = dot(d_pre_1_ref[here, :], weights[1, :, :width], ((1,), (1,)))
        pulled = norm_vjp(hat_1_s[here, :], rstd_1_s[here, :], d_normed * gain_1[:, :c])
        up = cot_ref[here, :].astype(F32) + pulled
        up_ref[here, :] = up
        d_branch, d_gate, d_product = unmix(
            up,
            gate_s[here, :],
            branch_s[here, :],
            p_hat_s[here, :],
            p_rstd_s[here, :],
            gain[:, c:],
            weights[0, :, width:],
        )
        d_out = dot(mixed_s[here, :], d_branch, ((0,), (0,)))
        d_pre_ref[here, 2 * h :] = d_gate
        d_product_s[here, :] = d_product
        store_swapped(d_product_t_ref, STEP_ROWS, n, t * STEP_ROWS, d_product)
        grads_ref[:, 2 * h + c :] = d_out.astype(BF16)

    one_side(n, 0, d_product_s, edges_s, slopes_s, d_edge_s, d_pre_ref)
    d_pre = dot(normed_s[...], d_pre_ref[...], ((0,), (0,)))
    grads_ref[:, : 2 * h + c] = d_pre.astype(BF16)


def backward_right(n, d_product_t_ref, *refs):
    (edges_s, slopes_s, *kept) = kept_parts(refs, 0)
    normed_s = kept[-2]
    d_pre_ref, grads_ref, d_edge_s = refs[KEPT:]
    one_side(n, 1, d_product_t_ref, edges_s, slopes_s, d_edge_s, d_pre_ref)
    grads_ref[...] = dot(normed_s[...], d_pre_ref[...], ((0,), (0,))).astype(BF16)


def one_side(n, side, x, edges_s, slopes_s, d_edge_s, d_pre_ref):
    h = edges_s.shape[2]

    @pl.loop(0, n // BLOCK_ROWS)
    def _(t):
        d_edge_s[block(t, BLOCK_ROWS, n), :] = contract(
            n, t * BLOCK_ROWS, x, edges_s.at[1 - side]
        )

    @pl.loop(0, n // STEP_ROWS)
    def _(t):
        here = block(t, STEP_ROWS, n)
        d_pre_ref[here, : 2 * h] = edge_grads(
            d_edge_s[here, :], slopes_s[side, here, :], edges_s[side, here, :]
        )


def own_rows(
    pair_ref, up_ref, d_left_ref, d_right_ref, weights, vectors, hat_ref, rstd_ref, out_ref
):
    cells, c = out_ref.shape
    half = d_right_ref.shape[1]
    place = own_place(pair_ref)
    own = pl.ds(pl.multiple_of(place * cells, cells), cells)
    width = d_left_ref.shape[1] + half
    gain = vector_parts(vectors[0:1, :], c, width)[1]
    d_left, d_right = d_left_ref[own, :], d_right_ref[own, :]
    d_pre = jnp.concatenate([d_left[:, :half], d_right, d_left[:, half:]], axis=1)
    d_normed = dot(d_pre, weights[0, :, :width], ((1,), (1,))) * gain[:, :c]
    pulled = norm_vjp(hat_ref[0, own, :], rstd_ref[0, own, :], d_normed)
    out_ref[...] = (up_ref[own, :] + pulled).astype(BF16)


def exchange(value, axis, size, step):
    return lax.ppermute(value, axis, [(d, d ^ step) for d in range(size)])


def near_rounds(value, groups):
    other = exchange(value, "dp", groups, 1)
    step = 2
    while step < groups // 2:
        value = add_narrow(value, other)
        other = exchange(value, "dp", groups, step)
        step *= 2
    return value, other


def add_narrow(a, b):
    return (a.astype(F32) + b.astype(F32)).astype(BF16)


def prepare(
    index_ref, mask_ref, state_ref, cot_ref, w, w_out, b, gain, shift, b_out, *refs
):
    sent_ref, weights_ref, vectors_ref, mask_s, sems = refs
    cells, c = state_ref.shape
    below, width = cells + TAIL_ROWS, w.shape[2]
    copies = [(mask_ref, mask_s), (state_ref, sent_ref.at[:cells]), (cot_ref, sent_ref.at[below:])]
    copies += [(w, weights_ref.at[:, :, :width]), (w_out, weights_ref.at[:, :, width:])]
    first = 0
    for vector in (b, gain, shift, b_out):
        last = first + vector.shape[1]
        copies.append((vector, vectors_ref.at[:, first:last]))
        first = last
    copies = [pltpu.make_async_copy(*pair, sems.at[k]) for k, pair in enumerate(copies)]
    for copy in copies:
        copy.start()
    copies[0].wait()
    length = jnp.max(jnp.sum(mask_s[...].astype(F32), axis=1, keepdims=True))
    in_length = lax.broadcasted_iota(jnp.int32, (TAIL_ROWS, c), 1) < 64
    place = index_ref[0].astype(F32)
    sent_ref[cells:below, :] = jnp.where(in_length, length, place).astype(BF16)
    for copy in copies[1:]:
        copy.wait()


def pair_up(near_ref, far_ref, state_ref, cot_ref):
    split = state_ref.shape[1]
    for side, ref in enumerate((near_ref, far_ref)):
        state_ref[side] = ref[:split, :]
        cot_ref[side] = ref[split:, :]


def hold(weights_in, vectors_in, weights_out, vectors_out):
    weights_out[...] = weights_in[...]
    vectors_out[...] = vectors_in[...]


def vector_parts(row, c, width):
    ends = [width, width + 2 * c, width + 4 * c, width + 5 * c]
    return [row[:, first:last] for first, last in zip([0] + ends, ends)]


def add_grads(rest, rest_near, left, left_near, right, right_far, proj_ref, out_ref):
    width = proj_ref.shape[2]
    c = out_ref.shape[2]
    half = (width - c) // 2
    total = rest[:, : width + c].astype(F32) + rest_near[:, : width + c].astype(F32)
    proj_ref[1] = total[:, :width]
    out_ref[1] = total[:, width:]
    total = left[...].astype(F32) + left_near[...].astype(F32)
    proj_ref[0, :, :half] = total[:, :half]
    proj_ref[0, :, 2 * half :] = total[:, half : half + c]
    out_ref[0] = total[:, half + c :]
    proj_ref[0, :, half : 2 * half] = right[...].astype(F32) + right_far[...].astype(F32)


def crop_shards(
    groups,
    parts,
    pair_repr,
    pair_mask,
    cotangent,
    proj_weight,
    proj_bias,
    norm_gain,
    norm_shift,
    out_weight,
    out_bias,
):
    _, rows, n, c = pair_repr.shape
    h = out_weight.shape[1]
    width = proj_weight.shape[2]
    cells, pairs = rows * n, n * n
    plane = (pairs + 8, h)
    kept = [jax.ShapeDtypeStruct((2, 4) + plane, F32), jax.ShapeDtypeStruct((2, 2) + plane, F32)]
    kept += [jax.ShapeDtypeStruct((2,) + plane, F32)] * 6
    kept += [jax.ShapeDtypeStruct((2, pairs, h), BF16)] * 2
    grads = jax.ShapeDtypeStruct((c, width + c), BF16)
    vmem = pl.BlockSpec(memory_space=pltpu.VMEM)
    main = pl.BlockSpec(memory_space=pltpu.HBM)
    params = pltpu.CompilerParams(vmem_limit_bytes=VMEM_BYTES)

    def cost(planes):
        flops = 4 * pairs * width * c
        return pl.CostEstimate(
            flops=flops, bytes_accessed=planes * pairs * c * 4, transcendentals=0
        )

    packed = (
        jax.ShapeDtypeStruct((2, c, width + c), BF16),
        jax.ShapeDtypeStruct((2, width + 5 * c), F32),
    )
    sent, *weights = pl.pallas_call(
        prepare,
        out_shape=(jax.ShapeDtypeStruct((2 * cells + TAIL_ROWS, c), BF16),) + packed,
        in_specs=[pl.BlockSpec(memory_space=pltpu.SMEM)] + [main] * 9,
        out_specs=[vmem] * 3,
        scratch_shapes=[pltpu.VMEM((rows, n), jnp.int32), pltpu.SemaphoreType.DMA((9,))],
        compiler_params=pltpu.CompilerParams(vmem_limit_bytes=PREPARE_BYTES),
        name="prepare",
    )(
        lax.axis_index("dap").astype(jnp.int32)[None],
        pair_mask[0],
        pair_repr.reshape(cells, c),
        cotangent.reshape(cells, c),
        proj_weight,
        out_weight,
        proj_bias,
        norm_gain,
        norm_shift,
        out_bias,
    )
    weights = pl.pallas_call(
        hold,
        out_shape=packed,
        in_specs=[vmem] * 2,
        out_specs=[vmem] * 2,
        compiler_params=params,
        cost_estimate=cost(8),
        name="hold",
    )(*weights)
    beside = exchange(sent, "dap", parts, 1)
    beside, *weights = lax.optimization_barrier((beside, *weights))
    state, cot = pl.pallas_call(
        pair_up,
        out_shape=(
            jax.ShapeDtypeStruct((2, cells + TAIL_ROWS, c), BF16),
            jax.ShapeDtypeStruct((2, cells, c), BF16),
        ),
        in_specs=[vmem] * 2,
        out_specs=[vmem] * 2,
        compiler_params=params,
        name="pair_up",
    )(sent, beside)
    states, cots = [state], [cot]
    half = parts // 2
    jumps = [0, *range(1, half // 2), *reversed(range(half // 2, half))]
    states += [exchange(state, "dap", parts, 2 * jump) for jump in jumps[1:]]
    cot_jumps = [0, *reversed(range(1, half))]
    cots += [exchange(cot, "dap", parts, 2 * jump) for jump in cot_jumps[1:]]

    held = pl.pallas_call(
        functools.partial(forward, n, jumps),
        out_shape=kept,
        in_specs=[vmem] * (half + 2),
        out_specs=(vmem,) * KEPT,
        scratch_shapes=[pltpu.VMEM((pairs, c), BF16)],
        compiler_params=params,
        cost_estimate=cost(64),
        name="forward",
    )(*states, *weights)

    double, single = pltpu.VMEM((2,) + plane, F32), pltpu.VMEM(plane, F32)
    d_pre_1, cot, grads_1 = pl.pallas_call(
        functools.partial(backward_second, n, cot_jumps),
        out_shape=(
            jax.ShapeDtypeStruct((pairs, width), BF16),
            jax.ShapeDtypeStruct((pairs, c), BF16),
            grads,
        ),
        in_specs=[vmem] * (3 + half + KEPT),
        out_specs=[vmem] * 3,
        scratch_shapes=[double, double],
        compiler_params=params,
        cost_estimate=cost(48),
        name="backward_second",
    )(states[0], *cots, *weights, *held)
    far = groups // 2
    others_1 = exchange(grads_1, "dp", groups, far)

    up_1, d_left, d_product_t, grads_left = pl.pallas_call(
        functools.partial(backward_left, n),
        out_shape=(
            jax.ShapeDtypeStruct((pairs, c), F32),
            jax.ShapeDtypeStruct((pairs, 2 * h + c), BF16),
            jax.ShapeDtypeStruct(plane, F32),
            jax.ShapeDtypeStruct((c, 2 * h + 2 * c), BF16),
        ),
        in_specs=[vmem] * (4 + KEPT),
        out_specs=[vmem] * 4,
        scratch_shapes=[single, single],
        compiler_params=params,
        cost_estimate=cost(24),
        name="backward_left",
    )(d_pre_1, cot, *weights, *held)
    others_left = exchange(grads_left, "dp", groups, far)

    d_right, grads_right = pl.pallas_call(
        functools.partial(backward_right, n),
        out_shape=(
            jax.ShapeDtypeStruct((pairs, 2 * h), BF16),
            jax.ShapeDtypeStruct((c, 2 * h), BF16),
        ),
        in_specs=[vmem] * (1 + KEPT),
        out_specs=[vmem] * 2,
        scratch_shapes=[single],
        compiler_params=params,
        cost_estimate=cost(24),
        name="backward_right",
    )(d_product_t, *held)
    pair_grad = pl.pallas_call(
        own_rows,
        out_shape=jax.ShapeDtypeStruct((cells, c), BF16),
        in_specs=[vmem] * 8,
        out_specs=vmem,
        compiler_params=params,
        cost_estimate=cost(8),
        name="own_rows",
    )(states[0], up_1, d_left, d_right, *weights, held[3], held[4])

    rest, rest_near = near_rounds(
        jnp.concatenate([add_narrow(grads_1, others_1), grads_right], axis=1), groups
    )
    right = add_narrow(rest[:, width + c :], rest_near[:, width + c :])
    right_far = exchange(right, "dp", groups, far)
    ends_left = near_rounds(add_narrow(grads_left, others_left), groups)

    proj_total, out_total = pl.pallas_call(
        add_grads,
        out_shape=(
            jax.ShapeDtypeStruct((2, c, width), F32),
            jax.ShapeDtypeStruct((2, h, c), F32),
        ),
        in_specs=[vmem] * 6,
        out_specs=(vmem, vmem),
        compiler_params=params,
        name="add_grads",
    )(rest, rest_near, *ends_left, right, right_far)
    return pair_grad.reshape(pair_repr.shape), proj_total, out_total


def layer_norm(values, gain_vec, shift_vec, norm_axis):
    mean_value = jnp.mean(values, axis=norm_axis, keepdims=True)
    centred = values - mean_value
    variance = jnp.mean(centred * centred, axis=norm_axis, keepdims=True)
    return centred * lax.rsqrt(variance + NORM_EPSILON) * gain_vec + shift_vec


def norm_pullback(values, gain_vec, shift_vec, norm_axis, upstream):
    _, pull_back = jax.vjp(
        lambda inner_value: layer_norm(inner_value, gain_vec, shift_vec, norm_axis), values
    )
    return pull_back(upstream)[0]


def edge_pair(edge_pre, cell_mask):
    left_edge = jax.nn.sigmoid(edge_pre[1]) * edge_pre[0] * cell_mask
    right_edge = jax.nn.sigmoid(edge_pre[3]) * edge_pre[2] * cell_mask
    return jnp.stack([left_edge, right_edge]).astype(jnp.bfloat16)


def edge_pullback(edge_pre, cell_mask, grad_pair):
    sig_left = jax.nn.sigmoid(edge_pre[1])
    sig_right = jax.nn.sigmoid(edge_pre[3])
    grad_left = grad_pair[0].astype(jnp.float32) * cell_mask
    grad_right = grad_pair[1].astype(jnp.float32) * cell_mask
    return jnp.stack(
        [
            grad_left * sig_left,
            grad_left * edge_pre[0] * sig_left * (1.0 - sig_left),
            grad_right * sig_right,
            grad_right * edge_pre[2] * sig_right * (1.0 - sig_right),
        ]
    ).astype(jnp.bfloat16)


def triangle(pair_edges, outgoing):
    if outgoing:
        einsum_form = "cik,cjk->cij"
    else:
        einsum_form = "cki,ckj->cij"
    return jnp.einsum(
        einsum_form, pair_edges[0], pair_edges[1], preferred_element_type=jnp.float32
    ).astype(jnp.bfloat16)


def triangle_pullback(pair_edges, grad_product, outgoing):
    left_edge = pair_edges[0]
    right_edge = pair_edges[1]
    if outgoing:
        grad_left = jnp.einsum(
            "cij,cjk->cik", grad_product, right_edge, preferred_element_type=jnp.float32
        )
        grad_right = jnp.einsum(
            "cij,cik->cjk", grad_product, left_edge, preferred_element_type=jnp.float32
        )
    else:
        grad_left = jnp.einsum(
            "ckj,cij->cki", right_edge, grad_product, preferred_element_type=jnp.float32
        )
        grad_right = jnp.einsum(
            "cki,cij->ckj", left_edge, grad_product, preferred_element_type=jnp.float32
        )
    return jnp.stack([grad_left, grad_right]).astype(jnp.bfloat16)


def update_weights(proj_weight, proj_bias, norm_gain, norm_shift, update, channels, hidden):
    w_edge = proj_weight[update, :, : 4 * hidden].reshape(channels, 4, hidden)
    w_gate = proj_weight[update, :, 4 * hidden :]
    bias_edge = proj_bias[update, : 4 * hidden].reshape(4, hidden, 1, 1)
    bias_gate = proj_bias[update, 4 * hidden :]
    gain_in = norm_gain[update, :channels]
    shift_in = norm_shift[update, :channels]
    gain_out = norm_gain[update, channels:][:, None, None]
    shift_out = norm_shift[update, channels:][:, None, None]
    return (w_edge, w_gate, bias_edge, bias_gate, gain_in, shift_in, gain_out, shift_out)


def shards(
    pair_repr,
    pair_mask,
    cotangent,
    proj_weight,
    proj_bias,
    norm_gain,
    norm_shift,
    out_weight,
    out_bias,
):
    channels = pair_repr.shape[3]
    hidden = out_weight.shape[1]
    pair_state = pair_repr[0]
    cell_mask = pair_mask[0].astype(jnp.float32)
    records = []
    for update in range(2):
        w_edge, w_gate, bias_edge, bias_gate, gain_in, shift_in, gain_out, shift_out = (
            update_weights(proj_weight, proj_bias, norm_gain, norm_shift, update, channels, hidden)
        )
        state_f = pair_state.astype(jnp.float32)
        normed = layer_norm(state_f, gain_in, shift_in, -1).astype(jnp.bfloat16)
        edge_pre = (
            jnp.einsum("rnc,cgh->ghrn", normed, w_edge, preferred_element_type=jnp.float32)
            + bias_edge
        )
        gate_pre = (
            jnp.einsum("rnc,cd->rnd", normed, w_gate, preferred_element_type=jnp.float32)
            + bias_gate
        )
        pair_edges = edge_pair(edge_pre, cell_mask)
        spread = lax.all_to_all(pair_edges, "dap", split_axis=1, concat_axis=2, tiled=True)
        product = lax.all_to_all(
            triangle(spread, update == 0), "dap", split_axis=1, concat_axis=0, tiled=True
        )
        mixed_norm = layer_norm(product.astype(jnp.float32), gain_out, shift_out, 0).astype(
            jnp.bfloat16
        )
        branch = (
            jnp.einsum(
                "hrn,hd->rnd", mixed_norm, out_weight[update], preferred_element_type=jnp.float32
            )
            + out_bias[update]
        )
        records.append(
            (state_f, normed, edge_pre, gate_pre, pair_edges, spread, product, mixed_norm, branch)
        )
        pair_state = (state_f + jax.nn.sigmoid(gate_pre) * branch).astype(jnp.bfloat16)
    upstream = cotangent[0].astype(jnp.float32)
    proj_grads = []
    out_grads = []
    for update in (1, 0):
        state_f, normed, edge_pre, gate_pre, pair_edges, spread, product, mixed_norm, branch = (
            records[update]
        )
        w_edge, w_gate, bias_edge, bias_gate, gain_in, shift_in, gain_out, shift_out = (
            update_weights(proj_weight, proj_bias, norm_gain, norm_shift, update, channels, hidden)
        )
        gate_value = jax.nn.sigmoid(gate_pre)
        grad_branch = (upstream * gate_value).astype(jnp.bfloat16)
        grad_gate = (upstream * branch * gate_value * (1.0 - gate_value)).astype(jnp.bfloat16)
        out_grad = jnp.einsum(
            "hrn,rnd->hd", mixed_norm, grad_branch, preferred_element_type=jnp.float32
        )
        grad_mixed = jnp.einsum(
            "rnd,hd->hrn", grad_branch, out_weight[update], preferred_element_type=jnp.float32
        )
        grad_product = norm_pullback(
            product.astype(jnp.float32), gain_out, shift_out, 0, grad_mixed
        ).astype(jnp.bfloat16)
        column_edges = spread
        column_grad = lax.all_to_all(
            grad_product[None], "dap", split_axis=1, concat_axis=2, tiled=True
        )[0]
        grad_pair = lax.all_to_all(
            triangle_pullback(column_edges, column_grad, update == 0),
            "dap",
            split_axis=2,
            concat_axis=1,
            tiled=True,
        )
        grad_edge = edge_pullback(edge_pre, cell_mask, grad_pair)
        edge_grad = jnp.einsum(
            "rnc,ghrn->cgh", normed, grad_edge, preferred_element_type=jnp.float32
        ).reshape(channels, 4 * hidden)
        gate_grad = jnp.einsum("rnc,rnd->cd", normed, grad_gate, preferred_element_type=jnp.float32)
        grad_normed = jnp.einsum(
            "ghrn,cgh->rnc", grad_edge, w_edge, preferred_element_type=jnp.float32
        )
        grad_normed = grad_normed + jnp.einsum(
            "rnd,cd->rnc", grad_gate, w_gate, preferred_element_type=jnp.float32
        )
        upstream = upstream + norm_pullback(state_f, gain_in, shift_in, -1, grad_normed)
        proj_part = jnp.concatenate([edge_grad, gate_grad], axis=1)
        proj_grads.append(proj_part)
        out_grads.append(out_grad)
    proj_total = jnp.stack(proj_grads[::-1])
    out_total = jnp.stack(out_grads[::-1])
    proj_total, out_total = lax.psum((proj_total, out_total), ("dp", "dap"))
    return (upstream.astype(jnp.bfloat16)[None], proj_total, out_total)


def solution(mesh):
    placed = (
        P("dp", "dap", None, None),
        P("dp", "dap", None),
        P("dp", "dap", None, None),
        P(),
        P(),
        P(),
        P(),
        P(),
        P(),
    )
    groups, parts = mesh.shape["dp"], mesh.shape["dap"]

    def program(*args):
        n, c = args[0].shape[2:]
        rows = n // parts
        fits = 20 * n * n * c * 4 <= CROP_BUDGET
        paired = all(size >= 4 and size & (size - 1) == 0 for size in (groups, parts))
        even = args[7].shape[1] == c == 128 and STEP_ROWS % rows == 0 and n == STEP_ROWS
        body = functools.partial(crop_shards, groups, parts) if fits and even and paired else shards
        return spread_over(body)(*args)

    def spread_over(body):
        return jax.shard_map(
            body,
            mesh=mesh,
            in_specs=placed,
            out_specs=(P("dp", "dap", None, None), P(), P()),
            check_vma=False,
        )

    return program
```

```python
import functools

import jax
import jax.numpy as jnp
from jax import lax
from jax.experimental import pallas as pl
from jax.experimental.pallas import tpu as pltpu
from jax.sharding import PartitionSpec as P

NORM_EPSILON = 1e-05
VMEM_BYTES = 16 * 1024 * 1024
PREPARE_BYTES = 63 * 1024 * 1024
CROP_BUDGET = 32 * 1024 * 1024
BLOCK_ROWS = 8
STEP_ROWS = 32
KEPT = 10
TAIL_ROWS = 16
F32 = jnp.float32
BF16 = jnp.bfloat16


def sigmoid(x):
    return 0.5 * jnp.tanh(0.5 * x) + 0.5


def dot(a, b, dims=((1,), (0,))):
    return lax.dot_general(a, b, (dims, ((), ())), preferred_element_type=F32)


def norm_parts(x):
    x = x.astype(F32)
    centred = x - jnp.mean(x, axis=-1, keepdims=True)
    rstd = lax.rsqrt(jnp.mean(centred * centred, axis=-1, keepdims=True) + NORM_EPSILON)
    return centred * rstd, jnp.broadcast_to(rstd, x.shape)


def norm_vjp(x_hat, rstd, grad):
    mean_grad = jnp.mean(grad, axis=-1, keepdims=True)
    mean_prod = jnp.mean(grad * x_hat, axis=-1, keepdims=True)
    return rstd * (grad - mean_grad - x_hat * mean_prod)


def pair_mask_block(length, first_row, rows, n, lanes):
    shape = (rows, n, lanes)
    i = lax.broadcasted_iota(jnp.int32, shape, 0) + first_row
    j = lax.broadcasted_iota(jnp.int32, shape, 1)
    inside = jnp.where((i < length) & (j < length), 1.0, 0.0)
    return inside.reshape(rows * n, lanes)


def project(x, mask, w, b, gain, shift):
    x_hat, rstd = norm_parts(x)
    normed = (x_hat * gain + shift).astype(BF16)
    pre = dot(normed, w) + b
    h = (pre.shape[1] - x.shape[1]) // 4
    s_left = sigmoid(pre[:, h : 2 * h]) * mask
    s_right = sigmoid(pre[:, 3 * h : 4 * h]) * mask
    left = s_left * pre[:, :h]
    right = s_right * pre[:, 2 * h : 3 * h]
    gate = sigmoid(pre[:, 4 * h :])
    return x_hat, rstd, normed, s_left, s_right, left, right, gate


def mix(product, gain, shift, w_out, b_out):
    p_hat, p_rstd = norm_parts(product)
    mixed = (p_hat * gain + shift).astype(BF16)
    return p_hat, p_rstd, mixed, dot(mixed, w_out) + b_out


def unmix(up, gate, branch, p_hat, p_rstd, gain, w_out):
    d_branch = up * gate
    d_gate = (d_branch * branch * (1.0 - gate)).astype(BF16)
    d_branch = d_branch.astype(BF16)
    d_mixed = dot(d_branch, w_out, ((1,), (1,))) * gain
    return d_branch, d_gate, norm_vjp(p_hat, p_rstd, d_mixed)


def contract(n, first, x, y):
    lanes = y.shape[1]
    tiles = (n // 8, 8, lanes)

    def step(e, totals):
        block = y[pl.ds(pl.multiple_of(e * n, n), n), :].reshape(tiles)
        return tuple(
            totals[a] + x[pl.ds((first + a) * n + e, 8, stride=0), :][None] * block
            for a in range(BLOCK_ROWS)
        )

    zero = jnp.zeros(tiles, F32)
    totals = lax.fori_loop(0, n, step, (zero,) * BLOCK_ROWS, unroll=True)
    return jnp.stack(totals).reshape(BLOCK_ROWS * n, lanes)


def edge_grads(d_edge, slope, edge):
    grads = (d_edge * slope).astype(BF16), (d_edge * edge * (1.0 - slope)).astype(BF16)
    return jnp.concatenate(grads, axis=1)


def tail_values(block, lanes_from, lanes_to):
    lane = lax.broadcasted_iota(jnp.int32, block.shape, block.ndim - 1)
    inside = (lane >= lanes_from) & (lane < lanes_to)
    return jnp.max(jnp.where(inside, block.astype(F32), 0.0)).astype(jnp.int32)


def own_place(pair_ref):
    return tail_values(pair_ref[0, -TAIL_ROWS:, :], 64, 128)


def place_of(own, jump, side):
    return own ^ (2 * jump) ^ side


def block(t, rows, n):
    return pl.ds(pl.multiple_of(t * rows * n, rows * n), rows * n)


def forward(n, jumps, *refs):
    pairs, refs = refs[: len(jumps)], refs[len(jumps) :]
    (weights, vectors), refs = refs[:2], refs[2:]
    (edges_s, slopes_s, gate_s, hat_s, rstd_s) = refs[:5]
    (p_hat_s, p_rstd_s, branch_s, normed_s, mixed_s) = refs[5:KEPT]
    (next_s,) = refs[KEPT:]
    c = weights.shape[1]
    width = weights.shape[2] - c
    rows = n // (2 * len(jumps))
    cells = rows * n
    tails = jnp.stack([pair[:, cells:, :] for pair in pairs])
    length = tail_values(tails, 0, 64)
    own = own_place(pairs[0])
    for pair, jump in zip(pairs, jumps):
        for side in range(2):
            next_s[block(place_of(own, jump, side), rows, n), :] = pair[side, :cells, :]
    steps = n // STEP_ROWS

    @pl.loop(0, 2)
    def _(u):
        row = jnp.where(u == 0, vectors[0:1, :], vectors[1:2, :])
        bias, gains, shifts, bias_out = vector_parts(row, c, width)

        @pl.loop(0, steps)
        def _(t):
            first = t * STEP_ROWS
            here = block(t, STEP_ROWS, n)
            mask = pair_mask_block(length, first, STEP_ROWS, n, c)
            x_hat, rstd, normed, s_left, s_right, left, right, gate = project(
                next_s[here, :], mask, weights[u, :, :width], bias, gains[:, :c], shifts[:, :c]
            )
            edges_s[u, 0, here, :] = left
            edges_s[u, 1, here, :] = right
            for r in range(STEP_ROWS):
                swapped = pl.ds(first + r, n, stride=n)
                edges_s[u, 2, swapped, :] = right[r * n : (r + 1) * n]
                edges_s[u, 3, swapped, :] = left[r * n : (r + 1) * n]
            slopes_s[u, 0, here, :] = s_left
            slopes_s[u, 1, here, :] = s_right
            gate_s[u, here, :] = gate
            hat_s[u, here, :] = x_hat
            rstd_s[u, here, :] = rstd
            normed_s[u, here, :] = normed

        @pl.loop(0, steps)
        def _(t):
            here = block(t, STEP_ROWS, n)
            x, y = edges_s.at[u, 3 * u], edges_s.at[u, 2 - u]
            product = [
                contract(n, t * STEP_ROWS + r, x, y) for r in range(0, STEP_ROWS, BLOCK_ROWS)
            ]
            p_hat, p_rstd, mixed, branch = mix(
                jnp.concatenate(product).astype(BF16), gains[:, c:], shifts[:, c:], weights[u, :, width:], bias_out
            )
            p_hat_s[u, here, :] = p_hat
            p_rstd_s[u, here, :] = p_rstd
            mixed_s[u, here, :] = mixed
            branch_s[u, here, :] = branch
            x = next_s[here, :].astype(F32)
            next_s[here, :] = (x + gate_s[u, here, :] * branch).astype(BF16)


def kept_parts(refs, u):
    return [ref.at[u] for ref in refs[:KEPT]]


def store_swapped(ref, rows, n, first, values):
    for r in range(rows):
        ref[pl.ds(first + r, n, stride=n), :] = values[r * n : (r + 1) * n]


def backward_second(n, jumps, pair, *refs):
    parted, refs = refs[: len(jumps)], refs[len(jumps) :]
    weights, vectors = refs[:2]
    (edges_s, slopes_s, gate_s, hat_s, rstd_s, *kept) = kept_parts(refs[2:], 1)
    (p_hat_s, p_rstd_s, branch_s, normed_s, mixed_s) = kept
    up_ref, grads_ref, d_product_s, d_edges_s, d_pre_s, cot_s = refs[2 + KEPT :]
    c, h = weights.shape[1], edges_s.shape[2]
    width = 4 * h + c
    gain = vector_parts(vectors[1:2, :], c, width)[1]
    own = own_place(pair)
    for part, jump in zip(parted, jumps):
        for side in range(2):
            cot_s[block(place_of(own, jump, side), part.shape[1] // n, n), :] = part[side]

    @pl.loop(0, n // STEP_ROWS)
    def _(t):
        here = block(t, STEP_ROWS, n)
        d_branch, d_gate, d_product = unmix(
            cot_s[here, :].astype(F32),
            gate_s[here, :],
            branch_s[here, :],
            p_hat_s[here, :],
            p_rstd_s[here, :],
            gain[:, c:],
            weights[1, :, width:],
        )
        d_out = dot(mixed_s[here, :], d_branch, ((0,), (0,)))
        d_pre_s[here, 4 * h :] = d_gate
        d_product_s[1, here, :] = d_product
        store_swapped(d_product_s.at[0], STEP_ROWS, n, t * STEP_ROWS, d_product)
        grads_ref[:, width:] = d_out.astype(BF16)

    blocks = n // BLOCK_ROWS

    @pl.loop(0, 2 * blocks)
    def _(step):
        side, t = step // blocks, step % blocks
        d_edges_s[side, block(t, BLOCK_ROWS, n), :] = contract(
            n, t * BLOCK_ROWS, edges_s.at[1 - side], d_product_s.at[side]
        )

    @pl.loop(0, n // STEP_ROWS)
    def _(t):
        here = block(t, STEP_ROWS, n)
        grads = [
            edge_grads(d_edges_s[side, here, :], slopes_s[side, here, :], edges_s[side, here, :])
            for side in range(2)
        ]
        d_pre = jnp.concatenate([*grads, d_pre_s[here, 4 * h :]], axis=1)
        normed = normed_s[here, :]
        d_normed = dot(d_pre, weights[1, :, :width], ((1,), (1,))) * gain[:, :c]
        pulled = norm_vjp(hat_s[here, :], rstd_s[here, :], d_normed)
        up_ref[here, :] = cot_s[here, :].astype(F32) + pulled
        grads_ref[:, :width] = dot(normed, d_pre, ((0,), (0,))).astype(BF16)


def backward_left(n, up_in_ref, weights, vectors, *refs):
    (edges_s, slopes_s, gate_s, _, _, *kept) = kept_parts(refs, 0)
    (p_hat_s, p_rstd_s, branch_s, normed_s, mixed_s) = kept
    d_pre_ref, d_product_t_ref, grads_ref, d_product_s, d_edge_s = refs[KEPT:]
    c, h = weights.shape[1], edges_s.shape[2]
    width = 4 * h + c
    gain = vector_parts(vectors[0:1, :], c, width)[1]

    @pl.loop(0, n // STEP_ROWS)
    def _(t):
        here = block(t, STEP_ROWS, n)
        d_branch, d_gate, d_product = unmix(
            up_in_ref[here, :],
            gate_s[here, :],
            branch_s[here, :],
            p_hat_s[here, :],
            p_rstd_s[here, :],
            gain[:, c:],
            weights[0, :, width:],
        )
        d_out = dot(mixed_s[here, :], d_branch, ((0,), (0,)))
        d_pre_ref[here, 2 * h :] = d_gate
        d_product_s[here, :] = d_product
        store_swapped(d_product_t_ref, STEP_ROWS, n, t * STEP_ROWS, d_product)
        grads_ref[:, 2 * h + c :] = d_out.astype(BF16)

    one_side(n, 0, d_product_s, edges_s, slopes_s, d_edge_s, d_pre_ref)
    d_pre = dot(normed_s[...], d_pre_ref[...], ((0,), (0,)))
    grads_ref[:, : 2 * h + c] = d_pre.astype(BF16)


def backward_right(n, d_product_t_ref, *refs):
    (edges_s, slopes_s, *kept) = kept_parts(refs, 0)
    normed_s = kept[-2]
    d_pre_ref, grads_ref, d_edge_s = refs[KEPT:]
    one_side(n, 1, d_product_t_ref, edges_s, slopes_s, d_edge_s, d_pre_ref)
    grads_ref[...] = dot(normed_s[...], d_pre_ref[...], ((0,), (0,))).astype(BF16)


def one_side(n, side, x, edges_s, slopes_s, d_edge_s, d_pre_ref):
    h = edges_s.shape[2]

    @pl.loop(0, n // BLOCK_ROWS)
    def _(t):
        d_edge_s[block(t, BLOCK_ROWS, n), :] = contract(
            n, t * BLOCK_ROWS, x, edges_s.at[1 - side]
        )

    @pl.loop(0, n // STEP_ROWS)
    def _(t):
        here = block(t, STEP_ROWS, n)
        d_pre_ref[here, : 2 * h] = edge_grads(
            d_edge_s[here, :], slopes_s[side, here, :], edges_s[side, here, :]
        )


def own_rows(
    pair_ref, up_ref, d_left_ref, d_right_ref, weights, vectors, hat_ref, rstd_ref, out_ref
):
    cells, c = out_ref.shape
    half = d_right_ref.shape[1]
    place = own_place(pair_ref)
    own = pl.ds(pl.multiple_of(place * cells, cells), cells)
    width = d_left_ref.shape[1] + half
    gain = vector_parts(vectors[0:1, :], c, width)[1]
    d_left, d_right = d_left_ref[own, :], d_right_ref[own, :]
    d_pre = jnp.concatenate([d_left[:, :half], d_right, d_left[:, half:]], axis=1)
    d_normed = dot(d_pre, weights[0, :, :width], ((1,), (1,))) * gain[:, :c]
    pulled = norm_vjp(hat_ref[0, own, :], rstd_ref[0, own, :], d_normed)
    out_ref[...] = (up_ref[own, :] + pulled).astype(BF16)


def exchange(value, axis, size, step):
    return lax.ppermute(value, axis, [(d, d ^ step) for d in range(size)])


def near_rounds(value, groups):
    other = exchange(value, "dp", groups, 1)
    step = 2
    while step < groups // 2:
        value = add_narrow(value, other)
        other = exchange(value, "dp", groups, step)
        step *= 2
    return value, other


def add_narrow(a, b):
    return (a.astype(F32) + b.astype(F32)).astype(BF16)


def prepare(
    index_ref, mask_ref, state_ref, cot_ref, w, w_out, b, gain, shift, b_out, *refs
):
    sent_ref, weights_ref, vectors_ref, mask_s, sems = refs
    cells, c = state_ref.shape
    below, width = cells + TAIL_ROWS, w.shape[2]
    copies = [(mask_ref, mask_s), (state_ref, sent_ref.at[:cells]), (cot_ref, sent_ref.at[below:])]
    copies += [(w, weights_ref.at[:, :, :width]), (w_out, weights_ref.at[:, :, width:])]
    first = 0
    for vector in (b, gain, shift, b_out):
        last = first + vector.shape[1]
        copies.append((vector, vectors_ref.at[:, first:last]))
        first = last
    copies = [pltpu.make_async_copy(*pair, sems.at[k]) for k, pair in enumerate(copies)]
    for copy in copies:
        copy.start()
    copies[0].wait()
    length = jnp.max(jnp.sum(mask_s[...].astype(F32), axis=1, keepdims=True))
    in_length = lax.broadcasted_iota(jnp.int32, (TAIL_ROWS, c), 1) < 64
    place = index_ref[0].astype(F32)
    sent_ref[cells:below, :] = jnp.where(in_length, length, place).astype(BF16)
    for copy in copies[1:]:
        copy.wait()


def pair_up(near_ref, far_ref, state_ref, cot_ref):
    split = state_ref.shape[1]
    for side, ref in enumerate((near_ref, far_ref)):
        state_ref[side] = ref[:split, :]
        cot_ref[side] = ref[split:, :]


def hold(weights_in, vectors_in, weights_out, vectors_out):
    weights_out[...] = weights_in[...]
    vectors_out[...] = vectors_in[...]


def vector_parts(row, c, width):
    ends = [width, width + 2 * c, width + 4 * c, width + 5 * c]
    return [row[:, first:last] for first, last in zip([0] + ends, ends)]


def add_grads(second, second_far, left, left_far, right, right_far, proj_ref, out_ref):
    width = proj_ref.shape[2]
    c = out_ref.shape[2]
    half = (width - c) // 2
    total = second[...].astype(F32) + second_far[...].astype(F32)
    proj_ref[1] = total[:, :width]
    out_ref[1] = total[:, width:]
    total = left[...].astype(F32) + left_far[...].astype(F32)
    proj_ref[0, :, :half] = total[:, :half]
    proj_ref[0, :, 2 * half :] = total[:, half : half + c]
    out_ref[0] = total[:, half + c :]
    proj_ref[0, :, half : 2 * half] = right[...].astype(F32) + right_far[...].astype(F32)


def crop_shards(
    groups,
    parts,
    pair_repr,
    pair_mask,
    cotangent,
    proj_weight,
    proj_bias,
    norm_gain,
    norm_shift,
    out_weight,
    out_bias,
):
    _, rows, n, c = pair_repr.shape
    h = out_weight.shape[1]
    width = proj_weight.shape[2]
    cells, pairs = rows * n, n * n
    plane = (pairs + 8, h)
    kept = [jax.ShapeDtypeStruct((2, 4) + plane, F32), jax.ShapeDtypeStruct((2, 2) + plane, F32)]
    kept += [jax.ShapeDtypeStruct((2,) + plane, F32)] * 6
    kept += [jax.ShapeDtypeStruct((2, pairs, h), BF16)] * 2
    grads = jax.ShapeDtypeStruct((c, width + c), BF16)
    vmem = pl.BlockSpec(memory_space=pltpu.VMEM)
    main = pl.BlockSpec(memory_space=pltpu.HBM)
    params = pltpu.CompilerParams(vmem_limit_bytes=VMEM_BYTES)

    def cost(planes):
        flops = 4 * pairs * width * c
        return pl.CostEstimate(
            flops=flops, bytes_accessed=planes * pairs * c * 4, transcendentals=0
        )

    packed = (
        jax.ShapeDtypeStruct((2, c, width + c), BF16),
        jax.ShapeDtypeStruct((2, width + 5 * c), F32),
    )
    sent, *weights = pl.pallas_call(
        prepare,
        out_shape=(jax.ShapeDtypeStruct((2 * cells + TAIL_ROWS, c), BF16),) + packed,
        in_specs=[pl.BlockSpec(memory_space=pltpu.SMEM)] + [main] * 9,
        out_specs=[vmem] * 3,
        scratch_shapes=[pltpu.VMEM((rows, n), jnp.int32), pltpu.SemaphoreType.DMA((9,))],
        compiler_params=pltpu.CompilerParams(vmem_limit_bytes=PREPARE_BYTES),
        name="prepare",
    )(
        lax.axis_index("dap").astype(jnp.int32)[None],
        pair_mask[0],
        pair_repr.reshape(cells, c),
        cotangent.reshape(cells, c),
        proj_weight,
        out_weight,
        proj_bias,
        norm_gain,
        norm_shift,
        out_bias,
    )
    weights = pl.pallas_call(
        hold,
        out_shape=packed,
        in_specs=[vmem] * 2,
        out_specs=[vmem] * 2,
        compiler_params=params,
        cost_estimate=cost(8),
        name="hold",
    )(*weights)
    beside = exchange(sent, "dap", parts, 1)
    beside, *weights = lax.optimization_barrier((beside, *weights))
    state, cot = pl.pallas_call(
        pair_up,
        out_shape=(
            jax.ShapeDtypeStruct((2, cells + TAIL_ROWS, c), BF16),
            jax.ShapeDtypeStruct((2, cells, c), BF16),
        ),
        in_specs=[vmem] * 2,
        out_specs=[vmem] * 2,
        compiler_params=params,
        name="pair_up",
    )(sent, beside)
    states, cots = [state], [cot]
    half = parts // 2
    jumps = [0, *range(1, half // 2), *reversed(range(half // 2, half))]
    for group in (states, cots):
        group += [exchange(group[0], "dap", parts, 2 * jump) for jump in jumps[1:]]

    held = pl.pallas_call(
        functools.partial(forward, n, jumps),
        out_shape=kept,
        in_specs=[vmem] * (half + 2),
        out_specs=(vmem,) * KEPT,
        scratch_shapes=[pltpu.VMEM((pairs, c), BF16)],
        compiler_params=params,
        cost_estimate=cost(64),
        name="forward",
    )(*states, *weights)

    double, single = pltpu.VMEM((2,) + plane, F32), pltpu.VMEM(plane, F32)
    up_1, grads_1 = pl.pallas_call(
        functools.partial(backward_second, n, jumps),
        out_shape=(jax.ShapeDtypeStruct((pairs, c), F32), grads),
        in_specs=[vmem] * (3 + half + KEPT),
        out_specs=(vmem, vmem),
        scratch_shapes=[
            double,
            double,
            pltpu.VMEM((pairs, width), BF16),
            pltpu.VMEM((pairs, c), BF16),
        ],
        compiler_params=params,
        cost_estimate=cost(48),
        name="backward_second",
    )(states[0], *cots, *weights, *held)
    far = groups // 2
    near_1 = near_rounds(grads_1, groups)

    d_left, d_product_t, grads_left = pl.pallas_call(
        functools.partial(backward_left, n),
        out_shape=(
            jax.ShapeDtypeStruct((pairs, 2 * h + c), BF16),
            jax.ShapeDtypeStruct(plane, F32),
            jax.ShapeDtypeStruct((c, 2 * h + 2 * c), BF16),
        ),
        in_specs=[vmem] * (3 + KEPT),
        out_specs=[vmem] * 3,
        scratch_shapes=[single, single],
        compiler_params=params,
        cost_estimate=cost(24),
        name="backward_left",
    )(up_1, *weights, *held)
    near_left = near_rounds(grads_left, groups)
    second = add_narrow(*near_1)
    second, d_product_t = lax.optimization_barrier((second, d_product_t))
    second_far = exchange(second, "dp", groups, far)

    d_right, grads_right = pl.pallas_call(
        functools.partial(backward_right, n),
        out_shape=(
            jax.ShapeDtypeStruct((pairs, 2 * h), BF16),
            jax.ShapeDtypeStruct((c, 2 * h), BF16),
        ),
        in_specs=[vmem] * (1 + KEPT),
        out_specs=[vmem] * 2,
        scratch_shapes=[single],
        compiler_params=params,
        cost_estimate=cost(24),
        name="backward_right",
    )(d_product_t, *held)
    pair_grad = pl.pallas_call(
        own_rows,
        out_shape=jax.ShapeDtypeStruct((cells, c), BF16),
        in_specs=[vmem] * 8,
        out_specs=vmem,
        compiler_params=params,
        cost_estimate=cost(8),
        name="own_rows",
    )(states[0], up_1, d_left, d_right, *weights, held[3], held[4])

    left = add_narrow(*near_left)
    left_far = exchange(left, "dp", groups, far)
    grads_right, second_far = lax.optimization_barrier((grads_right, second_far))
    right = add_narrow(*near_rounds(grads_right, groups))
    right_far = exchange(right, "dp", groups, far)

    proj_total, out_total = pl.pallas_call(
        add_grads,
        out_shape=(
            jax.ShapeDtypeStruct((2, c, width), F32),
            jax.ShapeDtypeStruct((2, h, c), F32),
        ),
        in_specs=[vmem] * 6,
        out_specs=(vmem, vmem),
        compiler_params=params,
        name="add_grads",
    )(second, second_far, left, left_far, right, right_far)
    return pair_grad.reshape(pair_repr.shape), proj_total, out_total


def layer_norm(values, gain_vec, shift_vec, norm_axis):
    mean_value = jnp.mean(values, axis=norm_axis, keepdims=True)
    centred = values - mean_value
    variance = jnp.mean(centred * centred, axis=norm_axis, keepdims=True)
    return centred * lax.rsqrt(variance + NORM_EPSILON) * gain_vec + shift_vec


def norm_pullback(values, gain_vec, shift_vec, norm_axis, upstream):
    _, pull_back = jax.vjp(
        lambda inner_value: layer_norm(inner_value, gain_vec, shift_vec, norm_axis), values
    )
    return pull_back(upstream)[0]


def edge_pair(edge_pre, cell_mask):
    left_edge = jax.nn.sigmoid(edge_pre[1]) * edge_pre[0] * cell_mask
    right_edge = jax.nn.sigmoid(edge_pre[3]) * edge_pre[2] * cell_mask
    return jnp.stack([left_edge, right_edge]).astype(jnp.bfloat16)


def edge_pullback(edge_pre, cell_mask, grad_pair):
    sig_left = jax.nn.sigmoid(edge_pre[1])
    sig_right = jax.nn.sigmoid(edge_pre[3])
    grad_left = grad_pair[0].astype(jnp.float32) * cell_mask
    grad_right = grad_pair[1].astype(jnp.float32) * cell_mask
    return jnp.stack(
        [
            grad_left * sig_left,
            grad_left * edge_pre[0] * sig_left * (1.0 - sig_left),
            grad_right * sig_right,
            grad_right * edge_pre[2] * sig_right * (1.0 - sig_right),
        ]
    ).astype(jnp.bfloat16)


def triangle(pair_edges, outgoing):
    if outgoing:
        einsum_form = "cik,cjk->cij"
    else:
        einsum_form = "cki,ckj->cij"
    return jnp.einsum(
        einsum_form, pair_edges[0], pair_edges[1], preferred_element_type=jnp.float32
    ).astype(jnp.bfloat16)


def triangle_pullback(pair_edges, grad_product, outgoing):
    left_edge = pair_edges[0]
    right_edge = pair_edges[1]
    if outgoing:
        grad_left = jnp.einsum(
            "cij,cjk->cik", grad_product, right_edge, preferred_element_type=jnp.float32
        )
        grad_right = jnp.einsum(
            "cij,cik->cjk", grad_product, left_edge, preferred_element_type=jnp.float32
        )
    else:
        grad_left = jnp.einsum(
            "ckj,cij->cki", right_edge, grad_product, preferred_element_type=jnp.float32
        )
        grad_right = jnp.einsum(
            "cki,cij->ckj", left_edge, grad_product, preferred_element_type=jnp.float32
        )
    return jnp.stack([grad_left, grad_right]).astype(jnp.bfloat16)


def update_weights(proj_weight, proj_bias, norm_gain, norm_shift, update, channels, hidden):
    w_edge = proj_weight[update, :, : 4 * hidden].reshape(channels, 4, hidden)
    w_gate = proj_weight[update, :, 4 * hidden :]
    bias_edge = proj_bias[update, : 4 * hidden].reshape(4, hidden, 1, 1)
    bias_gate = proj_bias[update, 4 * hidden :]
    gain_in = norm_gain[update, :channels]
    shift_in = norm_shift[update, :channels]
    gain_out = norm_gain[update, channels:][:, None, None]
    shift_out = norm_shift[update, channels:][:, None, None]
    return (w_edge, w_gate, bias_edge, bias_gate, gain_in, shift_in, gain_out, shift_out)


def shards(
    pair_repr,
    pair_mask,
    cotangent,
    proj_weight,
    proj_bias,
    norm_gain,
    norm_shift,
    out_weight,
    out_bias,
):
    channels = pair_repr.shape[3]
    hidden = out_weight.shape[1]
    pair_state = pair_repr[0]
    cell_mask = pair_mask[0].astype(jnp.float32)
    records = []
    for update in range(2):
        w_edge, w_gate, bias_edge, bias_gate, gain_in, shift_in, gain_out, shift_out = (
            update_weights(proj_weight, proj_bias, norm_gain, norm_shift, update, channels, hidden)
        )
        state_f = pair_state.astype(jnp.float32)
        normed = layer_norm(state_f, gain_in, shift_in, -1).astype(jnp.bfloat16)
        edge_pre = (
            jnp.einsum("rnc,cgh->ghrn", normed, w_edge, preferred_element_type=jnp.float32)
            + bias_edge
        )
        gate_pre = (
            jnp.einsum("rnc,cd->rnd", normed, w_gate, preferred_element_type=jnp.float32)
            + bias_gate
        )
        pair_edges = edge_pair(edge_pre, cell_mask)
        spread = lax.all_to_all(pair_edges, "dap", split_axis=1, concat_axis=2, tiled=True)
        product = lax.all_to_all(
            triangle(spread, update == 0), "dap", split_axis=1, concat_axis=0, tiled=True
        )
        mixed_norm = layer_norm(product.astype(jnp.float32), gain_out, shift_out, 0).astype(
            jnp.bfloat16
        )
        branch = (
            jnp.einsum(
                "hrn,hd->rnd", mixed_norm, out_weight[update], preferred_element_type=jnp.float32
            )
            + out_bias[update]
        )
        records.append(
            (state_f, normed, edge_pre, gate_pre, pair_edges, spread, product, mixed_norm, branch)
        )
        pair_state = (state_f + jax.nn.sigmoid(gate_pre) * branch).astype(jnp.bfloat16)
    upstream = cotangent[0].astype(jnp.float32)
    proj_grads = []
    out_grads = []
    for update in (1, 0):
        state_f, normed, edge_pre, gate_pre, pair_edges, spread, product, mixed_norm, branch = (
            records[update]
        )
        w_edge, w_gate, bias_edge, bias_gate, gain_in, shift_in, gain_out, shift_out = (
            update_weights(proj_weight, proj_bias, norm_gain, norm_shift, update, channels, hidden)
        )
        gate_value = jax.nn.sigmoid(gate_pre)
        grad_branch = (upstream * gate_value).astype(jnp.bfloat16)
        grad_gate = (upstream * branch * gate_value * (1.0 - gate_value)).astype(jnp.bfloat16)
        out_grad = jnp.einsum(
            "hrn,rnd->hd", mixed_norm, grad_branch, preferred_element_type=jnp.float32
        )
        grad_mixed = jnp.einsum(
            "rnd,hd->hrn", grad_branch, out_weight[update], preferred_element_type=jnp.float32
        )
        grad_product = norm_pullback(
            product.astype(jnp.float32), gain_out, shift_out, 0, grad_mixed
        ).astype(jnp.bfloat16)
        column_edges = spread
        column_grad = lax.all_to_all(
            grad_product[None], "dap", split_axis=1, concat_axis=2, tiled=True
        )[0]
        grad_pair = lax.all_to_all(
            triangle_pullback(column_edges, column_grad, update == 0),
            "dap",
            split_axis=2,
            concat_axis=1,
            tiled=True,
        )
        grad_edge = edge_pullback(edge_pre, cell_mask, grad_pair)
        edge_grad = jnp.einsum(
            "rnc,ghrn->cgh", normed, grad_edge, preferred_element_type=jnp.float32
        ).reshape(channels, 4 * hidden)
        gate_grad = jnp.einsum("rnc,rnd->cd", normed, grad_gate, preferred_element_type=jnp.float32)
        grad_normed = jnp.einsum(
            "ghrn,cgh->rnc", grad_edge, w_edge, preferred_element_type=jnp.float32
        )
        grad_normed = grad_normed + jnp.einsum(
            "rnd,cd->rnc", grad_gate, w_gate, preferred_element_type=jnp.float32
        )
        upstream = upstream + norm_pullback(state_f, gain_in, shift_in, -1, grad_normed)
        proj_part = jnp.concatenate([edge_grad, gate_grad], axis=1)
        proj_grads.append(proj_part)
        out_grads.append(out_grad)
    proj_total = jnp.stack(proj_grads[::-1])
    out_total = jnp.stack(out_grads[::-1])
    proj_total, out_total = lax.psum((proj_total, out_total), ("dp", "dap"))
    return (upstream.astype(jnp.bfloat16)[None], proj_total, out_total)


def solution(mesh):
    placed = (
        P("dp", "dap", None, None),
        P("dp", "dap", None),
        P("dp", "dap", None, None),
        P(),
        P(),
        P(),
        P(),
        P(),
        P(),
    )
    groups, parts = mesh.shape["dp"], mesh.shape["dap"]

    def program(*args):
        n, c = args[0].shape[2:]
        rows = n // parts
        fits = 20 * n * n * c * 4 <= CROP_BUDGET
        paired = all(size >= 4 and size & (size - 1) == 0 for size in (groups, parts))
        even = args[7].shape[1] == c == 128 and STEP_ROWS % rows == 0 and n == STEP_ROWS
        body = functools.partial(crop_shards, groups, parts) if fits and even and paired else shards
        return spread_over(body)(*args)

    def spread_over(body):
        return jax.shard_map(
            body,
            mesh=mesh,
            in_specs=placed,
            out_specs=(P("dp", "dap", None, None), P(), P()),
            check_vma=False,
        )

    return program
```

```python
import functools

import jax
import jax.numpy as jnp
from jax import lax
from jax.experimental import pallas as pl
from jax.experimental.pallas import tpu as pltpu
from jax.sharding import PartitionSpec as P

NORM_EPSILON = 1e-05
VMEM_BYTES = 16 * 1024 * 1024
PREPARE_BYTES = 63 * 1024 * 1024
CROP_BUDGET = 32 * 1024 * 1024
BLOCK_ROWS = 8
STEP_ROWS = 32
KEPT = 10
TAIL_ROWS = 16
F32 = jnp.float32
BF16 = jnp.bfloat16


def sigmoid(x):
    return 0.5 * jnp.tanh(0.5 * x) + 0.5


def dot(a, b, dims=((1,), (0,))):
    return lax.dot_general(a, b, (dims, ((), ())), preferred_element_type=F32)


def norm_parts(x):
    x = x.astype(F32)
    centred = x - jnp.mean(x, axis=-1, keepdims=True)
    rstd = lax.rsqrt(jnp.mean(centred * centred, axis=-1, keepdims=True) + NORM_EPSILON)
    return centred * rstd, jnp.broadcast_to(rstd, x.shape)


def norm_vjp(x_hat, rstd, grad):
    mean_grad = jnp.mean(grad, axis=-1, keepdims=True)
    mean_prod = jnp.mean(grad * x_hat, axis=-1, keepdims=True)
    return rstd * (grad - mean_grad - x_hat * mean_prod)


def pair_mask_block(length, first_row, rows, n, lanes):
    shape = (rows, n, lanes)
    i = lax.broadcasted_iota(jnp.int32, shape, 0) + first_row
    j = lax.broadcasted_iota(jnp.int32, shape, 1)
    inside = jnp.where((i < length) & (j < length), 1.0, 0.0)
    return inside.reshape(rows * n, lanes)


def project(x, mask, w, b, gain, shift):
    x_hat, rstd = norm_parts(x)
    normed = (x_hat * gain + shift).astype(BF16)
    pre = dot(normed, w) + b
    h = (pre.shape[1] - x.shape[1]) // 4
    s_left = sigmoid(pre[:, h : 2 * h]) * mask
    s_right = sigmoid(pre[:, 3 * h : 4 * h]) * mask
    left = s_left * pre[:, :h]
    right = s_right * pre[:, 2 * h : 3 * h]
    gate = sigmoid(pre[:, 4 * h :])
    return x_hat, rstd, normed, s_left, s_right, left, right, gate


def mix(product, gain, shift, w_out, b_out):
    p_hat, p_rstd = norm_parts(product)
    mixed = (p_hat * gain + shift).astype(BF16)
    return p_hat, p_rstd, mixed, dot(mixed, w_out) + b_out


def unmix(up, gate, branch, p_hat, p_rstd, gain, w_out):
    d_branch = up * gate
    d_gate = (d_branch * branch * (1.0 - gate)).astype(BF16)
    d_branch = d_branch.astype(BF16)
    d_mixed = dot(d_branch, w_out, ((1,), (1,))) * gain
    return d_branch, d_gate, norm_vjp(p_hat, p_rstd, d_mixed)


def contract(n, first, x, y, swapped=False):
    lanes = y.shape[1]
    tiles = (n // 8, 8, lanes)

    def row(a, e):
        return e * n + first + a if swapped else (first + a) * n + e

    def step(e, totals):
        block = y[pl.ds(pl.multiple_of(e * n, n), n), :].reshape(tiles)
        return tuple(
            totals[a] + x[pl.ds(row(a, e), 8, stride=0), :][None] * block
            for a in range(BLOCK_ROWS)
        )

    zero = jnp.zeros(tiles, F32)
    totals = lax.fori_loop(0, n, step, (zero,) * BLOCK_ROWS, unroll=True)
    return jnp.stack(totals).reshape(BLOCK_ROWS * n, lanes)


def edge_grads(d_edge, slope, edge):
    grads = (d_edge * slope).astype(BF16), (d_edge * edge * (1.0 - slope)).astype(BF16)
    return jnp.concatenate(grads, axis=1)


def tail_values(block, lanes_from, lanes_to):
    lane = lax.broadcasted_iota(jnp.int32, block.shape, block.ndim - 1)
    inside = (lane >= lanes_from) & (lane < lanes_to)
    return jnp.max(jnp.where(inside, block.astype(F32), 0.0)).astype(jnp.int32)


def own_place(pair_ref):
    return tail_values(pair_ref[0, -TAIL_ROWS:, :], 64, 128)


def place_of(own, jump, side):
    return own ^ (2 * jump) ^ side


def block(t, rows, n):
    return pl.ds(pl.multiple_of(t * rows * n, rows * n), rows * n)


def forward(n, jumps, *refs):
    pairs, refs = refs[: len(jumps)], refs[len(jumps) :]
    (weights, vectors), refs = refs[:2], refs[2:]
    (edges_s, slopes_s, gate_s, hat_s, rstd_s) = refs[:5]
    (p_hat_s, p_rstd_s, branch_s, normed_s, mixed_s) = refs[5:KEPT]
    next_s, right_t_s = refs[KEPT:]
    c = weights.shape[1]
    width = weights.shape[2] - c
    rows = n // (2 * len(jumps))
    cells = rows * n
    tails = jnp.stack([pair[:, cells:, :] for pair in pairs])
    length = tail_values(tails, 0, 64)
    own = own_place(pairs[0])
    for pair, jump in zip(pairs, jumps):
        for side in range(2):
            next_s[block(place_of(own, jump, side), rows, n), :] = pair[side, :cells, :]
    steps = n // STEP_ROWS

    for u in range(2):
        bias, gains, shifts, bias_out = vector_parts(vectors[u : u + 1, :], c, width)

        @pl.loop(0, steps)
        def _(t):
            first = t * STEP_ROWS
            here = block(t, STEP_ROWS, n)
            mask = pair_mask_block(length, first, STEP_ROWS, n, c)
            x_hat, rstd, normed, s_left, s_right, left, right, gate = project(
                next_s[here, :], mask, weights[u, :, :width], bias, gains[:, :c], shifts[:, :c]
            )
            edges_s[u, 0, here, :] = left
            edges_s[u, 1, here, :] = right
            if u == 0:
                store_swapped(right_t_s, STEP_ROWS, n, first, right)
            slopes_s[u, 0, here, :] = s_left
            slopes_s[u, 1, here, :] = s_right
            gate_s[u, here, :] = gate
            hat_s[u, here, :] = x_hat
            rstd_s[u, here, :] = rstd
            normed_s[u, here, :] = normed

        @pl.loop(0, steps)
        def _(t):
            here = block(t, STEP_ROWS, n)
            x, y = edges_s.at[u, 0], edges_s.at[1, 1] if u == 1 else right_t_s
            product = [
                contract(n, t * STEP_ROWS + r, x, y, u == 1)
                for r in range(0, STEP_ROWS, BLOCK_ROWS)
            ]
            p_hat, p_rstd, mixed, branch = mix(
                jnp.concatenate(product).astype(BF16),
                gains[:, c:],
                shifts[:, c:],
                weights[u, :, width:],
                bias_out,
            )
            p_hat_s[u, here, :] = p_hat
            p_rstd_s[u, here, :] = p_rstd
            mixed_s[u, here, :] = mixed
            branch_s[u, here, :] = branch
            if u == 0:
                x = next_s[here, :].astype(F32)
                next_s[here, :] = (x + gate_s[u, here, :] * branch).astype(BF16)


def kept_parts(refs, u):
    return [ref.at[u] for ref in refs[:KEPT]]


def store_swapped(ref, rows, n, first, values):
    for r in range(rows):
        ref[pl.ds(first + r, n, stride=n), :] = values[r * n : (r + 1) * n]


def backward_second(n, jumps, pair, *refs):
    parted, refs = refs[: len(jumps)], refs[len(jumps) :]
    weights, vectors = refs[:2]
    (edges_s, slopes_s, gate_s, hat_s, rstd_s, *kept) = kept_parts(refs[2:], 1)
    (p_hat_s, p_rstd_s, branch_s, normed_s, mixed_s) = kept
    up_ref, grads_ref, d_product_s, d_edges_s, d_pre_s, cot_s = refs[2 + KEPT :]
    c, h = weights.shape[1], edges_s.shape[2]
    width = 4 * h + c
    gain = vector_parts(vectors[1:2, :], c, width)[1]
    own = own_place(pair)
    for part, jump in zip(parted, jumps):
        for side in range(2):
            cot_s[block(place_of(own, jump, side), part.shape[1] // n, n), :] = part[side]

    @pl.loop(0, n // STEP_ROWS)
    def _(t):
        here = block(t, STEP_ROWS, n)
        d_branch, d_gate, d_product = unmix(
            cot_s[here, :].astype(F32),
            gate_s[here, :],
            branch_s[here, :],
            p_hat_s[here, :],
            p_rstd_s[here, :],
            gain[:, c:],
            weights[1, :, width:],
        )
        d_out = dot(mixed_s[here, :], d_branch, ((0,), (0,)))
        d_pre_s[here, 4 * h :] = d_gate
        d_product_s[1, here, :] = d_product
        store_swapped(d_product_s.at[0], STEP_ROWS, n, t * STEP_ROWS, d_product)
        grads_ref[:, width:] = d_out.astype(BF16)

    blocks = n // BLOCK_ROWS

    @pl.loop(0, 2 * blocks)
    def _(step):
        side, t = step // blocks, step % blocks
        d_edges_s[side, block(t, BLOCK_ROWS, n), :] = contract(
            n, t * BLOCK_ROWS, edges_s.at[1 - side], d_product_s.at[side]
        )

    @pl.loop(0, n // STEP_ROWS)
    def _(t):
        here = block(t, STEP_ROWS, n)
        grads = [
            edge_grads(d_edges_s[side, here, :], slopes_s[side, here, :], edges_s[side, here, :])
            for side in range(2)
        ]
        d_pre = jnp.concatenate([*grads, d_pre_s[here, 4 * h :]], axis=1)
        normed = normed_s[here, :]
        d_normed = dot(d_pre, weights[1, :, :width], ((1,), (1,))) * gain[:, :c]
        pulled = norm_vjp(hat_s[here, :], rstd_s[here, :], d_normed)
        up_ref[here, :] = cot_s[here, :].astype(F32) + pulled
        grads_ref[:, :width] = dot(normed, d_pre, ((0,), (0,))).astype(BF16)


def backward_left(n, up_in_ref, weights, vectors, *refs):
    (edges_s, slopes_s, gate_s, _, _, *kept) = kept_parts(refs, 0)
    (p_hat_s, p_rstd_s, branch_s, normed_s, mixed_s) = kept
    d_pre_ref, d_product_ref, grads_ref, d_edge_s = refs[KEPT:]
    c, h = weights.shape[1], edges_s.shape[2]
    width = 4 * h + c
    gain = vector_parts(vectors[0:1, :], c, width)[1]

    @pl.loop(0, n // STEP_ROWS)
    def _(t):
        here = block(t, STEP_ROWS, n)
        d_branch, d_gate, d_product = unmix(
            up_in_ref[here, :],
            gate_s[here, :],
            branch_s[here, :],
            p_hat_s[here, :],
            p_rstd_s[here, :],
            gain[:, c:],
            weights[0, :, width:],
        )
        d_out = dot(mixed_s[here, :], d_branch, ((0,), (0,)))
        d_pre_ref[here, 2 * h :] = d_gate
        d_product_ref[here, :] = d_product
        grads_ref[:, 2 * h + c :] = d_out.astype(BF16)

    one_side(n, 0, d_product_ref, edges_s, slopes_s, d_edge_s, d_pre_ref)
    d_pre = dot(normed_s[...], d_pre_ref[...], ((0,), (0,)))
    grads_ref[:, : 2 * h + c] = d_pre.astype(BF16)


def backward_right(n, d_product_ref, *refs):
    (edges_s, slopes_s, *kept) = kept_parts(refs, 0)
    normed_s = kept[-2]
    d_pre_ref, grads_ref, d_edge_s = refs[KEPT:]
    one_side(n, 1, d_product_ref, edges_s, slopes_s, d_edge_s, d_pre_ref)
    grads_ref[...] = dot(normed_s[...], d_pre_ref[...], ((0,), (0,))).astype(BF16)


def one_side(n, side, x, edges_s, slopes_s, d_edge_s, d_pre_ref):
    h = edges_s.shape[2]

    @pl.loop(0, n // BLOCK_ROWS)
    def _(t):
        d_edge_s[block(t, BLOCK_ROWS, n), :] = contract(
            n, t * BLOCK_ROWS, x, edges_s.at[1 - side], side == 1
        )

    @pl.loop(0, n // STEP_ROWS)
    def _(t):
        here = block(t, STEP_ROWS, n)
        d_pre_ref[here, : 2 * h] = edge_grads(
            d_edge_s[here, :], slopes_s[side, here, :], edges_s[side, here, :]
        )


def own_rows(
    pair_ref, up_ref, d_left_ref, d_right_ref, weights, vectors, hat_ref, rstd_ref, out_ref
):
    cells, c = out_ref.shape
    half = d_right_ref.shape[1]
    place = own_place(pair_ref)
    own = pl.ds(pl.multiple_of(place * cells, cells), cells)
    width = d_left_ref.shape[1] + half
    gain = vector_parts(vectors[0:1, :], c, width)[1]
    d_left, d_right = d_left_ref[own, :], d_right_ref[own, :]
    d_pre = jnp.concatenate([d_left[:, :half], d_right, d_left[:, half:]], axis=1)
    d_normed = dot(d_pre, weights[0, :, :width], ((1,), (1,))) * gain[:, :c]
    pulled = norm_vjp(hat_ref[0, own, :], rstd_ref[0, own, :], d_normed)
    out_ref[...] = (up_ref[own, :] + pulled).astype(BF16)


def exchange(value, axis, size, step):
    return lax.ppermute(value, axis, [(d, d ^ step) for d in range(size)])


def near_rounds(value, groups):
    other = exchange(value, "dp", groups, 1)
    step = 2
    while step < groups // 2:
        value = add_narrow(value, other)
        other = exchange(value, "dp", groups, step)
        step *= 2
    return value, other


def add_narrow(a, b):
    return (a.astype(F32) + b.astype(F32)).astype(BF16)


def prepare(
    index_ref, mask_ref, state_ref, cot_ref, w, w_out, b, gain, shift, b_out, *refs
):
    sent_ref, weights_ref, vectors_ref, mask_s, sems = refs
    cells, c = state_ref.shape
    below, width = cells + TAIL_ROWS, w.shape[2]
    copies = [(mask_ref, mask_s), (state_ref, sent_ref.at[:cells]), (cot_ref, sent_ref.at[below:])]
    copies += [(w, weights_ref.at[:, :, :width]), (w_out, weights_ref.at[:, :, width:])]
    first = 0
    for vector in (b, gain, shift, b_out):
        last = first + vector.shape[1]
        copies.append((vector, vectors_ref.at[:, first:last]))
        first = last
    copies = [pltpu.make_async_copy(*pair, sems.at[k]) for k, pair in enumerate(copies)]
    for copy in copies:
        copy.start()
    copies[0].wait()
    length = jnp.max(jnp.sum(mask_s[...].astype(F32), axis=1, keepdims=True))
    in_length = lax.broadcasted_iota(jnp.int32, (TAIL_ROWS, c), 1) < 64
    place = index_ref[0].astype(F32)
    sent_ref[cells:below, :] = jnp.where(in_length, length, place).astype(BF16)
    for copy in copies[1:]:
        copy.wait()


def pair_up(near_ref, far_ref, state_ref, cot_ref):
    split = state_ref.shape[1]
    for side, ref in enumerate((near_ref, far_ref)):
        state_ref[side] = ref[:split, :]
        cot_ref[side] = ref[split:, :]


def hold(weights_in, vectors_in, weights_out, vectors_out):
    weights_out[...] = weights_in[...]
    vectors_out[...] = vectors_in[...]


def vector_parts(row, c, width):
    ends = [width, width + 2 * c, width + 4 * c, width + 5 * c]
    return [row[:, first:last] for first, last in zip([0] + ends, ends)]


def add_grads(rest, rest_near, left, left_near, right, right_far, proj_ref, out_ref):
    width = proj_ref.shape[2]
    c = out_ref.shape[2]
    half = (width - c) // 2
    total = rest[:, : width + c].astype(F32) + rest_near[:, : width + c].astype(F32)
    proj_ref[1] = total[:, :width]
    out_ref[1] = total[:, width:]
    total = left[...].astype(F32) + left_near[...].astype(F32)
    proj_ref[0, :, :half] = total[:, :half]
    proj_ref[0, :, 2 * half :] = total[:, half : half + c]
    out_ref[0] = total[:, half + c :]
    proj_ref[0, :, half : 2 * half] = right[...].astype(F32) + right_far[...].astype(F32)


def crop_shards(
    groups,
    parts,
    pair_repr,
    pair_mask,
    cotangent,
    proj_weight,
    proj_bias,
    norm_gain,
    norm_shift,
    out_weight,
    out_bias,
):
    _, rows, n, c = pair_repr.shape
    h = out_weight.shape[1]
    width = proj_weight.shape[2]
    cells, pairs = rows * n, n * n
    plane = (pairs + 8, h)
    kept = [jax.ShapeDtypeStruct((2, 2) + plane, F32)] * 2
    kept += [jax.ShapeDtypeStruct((2,) + plane, F32)] * 6
    kept += [jax.ShapeDtypeStruct((2, pairs, h), BF16)] * 2
    grads = jax.ShapeDtypeStruct((c, width + c), BF16)
    vmem = pl.BlockSpec(memory_space=pltpu.VMEM)
    main = pl.BlockSpec(memory_space=pltpu.HBM)
    params = pltpu.CompilerParams(vmem_limit_bytes=VMEM_BYTES)

    def cost(planes):
        flops = 4 * pairs * width * c
        return pl.CostEstimate(
            flops=flops, bytes_accessed=planes * pairs * c * 4, transcendentals=0
        )

    packed = (
        jax.ShapeDtypeStruct((2, c, width + c), BF16),
        jax.ShapeDtypeStruct((2, width + 5 * c), F32),
    )
    sent, *weights = pl.pallas_call(
        prepare,
        out_shape=(jax.ShapeDtypeStruct((2 * cells + TAIL_ROWS, c), BF16),) + packed,
        in_specs=[pl.BlockSpec(memory_space=pltpu.SMEM)] + [main] * 9,
        out_specs=[vmem] * 3,
        scratch_shapes=[pltpu.VMEM((rows, n), jnp.int32), pltpu.SemaphoreType.DMA((9,))],
        compiler_params=pltpu.CompilerParams(vmem_limit_bytes=PREPARE_BYTES),
        name="prepare",
    )(
        lax.axis_index("dap").astype(jnp.int32)[None],
        pair_mask[0],
        pair_repr.reshape(cells, c),
        cotangent.reshape(cells, c),
        proj_weight,
        out_weight,
        proj_bias,
        norm_gain,
        norm_shift,
        out_bias,
    )
    weights = pl.pallas_call(
        hold,
        out_shape=packed,
        in_specs=[vmem] * 2,
        out_specs=[vmem] * 2,
        compiler_params=params,
        cost_estimate=cost(8),
        name="hold",
    )(*weights)
    beside = exchange(sent, "dap", parts, 1)
    beside, *weights = lax.optimization_barrier((beside, *weights))
    state, cot = pl.pallas_call(
        pair_up,
        out_shape=(
            jax.ShapeDtypeStruct((2, cells + TAIL_ROWS, c), BF16),
            jax.ShapeDtypeStruct((2, cells, c), BF16),
        ),
        in_specs=[vmem] * 2,
        out_specs=[vmem] * 2,
        compiler_params=params,
        name="pair_up",
    )(sent, beside)
    states, cots = [state], [cot]
    half = parts // 2
    jumps = [0, *range(1, half // 2), *reversed(range(half // 2, half))]
    for group in (states, cots):
        group += [exchange(group[0], "dap", parts, 2 * jump) for jump in jumps[1:]]

    held = pl.pallas_call(
        functools.partial(forward, n, jumps),
        out_shape=kept,
        in_specs=[vmem] * (half + 2),
        out_specs=(vmem,) * KEPT,
        scratch_shapes=[pltpu.VMEM((pairs, c), BF16), pltpu.VMEM(plane, F32)],
        compiler_params=params,
        cost_estimate=cost(64),
        name="forward",
    )(*states, *weights)

    double, single = pltpu.VMEM((2,) + plane, F32), pltpu.VMEM(plane, F32)
    up_1, grads_1 = pl.pallas_call(
        functools.partial(backward_second, n, jumps),
        out_shape=(jax.ShapeDtypeStruct((pairs, c), F32), grads),
        in_specs=[vmem] * (3 + half + KEPT),
        out_specs=(vmem, vmem),
        scratch_shapes=[
            double,
            double,
            pltpu.VMEM((pairs, width), BF16),
            pltpu.VMEM((pairs, c), BF16),
        ],
        compiler_params=params,
        cost_estimate=cost(48),
        name="backward_second",
    )(states[0], *cots, *weights, *held)
    far = groups // 2
    others_1 = exchange(grads_1, "dp", groups, far)

    d_left, d_product, grads_left = pl.pallas_call(
        functools.partial(backward_left, n),
        out_shape=(
            jax.ShapeDtypeStruct((pairs, 2 * h + c), BF16),
            jax.ShapeDtypeStruct(plane, F32),
            jax.ShapeDtypeStruct((c, 2 * h + 2 * c), BF16),
        ),
        in_specs=[vmem] * (3 + KEPT),
        out_specs=[vmem] * 3,
        scratch_shapes=[single],
        compiler_params=params,
        cost_estimate=cost(24),
        name="backward_left",
    )(up_1, *weights, *held)
    others_left = exchange(grads_left, "dp", groups, far)

    d_right, grads_right = pl.pallas_call(
        functools.partial(backward_right, n),
        out_shape=(
            jax.ShapeDtypeStruct((pairs, 2 * h), BF16),
            jax.ShapeDtypeStruct((c, 2 * h), BF16),
        ),
        in_specs=[vmem] * (1 + KEPT),
        out_specs=[vmem] * 2,
        scratch_shapes=[single],
        compiler_params=params,
        cost_estimate=cost(24),
        name="backward_right",
    )(d_product, *held)
    pair_grad = pl.pallas_call(
        own_rows,
        out_shape=jax.ShapeDtypeStruct((cells, c), BF16),
        in_specs=[vmem] * 8,
        out_specs=vmem,
        compiler_params=params,
        cost_estimate=cost(8),
        name="own_rows",
    )(states[0], up_1, d_left, d_right, *weights, held[3], held[4])

    rest, rest_near = near_rounds(
        jnp.concatenate([add_narrow(grads_1, others_1), grads_right], axis=1), groups
    )
    right = add_narrow(rest[:, width + c :], rest_near[:, width + c :])
    right_far = exchange(right, "dp", groups, far)
    ends_left = near_rounds(add_narrow(grads_left, others_left), groups)

    proj_total, out_total = pl.pallas_call(
        add_grads,
        out_shape=(
            jax.ShapeDtypeStruct((2, c, width), F32),
            jax.ShapeDtypeStruct((2, h, c), F32),
        ),
        in_specs=[vmem] * 6,
        out_specs=(vmem, vmem),
        compiler_params=params,
        name="add_grads",
    )(rest, rest_near, *ends_left, right, right_far)
    return pair_grad.reshape(pair_repr.shape), proj_total, out_total


def layer_norm(values, gain_vec, shift_vec, norm_axis):
    mean_value = jnp.mean(values, axis=norm_axis, keepdims=True)
    centred = values - mean_value
    variance = jnp.mean(centred * centred, axis=norm_axis, keepdims=True)
    return centred * lax.rsqrt(variance + NORM_EPSILON) * gain_vec + shift_vec


def norm_pullback(values, gain_vec, shift_vec, norm_axis, upstream):
    _, pull_back = jax.vjp(
        lambda inner_value: layer_norm(inner_value, gain_vec, shift_vec, norm_axis), values
    )
    return pull_back(upstream)[0]


def edge_pair(edge_pre, cell_mask):
    left_edge = jax.nn.sigmoid(edge_pre[1]) * edge_pre[0] * cell_mask
    right_edge = jax.nn.sigmoid(edge_pre[3]) * edge_pre[2] * cell_mask
    return jnp.stack([left_edge, right_edge]).astype(jnp.bfloat16)


def edge_pullback(edge_pre, cell_mask, grad_pair):
    sig_left = jax.nn.sigmoid(edge_pre[1])
    sig_right = jax.nn.sigmoid(edge_pre[3])
    grad_left = grad_pair[0].astype(jnp.float32) * cell_mask
    grad_right = grad_pair[1].astype(jnp.float32) * cell_mask
    return jnp.stack(
        [
            grad_left * sig_left,
            grad_left * edge_pre[0] * sig_left * (1.0 - sig_left),
            grad_right * sig_right,
            grad_right * edge_pre[2] * sig_right * (1.0 - sig_right),
        ]
    ).astype(jnp.bfloat16)


def triangle(pair_edges, outgoing):
    if outgoing:
        einsum_form = "cik,cjk->cij"
    else:
        einsum_form = "cki,ckj->cij"
    return jnp.einsum(
        einsum_form, pair_edges[0], pair_edges[1], preferred_element_type=jnp.float32
    ).astype(jnp.bfloat16)


def triangle_pullback(pair_edges, grad_product, outgoing):
    left_edge = pair_edges[0]
    right_edge = pair_edges[1]
    if outgoing:
        grad_left = jnp.einsum(
            "cij,cjk->cik", grad_product, right_edge, preferred_element_type=jnp.float32
        )
        grad_right = jnp.einsum(
            "cij,cik->cjk", grad_product, left_edge, preferred_element_type=jnp.float32
        )
    else:
        grad_left = jnp.einsum(
            "ckj,cij->cki", right_edge, grad_product, preferred_element_type=jnp.float32
        )
        grad_right = jnp.einsum(
            "cki,cij->ckj", left_edge, grad_product, preferred_element_type=jnp.float32
        )
    return jnp.stack([grad_left, grad_right]).astype(jnp.bfloat16)


def update_weights(proj_weight, proj_bias, norm_gain, norm_shift, update, channels, hidden):
    w_edge = proj_weight[update, :, : 4 * hidden].reshape(channels, 4, hidden)
    w_gate = proj_weight[update, :, 4 * hidden :]
    bias_edge = proj_bias[update, : 4 * hidden].reshape(4, hidden, 1, 1)
    bias_gate = proj_bias[update, 4 * hidden :]
    gain_in = norm_gain[update, :channels]
    shift_in = norm_shift[update, :channels]
    gain_out = norm_gain[update, channels:][:, None, None]
    shift_out = norm_shift[update, channels:][:, None, None]
    return (w_edge, w_gate, bias_edge, bias_gate, gain_in, shift_in, gain_out, shift_out)


def shards(
    pair_repr,
    pair_mask,
    cotangent,
    proj_weight,
    proj_bias,
    norm_gain,
    norm_shift,
    out_weight,
    out_bias,
):
    channels = pair_repr.shape[3]
    hidden = out_weight.shape[1]
    pair_state = pair_repr[0]
    cell_mask = pair_mask[0].astype(jnp.float32)
    records = []
    for update in range(2):
        w_edge, w_gate, bias_edge, bias_gate, gain_in, shift_in, gain_out, shift_out = (
            update_weights(proj_weight, proj_bias, norm_gain, norm_shift, update, channels, hidden)
        )
        state_f = pair_state.astype(jnp.float32)
        normed = layer_norm(state_f, gain_in, shift_in, -1).astype(jnp.bfloat16)
        edge_pre = (
            jnp.einsum("rnc,cgh->ghrn", normed, w_edge, preferred_element_type=jnp.float32)
            + bias_edge
        )
        gate_pre = (
            jnp.einsum("rnc,cd->rnd", normed, w_gate, preferred_element_type=jnp.float32)
            + bias_gate
        )
        pair_edges = edge_pair(edge_pre, cell_mask)
        spread = lax.all_to_all(pair_edges, "dap", split_axis=1, concat_axis=2, tiled=True)
        product = lax.all_to_all(
            triangle(spread, update == 0), "dap", split_axis=1, concat_axis=0, tiled=True
        )
        mixed_norm = layer_norm(product.astype(jnp.float32), gain_out, shift_out, 0).astype(
            jnp.bfloat16
        )
        branch = (
            jnp.einsum(
                "hrn,hd->rnd", mixed_norm, out_weight[update], preferred_element_type=jnp.float32
            )
            + out_bias[update]
        )
        records.append(
            (state_f, normed, edge_pre, gate_pre, pair_edges, spread, product, mixed_norm, branch)
        )
        pair_state = (state_f + jax.nn.sigmoid(gate_pre) * branch).astype(jnp.bfloat16)
    upstream = cotangent[0].astype(jnp.float32)
    proj_grads = []
    out_grads = []
    for update in (1, 0):
        state_f, normed, edge_pre, gate_pre, pair_edges, spread, product, mixed_norm, branch = (
            records[update]
        )
        w_edge, w_gate, bias_edge, bias_gate, gain_in, shift_in, gain_out, shift_out = (
            update_weights(proj_weight, proj_bias, norm_gain, norm_shift, update, channels, hidden)
        )
        gate_value = jax.nn.sigmoid(gate_pre)
        grad_branch = (upstream * gate_value).astype(jnp.bfloat16)
        grad_gate = (upstream * branch * gate_value * (1.0 - gate_value)).astype(jnp.bfloat16)
        out_grad = jnp.einsum(
            "hrn,rnd->hd", mixed_norm, grad_branch, preferred_element_type=jnp.float32
        )
        grad_mixed = jnp.einsum(
            "rnd,hd->hrn", grad_branch, out_weight[update], preferred_element_type=jnp.float32
        )
        grad_product = norm_pullback(
            product.astype(jnp.float32), gain_out, shift_out, 0, grad_mixed
        ).astype(jnp.bfloat16)
        column_edges = spread
        column_grad = lax.all_to_all(
            grad_product[None], "dap", split_axis=1, concat_axis=2, tiled=True
        )[0]
        grad_pair = lax.all_to_all(
            triangle_pullback(column_edges, column_grad, update == 0),
            "dap",
            split_axis=2,
            concat_axis=1,
            tiled=True,
        )
        grad_edge = edge_pullback(edge_pre, cell_mask, grad_pair)
        edge_grad = jnp.einsum(
            "rnc,ghrn->cgh", normed, grad_edge, preferred_element_type=jnp.float32
        ).reshape(channels, 4 * hidden)
        gate_grad = jnp.einsum("rnc,rnd->cd", normed, grad_gate, preferred_element_type=jnp.float32)
        grad_normed = jnp.einsum(
            "ghrn,cgh->rnc", grad_edge, w_edge, preferred_element_type=jnp.float32
        )
        grad_normed = grad_normed + jnp.einsum(
            "rnd,cd->rnc", grad_gate, w_gate, preferred_element_type=jnp.float32
        )
        upstream = upstream + norm_pullback(state_f, gain_in, shift_in, -1, grad_normed)
        proj_part = jnp.concatenate([edge_grad, gate_grad], axis=1)
        proj_grads.append(proj_part)
        out_grads.append(out_grad)
    proj_total = jnp.stack(proj_grads[::-1])
    out_total = jnp.stack(out_grads[::-1])
    proj_total, out_total = lax.psum((proj_total, out_total), ("dp", "dap"))
    return (upstream.astype(jnp.bfloat16)[None], proj_total, out_total)


def solution(mesh):
    placed = (
        P("dp", "dap", None, None),
        P("dp", "dap", None),
        P("dp", "dap", None, None),
        P(),
        P(),
        P(),
        P(),
        P(),
        P(),
    )
    groups, parts = mesh.shape["dp"], mesh.shape["dap"]

    def program(*args):
        n, c = args[0].shape[2:]
        rows = n // parts
        fits = 20 * n * n * c * 4 <= CROP_BUDGET
        paired = all(size >= 4 and size & (size - 1) == 0 for size in (groups, parts))
        even = args[7].shape[1] == c == 128 and STEP_ROWS % rows == 0 and n == STEP_ROWS
        body = functools.partial(crop_shards, groups, parts) if fits and even and paired else shards
        return spread_over(body)(*args)

    def spread_over(body):
        return jax.shard_map(
            body,
            mesh=mesh,
            in_specs=placed,
            out_specs=(P("dp", "dap", None, None), P(), P()),
            check_vma=False,
        )

    return program
```

```python
import functools

import jax
import jax.numpy as jnp
from jax import lax
from jax.experimental import pallas as pl
from jax.experimental.pallas import tpu as pltpu
from jax.sharding import PartitionSpec as P

NORM_EPSILON = 1e-05
VMEM_BYTES = 16 * 1024 * 1024
PREPARE_BYTES = 63 * 1024 * 1024
CROP_BUDGET = 32 * 1024 * 1024
BLOCK_ROWS = 8
STEP_ROWS = 32
KEPT = 10
TAIL_ROWS = 16
F32 = jnp.float32
BF16 = jnp.bfloat16


def sigmoid(x):
    return 0.5 * jnp.tanh(0.5 * x) + 0.5


def dot(a, b, dims=((1,), (0,))):
    return lax.dot_general(a, b, (dims, ((), ())), preferred_element_type=F32)


def norm_parts(x):
    x = x.astype(F32)
    centred = x - jnp.mean(x, axis=-1, keepdims=True)
    rstd = lax.rsqrt(jnp.mean(centred * centred, axis=-1, keepdims=True) + NORM_EPSILON)
    return centred * rstd, jnp.broadcast_to(rstd, x.shape)


def norm_vjp(x_hat, rstd, grad):
    mean_grad = jnp.mean(grad, axis=-1, keepdims=True)
    mean_prod = jnp.mean(grad * x_hat, axis=-1, keepdims=True)
    return rstd * (grad - mean_grad - x_hat * mean_prod)


def pair_mask_block(length, first_row, rows, n, lanes):
    shape = (rows, n, lanes)
    i = lax.broadcasted_iota(jnp.int32, shape, 0) + first_row
    j = lax.broadcasted_iota(jnp.int32, shape, 1)
    inside = jnp.where((i < length) & (j < length), 1.0, 0.0)
    return inside.reshape(rows * n, lanes)


def project(x, mask, w, b, gain, shift):
    x_hat, rstd = norm_parts(x)
    normed = (x_hat * gain + shift).astype(BF16)
    pre = dot(normed, w) + b
    h = (pre.shape[1] - x.shape[1]) // 4
    s_left = sigmoid(pre[:, h : 2 * h]) * mask
    s_right = sigmoid(pre[:, 3 * h : 4 * h]) * mask
    left = s_left * pre[:, :h]
    right = s_right * pre[:, 2 * h : 3 * h]
    gate = sigmoid(pre[:, 4 * h :])
    return x_hat, rstd, normed, s_left, s_right, left, right, gate


def mix(product, gain, shift, w_out, b_out):
    p_hat, p_rstd = norm_parts(product)
    mixed = (p_hat * gain + shift).astype(BF16)
    return p_hat, p_rstd, mixed, dot(mixed, w_out) + b_out


def unmix(up, gate, branch, p_hat, p_rstd, gain, w_out):
    d_branch = up * gate
    d_gate = (d_branch * branch * (1.0 - gate)).astype(BF16)
    d_branch = d_branch.astype(BF16)
    d_mixed = dot(d_branch, w_out, ((1,), (1,))) * gain
    return d_branch, d_gate, norm_vjp(p_hat, p_rstd, d_mixed)


def contract(n, first, x, y, swapped=False):
    lanes = y.shape[1]
    tiles = (n // 8, 8, lanes)

    def row(a, e):
        return e * n + first + a if swapped else (first + a) * n + e

    def step(e, totals):
        block = y[pl.ds(pl.multiple_of(e * n, n), n), :].reshape(tiles)
        return tuple(
            totals[a] + x[pl.ds(row(a, e), 8, stride=0), :][None] * block
            for a in range(BLOCK_ROWS)
        )

    zero = jnp.zeros(tiles, F32)
    totals = lax.fori_loop(0, n, step, (zero,) * BLOCK_ROWS, unroll=True)
    return jnp.stack(totals).reshape(BLOCK_ROWS * n, lanes)


def edge_grads(d_edge, slope, edge):
    grads = (d_edge * slope).astype(BF16), (d_edge * edge * (1.0 - slope)).astype(BF16)
    return jnp.concatenate(grads, axis=1)


def tail_values(block, lanes_from, lanes_to):
    lane = lax.broadcasted_iota(jnp.int32, block.shape, block.ndim - 1)
    inside = (lane >= lanes_from) & (lane < lanes_to)
    return jnp.max(jnp.where(inside, block.astype(F32), 0.0)).astype(jnp.int32)


def own_place(pair_ref):
    return tail_values(pair_ref[0, -TAIL_ROWS:, :], 64, 128)


def place_of(own, jump, side):
    return own ^ (2 * jump) ^ side


def block(t, rows, n):
    return pl.ds(pl.multiple_of(t * rows * n, rows * n), rows * n)


def forward(n, jumps, *refs):
    pairs, refs = refs[: len(jumps)], refs[len(jumps) :]
    (weights, vectors), refs = refs[:2], refs[2:]
    (edges_s, slopes_s, gate_s, hat_s, rstd_s) = refs[:5]
    (p_hat_s, p_rstd_s, branch_s, normed_s, mixed_s) = refs[5:KEPT]
    next_s, right_t_s = refs[KEPT:]
    c = weights.shape[1]
    width = weights.shape[2] - c
    rows = n // (2 * len(jumps))
    cells = rows * n
    tails = jnp.stack([pair[:, cells:, :] for pair in pairs])
    length = tail_values(tails, 0, 64)
    own = own_place(pairs[0])
    for pair, jump in zip(pairs, jumps):
        for side in range(2):
            next_s[block(place_of(own, jump, side), rows, n), :] = pair[side, :cells, :]
    steps = n // STEP_ROWS

    for u in range(2):
        bias, gains, shifts, bias_out = vector_parts(vectors[u : u + 1, :], c, width)

        @pl.loop(0, steps)
        def _(t):
            first = t * STEP_ROWS
            here = block(t, STEP_ROWS, n)
            mask = pair_mask_block(length, first, STEP_ROWS, n, c)
            x_hat, rstd, normed, s_left, s_right, left, right, gate = project(
                next_s[here, :], mask, weights[u, :, :width], bias, gains[:, :c], shifts[:, :c]
            )
            edges_s[u, 0, here, :] = left
            edges_s[u, 1, here, :] = right
            if u == 0:
                store_swapped(right_t_s, STEP_ROWS, n, first, right)
            slopes_s[u, 0, here, :] = s_left
            slopes_s[u, 1, here, :] = s_right
            gate_s[u, here, :] = gate
            if u == 1:
                hat_s[here, :] = x_hat
                rstd_s[here, :] = rstd
            normed_s[u, here, :] = normed

        @pl.loop(0, steps)
        def _(t):
            here = block(t, STEP_ROWS, n)
            x, y = edges_s.at[u, 0], edges_s.at[1, 1] if u == 1 else right_t_s
            product = [
                contract(n, t * STEP_ROWS + r, x, y, u == 1)
                for r in range(0, STEP_ROWS, BLOCK_ROWS)
            ]
            p_hat, p_rstd, mixed, branch = mix(
                jnp.concatenate(product).astype(BF16),
                gains[:, c:],
                shifts[:, c:],
                weights[u, :, width:],
                bias_out,
            )
            p_hat_s[u, here, :] = p_hat
            p_rstd_s[u, here, :] = p_rstd
            mixed_s[u, here, :] = mixed
            branch_s[u, here, :] = branch
            if u == 0:
                x = next_s[here, :].astype(F32)
                next_s[here, :] = (x + gate_s[u, here, :] * branch).astype(BF16)


def kept_parts(refs, u):
    return [ref if ref.shape[0] != 2 else ref.at[u] for ref in refs[:KEPT]]


def store_swapped(ref, rows, n, first, values):
    for r in range(rows):
        ref[pl.ds(first + r, n, stride=n), :] = values[r * n : (r + 1) * n]


def backward_second(n, jumps, pair, *refs):
    parted, refs = refs[: len(jumps)], refs[len(jumps) :]
    weights, vectors = refs[:2]
    (edges_s, slopes_s, gate_s, hat_s, rstd_s, *kept) = kept_parts(refs[2:], 1)
    (p_hat_s, p_rstd_s, branch_s, normed_s, mixed_s) = kept
    up_ref, grads_ref, d_product_s, d_edges_s, d_pre_s, cot_s = refs[2 + KEPT :]
    c, h = weights.shape[1], edges_s.shape[2]
    width = 4 * h + c
    gain = vector_parts(vectors[1:2, :], c, width)[1]
    own = own_place(pair)
    for part, jump in zip(parted, jumps):
        for side in range(2):
            cot_s[block(place_of(own, jump, side), part.shape[1] // n, n), :] = part[side]

    @pl.loop(0, n // STEP_ROWS)
    def _(t):
        here = block(t, STEP_ROWS, n)
        d_branch, d_gate, d_product = unmix(
            cot_s[here, :].astype(F32),
            gate_s[here, :],
            branch_s[here, :],
            p_hat_s[here, :],
            p_rstd_s[here, :],
            gain[:, c:],
            weights[1, :, width:],
        )
        d_out = dot(mixed_s[here, :], d_branch, ((0,), (0,)))
        d_pre_s[here, 4 * h :] = d_gate
        d_product_s[1, here, :] = d_product
        store_swapped(d_product_s.at[0], STEP_ROWS, n, t * STEP_ROWS, d_product)
        grads_ref[:, width:] = d_out.astype(BF16)

    blocks = n // BLOCK_ROWS

    @pl.loop(0, 2 * blocks)
    def _(step):
        side, t = step // blocks, step % blocks
        d_edges_s[side, block(t, BLOCK_ROWS, n), :] = contract(
            n, t * BLOCK_ROWS, edges_s.at[1 - side], d_product_s.at[side]
        )

    @pl.loop(0, n // STEP_ROWS)
    def _(t):
        here = block(t, STEP_ROWS, n)
        grads = [
            edge_grads(d_edges_s[side, here, :], slopes_s[side, here, :], edges_s[side, here, :])
            for side in range(2)
        ]
        d_pre = jnp.concatenate([*grads, d_pre_s[here, 4 * h :]], axis=1)
        normed = normed_s[here, :]
        d_normed = dot(d_pre, weights[1, :, :width], ((1,), (1,))) * gain[:, :c]
        pulled = norm_vjp(hat_s[here, :], rstd_s[here, :], d_normed)
        up_ref[here, :] = cot_s[here, :].astype(F32) + pulled
        grads_ref[:, :width] = dot(normed, d_pre, ((0,), (0,))).astype(BF16)


def backward_left(n, up_in_ref, weights, vectors, *refs):
    (edges_s, slopes_s, gate_s, _, _, *kept) = kept_parts(refs, 0)
    (p_hat_s, p_rstd_s, branch_s, normed_s, mixed_s) = kept
    d_pre_ref, d_product_ref, grads_ref = refs[KEPT:]
    c, h = weights.shape[1], edges_s.shape[2]
    width = 4 * h + c
    gain = vector_parts(vectors[0:1, :], c, width)[1]

    @pl.loop(0, n // STEP_ROWS)
    def _(t):
        here = block(t, STEP_ROWS, n)
        d_branch, d_gate, d_product = unmix(
            up_in_ref[here, :],
            gate_s[here, :],
            branch_s[here, :],
            p_hat_s[here, :],
            p_rstd_s[here, :],
            gain[:, c:],
            weights[0, :, width:],
        )
        d_out = dot(mixed_s[here, :], d_branch, ((0,), (0,)))
        d_pre_ref[here, 2 * h :] = d_gate
        d_product_ref[here, :] = d_product
        grads_ref[:, 2 * h + c :] = d_out.astype(BF16)

    one_side(n, 0, d_product_ref, edges_s, slopes_s, d_pre_ref)
    d_pre = dot(normed_s[...], d_pre_ref[...], ((0,), (0,)))
    grads_ref[:, : 2 * h + c] = d_pre.astype(BF16)


def backward_right(n, d_product_ref, *refs):
    (edges_s, slopes_s, *kept) = kept_parts(refs, 0)
    normed_s = kept[-2]
    d_pre_ref, grads_ref = refs[KEPT:]
    one_side(n, 1, d_product_ref, edges_s, slopes_s, d_pre_ref)
    grads_ref[...] = dot(normed_s[...], d_pre_ref[...], ((0,), (0,))).astype(BF16)


def one_side(n, side, x, edges_s, slopes_s, d_pre_ref):
    h = edges_s.shape[2]

    @pl.loop(0, n // STEP_ROWS)
    def _(t):
        here = block(t, STEP_ROWS, n)
        d_edge = [
            contract(n, t * STEP_ROWS + r, x, edges_s.at[1 - side], side == 1)
            for r in range(0, STEP_ROWS, BLOCK_ROWS)
        ]
        d_pre_ref[here, : 2 * h] = edge_grads(
            jnp.concatenate(d_edge), slopes_s[side, here, :], edges_s[side, here, :]
        )


def own_rows(
    pair_ref, up_ref, d_left_ref, d_right_ref, weights, vectors, out_ref
):
    cells, c = out_ref.shape
    half = d_right_ref.shape[1]
    place = own_place(pair_ref)
    own = pl.ds(pl.multiple_of(place * cells, cells), cells)
    width = d_left_ref.shape[1] + half
    gain = vector_parts(vectors[0:1, :], c, width)[1]
    d_left, d_right = d_left_ref[own, :], d_right_ref[own, :]
    d_pre = jnp.concatenate([d_left[:, :half], d_right, d_left[:, half:]], axis=1)
    d_normed = dot(d_pre, weights[0, :, :width], ((1,), (1,))) * gain[:, :c]
    pulled = norm_vjp(*norm_parts(pair_ref[0, :cells, :]), d_normed)
    out_ref[...] = (up_ref[own, :] + pulled).astype(BF16)


def exchange(value, axis, size, step):
    return lax.ppermute(value, axis, [(d, d ^ step) for d in range(size)])


def near_rounds(value, groups):
    other = exchange(value, "dp", groups, 1)
    step = 2
    while step < groups // 2:
        value = add_narrow(value, other)
        other = exchange(value, "dp", groups, step)
        step *= 2
    return value, other


def add_narrow(a, b):
    return (a.astype(F32) + b.astype(F32)).astype(BF16)


def prepare(
    index_ref, mask_ref, state_ref, cot_ref, w, w_out, b, gain, shift, b_out, *refs
):
    sent_ref, weights_ref, vectors_ref, mask_s, sems = refs
    cells, c = state_ref.shape
    below, width = cells + TAIL_ROWS, w.shape[2]
    copies = [(mask_ref, mask_s), (state_ref, sent_ref.at[:cells]), (cot_ref, sent_ref.at[below:])]
    copies += [(w, weights_ref.at[:, :, :width]), (w_out, weights_ref.at[:, :, width:])]
    first = 0
    for vector in (b, gain, shift, b_out):
        last = first + vector.shape[1]
        copies.append((vector, vectors_ref.at[:, first:last]))
        first = last
    copies = [pltpu.make_async_copy(*pair, sems.at[k]) for k, pair in enumerate(copies)]
    for copy in copies:
        copy.start()
    copies[0].wait()
    length = jnp.max(jnp.sum(mask_s[...].astype(F32), axis=1, keepdims=True))
    in_length = lax.broadcasted_iota(jnp.int32, (TAIL_ROWS, c), 1) < 64
    place = index_ref[0].astype(F32)
    sent_ref[cells:below, :] = jnp.where(in_length, length, place).astype(BF16)
    for copy in copies[1:]:
        copy.wait()


def pair_up(near_ref, far_ref, state_ref, cot_ref):
    split = state_ref.shape[1]
    for side, ref in enumerate((near_ref, far_ref)):
        state_ref[side] = ref[:split, :]
        cot_ref[side] = ref[split:, :]


def hold(weights_in, vectors_in, weights_out, vectors_out):
    weights_out[...] = weights_in[...]
    vectors_out[...] = vectors_in[...]


def vector_parts(row, c, width):
    ends = [width, width + 2 * c, width + 4 * c, width + 5 * c]
    return [row[:, first:last] for first, last in zip([0] + ends, ends)]


def add_grads(rest, rest_near, left, left_near, right, right_far, proj_ref, out_ref):
    width = proj_ref.shape[2]
    c = out_ref.shape[2]
    half = (width - c) // 2
    total = rest[:, : width + c].astype(F32) + rest_near[:, : width + c].astype(F32)
    proj_ref[1] = total[:, :width]
    out_ref[1] = total[:, width:]
    total = left[...].astype(F32) + left_near[...].astype(F32)
    proj_ref[0, :, :half] = total[:, :half]
    proj_ref[0, :, 2 * half :] = total[:, half : half + c]
    out_ref[0] = total[:, half + c :]
    proj_ref[0, :, half : 2 * half] = right[...].astype(F32) + right_far[...].astype(F32)


def crop_shards(
    groups,
    parts,
    pair_repr,
    pair_mask,
    cotangent,
    proj_weight,
    proj_bias,
    norm_gain,
    norm_shift,
    out_weight,
    out_bias,
):
    _, rows, n, c = pair_repr.shape
    h = out_weight.shape[1]
    width = proj_weight.shape[2]
    cells, pairs = rows * n, n * n
    plane = (pairs + 8, h)
    kept = [jax.ShapeDtypeStruct((2, 2) + plane, F32)] * 2
    two = jax.ShapeDtypeStruct((2,) + plane, F32)
    kept += [two] + [jax.ShapeDtypeStruct(plane, F32)] * 2 + [two] * 3
    kept += [jax.ShapeDtypeStruct((2, pairs, h), BF16)] * 2
    grads = jax.ShapeDtypeStruct((c, width + c), BF16)
    vmem = pl.BlockSpec(memory_space=pltpu.VMEM)
    main = pl.BlockSpec(memory_space=pltpu.HBM)
    params = pltpu.CompilerParams(vmem_limit_bytes=VMEM_BYTES)

    def cost(planes):
        flops = 4 * pairs * width * c
        return pl.CostEstimate(
            flops=flops, bytes_accessed=planes * pairs * c * 4, transcendentals=0
        )

    packed = (
        jax.ShapeDtypeStruct((2, c, width + c), BF16),
        jax.ShapeDtypeStruct((2, width + 5 * c), F32),
    )
    sent, *weights = pl.pallas_call(
        prepare,
        out_shape=(jax.ShapeDtypeStruct((2 * cells + TAIL_ROWS, c), BF16),) + packed,
        in_specs=[pl.BlockSpec(memory_space=pltpu.SMEM)] + [main] * 9,
        out_specs=[vmem] * 3,
        scratch_shapes=[pltpu.VMEM((rows, n), jnp.int32), pltpu.SemaphoreType.DMA((9,))],
        compiler_params=pltpu.CompilerParams(vmem_limit_bytes=PREPARE_BYTES),
        name="prepare",
    )(
        lax.axis_index("dap").astype(jnp.int32)[None],
        pair_mask[0],
        pair_repr.reshape(cells, c),
        cotangent.reshape(cells, c),
        proj_weight,
        out_weight,
        proj_bias,
        norm_gain,
        norm_shift,
        out_bias,
    )
    weights = pl.pallas_call(
        hold,
        out_shape=packed,
        in_specs=[vmem] * 2,
        out_specs=[vmem] * 2,
        compiler_params=params,
        cost_estimate=cost(8),
        name="hold",
    )(*weights)
    beside = exchange(sent, "dap", parts, 1)
    beside, *weights = lax.optimization_barrier((beside, *weights))
    state, cot = pl.pallas_call(
        pair_up,
        out_shape=(
            jax.ShapeDtypeStruct((2, cells + TAIL_ROWS, c), BF16),
            jax.ShapeDtypeStruct((2, cells, c), BF16),
        ),
        in_specs=[vmem] * 2,
        out_specs=[vmem] * 2,
        compiler_params=params,
        name="pair_up",
    )(sent, beside)
    states, cots = [state], [cot]
    half = parts // 2
    jumps = [0, *range(1, half // 2), *reversed(range(half // 2, half))]
    for group in (states, cots):
        group += [exchange(group[0], "dap", parts, 2 * jump) for jump in jumps[1:]]

    held = pl.pallas_call(
        functools.partial(forward, n, jumps),
        out_shape=kept,
        in_specs=[vmem] * (half + 2),
        out_specs=(vmem,) * KEPT,
        scratch_shapes=[pltpu.VMEM((pairs, c), BF16), pltpu.VMEM(plane, F32)],
        compiler_params=params,
        cost_estimate=cost(64),
        name="forward",
    )(*states, *weights)

    double = pltpu.VMEM((2,) + plane, F32)
    up_1, grads_1 = pl.pallas_call(
        functools.partial(backward_second, n, jumps),
        out_shape=(jax.ShapeDtypeStruct((pairs, c), F32), grads),
        in_specs=[vmem] * (3 + half + KEPT),
        out_specs=(vmem, vmem),
        scratch_shapes=[
            double,
            double,
            pltpu.VMEM((pairs, width), BF16),
            pltpu.VMEM((pairs, c), BF16),
        ],
        compiler_params=params,
        cost_estimate=cost(48),
        name="backward_second",
    )(states[0], *cots, *weights, *held)
    far = groups // 2
    others_1 = exchange(grads_1, "dp", groups, far)

    d_left, d_product, grads_left = pl.pallas_call(
        functools.partial(backward_left, n),
        out_shape=(
            jax.ShapeDtypeStruct((pairs, 2 * h + c), BF16),
            jax.ShapeDtypeStruct(plane, F32),
            jax.ShapeDtypeStruct((c, 2 * h + 2 * c), BF16),
        ),
        in_specs=[vmem] * (3 + KEPT),
        out_specs=[vmem] * 3,
        compiler_params=params,
        cost_estimate=cost(24),
        name="backward_left",
    )(up_1, *weights, *held)
    others_left = exchange(grads_left, "dp", groups, far)

    d_right, grads_right = pl.pallas_call(
        functools.partial(backward_right, n),
        out_shape=(
            jax.ShapeDtypeStruct((pairs, 2 * h), BF16),
            jax.ShapeDtypeStruct((c, 2 * h), BF16),
        ),
        in_specs=[vmem] * (1 + KEPT),
        out_specs=[vmem] * 2,
        compiler_params=params,
        cost_estimate=cost(24),
        name="backward_right",
    )(d_product, *held)
    pair_grad = pl.pallas_call(
        own_rows,
        out_shape=jax.ShapeDtypeStruct((cells, c), BF16),
        in_specs=[vmem] * 6,
        out_specs=vmem,
        compiler_params=params,
        cost_estimate=cost(8),
        name="own_rows",
    )(states[0], up_1, d_left, d_right, *weights)

    rest, rest_near = near_rounds(
        jnp.concatenate([add_narrow(grads_1, others_1), grads_right], axis=1), groups
    )
    right = add_narrow(rest[:, width + c :], rest_near[:, width + c :])
    right_far = exchange(right, "dp", groups, far)
    ends_left = near_rounds(add_narrow(grads_left, others_left), groups)

    proj_total, out_total = pl.pallas_call(
        add_grads,
        out_shape=(
            jax.ShapeDtypeStruct((2, c, width), F32),
            jax.ShapeDtypeStruct((2, h, c), F32),
        ),
        in_specs=[vmem] * 6,
        out_specs=(vmem, vmem),
        compiler_params=params,
        name="add_grads",
    )(rest, rest_near, *ends_left, right, right_far)
    return pair_grad.reshape(pair_repr.shape), proj_total, out_total


def layer_norm(values, gain_vec, shift_vec, norm_axis):
    mean_value = jnp.mean(values, axis=norm_axis, keepdims=True)
    centred = values - mean_value
    variance = jnp.mean(centred * centred, axis=norm_axis, keepdims=True)
    return centred * lax.rsqrt(variance + NORM_EPSILON) * gain_vec + shift_vec


def norm_pullback(values, gain_vec, shift_vec, norm_axis, upstream):
    _, pull_back = jax.vjp(
        lambda inner_value: layer_norm(inner_value, gain_vec, shift_vec, norm_axis), values
    )
    return pull_back(upstream)[0]


def edge_pair(edge_pre, cell_mask):
    left_edge = jax.nn.sigmoid(edge_pre[1]) * edge_pre[0] * cell_mask
    right_edge = jax.nn.sigmoid(edge_pre[3]) * edge_pre[2] * cell_mask
    return jnp.stack([left_edge, right_edge]).astype(jnp.bfloat16)


def edge_pullback(edge_pre, cell_mask, grad_pair):
    sig_left = jax.nn.sigmoid(edge_pre[1])
    sig_right = jax.nn.sigmoid(edge_pre[3])
    grad_left = grad_pair[0].astype(jnp.float32) * cell_mask
    grad_right = grad_pair[1].astype(jnp.float32) * cell_mask
    return jnp.stack(
        [
            grad_left * sig_left,
            grad_left * edge_pre[0] * sig_left * (1.0 - sig_left),
            grad_right * sig_right,
            grad_right * edge_pre[2] * sig_right * (1.0 - sig_right),
        ]
    ).astype(jnp.bfloat16)


def triangle(pair_edges, outgoing):
    if outgoing:
        einsum_form = "cik,cjk->cij"
    else:
        einsum_form = "cki,ckj->cij"
    return jnp.einsum(
        einsum_form, pair_edges[0], pair_edges[1], preferred_element_type=jnp.float32
    ).astype(jnp.bfloat16)


def triangle_pullback(pair_edges, grad_product, outgoing):
    left_edge = pair_edges[0]
    right_edge = pair_edges[1]
    if outgoing:
        grad_left = jnp.einsum(
            "cij,cjk->cik", grad_product, right_edge, preferred_element_type=jnp.float32
        )
        grad_right = jnp.einsum(
            "cij,cik->cjk", grad_product, left_edge, preferred_element_type=jnp.float32
        )
    else:
        grad_left = jnp.einsum(
            "ckj,cij->cki", right_edge, grad_product, preferred_element_type=jnp.float32
        )
        grad_right = jnp.einsum(
            "cki,cij->ckj", left_edge, grad_product, preferred_element_type=jnp.float32
        )
    return jnp.stack([grad_left, grad_right]).astype(jnp.bfloat16)


def update_weights(proj_weight, proj_bias, norm_gain, norm_shift, update, channels, hidden):
    w_edge = proj_weight[update, :, : 4 * hidden].reshape(channels, 4, hidden)
    w_gate = proj_weight[update, :, 4 * hidden :]
    bias_edge = proj_bias[update, : 4 * hidden].reshape(4, hidden, 1, 1)
    bias_gate = proj_bias[update, 4 * hidden :]
    gain_in = norm_gain[update, :channels]
    shift_in = norm_shift[update, :channels]
    gain_out = norm_gain[update, channels:][:, None, None]
    shift_out = norm_shift[update, channels:][:, None, None]
    return (w_edge, w_gate, bias_edge, bias_gate, gain_in, shift_in, gain_out, shift_out)


def shards(
    pair_repr,
    pair_mask,
    cotangent,
    proj_weight,
    proj_bias,
    norm_gain,
    norm_shift,
    out_weight,
    out_bias,
):
    channels = pair_repr.shape[3]
    hidden = out_weight.shape[1]
    pair_state = pair_repr[0]
    cell_mask = pair_mask[0].astype(jnp.float32)
    records = []
    for update in range(2):
        w_edge, w_gate, bias_edge, bias_gate, gain_in, shift_in, gain_out, shift_out = (
            update_weights(proj_weight, proj_bias, norm_gain, norm_shift, update, channels, hidden)
        )
        state_f = pair_state.astype(jnp.float32)
        normed = layer_norm(state_f, gain_in, shift_in, -1).astype(jnp.bfloat16)
        edge_pre = (
            jnp.einsum("rnc,cgh->ghrn", normed, w_edge, preferred_element_type=jnp.float32)
            + bias_edge
        )
        gate_pre = (
            jnp.einsum("rnc,cd->rnd", normed, w_gate, preferred_element_type=jnp.float32)
            + bias_gate
        )
        pair_edges = edge_pair(edge_pre, cell_mask)
        spread = lax.all_to_all(pair_edges, "dap", split_axis=1, concat_axis=2, tiled=True)
        product = lax.all_to_all(
            triangle(spread, update == 0), "dap", split_axis=1, concat_axis=0, tiled=True
        )
        mixed_norm = layer_norm(product.astype(jnp.float32), gain_out, shift_out, 0).astype(
            jnp.bfloat16
        )
        branch = (
            jnp.einsum(
                "hrn,hd->rnd", mixed_norm, out_weight[update], preferred_element_type=jnp.float32
            )
            + out_bias[update]
        )
        records.append(
            (state_f, normed, edge_pre, gate_pre, pair_edges, spread, product, mixed_norm, branch)
        )
        pair_state = (state_f + jax.nn.sigmoid(gate_pre) * branch).astype(jnp.bfloat16)
    upstream = cotangent[0].astype(jnp.float32)
    proj_grads = []
    out_grads = []
    for update in (1, 0):
        state_f, normed, edge_pre, gate_pre, pair_edges, spread, product, mixed_norm, branch = (
            records[update]
        )
        w_edge, w_gate, bias_edge, bias_gate, gain_in, shift_in, gain_out, shift_out = (
            update_weights(proj_weight, proj_bias, norm_gain, norm_shift, update, channels, hidden)
        )
        gate_value = jax.nn.sigmoid(gate_pre)
        grad_branch = (upstream * gate_value).astype(jnp.bfloat16)
        grad_gate = (upstream * branch * gate_value * (1.0 - gate_value)).astype(jnp.bfloat16)
        out_grad = jnp.einsum(
            "hrn,rnd->hd", mixed_norm, grad_branch, preferred_element_type=jnp.float32
        )
        grad_mixed = jnp.einsum(
            "rnd,hd->hrn", grad_branch, out_weight[update], preferred_element_type=jnp.float32
        )
        grad_product = norm_pullback(
            product.astype(jnp.float32), gain_out, shift_out, 0, grad_mixed
        ).astype(jnp.bfloat16)
        column_edges = spread
        column_grad = lax.all_to_all(
            grad_product[None], "dap", split_axis=1, concat_axis=2, tiled=True
        )[0]
        grad_pair = lax.all_to_all(
            triangle_pullback(column_edges, column_grad, update == 0),
            "dap",
            split_axis=2,
            concat_axis=1,
            tiled=True,
        )
        grad_edge = edge_pullback(edge_pre, cell_mask, grad_pair)
        edge_grad = jnp.einsum(
            "rnc,ghrn->cgh", normed, grad_edge, preferred_element_type=jnp.float32
        ).reshape(channels, 4 * hidden)
        gate_grad = jnp.einsum("rnc,rnd->cd", normed, grad_gate, preferred_element_type=jnp.float32)
        grad_normed = jnp.einsum(
            "ghrn,cgh->rnc", grad_edge, w_edge, preferred_element_type=jnp.float32
        )
        grad_normed = grad_normed + jnp.einsum(
            "rnd,cd->rnc", grad_gate, w_gate, preferred_element_type=jnp.float32
        )
        upstream = upstream + norm_pullback(state_f, gain_in, shift_in, -1, grad_normed)
        proj_part = jnp.concatenate([edge_grad, gate_grad], axis=1)
        proj_grads.append(proj_part)
        out_grads.append(out_grad)
    proj_total = jnp.stack(proj_grads[::-1])
    out_total = jnp.stack(out_grads[::-1])
    proj_total, out_total = lax.psum((proj_total, out_total), ("dp", "dap"))
    return (upstream.astype(jnp.bfloat16)[None], proj_total, out_total)


def solution(mesh):
    placed = (
        P("dp", "dap", None, None),
        P("dp", "dap", None),
        P("dp", "dap", None, None),
        P(),
        P(),
        P(),
        P(),
        P(),
        P(),
    )
    groups, parts = mesh.shape["dp"], mesh.shape["dap"]

    def program(*args):
        n, c = args[0].shape[2:]
        rows = n // parts
        fits = 20 * n * n * c * 4 <= CROP_BUDGET
        paired = all(size >= 4 and size & (size - 1) == 0 for size in (groups, parts))
        even = args[7].shape[1] == c == 128 and STEP_ROWS % rows == 0 and n == STEP_ROWS
        body = functools.partial(crop_shards, groups, parts) if fits and even and paired else shards
        return spread_over(body)(*args)

    def spread_over(body):
        return jax.shard_map(
            body,
            mesh=mesh,
            in_specs=placed,
            out_specs=(P("dp", "dap", None, None), P(), P()),
            check_vma=False,
        )

    return program
```

```python
import functools

import jax
import jax.numpy as jnp
from jax import lax
from jax.experimental import pallas as pl
from jax.experimental.pallas import tpu as pltpu
from jax.sharding import PartitionSpec as P

NORM_EPSILON = 1e-05
VMEM_BYTES = 16 * 1024 * 1024
PREPARE_BYTES = 63 * 1024 * 1024
CROP_BUDGET = 32 * 1024 * 1024
BLOCK_ROWS = 8
STEP_ROWS = 32
KEPT = 10
TAIL_ROWS = 16
F32 = jnp.float32
BF16 = jnp.bfloat16


def sigmoid(x):
    return 0.5 * jnp.tanh(0.5 * x) + 0.5


def dot(a, b, dims=((1,), (0,))):
    return lax.dot_general(a, b, (dims, ((), ())), preferred_element_type=F32)


def norm_parts(x):
    x = x.astype(F32)
    centred = x - jnp.mean(x, axis=-1, keepdims=True)
    rstd = lax.rsqrt(jnp.mean(centred * centred, axis=-1, keepdims=True) + NORM_EPSILON)
    return centred * rstd, jnp.broadcast_to(rstd, x.shape)


def norm_vjp(x_hat, rstd, grad):
    mean_grad = jnp.mean(grad, axis=-1, keepdims=True)
    mean_prod = jnp.mean(grad * x_hat, axis=-1, keepdims=True)
    return rstd * (grad - mean_grad - x_hat * mean_prod)


def pair_mask_block(length, first_row, rows, n, lanes):
    shape = (rows, n, lanes)
    i = lax.broadcasted_iota(jnp.int32, shape, 0) + first_row
    j = lax.broadcasted_iota(jnp.int32, shape, 1)
    inside = jnp.where((i < length) & (j < length), 1.0, 0.0)
    return inside.reshape(rows * n, lanes)


def project(x, mask, w, b, gain, shift):
    x_hat, rstd = norm_parts(x)
    normed = (x_hat * gain + shift).astype(BF16)
    pre = dot(normed, w) + b
    h = (pre.shape[1] - x.shape[1]) // 4
    s_left = sigmoid(pre[:, h : 2 * h]) * mask
    s_right = sigmoid(pre[:, 3 * h : 4 * h]) * mask
    left = s_left * pre[:, :h]
    right = s_right * pre[:, 2 * h : 3 * h]
    gate = sigmoid(pre[:, 4 * h :])
    return x_hat, rstd, normed, s_left, s_right, left, right, gate


def mix(product, gain, shift, w_out, b_out):
    p_hat, p_rstd = norm_parts(product)
    mixed = (p_hat * gain + shift).astype(BF16)
    return p_hat, p_rstd, mixed, dot(mixed, w_out) + b_out


def unmix(up, gate, branch, p_hat, p_rstd, gain, w_out):
    d_branch = up * gate
    d_gate = (d_branch * branch * (1.0 - gate)).astype(BF16)
    d_branch = d_branch.astype(BF16)
    d_mixed = dot(d_branch, w_out, ((1,), (1,))) * gain
    return d_branch, d_gate, norm_vjp(p_hat, p_rstd, d_mixed)


def contract(n, first, x, y, swapped=False, pitch=0):
    lanes = y.shape[1]
    tiles = (n // 8, 8, lanes)

    def row(a, e):
        return e * n + first + a if swapped else (first + a) * n + e

    def step(e, totals):
        block = y[pl.ds(pl.multiple_of(e * (pitch or n), 8), n), :].reshape(tiles)
        return tuple(
            totals[a] + x[pl.ds(row(a, e), 8, stride=0), :][None] * block
            for a in range(BLOCK_ROWS)
        )

    zero = jnp.zeros(tiles, F32)
    totals = lax.fori_loop(0, n, step, (zero,) * BLOCK_ROWS, unroll=True)
    return jnp.stack(totals).reshape(BLOCK_ROWS * n, lanes)


def edge_grads(d_edge, slope, edge):
    grads = (d_edge * slope).astype(BF16), (d_edge * edge * (1.0 - slope)).astype(BF16)
    return jnp.concatenate(grads, axis=1)


def tail_values(block, lanes_from, lanes_to):
    lane = lax.broadcasted_iota(jnp.int32, block.shape, block.ndim - 1)
    inside = (lane >= lanes_from) & (lane < lanes_to)
    return jnp.max(jnp.where(inside, block.astype(F32), 0.0)).astype(jnp.int32)


def own_place(pair_ref):
    return tail_values(pair_ref[0, -TAIL_ROWS:, :], 64, 128)


def place_of(own, jump, side):
    return own ^ (2 * jump) ^ side


def block(t, rows, n):
    return pl.ds(pl.multiple_of(t * rows * n, rows * n), rows * n)


def forward(n, jumps, *refs):
    pairs, refs = refs[: len(jumps)], refs[len(jumps) :]
    (weights, vectors), refs = refs[:2], refs[2:]
    (edges_s, slopes_s, gate_s, hat_s, rstd_s) = refs[:5]
    (p_hat_s, p_rstd_s, branch_s, normed_s, mixed_s) = refs[5:KEPT]
    next_s, right_t_s = refs[KEPT:]
    c = weights.shape[1]
    width = weights.shape[2] - c
    rows = n // (2 * len(jumps))
    cells = rows * n
    tails = jnp.stack([pair[:, cells:, :] for pair in pairs])
    length = tail_values(tails, 0, 64)
    own = own_place(pairs[0])
    for pair, jump in zip(pairs, jumps):
        for side in range(2):
            next_s[block(place_of(own, jump, side), rows, n), :] = pair[side, :cells, :]
    steps = n // STEP_ROWS

    for u in range(2):
        bias, gains, shifts, bias_out = vector_parts(vectors[u : u + 1, :], c, width)

        @pl.loop(0, steps)
        def _(t):
            first = t * STEP_ROWS
            here = block(t, STEP_ROWS, n)
            mask = pair_mask_block(length, first, STEP_ROWS, n, c)
            x_hat, rstd, normed, s_left, s_right, left, right, gate = project(
                next_s[here, :], mask, weights[u, :, :width], bias, gains[:, :c], shifts[:, :c]
            )
            edges_s[u, 0, here, :] = left
            edges_s[u, 1, here, :] = right
            if u == 0:
                store_swapped(right_t_s, STEP_ROWS, n, first, right)
            slopes_s[u, 0, here, :] = s_left
            slopes_s[u, 1, here, :] = s_right
            gate_s[u, here, :] = gate
            hat_s[u, here, :] = x_hat
            rstd_s[u, here, :] = rstd
            normed_s[u, here, :] = normed

        @pl.loop(0, steps)
        def _(t):
            here = block(t, STEP_ROWS, n)
            x, y = edges_s.at[u, 0], edges_s.at[1, 1] if u == 1 else right_t_s
            product = [
                contract(n, t * STEP_ROWS + r, x, y, u == 1, (1 - u) * (n + 8))
                for r in range(0, STEP_ROWS, BLOCK_ROWS)
            ]
            p_hat, p_rstd, mixed, branch = mix(
                jnp.concatenate(product).astype(BF16),
                gains[:, c:],
                shifts[:, c:],
                weights[u, :, width:],
                bias_out,
            )
            p_hat_s[u, here, :] = p_hat
            p_rstd_s[u, here, :] = p_rstd
            mixed_s[u, here, :] = mixed
            branch_s[u, here, :] = branch
            if u == 0:
                x = next_s[here, :].astype(F32)
                next_s[here, :] = (x + gate_s[u, here, :] * branch).astype(BF16)


def kept_parts(refs, u):
    return [ref.at[u] for ref in refs[:KEPT]]


def store_swapped(ref, rows, n, first, values):
    for r in range(rows):
        ref[pl.ds(first + r, n, stride=n + 8), :] = values[r * n : (r + 1) * n]


def backward_second(n, jumps, pair, *refs):
    parted, refs = refs[: len(jumps)], refs[len(jumps) :]
    weights, vectors = refs[:2]
    (edges_s, slopes_s, gate_s, hat_s, rstd_s, *kept) = kept_parts(refs[2:], 1)
    (p_hat_s, p_rstd_s, branch_s, normed_s, mixed_s) = kept
    up_ref, grads_ref, d_product_s, d_edges_s, d_pre_s, cot_s = refs[2 + KEPT :]
    c, h = weights.shape[1], edges_s.shape[2]
    width = 4 * h + c
    gain = vector_parts(vectors[1:2, :], c, width)[1]
    own = own_place(pair)
    for part, jump in zip(parted, jumps):
        for side in range(2):
            cot_s[block(place_of(own, jump, side), part.shape[1] // n, n), :] = part[side]

    @pl.loop(0, n // STEP_ROWS)
    def _(t):
        here = block(t, STEP_ROWS, n)
        d_branch, d_gate, d_product = unmix(
            cot_s[here, :].astype(F32),
            gate_s[here, :],
            branch_s[here, :],
            p_hat_s[here, :],
            p_rstd_s[here, :],
            gain[:, c:],
            weights[1, :, width:],
        )
        d_out = dot(mixed_s[here, :], d_branch, ((0,), (0,)))
        d_pre_s[here, 4 * h :] = d_gate
        for r in range(STEP_ROWS):
            row = pl.ds(pl.multiple_of((t * STEP_ROWS + r) * (n + 8), 8), n)
            d_product_s[1, row, :] = d_product[r * n : (r + 1) * n]
        store_swapped(d_product_s.at[0], STEP_ROWS, n, t * STEP_ROWS, d_product)
        grads_ref[:, width:] = d_out.astype(BF16)

    blocks = n // BLOCK_ROWS

    @pl.loop(0, 2 * blocks)
    def _(step):
        side, t = step // blocks, step % blocks
        d_edges_s[side, block(t, BLOCK_ROWS, n), :] = contract(
            n, t * BLOCK_ROWS, edges_s.at[1 - side], d_product_s.at[side], pitch=n + 8
        )

    @pl.loop(0, n // STEP_ROWS)
    def _(t):
        here = block(t, STEP_ROWS, n)
        grads = [
            edge_grads(d_edges_s[side, here, :], slopes_s[side, here, :], edges_s[side, here, :])
            for side in range(2)
        ]
        d_pre = jnp.concatenate([*grads, d_pre_s[here, 4 * h :]], axis=1)
        normed = normed_s[here, :]
        d_normed = dot(d_pre, weights[1, :, :width], ((1,), (1,))) * gain[:, :c]
        pulled = norm_vjp(hat_s[here, :], rstd_s[here, :], d_normed)
        up_ref[here, :] = cot_s[here, :].astype(F32) + pulled
        grads_ref[:, :width] = dot(normed, d_pre, ((0,), (0,))).astype(BF16)


def backward_left(n, up_in_ref, weights, vectors, *refs):
    (edges_s, slopes_s, gate_s, _, _, *kept) = kept_parts(refs, 0)
    (p_hat_s, p_rstd_s, branch_s, normed_s, mixed_s) = kept
    d_pre_ref, d_product_ref, grads_ref, d_edge_s = refs[KEPT:]
    c, h = weights.shape[1], edges_s.shape[2]
    width = 4 * h + c
    gain = vector_parts(vectors[0:1, :], c, width)[1]

    @pl.loop(0, n // STEP_ROWS)
    def _(t):
        here = block(t, STEP_ROWS, n)
        d_branch, d_gate, d_product = unmix(
            up_in_ref[here, :],
            gate_s[here, :],
            branch_s[here, :],
            p_hat_s[here, :],
            p_rstd_s[here, :],
            gain[:, c:],
            weights[0, :, width:],
        )
        d_out = dot(mixed_s[here, :], d_branch, ((0,), (0,)))
        d_pre_ref[here, 2 * h :] = d_gate
        d_product_ref[here, :] = d_product
        grads_ref[:, 2 * h + c :] = d_out.astype(BF16)

    one_side(n, 0, d_product_ref, edges_s, slopes_s, d_edge_s, d_pre_ref)
    d_pre = dot(normed_s[...], d_pre_ref[...], ((0,), (0,)))
    grads_ref[:, : 2 * h + c] = d_pre.astype(BF16)


def backward_right(n, d_product_ref, *refs):
    (edges_s, slopes_s, *kept) = kept_parts(refs, 0)
    normed_s = kept[-2]
    d_pre_ref, grads_ref, d_edge_s = refs[KEPT:]
    one_side(n, 1, d_product_ref, edges_s, slopes_s, d_edge_s, d_pre_ref)
    grads_ref[...] = dot(normed_s[...], d_pre_ref[...], ((0,), (0,))).astype(BF16)


def one_side(n, side, x, edges_s, slopes_s, d_edge_s, d_pre_ref):
    h = edges_s.shape[2]

    @pl.loop(0, n // BLOCK_ROWS)
    def _(t):
        d_edge_s[block(t, BLOCK_ROWS, n), :] = contract(
            n, t * BLOCK_ROWS, x, edges_s.at[1 - side], side == 1
        )

    @pl.loop(0, n // STEP_ROWS)
    def _(t):
        here = block(t, STEP_ROWS, n)
        d_pre_ref[here, : 2 * h] = edge_grads(
            d_edge_s[here, :], slopes_s[side, here, :], edges_s[side, here, :]
        )


def own_rows(
    pair_ref, up_ref, d_left_ref, d_right_ref, weights, vectors, hat_ref, rstd_ref, out_ref
):
    cells, c = out_ref.shape
    half = d_right_ref.shape[1]
    place = own_place(pair_ref)
    own = pl.ds(pl.multiple_of(place * cells, cells), cells)
    width = d_left_ref.shape[1] + half
    gain = vector_parts(vectors[0:1, :], c, width)[1]
    d_left, d_right = d_left_ref[own, :], d_right_ref[own, :]
    d_pre = jnp.concatenate([d_left[:, :half], d_right, d_left[:, half:]], axis=1)
    d_normed = dot(d_pre, weights[0, :, :width], ((1,), (1,))) * gain[:, :c]
    pulled = norm_vjp(hat_ref[0, own, :], rstd_ref[0, own, :], d_normed)
    out_ref[...] = (up_ref[own, :] + pulled).astype(BF16)


def exchange(value, axis, size, step):
    return lax.ppermute(value, axis, [(d, d ^ step) for d in range(size)])


def near_rounds(value, groups):
    other = exchange(value, "dp", groups, 1)
    step = 2
    while step < groups // 2:
        value = add_narrow(value, other)
        other = exchange(value, "dp", groups, step)
        step *= 2
    return value, other


def add_narrow(a, b):
    return (a.astype(F32) + b.astype(F32)).astype(BF16)


def prepare(
    index_ref, mask_ref, state_ref, cot_ref, w, w_out, b, gain, shift, b_out, *refs
):
    sent_ref, weights_ref, vectors_ref, mask_s, sems = refs
    cells, c = state_ref.shape
    below, width = cells + TAIL_ROWS, w.shape[2]
    copies = [(mask_ref, mask_s), (state_ref, sent_ref.at[:cells]), (cot_ref, sent_ref.at[below:])]
    copies += [(w, weights_ref.at[:, :, :width]), (w_out, weights_ref.at[:, :, width:])]
    first = 0
    for vector in (b, gain, shift, b_out):
        last = first + vector.shape[1]
        copies.append((vector, vectors_ref.at[:, first:last]))
        first = last
    copies = [pltpu.make_async_copy(*pair, sems.at[k]) for k, pair in enumerate(copies)]
    for copy in copies:
        copy.start()
    copies[0].wait()
    length = jnp.max(jnp.sum(mask_s[...].astype(F32), axis=1, keepdims=True))
    in_length = lax.broadcasted_iota(jnp.int32, (TAIL_ROWS, c), 1) < 64
    place = index_ref[0].astype(F32)
    sent_ref[cells:below, :] = jnp.where(in_length, length, place).astype(BF16)
    for copy in copies[1:]:
        copy.wait()


def pair_up(near_ref, far_ref, state_ref, cot_ref):
    split = state_ref.shape[1]
    for side, ref in enumerate((near_ref, far_ref)):
        state_ref[side] = ref[:split, :]
        cot_ref[side] = ref[split:, :]


def hold(weights_in, vectors_in, weights_out, vectors_out):
    weights_out[...] = weights_in[...]
    vectors_out[...] = vectors_in[...]


def vector_parts(row, c, width):
    ends = [width, width + 2 * c, width + 4 * c, width + 5 * c]
    return [row[:, first:last] for first, last in zip([0] + ends, ends)]


def add_grads(rest, rest_near, left, left_near, right, right_far, proj_ref, out_ref):
    width = proj_ref.shape[2]
    c = out_ref.shape[2]
    half = (width - c) // 2
    total = rest[:, : width + c].astype(F32) + rest_near[:, : width + c].astype(F32)
    proj_ref[1] = total[:, :width]
    out_ref[1] = total[:, width:]
    total = left[...].astype(F32) + left_near[...].astype(F32)
    proj_ref[0, :, :half] = total[:, :half]
    proj_ref[0, :, 2 * half :] = total[:, half : half + c]
    out_ref[0] = total[:, half + c :]
    proj_ref[0, :, half : 2 * half] = right[...].astype(F32) + right_far[...].astype(F32)


def crop_shards(
    groups,
    parts,
    pair_repr,
    pair_mask,
    cotangent,
    proj_weight,
    proj_bias,
    norm_gain,
    norm_shift,
    out_weight,
    out_bias,
):
    _, rows, n, c = pair_repr.shape
    h = out_weight.shape[1]
    width = proj_weight.shape[2]
    cells, pairs = rows * n, n * n
    plane = (pairs + 8, h)
    wide_plane = (n * (n + 8), h)
    kept = [jax.ShapeDtypeStruct((2, 2) + plane, F32)] * 2
    kept += [jax.ShapeDtypeStruct((2,) + plane, F32)] * 6
    kept += [jax.ShapeDtypeStruct((2, pairs, h), BF16)] * 2
    grads = jax.ShapeDtypeStruct((c, width + c), BF16)
    vmem = pl.BlockSpec(memory_space=pltpu.VMEM)
    main = pl.BlockSpec(memory_space=pltpu.HBM)
    params = pltpu.CompilerParams(vmem_limit_bytes=VMEM_BYTES)

    def cost(planes):
        flops = 4 * pairs * width * c
        return pl.CostEstimate(
            flops=flops, bytes_accessed=planes * pairs * c * 4, transcendentals=0
        )

    packed = (
        jax.ShapeDtypeStruct((2, c, width + c), BF16),
        jax.ShapeDtypeStruct((2, width + 5 * c), F32),
    )
    sent, *weights = pl.pallas_call(
        prepare,
        out_shape=(jax.ShapeDtypeStruct((2 * cells + TAIL_ROWS, c), BF16),) + packed,
        in_specs=[pl.BlockSpec(memory_space=pltpu.SMEM)] + [main] * 9,
        out_specs=[vmem] * 3,
        scratch_shapes=[pltpu.VMEM((rows, n), jnp.int32), pltpu.SemaphoreType.DMA((9,))],
        compiler_params=pltpu.CompilerParams(vmem_limit_bytes=PREPARE_BYTES),
        name="prepare",
    )(
        lax.axis_index("dap").astype(jnp.int32)[None],
        pair_mask[0],
        pair_repr.reshape(cells, c),
        cotangent.reshape(cells, c),
        proj_weight,
        out_weight,
        proj_bias,
        norm_gain,
        norm_shift,
        out_bias,
    )
    weights = pl.pallas_call(
        hold,
        out_shape=packed,
        in_specs=[vmem] * 2,
        out_specs=[vmem] * 2,
        compiler_params=params,
        cost_estimate=cost(8),
        name="hold",
    )(*weights)
    beside = exchange(sent, "dap", parts, 1)
    beside, *weights = lax.optimization_barrier((beside, *weights))
    state, cot = pl.pallas_call(
        pair_up,
        out_shape=(
            jax.ShapeDtypeStruct((2, cells + TAIL_ROWS, c), BF16),
            jax.ShapeDtypeStruct((2, cells, c), BF16),
        ),
        in_specs=[vmem] * 2,
        out_specs=[vmem] * 2,
        compiler_params=params,
        name="pair_up",
    )(sent, beside)
    states, cots = [state], [cot]
    half = parts // 2
    jumps = [0, *range(1, half // 2), *reversed(range(half // 2, half))]
    for group in (states, cots):
        group += [exchange(group[0], "dap", parts, 2 * jump) for jump in jumps[1:]]

    held = pl.pallas_call(
        functools.partial(forward, n, jumps),
        out_shape=kept,
        in_specs=[vmem] * (half + 2),
        out_specs=(vmem,) * KEPT,
        scratch_shapes=[pltpu.VMEM((pairs, c), BF16), pltpu.VMEM(wide_plane, F32)],
        compiler_params=params,
        cost_estimate=cost(64),
        name="forward",
    )(*states, *weights)

    double, single = pltpu.VMEM((2,) + plane, F32), pltpu.VMEM(plane, F32)
    up_1, grads_1 = pl.pallas_call(
        functools.partial(backward_second, n, jumps),
        out_shape=(jax.ShapeDtypeStruct((pairs, c), F32), grads),
        in_specs=[vmem] * (3 + half + KEPT),
        out_specs=(vmem, vmem),
        scratch_shapes=[
            pltpu.VMEM((2,) + wide_plane, F32),
            double,
            pltpu.VMEM((pairs, width), BF16),
            pltpu.VMEM((pairs, c), BF16),
        ],
        compiler_params=params,
        cost_estimate=cost(48),
        name="backward_second",
    )(states[0], *cots, *weights, *held)
    far = groups // 2
    others_1 = exchange(grads_1, "dp", groups, far)

    d_left, d_product, grads_left = pl.pallas_call(
        functools.partial(backward_left, n),
        out_shape=(
            jax.ShapeDtypeStruct((pairs, 2 * h + c), BF16),
            jax.ShapeDtypeStruct(plane, F32),
            jax.ShapeDtypeStruct((c, 2 * h + 2 * c), BF16),
        ),
        in_specs=[vmem] * (3 + KEPT),
        out_specs=[vmem] * 3,
        scratch_shapes=[single],
        compiler_params=params,
        cost_estimate=cost(24),
        name="backward_left",
    )(up_1, *weights, *held)
    others_left = exchange(grads_left, "dp", groups, far)

    d_right, grads_right = pl.pallas_call(
        functools.partial(backward_right, n),
        out_shape=(
            jax.ShapeDtypeStruct((pairs, 2 * h), BF16),
            jax.ShapeDtypeStruct((c, 2 * h), BF16),
        ),
        in_specs=[vmem] * (1 + KEPT),
        out_specs=[vmem] * 2,
        scratch_shapes=[single],
        compiler_params=params,
        cost_estimate=cost(24),
        name="backward_right",
    )(d_product, *held)
    pair_grad = pl.pallas_call(
        own_rows,
        out_shape=jax.ShapeDtypeStruct((cells, c), BF16),
        in_specs=[vmem] * 8,
        out_specs=vmem,
        compiler_params=params,
        cost_estimate=cost(8),
        name="own_rows",
    )(states[0], up_1, d_left, d_right, *weights, held[3], held[4])

    rest, rest_near = near_rounds(
        jnp.concatenate([add_narrow(grads_1, others_1), grads_right], axis=1), groups
    )
    right = add_narrow(rest[:, width + c :], rest_near[:, width + c :])
    right_far = exchange(right, "dp", groups, far)
    ends_left = near_rounds(add_narrow(grads_left, others_left), groups)

    proj_total, out_total = pl.pallas_call(
        add_grads,
        out_shape=(
            jax.ShapeDtypeStruct((2, c, width), F32),
            jax.ShapeDtypeStruct((2, h, c), F32),
        ),
        in_specs=[vmem] * 6,
        out_specs=(vmem, vmem),
        compiler_params=params,
        name="add_grads",
    )(rest, rest_near, *ends_left, right, right_far)
    return pair_grad.reshape(pair_repr.shape), proj_total, out_total


def layer_norm(values, gain_vec, shift_vec, norm_axis):
    mean_value = jnp.mean(values, axis=norm_axis, keepdims=True)
    centred = values - mean_value
    variance = jnp.mean(centred * centred, axis=norm_axis, keepdims=True)
    return centred * lax.rsqrt(variance + NORM_EPSILON) * gain_vec + shift_vec


def norm_pullback(values, gain_vec, shift_vec, norm_axis, upstream):
    _, pull_back = jax.vjp(
        lambda inner_value: layer_norm(inner_value, gain_vec, shift_vec, norm_axis), values
    )
    return pull_back(upstream)[0]


def edge_pair(edge_pre, cell_mask):
    left_edge = jax.nn.sigmoid(edge_pre[1]) * edge_pre[0] * cell_mask
    right_edge = jax.nn.sigmoid(edge_pre[3]) * edge_pre[2] * cell_mask
    return jnp.stack([left_edge, right_edge]).astype(jnp.bfloat16)


def edge_pullback(edge_pre, cell_mask, grad_pair):
    sig_left = jax.nn.sigmoid(edge_pre[1])
    sig_right = jax.nn.sigmoid(edge_pre[3])
    grad_left = grad_pair[0].astype(jnp.float32) * cell_mask
    grad_right = grad_pair[1].astype(jnp.float32) * cell_mask
    return jnp.stack(
        [
            grad_left * sig_left,
            grad_left * edge_pre[0] * sig_left * (1.0 - sig_left),
            grad_right * sig_right,
            grad_right * edge_pre[2] * sig_right * (1.0 - sig_right),
        ]
    ).astype(jnp.bfloat16)


def triangle(pair_edges, outgoing):
    if outgoing:
        einsum_form = "cik,cjk->cij"
    else:
        einsum_form = "cki,ckj->cij"
    return jnp.einsum(
        einsum_form, pair_edges[0], pair_edges[1], preferred_element_type=jnp.float32
    ).astype(jnp.bfloat16)


def triangle_pullback(pair_edges, grad_product, outgoing):
    left_edge = pair_edges[0]
    right_edge = pair_edges[1]
    if outgoing:
        grad_left = jnp.einsum(
            "cij,cjk->cik", grad_product, right_edge, preferred_element_type=jnp.float32
        )
        grad_right = jnp.einsum(
            "cij,cik->cjk", grad_product, left_edge, preferred_element_type=jnp.float32
        )
    else:
        grad_left = jnp.einsum(
            "ckj,cij->cki", right_edge, grad_product, preferred_element_type=jnp.float32
        )
        grad_right = jnp.einsum(
            "cki,cij->ckj", left_edge, grad_product, preferred_element_type=jnp.float32
        )
    return jnp.stack([grad_left, grad_right]).astype(jnp.bfloat16)


def update_weights(proj_weight, proj_bias, norm_gain, norm_shift, update, channels, hidden):
    w_edge = proj_weight[update, :, : 4 * hidden].reshape(channels, 4, hidden)
    w_gate = proj_weight[update, :, 4 * hidden :]
    bias_edge = proj_bias[update, : 4 * hidden].reshape(4, hidden, 1, 1)
    bias_gate = proj_bias[update, 4 * hidden :]
    gain_in = norm_gain[update, :channels]
    shift_in = norm_shift[update, :channels]
    gain_out = norm_gain[update, channels:][:, None, None]
    shift_out = norm_shift[update, channels:][:, None, None]
    return (w_edge, w_gate, bias_edge, bias_gate, gain_in, shift_in, gain_out, shift_out)


def shards(
    pair_repr,
    pair_mask,
    cotangent,
    proj_weight,
    proj_bias,
    norm_gain,
    norm_shift,
    out_weight,
    out_bias,
):
    channels = pair_repr.shape[3]
    hidden = out_weight.shape[1]
    pair_state = pair_repr[0]
    cell_mask = pair_mask[0].astype(jnp.float32)
    records = []
    for update in range(2):
        w_edge, w_gate, bias_edge, bias_gate, gain_in, shift_in, gain_out, shift_out = (
            update_weights(proj_weight, proj_bias, norm_gain, norm_shift, update, channels, hidden)
        )
        state_f = pair_state.astype(jnp.float32)
        normed = layer_norm(state_f, gain_in, shift_in, -1).astype(jnp.bfloat16)
        edge_pre = (
            jnp.einsum("rnc,cgh->ghrn", normed, w_edge, preferred_element_type=jnp.float32)
            + bias_edge
        )
        gate_pre = (
            jnp.einsum("rnc,cd->rnd", normed, w_gate, preferred_element_type=jnp.float32)
            + bias_gate
        )
        pair_edges = edge_pair(edge_pre, cell_mask)
        spread = lax.all_to_all(pair_edges, "dap", split_axis=1, concat_axis=2, tiled=True)
        product = lax.all_to_all(
            triangle(spread, update == 0), "dap", split_axis=1, concat_axis=0, tiled=True
        )
        mixed_norm = layer_norm(product.astype(jnp.float32), gain_out, shift_out, 0).astype(
            jnp.bfloat16
        )
        branch = (
            jnp.einsum(
                "hrn,hd->rnd", mixed_norm, out_weight[update], preferred_element_type=jnp.float32
            )
            + out_bias[update]
        )
        records.append(
            (state_f, normed, edge_pre, gate_pre, pair_edges, spread, product, mixed_norm, branch)
        )
        pair_state = (state_f + jax.nn.sigmoid(gate_pre) * branch).astype(jnp.bfloat16)
    upstream = cotangent[0].astype(jnp.float32)
    proj_grads = []
    out_grads = []
    for update in (1, 0):
        state_f, normed, edge_pre, gate_pre, pair_edges, spread, product, mixed_norm, branch = (
            records[update]
        )
        w_edge, w_gate, bias_edge, bias_gate, gain_in, shift_in, gain_out, shift_out = (
            update_weights(proj_weight, proj_bias, norm_gain, norm_shift, update, channels, hidden)
        )
        gate_value = jax.nn.sigmoid(gate_pre)
        grad_branch = (upstream * gate_value).astype(jnp.bfloat16)
        grad_gate = (upstream * branch * gate_value * (1.0 - gate_value)).astype(jnp.bfloat16)
        out_grad = jnp.einsum(
            "hrn,rnd->hd", mixed_norm, grad_branch, preferred_element_type=jnp.float32
        )
        grad_mixed = jnp.einsum(
            "rnd,hd->hrn", grad_branch, out_weight[update], preferred_element_type=jnp.float32
        )
        grad_product = norm_pullback(
            product.astype(jnp.float32), gain_out, shift_out, 0, grad_mixed
        ).astype(jnp.bfloat16)
        column_edges = spread
        column_grad = lax.all_to_all(
            grad_product[None], "dap", split_axis=1, concat_axis=2, tiled=True
        )[0]
        grad_pair = lax.all_to_all(
            triangle_pullback(column_edges, column_grad, update == 0),
            "dap",
            split_axis=2,
            concat_axis=1,
            tiled=True,
        )
        grad_edge = edge_pullback(edge_pre, cell_mask, grad_pair)
        edge_grad = jnp.einsum(
            "rnc,ghrn->cgh", normed, grad_edge, preferred_element_type=jnp.float32
        ).reshape(channels, 4 * hidden)
        gate_grad = jnp.einsum("rnc,rnd->cd", normed, grad_gate, preferred_element_type=jnp.float32)
        grad_normed = jnp.einsum(
            "ghrn,cgh->rnc", grad_edge, w_edge, preferred_element_type=jnp.float32
        )
        grad_normed = grad_normed + jnp.einsum(
            "rnd,cd->rnc", grad_gate, w_gate, preferred_element_type=jnp.float32
        )
        upstream = upstream + norm_pullback(state_f, gain_in, shift_in, -1, grad_normed)
        proj_part = jnp.concatenate([edge_grad, gate_grad], axis=1)
        proj_grads.append(proj_part)
        out_grads.append(out_grad)
    proj_total = jnp.stack(proj_grads[::-1])
    out_total = jnp.stack(out_grads[::-1])
    proj_total, out_total = lax.psum((proj_total, out_total), ("dp", "dap"))
    return (upstream.astype(jnp.bfloat16)[None], proj_total, out_total)


def solution(mesh):
    placed = (
        P("dp", "dap", None, None),
        P("dp", "dap", None),
        P("dp", "dap", None, None),
        P(),
        P(),
        P(),
        P(),
        P(),
        P(),
    )
    groups, parts = mesh.shape["dp"], mesh.shape["dap"]

    def program(*args):
        n, c = args[0].shape[2:]
        rows = n // parts
        fits = 20 * n * n * c * 4 <= CROP_BUDGET
        paired = all(size >= 4 and size & (size - 1) == 0 for size in (groups, parts))
        even = args[7].shape[1] == c == 128 and STEP_ROWS % rows == 0 and n == STEP_ROWS
        body = functools.partial(crop_shards, groups, parts) if fits and even and paired else shards
        return spread_over(body)(*args)

    def spread_over(body):
        return jax.shard_map(
            body,
            mesh=mesh,
            in_specs=placed,
            out_specs=(P("dp", "dap", None, None), P(), P()),
            check_vma=False,
        )

    return program
```

```python
import functools

import jax
import jax.numpy as jnp
from jax import lax
from jax.experimental import pallas as pl
from jax.experimental.pallas import tpu as pltpu
from jax.sharding import PartitionSpec as P

NORM_EPSILON = 1e-05
VMEM_BYTES = 16 * 1024 * 1024
PREPARE_BYTES = 63 * 1024 * 1024
CROP_BUDGET = 32 * 1024 * 1024
BLOCK_ROWS = 8
STEP_ROWS = 32
KEPT = 10
TAIL_ROWS = 16
F32 = jnp.float32
BF16 = jnp.bfloat16


def sigmoid(x):
    return 0.5 * jnp.tanh(0.5 * x) + 0.5


def dot(a, b, dims=((1,), (0,))):
    return lax.dot_general(a, b, (dims, ((), ())), preferred_element_type=F32)


def norm_parts(x):
    x = x.astype(F32)
    centred = x - jnp.mean(x, axis=-1, keepdims=True)
    rstd = lax.rsqrt(jnp.mean(centred * centred, axis=-1, keepdims=True) + NORM_EPSILON)
    return centred * rstd, jnp.broadcast_to(rstd, x.shape)


def norm_vjp(x_hat, rstd, grad):
    mean_grad = jnp.mean(grad, axis=-1, keepdims=True)
    mean_prod = jnp.mean(grad * x_hat, axis=-1, keepdims=True)
    return rstd * (grad - mean_grad - x_hat * mean_prod)


def pair_mask_block(length, first_row, rows, n, lanes):
    i = lax.broadcasted_iota(jnp.int32, (rows, 8, lanes), 0) + first_row
    j = lax.broadcasted_iota(jnp.int32, (n, lanes), 0)
    row_inside = jnp.where(i < length, 1.0, 0.0)
    column_inside = jnp.where(j < length, 1.0, 0.0).reshape(1, n // 8, 8, lanes)
    return (row_inside[:, None] * column_inside).reshape(rows * n, lanes)


def project(x, mask, w, b, gain, shift):
    x_hat, rstd = norm_parts(x)
    normed = (x_hat * gain + shift).astype(BF16)
    pre = dot(normed, w) + b
    h = (pre.shape[1] - x.shape[1]) // 4
    s_left = sigmoid(pre[:, h : 2 * h]) * mask
    s_right = sigmoid(pre[:, 3 * h : 4 * h]) * mask
    left = s_left * pre[:, :h]
    right = s_right * pre[:, 2 * h : 3 * h]
    gate = sigmoid(pre[:, 4 * h :])
    return x_hat, rstd, normed, s_left, s_right, left, right, gate


def mix(product, gain, shift, w_out, b_out):
    p_hat, p_rstd = norm_parts(product)
    mixed = (p_hat * gain + shift).astype(BF16)
    return p_hat, p_rstd, mixed, dot(mixed, w_out) + b_out


def unmix(up, gate, branch, p_hat, p_rstd, gain, w_out):
    d_branch = up * gate
    d_gate = (d_branch * branch * (1.0 - gate)).astype(BF16)
    d_branch = d_branch.astype(BF16)
    d_mixed = dot(d_branch, w_out, ((1,), (1,))) * gain
    return d_branch, d_gate, norm_vjp(p_hat, p_rstd, d_mixed)


def contract(n, first, x, y, swapped=False, pitch=0):
    lanes = y.shape[1]
    tiles = (n // 8, 8, lanes)

    def row(a, e):
        return e * n + first + a if swapped else (first + a) * n + e

    def step(e, totals):
        block = y[pl.ds(pl.multiple_of(e * (pitch or n), 8), n), :].reshape(tiles)
        return tuple(
            totals[a] + x[pl.ds(row(a, e), 8, stride=0), :][None] * block
            for a in range(BLOCK_ROWS)
        )

    zero = jnp.zeros(tiles, F32)
    totals = lax.fori_loop(0, n, step, (zero,) * BLOCK_ROWS, unroll=True)
    return jnp.stack(totals).reshape(BLOCK_ROWS * n, lanes)


def edge_grads(d_edge, slope, edge):
    grads = (d_edge * slope).astype(BF16), (d_edge * edge * (1.0 - slope)).astype(BF16)
    return jnp.concatenate(grads, axis=1)


def tail_values(block, lanes_from, lanes_to):
    lane = lax.broadcasted_iota(jnp.int32, block.shape, block.ndim - 1)
    inside = (lane >= lanes_from) & (lane < lanes_to)
    return jnp.max(jnp.where(inside, block.astype(F32), 0.0)).astype(jnp.int32)


def own_place(pair_ref):
    return tail_values(pair_ref[0, -TAIL_ROWS:, :], 64, 128)


def place_of(own, jump, side):
    return own ^ (2 * jump) ^ side


def block(t, rows, n):
    return pl.ds(pl.multiple_of(t * rows * n, rows * n), rows * n)


def forward(n, jumps, *refs):
    pairs, refs = refs[: len(jumps)], refs[len(jumps) :]
    (weights, vectors), refs = refs[:2], refs[2:]
    (edges_s, slopes_s, gate_s, hat_s, rstd_s) = refs[:5]
    (p_hat_s, p_rstd_s, branch_s, normed_s, mixed_s) = refs[5:KEPT]
    next_s, right_t_s = refs[KEPT:]
    c = weights.shape[1]
    width = weights.shape[2] - c
    rows = n // (2 * len(jumps))
    cells = rows * n
    tails = jnp.stack([pair[:, cells:, :] for pair in pairs])
    length = tail_values(tails, 0, 64)
    own = own_place(pairs[0])
    for pair, jump in zip(pairs, jumps):
        for side in range(2):
            next_s[block(place_of(own, jump, side), rows, n), :] = pair[side, :cells, :]
    steps = n // STEP_ROWS

    for u in range(2):
        bias, gains, shifts, bias_out = vector_parts(vectors[u : u + 1, :], c, width)

        @pl.loop(0, steps)
        def _(t):
            first = t * STEP_ROWS
            here = block(t, STEP_ROWS, n)
            mask = pair_mask_block(length, first, STEP_ROWS, n, c)
            x_hat, rstd, normed, s_left, s_right, left, right, gate = project(
                next_s[here, :], mask, weights[u, :, :width], bias, gains[:, :c], shifts[:, :c]
            )
            edges_s[u, 0, here, :] = left
            edges_s[u, 1, here, :] = right
            if u == 0:
                store_swapped(right_t_s, STEP_ROWS, n, first, right)
            slopes_s[u, 0, here, :] = s_left
            slopes_s[u, 1, here, :] = s_right
            gate_s[u, here, :] = gate
            hat_s[u, here, :] = x_hat
            rstd_s[u, here, :] = rstd
            normed_s[u, here, :] = normed

        @pl.loop(0, steps)
        def _(t):
            here = block(t, STEP_ROWS, n)
            x, y = edges_s.at[u, 0], edges_s.at[1, 1] if u == 1 else right_t_s
            product = [
                contract(n, t * STEP_ROWS + r, x, y, u == 1, (1 - u) * (n + 8))
                for r in range(0, STEP_ROWS, BLOCK_ROWS)
            ]
            p_hat, p_rstd, mixed, branch = mix(
                jnp.concatenate(product).astype(BF16),
                gains[:, c:],
                shifts[:, c:],
                weights[u, :, width:],
                bias_out,
            )
            p_hat_s[u, here, :] = p_hat
            p_rstd_s[u, here, :] = p_rstd
            mixed_s[u, here, :] = mixed
            branch_s[u, here, :] = branch
            if u == 0:
                x = next_s[here, :].astype(F32)
                next_s[here, :] = (x + gate_s[u, here, :] * branch).astype(BF16)


def kept_parts(refs, u):
    return [ref.at[u] for ref in refs[:KEPT]]


def store_swapped(ref, rows, n, first, values):
    for r in range(rows):
        ref[pl.ds(first + r, n, stride=n + 8), :] = values[r * n : (r + 1) * n]


def backward_second(n, jumps, pair, *refs):
    parted, refs = refs[: len(jumps)], refs[len(jumps) :]
    weights, vectors = refs[:2]
    (edges_s, slopes_s, gate_s, hat_s, rstd_s, *kept) = kept_parts(refs[2:], 1)
    (p_hat_s, p_rstd_s, branch_s, normed_s, mixed_s) = kept
    up_ref, grads_ref, d_product_s, d_edges_s, d_pre_s, cot_s = refs[2 + KEPT :]
    c, h = weights.shape[1], edges_s.shape[2]
    width = 4 * h + c
    gain = vector_parts(vectors[1:2, :], c, width)[1]
    own = own_place(pair)
    for part, jump in zip(parted, jumps):
        for side in range(2):
            cot_s[block(place_of(own, jump, side), part.shape[1] // n, n), :] = part[side]

    @pl.loop(0, n // STEP_ROWS)
    def _(t):
        here = block(t, STEP_ROWS, n)
        d_branch, d_gate, d_product = unmix(
            cot_s[here, :].astype(F32),
            gate_s[here, :],
            branch_s[here, :],
            p_hat_s[here, :],
            p_rstd_s[here, :],
            gain[:, c:],
            weights[1, :, width:],
        )
        d_out = dot(mixed_s[here, :], d_branch, ((0,), (0,)))
        d_pre_s[here, 4 * h :] = d_gate
        for r in range(STEP_ROWS):
            row = pl.ds(pl.multiple_of((t * STEP_ROWS + r) * (n + 8), 8), n)
            d_product_s[1, row, :] = d_product[r * n : (r + 1) * n]
        store_swapped(d_product_s.at[0], STEP_ROWS, n, t * STEP_ROWS, d_product)
        grads_ref[:, width:] = d_out.astype(BF16)

    blocks = n // BLOCK_ROWS

    @pl.loop(0, 2 * blocks)
    def _(step):
        side, t = step // blocks, step % blocks
        d_edges_s[side, block(t, BLOCK_ROWS, n), :] = contract(
            n, t * BLOCK_ROWS, edges_s.at[1 - side], d_product_s.at[side], pitch=n + 8
        )

    @pl.loop(0, n // STEP_ROWS)
    def _(t):
        here = block(t, STEP_ROWS, n)
        grads = [
            edge_grads(d_edges_s[side, here, :], slopes_s[side, here, :], edges_s[side, here, :])
            for side in range(2)
        ]
        d_pre = jnp.concatenate([*grads, d_pre_s[here, 4 * h :]], axis=1)
        normed = normed_s[here, :]
        d_normed = dot(d_pre, weights[1, :, :width], ((1,), (1,))) * gain[:, :c]
        pulled = norm_vjp(hat_s[here, :], rstd_s[here, :], d_normed)
        up_ref[here, :] = cot_s[here, :].astype(F32) + pulled
        grads_ref[:, :width] = dot(normed, d_pre, ((0,), (0,))).astype(BF16)


def backward_left(n, up_in_ref, weights, vectors, *refs):
    (edges_s, slopes_s, gate_s, _, _, *kept) = kept_parts(refs, 0)
    (p_hat_s, p_rstd_s, branch_s, normed_s, mixed_s) = kept
    d_pre_ref, d_product_ref, grads_ref, d_edge_s = refs[KEPT:]
    c, h = weights.shape[1], edges_s.shape[2]
    width = 4 * h + c
    gain = vector_parts(vectors[0:1, :], c, width)[1]

    @pl.loop(0, n // STEP_ROWS)
    def _(t):
        here = block(t, STEP_ROWS, n)
        d_branch, d_gate, d_product = unmix(
            up_in_ref[here, :],
            gate_s[here, :],
            branch_s[here, :],
            p_hat_s[here, :],
            p_rstd_s[here, :],
            gain[:, c:],
            weights[0, :, width:],
        )
        d_out = dot(mixed_s[here, :], d_branch, ((0,), (0,)))
        d_pre_ref[here, 2 * h :] = d_gate
        d_product_ref[here, :] = d_product
        grads_ref[:, 2 * h + c :] = d_out.astype(BF16)

    one_side(n, 0, d_product_ref, edges_s, slopes_s, d_edge_s, d_pre_ref)
    d_pre = dot(normed_s[...], d_pre_ref[...], ((0,), (0,)))
    grads_ref[:, : 2 * h + c] = d_pre.astype(BF16)


def backward_right(n, d_product_ref, *refs):
    (edges_s, slopes_s, *kept) = kept_parts(refs, 0)
    normed_s = kept[-2]
    d_pre_ref, grads_ref, d_edge_s = refs[KEPT:]
    one_side(n, 1, d_product_ref, edges_s, slopes_s, d_edge_s, d_pre_ref)
    grads_ref[...] = dot(normed_s[...], d_pre_ref[...], ((0,), (0,))).astype(BF16)


def one_side(n, side, x, edges_s, slopes_s, d_edge_s, d_pre_ref):
    h = edges_s.shape[2]

    @pl.loop(0, n // BLOCK_ROWS)
    def _(t):
        d_edge_s[block(t, BLOCK_ROWS, n), :] = contract(
            n, t * BLOCK_ROWS, x, edges_s.at[1 - side], side == 1
        )

    @pl.loop(0, n // STEP_ROWS)
    def _(t):
        here = block(t, STEP_ROWS, n)
        d_pre_ref[here, : 2 * h] = edge_grads(
            d_edge_s[here, :], slopes_s[side, here, :], edges_s[side, here, :]
        )


def own_rows(
    pair_ref, up_ref, d_left_ref, d_right_ref, weights, vectors, hat_ref, rstd_ref, out_ref
):
    cells, c = out_ref.shape
    half = d_right_ref.shape[1]
    place = own_place(pair_ref)
    own = pl.ds(pl.multiple_of(place * cells, cells), cells)
    width = d_left_ref.shape[1] + half
    gain = vector_parts(vectors[0:1, :], c, width)[1]
    d_left, d_right = d_left_ref[own, :], d_right_ref[own, :]
    d_pre = jnp.concatenate([d_left[:, :half], d_right, d_left[:, half:]], axis=1)
    d_normed = dot(d_pre, weights[0, :, :width], ((1,), (1,))) * gain[:, :c]
    pulled = norm_vjp(hat_ref[0, own, :], rstd_ref[0, own, :], d_normed)
    out_ref[...] = (up_ref[own, :] + pulled).astype(BF16)


def exchange(value, axis, size, step):
    return lax.ppermute(value, axis, [(d, d ^ step) for d in range(size)])


def near_rounds(value, groups):
    other = exchange(value, "dp", groups, 1)
    step = 2
    while step < groups // 2:
        value = add_narrow(value, other)
        other = exchange(value, "dp", groups, step)
        step *= 2
    return value, other


def add_narrow(a, b):
    return (a.astype(F32) + b.astype(F32)).astype(BF16)


def prepare(
    index_ref, mask_ref, state_ref, cot_ref, w, w_out, b, gain, shift, b_out, *refs
):
    sent_ref, weights_ref, vectors_ref, mask_s, sems = refs
    cells, c = state_ref.shape
    below, width = cells + TAIL_ROWS, w.shape[2]
    copies = [(mask_ref, mask_s), (state_ref, sent_ref.at[:cells]), (cot_ref, sent_ref.at[below:])]
    copies += [(w, weights_ref.at[:, :, :width]), (w_out, weights_ref.at[:, :, width:])]
    first = 0
    for vector in (b, gain, shift, b_out):
        last = first + vector.shape[1]
        copies.append((vector, vectors_ref.at[:, first:last]))
        first = last
    copies = [pltpu.make_async_copy(*pair, sems.at[k]) for k, pair in enumerate(copies)]
    for copy in copies:
        copy.start()
    copies[0].wait()
    length = jnp.max(jnp.sum(mask_s[...].astype(F32), axis=1, keepdims=True))
    in_length = lax.broadcasted_iota(jnp.int32, (TAIL_ROWS, c), 1) < 64
    place = index_ref[0].astype(F32)
    sent_ref[cells:below, :] = jnp.where(in_length, length, place).astype(BF16)
    for copy in copies[1:]:
        copy.wait()


def pair_up(near_ref, far_ref, state_ref, cot_ref):
    split = state_ref.shape[1]
    for side, ref in enumerate((near_ref, far_ref)):
        state_ref[side] = ref[:split, :]
        cot_ref[side] = ref[split:, :]


def hold(weights_in, vectors_in, weights_out, vectors_out):
    weights_out[...] = weights_in[...]
    vectors_out[...] = vectors_in[...]


def vector_parts(row, c, width):
    ends = [width, width + 2 * c, width + 4 * c, width + 5 * c]
    return [row[:, first:last] for first, last in zip([0] + ends, ends)]


def add_grads(rest, rest_near, left, left_near, right, right_far, proj_ref, out_ref):
    width = proj_ref.shape[2]
    c = out_ref.shape[2]
    half = (width - c) // 2
    total = rest[:, : width + c].astype(F32) + rest_near[:, : width + c].astype(F32)
    proj_ref[1] = total[:, :width]
    out_ref[1] = total[:, width:]
    total = left[...].astype(F32) + left_near[...].astype(F32)
    proj_ref[0, :, :half] = total[:, :half]
    proj_ref[0, :, 2 * half :] = total[:, half : half + c]
    out_ref[0] = total[:, half + c :]
    proj_ref[0, :, half : 2 * half] = right[...].astype(F32) + right_far[...].astype(F32)


def crop_shards(
    groups,
    parts,
    pair_repr,
    pair_mask,
    cotangent,
    proj_weight,
    proj_bias,
    norm_gain,
    norm_shift,
    out_weight,
    out_bias,
):
    _, rows, n, c = pair_repr.shape
    h = out_weight.shape[1]
    width = proj_weight.shape[2]
    cells, pairs = rows * n, n * n
    plane = (pairs + 8, h)
    wide_plane = (n * (n + 8), h)
    kept = [jax.ShapeDtypeStruct((2, 2) + plane, F32)] * 2
    kept += [jax.ShapeDtypeStruct((2,) + plane, F32)] * 6
    kept += [jax.ShapeDtypeStruct((2, pairs, h), BF16)] * 2
    grads = jax.ShapeDtypeStruct((c, width + c), BF16)
    vmem = pl.BlockSpec(memory_space=pltpu.VMEM)
    main = pl.BlockSpec(memory_space=pltpu.HBM)
    params = pltpu.CompilerParams(vmem_limit_bytes=VMEM_BYTES)

    def cost(planes):
        flops = 4 * pairs * width * c
        return pl.CostEstimate(
            flops=flops, bytes_accessed=planes * pairs * c * 4, transcendentals=0
        )

    packed = (
        jax.ShapeDtypeStruct((2, c, width + c), BF16),
        jax.ShapeDtypeStruct((2, width + 5 * c), F32),
    )
    sent, *weights = pl.pallas_call(
        prepare,
        out_shape=(jax.ShapeDtypeStruct((2 * cells + TAIL_ROWS, c), BF16),) + packed,
        in_specs=[pl.BlockSpec(memory_space=pltpu.SMEM)] + [main] * 9,
        out_specs=[vmem] * 3,
        scratch_shapes=[pltpu.VMEM((rows, n), jnp.int32), pltpu.SemaphoreType.DMA((9,))],
        compiler_params=pltpu.CompilerParams(vmem_limit_bytes=PREPARE_BYTES),
        name="prepare",
    )(
        lax.axis_index("dap").astype(jnp.int32)[None],
        pair_mask[0],
        pair_repr.reshape(cells, c),
        cotangent.reshape(cells, c),
        proj_weight,
        out_weight,
        proj_bias,
        norm_gain,
        norm_shift,
        out_bias,
    )
    weights = pl.pallas_call(
        hold,
        out_shape=packed,
        in_specs=[vmem] * 2,
        out_specs=[vmem] * 2,
        compiler_params=params,
        cost_estimate=cost(8),
        name="hold",
    )(*weights)
    beside = exchange(sent, "dap", parts, 1)
    beside, *weights = lax.optimization_barrier((beside, *weights))
    state, cot = pl.pallas_call(
        pair_up,
        out_shape=(
            jax.ShapeDtypeStruct((2, cells + TAIL_ROWS, c), BF16),
            jax.ShapeDtypeStruct((2, cells, c), BF16),
        ),
        in_specs=[vmem] * 2,
        out_specs=[vmem] * 2,
        compiler_params=params,
        name="pair_up",
    )(sent, beside)
    states, cots = [state], [cot]
    half = parts // 2
    jumps = [0, *range(1, half // 2), *reversed(range(half // 2, half))]
    for group in (states, cots):
        group += [exchange(group[0], "dap", parts, 2 * jump) for jump in jumps[1:]]

    held = pl.pallas_call(
        functools.partial(forward, n, jumps),
        out_shape=kept,
        in_specs=[vmem] * (half + 2),
        out_specs=(vmem,) * KEPT,
        scratch_shapes=[pltpu.VMEM((pairs, c), BF16), pltpu.VMEM(wide_plane, F32)],
        compiler_params=params,
        cost_estimate=cost(64),
        name="forward",
    )(*states, *weights)

    double, single = pltpu.VMEM((2,) + plane, F32), pltpu.VMEM(plane, F32)
    up_1, grads_1 = pl.pallas_call(
        functools.partial(backward_second, n, jumps),
        out_shape=(jax.ShapeDtypeStruct((pairs, c), F32), grads),
        in_specs=[vmem] * (3 + half + KEPT),
        out_specs=(vmem, vmem),
        scratch_shapes=[
            pltpu.VMEM((2,) + wide_plane, F32),
            double,
            pltpu.VMEM((pairs, width), BF16),
            pltpu.VMEM((pairs, c), BF16),
        ],
        compiler_params=params,
        cost_estimate=cost(48),
        name="backward_second",
    )(states[0], *cots, *weights, *held)
    far = groups // 2
    others_1 = exchange(grads_1, "dp", groups, far)

    d_left, d_product, grads_left = pl.pallas_call(
        functools.partial(backward_left, n),
        out_shape=(
            jax.ShapeDtypeStruct((pairs, 2 * h + c), BF16),
            jax.ShapeDtypeStruct(plane, F32),
            jax.ShapeDtypeStruct((c, 2 * h + 2 * c), BF16),
        ),
        in_specs=[vmem] * (3 + KEPT),
        out_specs=[vmem] * 3,
        scratch_shapes=[single],
        compiler_params=params,
        cost_estimate=cost(24),
        name="backward_left",
    )(up_1, *weights, *held)
    others_left = exchange(grads_left, "dp", groups, far)

    d_right, grads_right = pl.pallas_call(
        functools.partial(backward_right, n),
        out_shape=(
            jax.ShapeDtypeStruct((pairs, 2 * h), BF16),
            jax.ShapeDtypeStruct((c, 2 * h), BF16),
        ),
        in_specs=[vmem] * (1 + KEPT),
        out_specs=[vmem] * 2,
        scratch_shapes=[single],
        compiler_params=params,
        cost_estimate=cost(24),
        name="backward_right",
    )(d_product, *held)
    pair_grad = pl.pallas_call(
        own_rows,
        out_shape=jax.ShapeDtypeStruct((cells, c), BF16),
        in_specs=[vmem] * 8,
        out_specs=vmem,
        compiler_params=params,
        cost_estimate=cost(8),
        name="own_rows",
    )(states[0], up_1, d_left, d_right, *weights, held[3], held[4])

    rest, rest_near = near_rounds(
        jnp.concatenate([add_narrow(grads_1, others_1), grads_right], axis=1), groups
    )
    right = add_narrow(rest[:, width + c :], rest_near[:, width + c :])
    right_far = exchange(right, "dp", groups, far)
    ends_left = near_rounds(add_narrow(grads_left, others_left), groups)

    proj_total, out_total = pl.pallas_call(
        add_grads,
        out_shape=(
            jax.ShapeDtypeStruct((2, c, width), F32),
            jax.ShapeDtypeStruct((2, h, c), F32),
        ),
        in_specs=[vmem] * 6,
        out_specs=(vmem, vmem),
        compiler_params=params,
        name="add_grads",
    )(rest, rest_near, *ends_left, right, right_far)
    return pair_grad.reshape(pair_repr.shape), proj_total, out_total


def layer_norm(values, gain_vec, shift_vec, norm_axis):
    mean_value = jnp.mean(values, axis=norm_axis, keepdims=True)
    centred = values - mean_value
    variance = jnp.mean(centred * centred, axis=norm_axis, keepdims=True)
    return centred * lax.rsqrt(variance + NORM_EPSILON) * gain_vec + shift_vec


def norm_pullback(values, gain_vec, shift_vec, norm_axis, upstream):
    _, pull_back = jax.vjp(
        lambda inner_value: layer_norm(inner_value, gain_vec, shift_vec, norm_axis), values
    )
    return pull_back(upstream)[0]


def edge_pair(edge_pre, cell_mask):
    left_edge = jax.nn.sigmoid(edge_pre[1]) * edge_pre[0] * cell_mask
    right_edge = jax.nn.sigmoid(edge_pre[3]) * edge_pre[2] * cell_mask
    return jnp.stack([left_edge, right_edge]).astype(jnp.bfloat16)


def edge_pullback(edge_pre, cell_mask, grad_pair):
    sig_left = jax.nn.sigmoid(edge_pre[1])
    sig_right = jax.nn.sigmoid(edge_pre[3])
    grad_left = grad_pair[0].astype(jnp.float32) * cell_mask
    grad_right = grad_pair[1].astype(jnp.float32) * cell_mask
    return jnp.stack(
        [
            grad_left * sig_left,
            grad_left * edge_pre[0] * sig_left * (1.0 - sig_left),
            grad_right * sig_right,
            grad_right * edge_pre[2] * sig_right * (1.0 - sig_right),
        ]
    ).astype(jnp.bfloat16)


def triangle(pair_edges, outgoing):
    if outgoing:
        einsum_form = "cik,cjk->cij"
    else:
        einsum_form = "cki,ckj->cij"
    return jnp.einsum(
        einsum_form, pair_edges[0], pair_edges[1], preferred_element_type=jnp.float32
    ).astype(jnp.bfloat16)


def triangle_pullback(pair_edges, grad_product, outgoing):
    left_edge = pair_edges[0]
    right_edge = pair_edges[1]
    if outgoing:
        grad_left = jnp.einsum(
            "cij,cjk->cik", grad_product, right_edge, preferred_element_type=jnp.float32
        )
        grad_right = jnp.einsum(
            "cij,cik->cjk", grad_product, left_edge, preferred_element_type=jnp.float32
        )
    else:
        grad_left = jnp.einsum(
            "ckj,cij->cki", right_edge, grad_product, preferred_element_type=jnp.float32
        )
        grad_right = jnp.einsum(
            "cki,cij->ckj", left_edge, grad_product, preferred_element_type=jnp.float32
        )
    return jnp.stack([grad_left, grad_right]).astype(jnp.bfloat16)


def update_weights(proj_weight, proj_bias, norm_gain, norm_shift, update, channels, hidden):
    w_edge = proj_weight[update, :, : 4 * hidden].reshape(channels, 4, hidden)
    w_gate = proj_weight[update, :, 4 * hidden :]
    bias_edge = proj_bias[update, : 4 * hidden].reshape(4, hidden, 1, 1)
    bias_gate = proj_bias[update, 4 * hidden :]
    gain_in = norm_gain[update, :channels]
    shift_in = norm_shift[update, :channels]
    gain_out = norm_gain[update, channels:][:, None, None]
    shift_out = norm_shift[update, channels:][:, None, None]
    return (w_edge, w_gate, bias_edge, bias_gate, gain_in, shift_in, gain_out, shift_out)


def shards(
    pair_repr,
    pair_mask,
    cotangent,
    proj_weight,
    proj_bias,
    norm_gain,
    norm_shift,
    out_weight,
    out_bias,
):
    channels = pair_repr.shape[3]
    hidden = out_weight.shape[1]
    pair_state = pair_repr[0]
    cell_mask = pair_mask[0].astype(jnp.float32)
    records = []
    for update in range(2):
        w_edge, w_gate, bias_edge, bias_gate, gain_in, shift_in, gain_out, shift_out = (
            update_weights(proj_weight, proj_bias, norm_gain, norm_shift, update, channels, hidden)
        )
        state_f = pair_state.astype(jnp.float32)
        normed = layer_norm(state_f, gain_in, shift_in, -1).astype(jnp.bfloat16)
        edge_pre = (
            jnp.einsum("rnc,cgh->ghrn", normed, w_edge, preferred_element_type=jnp.float32)
            + bias_edge
        )
        gate_pre = (
            jnp.einsum("rnc,cd->rnd", normed, w_gate, preferred_element_type=jnp.float32)
            + bias_gate
        )
        pair_edges = edge_pair(edge_pre, cell_mask)
        spread = lax.all_to_all(pair_edges, "dap", split_axis=1, concat_axis=2, tiled=True)
        product = lax.all_to_all(
            triangle(spread, update == 0), "dap", split_axis=1, concat_axis=0, tiled=True
        )
        mixed_norm = layer_norm(product.astype(jnp.float32), gain_out, shift_out, 0).astype(
            jnp.bfloat16
        )
        branch = (
            jnp.einsum(
                "hrn,hd->rnd", mixed_norm, out_weight[update], preferred_element_type=jnp.float32
            )
            + out_bias[update]
        )
        records.append(
            (state_f, normed, edge_pre, gate_pre, pair_edges, spread, product, mixed_norm, branch)
        )
        pair_state = (state_f + jax.nn.sigmoid(gate_pre) * branch).astype(jnp.bfloat16)
    upstream = cotangent[0].astype(jnp.float32)
    proj_grads = []
    out_grads = []
    for update in (1, 0):
        state_f, normed, edge_pre, gate_pre, pair_edges, spread, product, mixed_norm, branch = (
            records[update]
        )
        w_edge, w_gate, bias_edge, bias_gate, gain_in, shift_in, gain_out, shift_out = (
            update_weights(proj_weight, proj_bias, norm_gain, norm_shift, update, channels, hidden)
        )
        gate_value = jax.nn.sigmoid(gate_pre)
        grad_branch = (upstream * gate_value).astype(jnp.bfloat16)
        grad_gate = (upstream * branch * gate_value * (1.0 - gate_value)).astype(jnp.bfloat16)
        out_grad = jnp.einsum(
            "hrn,rnd->hd", mixed_norm, grad_branch, preferred_element_type=jnp.float32
        )
        grad_mixed = jnp.einsum(
            "rnd,hd->hrn", grad_branch, out_weight[update], preferred_element_type=jnp.float32
        )
        grad_product = norm_pullback(
            product.astype(jnp.float32), gain_out, shift_out, 0, grad_mixed
        ).astype(jnp.bfloat16)
        column_edges = spread
        column_grad = lax.all_to_all(
            grad_product[None], "dap", split_axis=1, concat_axis=2, tiled=True
        )[0]
        grad_pair = lax.all_to_all(
            triangle_pullback(column_edges, column_grad, update == 0),
            "dap",
            split_axis=2,
            concat_axis=1,
            tiled=True,
        )
        grad_edge = edge_pullback(edge_pre, cell_mask, grad_pair)
        edge_grad = jnp.einsum(
            "rnc,ghrn->cgh", normed, grad_edge, preferred_element_type=jnp.float32
        ).reshape(channels, 4 * hidden)
        gate_grad = jnp.einsum("rnc,rnd->cd", normed, grad_gate, preferred_element_type=jnp.float32)
        grad_normed = jnp.einsum(
            "ghrn,cgh->rnc", grad_edge, w_edge, preferred_element_type=jnp.float32
        )
        grad_normed = grad_normed + jnp.einsum(
            "rnd,cd->rnc", grad_gate, w_gate, preferred_element_type=jnp.float32
        )
        upstream = upstream + norm_pullback(state_f, gain_in, shift_in, -1, grad_normed)
        proj_part = jnp.concatenate([edge_grad, gate_grad], axis=1)
        proj_grads.append(proj_part)
        out_grads.append(out_grad)
    proj_total = jnp.stack(proj_grads[::-1])
    out_total = jnp.stack(out_grads[::-1])
    proj_total, out_total = lax.psum((proj_total, out_total), ("dp", "dap"))
    return (upstream.astype(jnp.bfloat16)[None], proj_total, out_total)


def solution(mesh):
    placed = (
        P("dp", "dap", None, None),
        P("dp", "dap", None),
        P("dp", "dap", None, None),
        P(),
        P(),
        P(),
        P(),
        P(),
        P(),
    )
    groups, parts = mesh.shape["dp"], mesh.shape["dap"]

    def program(*args):
        n, c = args[0].shape[2:]
        rows = n // parts
        fits = 20 * n * n * c * 4 <= CROP_BUDGET
        paired = all(size >= 4 and size & (size - 1) == 0 for size in (groups, parts))
        even = args[7].shape[1] == c == 128 and STEP_ROWS % rows == 0 and n == STEP_ROWS
        body = functools.partial(crop_shards, groups, parts) if fits and even and paired else shards
        return spread_over(body)(*args)

    def spread_over(body):
        return jax.shard_map(
            body,
            mesh=mesh,
            in_specs=placed,
            out_specs=(P("dp", "dap", None, None), P(), P()),
            check_vma=False,
        )

    return program
```
